32 devices in a mesh: groups: 2 (over y), owner: 4 (over z), helper: 2 (over x), sub: 2 (over core).
Axes of the slice: x: 2, y: 2, z: 4, core: 2. Of those that a mesh axis runs over, the one named last changes fastest.
Arguments:
- embeddings: bfloat16 [8192, 1024], P(('groups', 'owner', 'helper', 'sub')), parts along dimension 0, may hold values from -128 to 128
- cluster_id: int32 [8192], P(('groups', 'owner', 'helper', 'sub')), parts along dimension 0, may hold values from 0 to 7, as said below
Outputs:
- dup_count: float32 [8192], P(('groups', 'owner', 'helper', 'sub')), parts along dimension 0
The draws below stay inside these ranges and needn't reach their ends.
There are 2 independent parts, one for each index of `groups`. The reference program is written for one: setup_inputs(seed, part) draws one part's arguments, and reference() takes and returns one part's arrays. A program takes and returns all parts, laid end to end along the dimension named above; each array names one. Nothing has to cross between parts.
Inputs may be any that keep to these rules, and one draw needn't show every extreme that they name: `cluster_id`: among the documents of one device no cluster is named more than 64 times, and on every device one cluster is named exactly 64 times. Among the documents of the 4 devices that share a helper and a sub index no cluster is named more than 256 times, and one cluster is named exactly 256 times.
All inputs are finite; a program needn't handle non-finite values.
Results may differ from the reference program's by a relative error of at most 0.0024.
Values may be sent and summed in bfloat16 or wider, within the bound.
No kernel may reach another device: no remote copies, remote signals or barrier semaphores. Data moves between devices by JAX's collectives and lax.ppermute only.
A program may use at most 64 MiB of HBM per device.

```python
import math
import jax
import jax.numpy as jnp
from jax import lax

D = 1024
CL_OWN = 2
DOC_DEV = 256
NC = 8
MEMB = 256
DOCS = 4096


def cluster_draw(key):
    key = jax.random.fold_in(key, 11)
    owner_count = NC // CL_OWN
    column_count = DOCS // (DOC_DEV * owner_count)
    column_total = owner_count * DOC_DEV
    slot_total = NC * MEMB
    lowest = max(1, MEMB // 4)
    slot_order = jnp.arange(slot_total, dtype=jnp.int32)
    slot_cluster = slot_order // MEMB
    slot_depth = slot_order % MEMB

    def one_column(column_key):
        caps_key, hot_key, score_key, shuffle_key = jax.random.split(column_key, 4)
        cluster_caps = lowest + jax.random.randint(caps_key, (NC,), 0, MEMB - lowest + 1)
        hottest = jax.random.randint(hot_key, (), 0, NC)
        active = slot_depth < cluster_caps[slot_cluster]
        scores = jax.random.randint(score_key, (slot_total,), 0, 32768) * slot_total + slot_order
        scores = jnp.where(active, scores, scores + 2 ** 29)
        scores = jnp.where(slot_cluster == hottest, scores + 2 ** 30, scores)
        chosen = jnp.sort(slot_cluster[jnp.argsort(scores)[:column_total - MEMB]].astype(jnp.int32))
        listing = jnp.concatenate([jnp.full((MEMB,), hottest, jnp.int32), chosen])
        dealt = listing.reshape(DOC_DEV, owner_count).T
        shuffle_keys = jax.random.split(shuffle_key, owner_count)
        return jax.vmap(lambda row, row_key: row[jax.random.permutation(row_key, DOC_DEV)])(dealt, shuffle_keys)
    columns = jax.vmap(one_column)(jax.random.split(key, column_count))
    return jnp.transpose(columns, (1, 0, 2)).reshape(DOCS).astype(jnp.int32)


def draw_cluster_id(key, part):
    return cluster_draw(key)


def draw_embeddings(key, part):
    assigned = cluster_draw(key)
    key = jax.random.fold_in(key, 23)
    center_key, family_key, pick_key, noise_key, level_key = jax.random.split(key, 5)
    families = 64
    centers = jax.random.normal(center_key, (NC, D), jnp.float32)
    family_vectors = jax.random.normal(family_key, (NC, families, D), jnp.float32)
    family_pick = jax.random.randint(pick_key, (DOCS,), 0, families)
    noise_level = jnp.exp(jax.random.uniform(level_key, (DOCS, 1), jnp.float32, math.log(0.2), math.log(0.8)))
    noise = jax.random.normal(noise_key, (DOCS, D), jnp.float32)
    mix_center = 0.55
    mix_family = 0.8
    vectors = mix_center * centers[assigned] + mix_family * family_vectors[assigned, family_pick] + noise_level * noise
    return vectors.astype(jnp.bfloat16)


def setup_inputs(seed: int = 0, part: int = 0) -> dict:
    key_of = jax.random.split(jax.random.key(seed), 3)
    part_splits = jax.random.split(jax.random.fold_in(key_of[2], part), 3)
    embeddings = draw_embeddings(jax.random.fold_in(jax.random.fold_in(key_of[2], part), 71), part)
    cluster_id = draw_cluster_id(jax.random.fold_in(jax.random.fold_in(key_of[2], part), 71), part)
    return {"embeddings": embeddings, "cluster_id": cluster_id}


epsilon = 1e-06
threshold = 0.8
sharpness = 0.05

def normalize(embeddings):
    widened = embeddings.astype(jnp.float32)
    factor = lax.rsqrt(lax.optimization_barrier(jnp.mean(widened * widened, axis=-1, keepdims=True)) + epsilon) * D ** (-0.5)
    return (widened * factor).astype(jnp.bfloat16)

def reference(embeddings, cluster_id):
    unit_rows = normalize(embeddings).astype(jnp.float32)
    positions = jnp.arange(DOCS, dtype=jnp.int32)

    def block_counts(block_index):
        first_row = (block_index * DOC_DEV).astype(jnp.int32)
        row_block = lax.dynamic_slice_in_dim(unit_rows, first_row, DOC_DEV, 0)
        row_ids = lax.dynamic_slice_in_dim(cluster_id, first_row, DOC_DEV, 0)
        row_pos = first_row + jnp.arange(DOC_DEV, dtype=jnp.int32)
        scores = jnp.dot(row_block, unit_rows.T, precision=lax.Precision.HIGHEST)
        keep_mask = (row_ids[:, None] == cluster_id[None, :]) & (row_pos[:, None] != positions[None, :])
        weights = jax.nn.sigmoid((scores - threshold) / sharpness)
        return lax.optimization_barrier(jnp.sum(jnp.where(keep_mask, weights, jnp.zeros_like(weights)), axis=1))
    totals = lax.map(block_counts, jnp.arange(DOCS // DOC_DEV, dtype=jnp.int32))
    return totals.reshape(DOCS)
```

```python
import functools
import math

import jax
import jax.numpy as jnp
from jax import lax
from jax.experimental import pallas as pl
from jax.experimental.pallas import tpu as pltpu
from jax.sharding import PartitionSpec as P

CL_OWN = 2

epsilon = 1e-06
threshold = 0.8
sharpness = 0.05

EMPTY = 4.0
TILE = 256
VMEM = pl.BlockSpec(memory_space=pltpu.VMEM)
ANY = pl.BlockSpec(memory_space=pl.ANY)


def route_kernel(clusters, capacity, by_chip, rows_ref, ids_ref, *out_refs):
    piece_refs, slot_ref = out_refs[:-1], out_refs[-1]
    doc_count, feature_count = rows_ref.shape
    widened = rows_ref[...].astype(jnp.float32)
    factor = lax.rsqrt(
        jnp.mean(widened * widened, axis=-1, keepdims=True) + epsilon
    ) * feature_count ** (-0.5)
    unit_rows = (widened * factor).astype(jnp.bfloat16)

    ids = ids_ref[...]
    member = lax.broadcasted_iota(jnp.int32, (clusters, doc_count), 0) == ids
    earlier = lax.broadcasted_iota(jnp.int32, (doc_count, doc_count), 0) < (
        lax.broadcasted_iota(jnp.int32, (doc_count, doc_count), 1)
    )
    ahead = jnp.dot(
        member.astype(jnp.bfloat16), earlier.astype(jnp.bfloat16), preferred_element_type=jnp.float32
    )
    rank = jnp.sum(jnp.where(member, ahead, 0.0), axis=0, keepdims=True).astype(jnp.int32)
    if by_chip:
        ids = ids ^ (lax.axis_index("owner") * CL_OWN + lax.axis_index("helper"))
    slot = ids * capacity + rank
    slot_ref[...] = slot

    slots = clusters * capacity
    dispatch = lax.broadcasted_iota(jnp.int32, (slots, doc_count), 0) == slot
    filled = jnp.sum(dispatch.astype(jnp.float32), axis=1, keepdims=True) > 0
    dispatch = dispatch.astype(jnp.bfloat16)
    piece_rows = slots // len(piece_refs)
    for first in range(0, feature_count, TILE):
        columns = slice(first, first + TILE)
        laid = jnp.dot(dispatch, unit_rows[:, columns], preferred_element_type=jnp.float32)
        if first == 0:
            lane = lax.broadcasted_iota(jnp.int32, (slots, TILE), 1)
            laid = jnp.where(filled | (lane > 0), laid, EMPTY)
        laid = laid.astype(jnp.bfloat16)
        for k, piece in enumerate(piece_refs):
            piece[:, columns] = laid[k * piece_rows : (k + 1) * piece_rows]


def route(embeddings, cluster_id, clusters, capacity, pieces, by_chip):
    doc_count, feature_count = embeddings.shape
    piece = jax.ShapeDtypeStruct((clusters * capacity // pieces, feature_count), jnp.bfloat16)
    *laid, slot = pl.pallas_call(
        functools.partial(route_kernel, clusters, capacity, by_chip),
        out_shape=[piece] * pieces + [jax.ShapeDtypeStruct((1, doc_count), jnp.int32)],
        in_specs=[VMEM, VMEM],
        out_specs=[VMEM] * (pieces + 1),
        compiler_params=pltpu.CompilerParams(vmem_limit_bytes=32 * 2**20),
        name="route",
    )(embeddings, cluster_id.reshape(1, doc_count))
    return laid, slot


def count_kernel(own_pieces, *refs):
    rows, sem = refs[-2:]
    count_refs = refs[-2 - own_pieces : -2]
    piece_refs = refs[: -2 - own_pieces]
    copies, first = [], 0
    for k, piece in enumerate(piece_refs):
        copies.append(
            pltpu.make_async_copy(piece, rows.at[pl.ds(first, piece.shape[0])], sem.at[k])
        )
        first += piece.shape[0]
    for copy in copies:
        copy.start()
    for copy in copies:
        copy.wait()
    own_count = sum(piece.shape[0] for piece in piece_refs[:own_pieces])
    own = rows[:own_count]
    slope = -math.log2(math.e) / sharpness
    total = jnp.zeros((1, own_count), jnp.float32)
    for first in range(0, first, TILE):
        other = rows[first : first + TILE]
        scores = lax.dot_general(
            other, own, (((1,), (1,)), ((), ())), preferred_element_type=jnp.float32
        )
        weights = 1.0 / (1.0 + jnp.exp2(scores * slope - threshold * slope))
        keep = other[:, :1].astype(jnp.float32) < 0.5 * EMPTY
        if first < own_count:
            keep = keep & (
                lax.broadcasted_iota(jnp.int32, scores.shape, 0) + first
                != lax.broadcasted_iota(jnp.int32, scores.shape, 1)
            )
        total = total + jnp.sum(jnp.where(keep, weights, 0.0), axis=0, keepdims=True)
    first = 0
    for count in count_refs:
        count[...] = total[:, first : first + count.shape[1]]
        first += count.shape[1]


def soft_counts(own, others):
    pieces = own + others
    total = sum(piece.shape[0] for piece in pieces)
    return pl.pallas_call(
        functools.partial(count_kernel, len(own)),
        out_shape=[jax.ShapeDtypeStruct((1, piece.shape[0]), jnp.float32) for piece in own],
        in_specs=[ANY] * len(pieces),
        out_specs=[VMEM] * len(own),
        scratch_shapes=[
            pltpu.VMEM((total, own[0].shape[1]), jnp.bfloat16),
            pltpu.SemaphoreType.DMA((len(pieces),)),
        ],
        compiler_params=pltpu.CompilerParams(vmem_limit_bytes=32 * 2**20),
        name="count",
    )(*pieces)


def select_kernel(capacity, *refs):
    *count_refs, slot_ref, out_ref = refs
    counts = jnp.concatenate([count[...] for count in count_refs], axis=0)
    slot = slot_ref[...]
    doc_count = slot.shape[1]
    block = slot // capacity
    rank = slot - block * capacity
    hot = (lax.broadcasted_iota(jnp.int32, (capacity, doc_count), 0) == rank).astype(jnp.float32)
    by_block = jnp.dot(
        counts, hot, precision=lax.Precision.HIGHEST, preferred_element_type=jnp.float32
    )
    chosen = lax.broadcasted_iota(jnp.int32, by_block.shape, 0) == block
    out_ref[...] = jnp.sum(jnp.where(chosen, by_block, 0.0), axis=0, keepdims=True)


def select(counts, slot, capacity):
    return pl.pallas_call(
        functools.partial(select_kernel, capacity),
        out_shape=jax.ShapeDtypeStruct(slot.shape, jnp.float32),
        in_specs=[VMEM] * (len(counts) + 1),
        out_specs=VMEM,
        name="select",
    )(*counts, slot)[0]


def swap_cores(x):
    cores = lax.axis_size("sub")
    return lax.ppermute(x, "sub", [(i, i ^ 1) for i in range(cores)])


def body_by_chip(embeddings, cluster_id):
    doc_count = embeddings.shape[0]
    clusters = CL_OWN * lax.axis_size("owner")
    capacity = 2 * doc_count // clusters

    def across(x, k):
        if k == 0:
            return x
        return lax.ppermute(x, ("owner", "helper"), [(i, i ^ k) for i in range(clusters)])

    pieces, slot = route(embeddings, cluster_id, clusters, capacity, clusters, True)
    order = list(range(clusters - 1, -1, -1))
    own = {k: across(pieces[k], k) for k in order}
    others = {k: swap_cores(own[k]) for k in own}
    counts = soft_counts([own[k] for k in range(clusters)], [others[k] for k in range(clusters)])
    back = [across(counts[k], k) for k in range(clusters)]
    return select(back, slot, capacity)


def body_by_owner(embeddings, cluster_id):
    doc_count, feature_count = embeddings.shape
    owners, helpers = lax.axis_size("owner"), lax.axis_size("helper")
    clusters = CL_OWN * owners
    capacity = 2 * doc_count // clusters
    mine = lax.axis_index("helper") % CL_OWN

    def partner(x):
        return lax.ppermute(x, "helper", [(i, i ^ 1) for i in range(helpers)])

    (outgoing,), slot = route(embeddings, cluster_id, clusters, capacity, 1, False)
    outgoing = outgoing.reshape(owners, CL_OWN, capacity, feature_count)
    arrived = lax.all_to_all(outgoing, "owner", split_axis=0, concat_axis=0, tiled=True)
    kept = lax.dynamic_index_in_dim(arrived, mine, 1, keepdims=False)
    given = partner(lax.dynamic_index_in_dim(arrived, 1 - mine, 1, keepdims=False))
    own = jnp.stack([kept, given]).reshape(CL_OWN * owners * capacity, feature_count)
    others = [swap_cores(own)]
    for step in range(CL_OWN, helpers, CL_OWN):
        turn = [(i, (i + step) % helpers) for i in range(helpers)]
        others += [lax.ppermute(x, "helper", turn) for x in (own, others[0])]
    (counts,) = soft_counts([own], others)
    counts = counts.reshape(CL_OWN, owners, capacity)
    kept, given = counts[0], partner(counts[1])
    counts = jnp.where(mine == 0, jnp.stack([kept, given], 1), jnp.stack([given, kept], 1))
    back = lax.all_to_all(counts, "owner", split_axis=0, concat_axis=0, tiled=True)
    return select([back.reshape(clusters, capacity)], slot, capacity)


def solution(mesh):
    in_specs = (
        P(("groups", "owner", "helper", "sub"), None),
        P(("groups", "owner", "helper", "sub")),
    )
    out_specs = P(("groups", "owner", "helper", "sub"))
    body = body_by_chip if mesh.shape["helper"] == CL_OWN else body_by_owner
    return jax.shard_map(body, mesh=mesh, in_specs=in_specs, out_specs=out_specs, check_vma=False)
```

```python
import functools
import math

import jax
import jax.numpy as jnp
from jax import lax
from jax.experimental import pallas as pl
from jax.experimental.pallas import tpu as pltpu
from jax.sharding import PartitionSpec as P

CL_OWN = 2

epsilon = 1e-06
threshold = 0.8
sharpness = 0.05

EMPTY = 4.0
TILE = 256
VMEM = pl.BlockSpec(memory_space=pltpu.VMEM)


def chip_index():
    return lax.axis_index("owner") * CL_OWN + lax.axis_index("helper")


def route_kernel(clusters, capacity, by_chip, rows_ref, ids_ref, *out_refs):
    piece_refs, slot_ref = out_refs[:-1], out_refs[-1]
    doc_count, feature_count = rows_ref.shape
    widened = rows_ref[...].astype(jnp.float32)
    factor = lax.rsqrt(
        jnp.mean(widened * widened, axis=-1, keepdims=True) + epsilon
    ) * feature_count ** (-0.5)
    unit_rows = (widened * factor).astype(jnp.bfloat16)

    ids = ids_ref[...]
    member = lax.broadcasted_iota(jnp.int32, (clusters, doc_count), 0) == ids
    earlier = lax.broadcasted_iota(jnp.int32, (doc_count, doc_count), 0) < (
        lax.broadcasted_iota(jnp.int32, (doc_count, doc_count), 1)
    )
    ahead = jnp.dot(
        member.astype(jnp.bfloat16), earlier.astype(jnp.bfloat16), preferred_element_type=jnp.float32
    )
    rank = jnp.sum(jnp.where(member, ahead, 0.0), axis=0, keepdims=True).astype(jnp.int32)
    slot_ref[...] = ids * capacity + rank
    if by_chip:
        ids = ids ^ chip_index()
    slot = ids * capacity + rank

    slots = clusters * capacity
    dispatch = lax.broadcasted_iota(jnp.int32, (slots, doc_count), 0) == slot
    filled = jnp.sum(dispatch.astype(jnp.float32), axis=1, keepdims=True) > 0
    dispatch = dispatch.astype(jnp.bfloat16)
    piece_rows = slots // len(piece_refs)
    for first in range(0, feature_count, TILE):
        columns = slice(first, first + TILE)
        laid = jnp.dot(dispatch, unit_rows[:, columns], preferred_element_type=jnp.float32)
        if first == 0:
            lane = lax.broadcasted_iota(jnp.int32, (slots, TILE), 1)
            laid = jnp.where(filled | (lane > 0), laid, EMPTY)
        laid = laid.astype(jnp.bfloat16)
        for k, piece in enumerate(piece_refs):
            piece[:, columns] = laid[k * piece_rows : (k + 1) * piece_rows]


def route(embeddings, cluster_id, clusters, capacity, pieces, by_chip):
    doc_count, feature_count = embeddings.shape
    piece = jax.ShapeDtypeStruct((clusters * capacity // pieces, feature_count), jnp.bfloat16)
    *laid, slot = pl.pallas_call(
        functools.partial(route_kernel, clusters, capacity, by_chip),
        out_shape=[piece] * pieces + [jax.ShapeDtypeStruct((1, doc_count), jnp.int32)],
        in_specs=[VMEM, VMEM],
        out_specs=[VMEM] * (pieces + 1),
        compiler_params=pltpu.CompilerParams(vmem_limit_bytes=32 * 2**20),
        name="route",
    )(embeddings, cluster_id.reshape(1, doc_count))
    return laid, slot


def count_kernel(distances, *refs):
    *piece_refs, count_ref = refs
    pieces = [piece[...] for piece in piece_refs]
    piece_rows = pieces[0].shape[0]
    own = jnp.concatenate(pieces[: len(distances)], axis=0)
    own_count = own.shape[0]
    slope = -math.log2(math.e) / sharpness
    total = jnp.zeros((1, own_count), jnp.float32)
    per_tile = max(1, TILE // piece_rows)
    for k in range(0, len(pieces), per_tile):
        other = jnp.concatenate(pieces[k : k + per_tile], axis=0)
        scores = lax.dot_general(
            other, own, (((1,), (1,)), ((), ())), preferred_element_type=jnp.float32
        )
        weights = 1.0 / (1.0 + jnp.exp2(scores * slope - threshold * slope))
        keep = other[:, :1].astype(jnp.float32) < 0.5 * EMPTY
        if k < len(distances):
            keep = keep & (
                lax.broadcasted_iota(jnp.int32, scores.shape, 0) + k * piece_rows
                != lax.broadcasted_iota(jnp.int32, scores.shape, 1)
            )
        total = total + jnp.sum(jnp.where(keep, weights, 0.0), axis=0, keepdims=True)
    for k, distance in enumerate(distances):
        place = chip_index() ^ distance if len(distances) > 1 else 0
        count_ref[pl.ds(place, 1), 0, :] = total[:, k * piece_rows : (k + 1) * piece_rows]


def soft_counts(own, others, distances):
    pieces = own + others
    return pl.pallas_call(
        functools.partial(count_kernel, distances),
        out_shape=jax.ShapeDtypeStruct((len(own), 1, own[0].shape[0]), jnp.float32),
        in_specs=[VMEM] * len(pieces),
        out_specs=VMEM,
        compiler_params=pltpu.CompilerParams(vmem_limit_bytes=32 * 2**20),
        name="count",
    )(*pieces)


def select_kernel(capacity, counts_ref, slot_ref, out_ref):
    counts = counts_ref[:, 0, :]
    slot = slot_ref[...]
    doc_count = slot.shape[1]
    block = slot // capacity
    rank = slot - block * capacity
    hot = (lax.broadcasted_iota(jnp.int32, (capacity, doc_count), 0) == rank).astype(jnp.float32)
    by_block = jnp.dot(
        counts, hot, precision=lax.Precision.HIGHEST, preferred_element_type=jnp.float32
    )
    chosen = lax.broadcasted_iota(jnp.int32, by_block.shape, 0) == block
    out_ref[...] = jnp.sum(jnp.where(chosen, by_block, 0.0), axis=0, keepdims=True)


def select(counts, slot, capacity):
    return pl.pallas_call(
        functools.partial(select_kernel, capacity),
        out_shape=jax.ShapeDtypeStruct(slot.shape, jnp.float32),
        in_specs=[VMEM, VMEM],
        out_specs=VMEM,
        compiler_params=pltpu.CompilerParams(vmem_limit_bytes=8 * 2**20),
        name="select",
    )(counts, slot)[0]


def swap_cores(x):
    cores = lax.axis_size("sub")
    return lax.ppermute(x, "sub", [(i, i ^ 1) for i in range(cores)])


def body_by_chip(embeddings, cluster_id):
    doc_count = embeddings.shape[0]
    clusters = CL_OWN * lax.axis_size("owner")
    capacity = 2 * doc_count // clusters

    def across(x, k):
        if k == 0:
            return x
        return lax.ppermute(x, ("owner", "helper"), [(i, i ^ k) for i in range(clusters)])

    pieces, slot = route(embeddings, cluster_id, clusters, capacity, clusters, True)
    distances = sorted(range(clusters), key=lambda k: (-(k // CL_OWN).bit_length(), k))
    own = [across(pieces[k], k) for k in distances]
    others = [swap_cores(piece) for piece in own]
    counts = soft_counts(own, others, distances)
    back = lax.all_to_all(counts, ("owner", "helper"), split_axis=0, concat_axis=0, tiled=True)
    return select(back, slot, capacity)


def body_by_owner(embeddings, cluster_id):
    doc_count, feature_count = embeddings.shape
    owners, helpers = lax.axis_size("owner"), lax.axis_size("helper")
    clusters = CL_OWN * owners
    capacity = 2 * doc_count // clusters
    mine = lax.axis_index("helper") % CL_OWN

    def partner(x):
        return lax.ppermute(x, "helper", [(i, i ^ 1) for i in range(helpers)])

    (outgoing,), slot = route(embeddings, cluster_id, clusters, capacity, 1, False)
    outgoing = outgoing.reshape(owners, CL_OWN, capacity, feature_count)
    arrived = lax.all_to_all(outgoing, "owner", split_axis=0, concat_axis=0, tiled=True)
    kept = lax.dynamic_index_in_dim(arrived, mine, 1, keepdims=False)
    given = partner(lax.dynamic_index_in_dim(arrived, 1 - mine, 1, keepdims=False))
    own = jnp.stack([kept, given]).reshape(CL_OWN * owners * capacity, feature_count)
    others = [swap_cores(own)]
    for step in range(CL_OWN, helpers, CL_OWN):
        turn = [(i, (i + step) % helpers) for i in range(helpers)]
        others += [lax.ppermute(x, "helper", turn) for x in (own, others[0])]
    counts = soft_counts([own], others, [0])
    counts = counts.reshape(CL_OWN, owners, capacity)
    kept, given = counts[0], partner(counts[1])
    counts = jnp.where(mine == 0, jnp.stack([kept, given], 1), jnp.stack([given, kept], 1))
    back = lax.all_to_all(counts, "owner", split_axis=0, concat_axis=0, tiled=True)
    return select(back.reshape(clusters, 1, capacity), slot, capacity)


def solution(mesh):
    in_specs = (
        P(("groups", "owner", "helper", "sub"), None),
        P(("groups", "owner", "helper", "sub")),
    )
    out_specs = P(("groups", "owner", "helper", "sub"))
    body = body_by_chip if mesh.shape["helper"] == CL_OWN else body_by_owner
    return jax.shard_map(body, mesh=mesh, in_specs=in_specs, out_specs=out_specs, check_vma=False)
```

```python
import functools
import math

import jax
import jax.numpy as jnp
from jax import lax
from jax.experimental import pallas as pl
from jax.experimental.pallas import tpu as pltpu
from jax.sharding import PartitionSpec as P

CL_OWN = 2

epsilon = 1e-06
threshold = 0.8
sharpness = 0.05

EMPTY = 4.0
TILE = 256
VMEM = pl.BlockSpec(memory_space=pltpu.VMEM)


def chip_index():
    return lax.axis_index("owner") * CL_OWN + lax.axis_index("helper")


def unit_rows_of(rows_ref):
    widened = rows_ref[...].astype(jnp.float32)
    factor = lax.rsqrt(
        jnp.mean(widened * widened, axis=-1, keepdims=True) + epsilon
    ) * rows_ref.shape[1] ** (-0.5)
    return (widened * factor).astype(jnp.bfloat16)


def slots_of(ids, clusters, capacity):
    doc_count = ids.shape[1]
    member = lax.broadcasted_iota(jnp.int32, (clusters, doc_count), 0) == ids
    earlier = lax.broadcasted_iota(jnp.int32, (doc_count, doc_count), 0) < (
        lax.broadcasted_iota(jnp.int32, (doc_count, doc_count), 1)
    )
    ahead = jnp.dot(
        member.astype(jnp.bfloat16), earlier.astype(jnp.bfloat16), preferred_element_type=jnp.float32
    )
    rank = jnp.sum(jnp.where(member, ahead, 0.0), axis=0, keepdims=True).astype(jnp.int32)
    return ids * capacity + rank


def lay(unit_rows, slot, slots):
    doc_count, feature_count = unit_rows.shape
    dispatch = lax.broadcasted_iota(jnp.int32, (slots, doc_count), 0) == slot
    filled = jnp.sum(dispatch.astype(jnp.float32), axis=1, keepdims=True) > 0
    dispatch = dispatch.astype(jnp.bfloat16)
    for column in range(0, feature_count, TILE):
        columns = slice(column, column + TILE)
        laid = jnp.dot(dispatch, unit_rows[:, columns], preferred_element_type=jnp.float32)
        if column == 0:
            lane = lax.broadcasted_iota(jnp.int32, (slots, TILE), 1)
            laid = jnp.where(filled | (lane > 0), laid, EMPTY)
        yield columns, laid.astype(jnp.bfloat16)


def route_chip_kernel(clusters, capacity, *refs):
    own_rows, other_rows, own_ids, other_ids, *piece_refs, slot_ref = refs
    core = lax.axis_index("sub")
    for part, (rows_ref, ids_ref) in enumerate(((own_rows, own_ids), (other_rows, other_ids))):
        slot = slots_of(ids_ref[...], clusters, capacity)
        if part == 0:
            slot_ref[...] = slot
        ids = ids_ref[...]
        rank = slot - ids * capacity
        distance = ids ^ chip_index()
        here = jnp.where((distance & 1) == core, (distance >> 1) * capacity + rank, -1)
        rows = slice(part * capacity, (part + 1) * capacity)
        for columns, laid in lay(unit_rows_of(rows_ref), here, len(piece_refs) * capacity):
            for p, piece in enumerate(piece_refs):
                piece[rows, columns] = laid[p * capacity : (p + 1) * capacity]


def route_kernel(clusters, capacity, rows_ref, ids_ref, piece_ref, slot_ref):
    slot = slots_of(ids_ref[...], clusters, capacity)
    slot_ref[...] = slot
    for columns, laid in lay(unit_rows_of(rows_ref), slot, piece_ref.shape[0]):
        piece_ref[:, columns] = laid


def call_kernel(name, kernel, out_shape, *args, limit=32):
    return pl.pallas_call(
        kernel,
        out_shape=out_shape,
        in_specs=[VMEM] * len(args),
        out_specs=jax.tree.map(lambda _: VMEM, out_shape),
        compiler_params=pltpu.CompilerParams(vmem_limit_bytes=limit * 2**20),
        name=name,
    )(*args)


def count_kernel(starts, places, *refs):
    *piece_refs, count_ref = refs
    rows = jnp.concatenate([piece[...] for piece in piece_refs], axis=0)
    size = count_ref.shape[2]
    own = jnp.concatenate([rows[start : start + size] for start in starts], axis=0)
    column = lax.broadcasted_iota(jnp.int32, (1, own.shape[0]), 1)
    itself = column
    for k, start in enumerate(starts):
        itself = jnp.where(column // size == k, column + (start - k * size), itself)
    slope = -math.log2(math.e) / sharpness
    total = jnp.zeros((1, own.shape[0]), jnp.float32)
    for first in range(0, rows.shape[0], TILE):
        other = rows[first : first + TILE]
        scores = lax.dot_general(
            other, own, (((1,), (1,)), ((), ())), preferred_element_type=jnp.float32
        )
        weights = 1.0 / (1.0 + jnp.exp2(scores * slope - threshold * slope))
        live = other[:, :1].astype(jnp.float32) < 0.5 * EMPTY
        keep = live & (lax.broadcasted_iota(jnp.int32, scores.shape, 0) + first != itself)
        total = total + jnp.sum(jnp.where(keep, weights, 0.0), axis=0, keepdims=True)
    for k, place in enumerate(places()):
        count_ref[pl.ds(place, 1), 0, :] = total[:, k * size : (k + 1) * size]


def soft_counts(pieces, size, starts, places):
    out_shape = jax.ShapeDtypeStruct((len(starts), 1, size), jnp.float32)
    return call_kernel("count", functools.partial(count_kernel, starts, places), out_shape, *pieces)


def select_kernel(capacity, counts_ref, slot_ref, out_ref):
    counts = counts_ref[:, 0, :]
    slot = slot_ref[...]
    doc_count = slot.shape[1]
    block = slot // capacity
    rank = slot - block * capacity
    hot = (lax.broadcasted_iota(jnp.int32, (capacity, doc_count), 0) == rank).astype(jnp.float32)
    by_block = jnp.dot(
        counts, hot, precision=lax.Precision.HIGHEST, preferred_element_type=jnp.float32
    )
    chosen = lax.broadcasted_iota(jnp.int32, by_block.shape, 0) == block
    out_ref[...] = jnp.sum(jnp.where(chosen, by_block, 0.0), axis=0, keepdims=True)


def select(counts, slot, capacity):
    out_shape = jax.ShapeDtypeStruct(slot.shape, jnp.float32)
    kernel = functools.partial(select_kernel, capacity)
    return call_kernel("select", kernel, out_shape, counts, slot, limit=8)[0]


def swap_cores(x):
    cores = lax.axis_size("sub")
    return lax.ppermute(x, "sub", [(i, i ^ 1) for i in range(cores)])


def body_by_chip(embeddings, cluster_id):
    doc_count, feature_count = embeddings.shape
    clusters = CL_OWN * lax.axis_size("owner")
    capacity = 2 * doc_count // clusters
    cores = lax.axis_size("sub")
    steps = clusters // cores

    def across(x, p):
        pairs = [
            (chip * cores + core, (chip ^ (p * cores + core)) * cores + core)
            for chip in range(clusters)
            for core in range(cores)
        ]
        return lax.ppermute(x, ("owner", "helper", "sub"), pairs)

    ids = cluster_id.reshape(1, doc_count)
    piece = jax.ShapeDtypeStruct((cores * capacity, feature_count), jnp.bfloat16)
    *pieces, slot = call_kernel(
        "route",
        functools.partial(route_chip_kernel, clusters, capacity),
        [piece] * steps + [jax.ShapeDtypeStruct((1, doc_count), jnp.int32)],
        embeddings,
        swap_cores(embeddings),
        ids,
        swap_cores(ids),
    )
    order = [steps // 2, *range(steps // 2), *range(steps // 2 + 1, steps)]
    arrived = [across(pieces[p], p) for p in order]
    swapped = [swap_cores(x) for x in arrived]

    def places():
        chip, core = chip_index(), lax.axis_index("sub")
        return [chip ^ (p * cores + core) for p in order] + [
            chip ^ (p * cores + 1 - core) for p in order
        ]

    span = cores * capacity
    starts = [k * span for k in range(steps)] + [k * span + capacity for k in range(steps, 2 * steps)]
    counts = soft_counts(arrived + swapped, capacity, starts, places)
    back = lax.all_to_all(counts, ("owner", "helper"), split_axis=0, concat_axis=0, tiled=True)
    return select(back, slot, capacity)


def body_by_owner(embeddings, cluster_id):
    doc_count, feature_count = embeddings.shape
    owners, helpers = lax.axis_size("owner"), lax.axis_size("helper")
    clusters = CL_OWN * owners
    capacity = 2 * doc_count // clusters
    mine = lax.axis_index("helper") % CL_OWN

    def partner(x):
        return lax.ppermute(x, "helper", [(i, i ^ 1) for i in range(helpers)])

    outgoing, slot = call_kernel(
        "route",
        functools.partial(route_kernel, clusters, capacity),
        [
            jax.ShapeDtypeStruct((clusters * capacity, feature_count), jnp.bfloat16),
            jax.ShapeDtypeStruct((1, doc_count), jnp.int32),
        ],
        embeddings,
        cluster_id.reshape(1, doc_count),
    )
    outgoing = outgoing.reshape(owners, CL_OWN, capacity, feature_count)
    arrived = lax.all_to_all(outgoing, "owner", split_axis=0, concat_axis=0, tiled=True)
    kept = lax.dynamic_index_in_dim(arrived, mine, 1, keepdims=False)
    given = partner(lax.dynamic_index_in_dim(arrived, 1 - mine, 1, keepdims=False))
    own = jnp.stack([kept, given]).reshape(CL_OWN * owners * capacity, feature_count)
    others = [swap_cores(own)]
    for step in range(CL_OWN, helpers, CL_OWN):
        turn = [(i, (i + step) % helpers) for i in range(helpers)]
        others += [lax.ppermute(x, "helper", turn) for x in (own, others[0])]
    counts = soft_counts([own, *others], own.shape[0], [0], lambda: [0])
    counts = counts.reshape(CL_OWN, owners, capacity)
    kept, given = counts[0], partner(counts[1])
    counts = jnp.where(mine == 0, jnp.stack([kept, given], 1), jnp.stack([given, kept], 1))
    back = lax.all_to_all(counts, "owner", split_axis=0, concat_axis=0, tiled=True)
    return select(back.reshape(clusters, 1, capacity), slot, capacity)


def solution(mesh):
    in_specs = (
        P(("groups", "owner", "helper", "sub"), None),
        P(("groups", "owner", "helper", "sub")),
    )
    out_specs = P(("groups", "owner", "helper", "sub"))
    body = body_by_chip if mesh.shape["helper"] == CL_OWN else body_by_owner
    return jax.shard_map(body, mesh=mesh, in_specs=in_specs, out_specs=out_specs, check_vma=False)
```

```python
import functools
import math

import jax
import jax.numpy as jnp
from jax import lax
from jax.experimental import pallas as pl
from jax.experimental.pallas import tpu as pltpu
from jax.sharding import PartitionSpec as P

CL_OWN = 2

epsilon = 1e-06
threshold = 0.8
sharpness = 0.05

EMPTY = 4.0
TILE = 256
VMEM = pl.BlockSpec(memory_space=pltpu.VMEM)


def chip_index():
    return lax.axis_index("owner") * CL_OWN + lax.axis_index("helper")


def slots_of(ids, clusters, capacity):
    doc_count = ids.shape[1]
    member = lax.broadcasted_iota(jnp.int32, (clusters, doc_count), 0) == ids
    earlier = lax.broadcasted_iota(jnp.int32, (doc_count, doc_count), 0) < (
        lax.broadcasted_iota(jnp.int32, (doc_count, doc_count), 1)
    )
    ahead = jnp.dot(
        member.astype(jnp.bfloat16), earlier.astype(jnp.bfloat16), preferred_element_type=jnp.float32
    )
    rank = jnp.sum(jnp.where(member, ahead, 0.0), axis=0, keepdims=True).astype(jnp.int32)
    return ids * capacity + rank


def lay(rows_ref, slot, slots):
    doc_count, feature_count = rows_ref.shape
    dispatch = lax.broadcasted_iota(jnp.int32, (slots, doc_count), 0) == slot
    filled = jnp.sum(dispatch.astype(jnp.float32), axis=1, keepdims=True) > 0
    laid = jnp.dot(
        dispatch.astype(jnp.bfloat16), rows_ref[...], preferred_element_type=jnp.float32
    )
    factor = lax.rsqrt(
        jnp.mean(laid * laid, axis=-1, keepdims=True) + epsilon
    ) * feature_count ** (-0.5)
    lane = lax.broadcasted_iota(jnp.int32, laid.shape, 1)
    return jnp.where(filled | (lane > 0), laid * factor, EMPTY).astype(jnp.bfloat16)


def slots_of_steps(slot, capacity, steps):
    cores = lax.axis_size("sub")
    by_distance = slot ^ (chip_index() * capacity)
    distance = by_distance // capacity
    rank = by_distance - distance * capacity
    step = jnp.full_like(slot, -1)
    for place, p in enumerate(steps):
        step = jnp.where(distance == p * cores + lax.axis_index("sub"), place, step)
    return jnp.where(step < 0, -1, step * capacity + rank)


def route_own_kernel(clusters, capacity, rows_ref, ids_ref, laid_ref, slot_ref):
    steps = range(laid_ref.shape[0] // capacity)
    slot = slots_of(ids_ref[...], clusters, capacity)
    slot_ref[...] = slot
    laid_ref[...] = lay(rows_ref, slots_of_steps(slot, capacity, steps), laid_ref.shape[0])


def route_other_kernel(clusters, capacity, rows_ref, ids_ref, laid_ref, *piece_refs):
    slot = slots_of(ids_ref[...], clusters, capacity)
    slot = slots_of_steps(slot, capacity, range(len(piece_refs)))
    laid = lay(rows_ref, slot, laid_ref.shape[0])
    for p, piece in enumerate(piece_refs):
        rows = slice(p * capacity, (p + 1) * capacity)
        piece[:capacity] = laid_ref[rows]
        piece[capacity:] = laid[rows]


def route_kernel(clusters, capacity, rows_ref, ids_ref, piece_ref, slot_ref):
    slot = slots_of(ids_ref[...], clusters, capacity)
    slot_ref[...] = slot
    piece_ref[...] = lay(rows_ref, slot, piece_ref.shape[0])


def call_kernel(name, kernel, out_shape, *args, limit=32 * 2**20):
    return pl.pallas_call(
        kernel,
        out_shape=out_shape,
        in_specs=[VMEM] * len(args),
        out_specs=jax.tree.map(lambda _: VMEM, out_shape),
        compiler_params=pltpu.CompilerParams(vmem_limit_bytes=limit),
        name=name,
    )(*args)


def blocks(rows, starts, size):
    return jnp.concatenate([rows[start : start + size] for start in starts], axis=0)


def count_against(rows, own, starts, size):
    column = lax.broadcasted_iota(jnp.int32, (1, own.shape[0]), 1)
    itself = jnp.full_like(column, -1)
    for k, start in enumerate(starts):
        itself = jnp.where(column // size == k, column + (start - k * size), itself)
    slope = -math.log2(math.e) / sharpness
    total = jnp.zeros((1, own.shape[0]), jnp.float32)
    for first in range(0, rows.shape[0], TILE):
        other = rows[first : first + TILE]
        scores = lax.dot_general(
            other, own, (((1,), (1,)), ((), ())), preferred_element_type=jnp.float32
        )
        weights = 1.0 / (1.0 + jnp.exp2(scores * slope - threshold * slope))
        keep = other[:, :1].astype(jnp.float32) < 0.5 * EMPTY
        if starts:
            keep = keep & (lax.broadcasted_iota(jnp.int32, scores.shape, 0) + first != itself)
        total = total + jnp.sum(jnp.where(keep, weights, 0.0), axis=0, keepdims=True)
    return total


def count_kernel(starts, size, *refs):
    *piece_refs, count_ref = refs
    rows = jnp.concatenate([piece[...] for piece in piece_refs], axis=0)
    count_ref[...] = count_against(rows, blocks(rows, starts, size), starts, size)


def soft_counts(pieces, starts, size):
    out_shape = jax.ShapeDtypeStruct((1, len(starts) * size), jnp.float32)
    return call_kernel("count", functools.partial(count_kernel, starts, size), out_shape, *pieces)


def finish_kernel(starts, late_pieces, late_starts, places, *refs):
    *piece_refs, early_ref, count_ref = refs
    size = count_ref.shape[2]
    early = jnp.concatenate([piece[...] for piece in piece_refs[:-late_pieces]], axis=0)
    late = jnp.concatenate([piece[...] for piece in piece_refs[-late_pieces:]], axis=0)
    own = blocks(early, starts, size)
    late_own = blocks(late, late_starts, size)
    total = early_ref[...] + count_against(late, own, [], size)
    late_total = count_against(early, late_own, [], size) + count_against(
        late, late_own, late_starts, size
    )
    for k, place in enumerate(places()):
        source, j = (total, k) if k < len(starts) else (late_total, k - len(starts))
        count_ref[pl.ds(place, 1), 0, :] = source[:, j * size : (j + 1) * size]


def select_kernel(capacity, counts_ref, slot_ref, out_ref):
    counts = counts_ref[:, 0, :]
    slot = slot_ref[...]
    doc_count = slot.shape[1]
    block = slot // capacity
    rank = slot - block * capacity
    hot = (lax.broadcasted_iota(jnp.int32, (capacity, doc_count), 0) == rank).astype(jnp.float32)
    by_block = jnp.dot(
        counts, hot, precision=lax.Precision.HIGHEST, preferred_element_type=jnp.float32
    )
    chosen = lax.broadcasted_iota(jnp.int32, by_block.shape, 0) == block
    out_ref[...] = jnp.sum(jnp.where(chosen, by_block, 0.0), axis=0, keepdims=True)


def select(counts, slot, capacity):
    out_shape = jax.ShapeDtypeStruct(slot.shape, jnp.float32)
    kernel = functools.partial(select_kernel, capacity)
    return call_kernel("select", kernel, out_shape, counts, slot, limit=8 * 2**20)[0]


def swap_cores(x):
    cores = lax.axis_size("sub")
    return lax.ppermute(x, "sub", [(i, i ^ 1) for i in range(cores)])


def body_by_chip(embeddings, cluster_id):
    doc_count, feature_count = embeddings.shape
    clusters = CL_OWN * lax.axis_size("owner")
    capacity = 2 * doc_count // clusters
    cores = lax.axis_size("sub")
    steps = clusters // cores

    def across(x, p):
        pairs = [
            (chip * cores + core, (chip ^ (p * cores + core)) * cores + core)
            for chip in range(clusters)
            for core in range(cores)
        ]
        return lax.ppermute(x, ("owner", "helper", "sub"), pairs)

    ids = cluster_id.reshape(1, doc_count)
    other_rows, other_ids = swap_cores(embeddings), swap_cores(ids)
    first, last = steps // 2, steps - 1
    middle = [p for p in range(steps) if p not in (first, last)]
    own_laid, slot = call_kernel(
        "route_own",
        functools.partial(route_own_kernel, clusters, capacity),
        [
            jax.ShapeDtypeStruct((steps * capacity, feature_count), jnp.bfloat16),
            jax.ShapeDtypeStruct((1, doc_count), jnp.int32),
        ],
        embeddings,
        ids,
    )
    pieces = call_kernel(
        "route_other",
        functools.partial(route_other_kernel, clusters, capacity),
        [jax.ShapeDtypeStruct((cores * capacity, feature_count), jnp.bfloat16)] * steps,
        other_rows,
        other_ids,
        own_laid,
    )
    arrived = [across(pieces[p], p) for p in (first, *middle, last)]
    swapped = [swap_cores(x) for x in arrived]

    early = arrived[:-1] + swapped[:-1]
    late = [arrived[-1], swapped[-1]]
    span = cores * capacity
    starts = [k * span for k in range(steps - 1)]
    starts += [k * span + capacity for k in range(steps - 1, 2 * (steps - 1))]
    late_starts = [0, span + capacity]

    def places():
        chip, core = chip_index(), lax.axis_index("sub")
        return (
            [chip ^ (p * cores + core) for p in (first, *middle)]
            + [chip ^ (p * cores + 1 - core) for p in (first, *middle)]
            + [chip ^ (last * cores + core), chip ^ (last * cores + 1 - core)]
        )

    counts = call_kernel(
        "finish",
        functools.partial(finish_kernel, starts, len(late), late_starts, places),
        jax.ShapeDtypeStruct((clusters, 1, capacity), jnp.float32),
        *early,
        *late,
        soft_counts(early, starts, capacity),
    )
    back = lax.all_to_all(counts, ("owner", "helper"), split_axis=0, concat_axis=0, tiled=True)
    return select(back, slot, capacity)


def body_by_owner(embeddings, cluster_id):
    doc_count, feature_count = embeddings.shape
    owners, helpers = lax.axis_size("owner"), lax.axis_size("helper")
    clusters = CL_OWN * owners
    capacity = 2 * doc_count // clusters
    mine = lax.axis_index("helper") % CL_OWN

    def partner(x):
        return lax.ppermute(x, "helper", [(i, i ^ 1) for i in range(helpers)])

    outgoing, slot = call_kernel(
        "route",
        functools.partial(route_kernel, clusters, capacity),
        [
            jax.ShapeDtypeStruct((clusters * capacity, feature_count), jnp.bfloat16),
            jax.ShapeDtypeStruct((1, doc_count), jnp.int32),
        ],
        embeddings,
        cluster_id.reshape(1, doc_count),
    )
    outgoing = outgoing.reshape(owners, CL_OWN, capacity, feature_count)
    arrived = lax.all_to_all(outgoing, "owner", split_axis=0, concat_axis=0, tiled=True)
    kept = lax.dynamic_index_in_dim(arrived, mine, 1, keepdims=False)
    given = partner(lax.dynamic_index_in_dim(arrived, 1 - mine, 1, keepdims=False))
    own = jnp.stack([kept, given]).reshape(CL_OWN * owners * capacity, feature_count)
    others = [swap_cores(own)]
    for step in range(CL_OWN, helpers, CL_OWN):
        turn = [(i, (i + step) % helpers) for i in range(helpers)]
        others += [lax.ppermute(x, "helper", turn) for x in (own, others[0])]
    counts = soft_counts([own, *others], [0], own.shape[0])
    counts = counts.reshape(CL_OWN, owners, capacity)
    kept, given = counts[0], partner(counts[1])
    counts = jnp.where(mine == 0, jnp.stack([kept, given], 1), jnp.stack([given, kept], 1))
    back = lax.all_to_all(counts, "owner", split_axis=0, concat_axis=0, tiled=True)
    return select(back.reshape(clusters, 1, capacity), slot, capacity)


def solution(mesh):
    in_specs = (
        P(("groups", "owner", "helper", "sub"), None),
        P(("groups", "owner", "helper", "sub")),
    )
    out_specs = P(("groups", "owner", "helper", "sub"))
    body = body_by_chip if mesh.shape["helper"] == CL_OWN else body_by_owner
    return jax.shard_map(body, mesh=mesh, in_specs=in_specs, out_specs=out_specs, check_vma=False)
```

```python
import functools
import math

import jax
import jax.numpy as jnp
from jax import lax
from jax.experimental import pallas as pl
from jax.experimental.pallas import tpu as pltpu
from jax.sharding import PartitionSpec as P

CL_OWN = 2

epsilon = 1e-06
threshold = 0.8
sharpness = 0.05

EMPTY = 4.0
TILE = 256
VMEM = pl.BlockSpec(memory_space=pltpu.VMEM)


def chip_index():
    return lax.axis_index("owner") * CL_OWN + lax.axis_index("helper")


def slots_of(ids, clusters, capacity):
    doc_count = ids.shape[1]
    member = lax.broadcasted_iota(jnp.int32, (clusters, doc_count), 0) == ids
    earlier = lax.broadcasted_iota(jnp.int32, (doc_count, doc_count), 0) < (
        lax.broadcasted_iota(jnp.int32, (doc_count, doc_count), 1)
    )
    ahead = jnp.dot(
        member.astype(jnp.bfloat16), earlier.astype(jnp.bfloat16), preferred_element_type=jnp.float32
    )
    rank = jnp.sum(jnp.where(member, ahead, 0.0), axis=0, keepdims=True).astype(jnp.int32)
    return ids * capacity + rank


def lay(rows_ref, slot, slots):
    doc_count, feature_count = rows_ref.shape
    dispatch = lax.broadcasted_iota(jnp.int32, (slots, doc_count), 0) == slot
    filled = jnp.sum(dispatch.astype(jnp.float32), axis=1, keepdims=True) > 0
    laid = jnp.dot(
        dispatch.astype(jnp.bfloat16), rows_ref[...], preferred_element_type=jnp.float32
    )
    factor = lax.rsqrt(
        jnp.mean(laid * laid, axis=-1, keepdims=True) + epsilon
    ) * feature_count ** (-0.5)
    lane = lax.broadcasted_iota(jnp.int32, laid.shape, 1)
    return jnp.where(filled | (lane > 0), laid * factor, EMPTY).astype(jnp.bfloat16)


def slots_of_steps(slot, capacity, steps):
    cores = lax.axis_size("sub")
    by_distance = slot ^ (chip_index() * capacity)
    distance = by_distance // capacity
    rank = by_distance - distance * capacity
    step = jnp.full_like(slot, -1)
    for place, p in enumerate(steps):
        step = jnp.where(distance == p * cores + lax.axis_index("sub"), place, step)
    return jnp.where(step < 0, -1, step * capacity + rank)


def route_own_kernel(clusters, capacity, rows_ref, ids_ref, laid_ref, slot_ref):
    steps = range(laid_ref.shape[0] // capacity)
    slot = slots_of(ids_ref[...], clusters, capacity)
    slot_ref[...] = slot
    laid_ref[...] = lay(rows_ref, slots_of_steps(slot, capacity, steps), laid_ref.shape[0])


def route_other_kernel(clusters, capacity, rows_ref, ids_ref, laid_ref, *piece_refs):
    slot = slots_of(ids_ref[...], clusters, capacity)
    slot = slots_of_steps(slot, capacity, range(len(piece_refs)))
    laid = lay(rows_ref, slot, laid_ref.shape[0])
    for p, piece in enumerate(piece_refs):
        rows = slice(p * capacity, (p + 1) * capacity)
        piece[:capacity] = laid_ref[rows]
        piece[capacity:] = laid[rows]


def route_kernel(clusters, capacity, rows_ref, ids_ref, piece_ref, slot_ref):
    slot = slots_of(ids_ref[...], clusters, capacity)
    slot_ref[...] = slot
    piece_ref[...] = lay(rows_ref, slot, piece_ref.shape[0])


def call_kernel(name, kernel, out_shape, *args, limit=32 * 2**20):
    return pl.pallas_call(
        kernel,
        out_shape=out_shape,
        in_specs=[VMEM] * len(args),
        out_specs=jax.tree.map(lambda _: VMEM, out_shape),
        compiler_params=pltpu.CompilerParams(vmem_limit_bytes=limit),
        name=name,
    )(*args)


def blocks(rows, starts, size):
    return jnp.concatenate([rows[start : start + size] for start in starts], axis=0)


def count_against(rows, own, starts, size):
    column = lax.broadcasted_iota(jnp.int32, (1, own.shape[0]), 1)
    itself = jnp.full_like(column, -1)
    for k, start in enumerate(starts):
        itself = jnp.where(column // size == k, column + (start - k * size), itself)
    slope = -math.log2(math.e) / sharpness
    total = jnp.zeros((1, own.shape[0]), jnp.float32)
    for first in range(0, rows.shape[0], TILE):
        other = rows[first : first + TILE]
        scores = lax.dot_general(
            other, own, (((1,), (1,)), ((), ())), preferred_element_type=jnp.float32
        )
        weights = 1.0 / (1.0 + jnp.exp2(scores * slope - threshold * slope))
        keep = other[:, :1].astype(jnp.float32) < 0.5 * EMPTY
        if starts:
            keep = keep & (lax.broadcasted_iota(jnp.int32, scores.shape, 0) + first != itself)
        total = total + jnp.sum(jnp.where(keep, weights, 0.0), axis=0, keepdims=True)
    return total


def count_kernel(starts, size, *refs):
    *piece_refs, count_ref = refs
    rows = jnp.concatenate([piece[...] for piece in piece_refs], axis=0)
    count_ref[...] = count_against(rows, blocks(rows, starts, size), starts, size)


def soft_counts(pieces, starts, size):
    out_shape = jax.ShapeDtypeStruct((1, len(starts) * size), jnp.float32)
    return call_kernel("count", functools.partial(count_kernel, starts, size), out_shape, *pieces)


def finish_kernel(starts, late_pieces, late_starts, places, *refs):
    *piece_refs, early_ref, count_ref = refs
    size = count_ref.shape[2]
    early = jnp.concatenate([piece[...] for piece in piece_refs[:-late_pieces]], axis=0)
    late = jnp.concatenate([piece[...] for piece in piece_refs[-late_pieces:]], axis=0)
    own = blocks(early, starts, size)
    late_own = blocks(late, late_starts, size)
    total = early_ref[...] + count_against(late, own, [], size)
    late_total = count_against(early, late_own, [], size) + count_against(
        late, late_own, late_starts, size
    )
    for k, place in enumerate(places()):
        source, j = (total, k) if k < len(starts) else (late_total, k - len(starts))
        count_ref[pl.ds(place, 1), 0, :] = source[:, j * size : (j + 1) * size]


def select_kernel(capacity, counts_ref, slot_ref, out_ref):
    counts = counts_ref[:, 0, :]
    slot = slot_ref[...]
    doc_count = slot.shape[1]
    block = slot // capacity
    rank = slot - block * capacity
    hot = (lax.broadcasted_iota(jnp.int32, (capacity, doc_count), 0) == rank).astype(jnp.float32)
    by_block = jnp.dot(
        counts, hot, precision=lax.Precision.HIGHEST, preferred_element_type=jnp.float32
    )
    chosen = lax.broadcasted_iota(jnp.int32, by_block.shape, 0) == block
    out_ref[...] = jnp.sum(jnp.where(chosen, by_block, 0.0), axis=0, keepdims=True)


def select(counts, slot, capacity):
    out_shape = jax.ShapeDtypeStruct(slot.shape, jnp.float32)
    kernel = functools.partial(select_kernel, capacity)
    return call_kernel("select", kernel, out_shape, counts, slot, limit=8 * 2**20)[0]


def swap_cores(x):
    cores = lax.axis_size("sub")
    return lax.ppermute(x, "sub", [(i, i ^ 1) for i in range(cores)])


def body_by_chip(embeddings, cluster_id):
    doc_count, feature_count = embeddings.shape
    clusters = CL_OWN * lax.axis_size("owner")
    capacity = 2 * doc_count // clusters
    cores = lax.axis_size("sub")
    steps = clusters // cores

    def across(x, p):
        pairs = [
            (chip * cores + core, (chip ^ (p * cores + core)) * cores + core)
            for chip in range(clusters)
            for core in range(cores)
        ]
        return lax.ppermute(x, ("owner", "helper", "sub"), pairs)

    ids = cluster_id.reshape(1, doc_count)
    other_rows, other_ids = swap_cores(embeddings), swap_cores(ids)
    first, last = steps - 1, steps // 2
    middle = [p for p in range(steps) if p not in (first, last)]
    own_laid, slot = call_kernel(
        "route_own",
        functools.partial(route_own_kernel, clusters, capacity),
        [
            jax.ShapeDtypeStruct((steps * capacity, feature_count), jnp.bfloat16),
            jax.ShapeDtypeStruct((1, doc_count), jnp.int32),
        ],
        embeddings,
        ids,
    )
    pieces = call_kernel(
        "route_other",
        functools.partial(route_other_kernel, clusters, capacity),
        [jax.ShapeDtypeStruct((cores * capacity, feature_count), jnp.bfloat16)] * steps,
        other_rows,
        other_ids,
        own_laid,
    )
    arrived = [across(pieces[p], p) for p in (first, *middle, last)]
    swapped = [swap_cores(x) for x in arrived]

    early = arrived[:-1] + swapped[:-1]
    late = [arrived[-1], swapped[-1]]
    span = cores * capacity
    starts = [k * span for k in range(steps - 1)]
    starts += [k * span + capacity for k in range(steps - 1, 2 * (steps - 1))]
    late_starts = [0, span + capacity]

    def places():
        chip, core = chip_index(), lax.axis_index("sub")
        return (
            [chip ^ (p * cores + core) for p in (first, *middle)]
            + [chip ^ (p * cores + 1 - core) for p in (first, *middle)]
            + [chip ^ (last * cores + core), chip ^ (last * cores + 1 - core)]
        )

    counts = call_kernel(
        "finish",
        functools.partial(finish_kernel, starts, len(late), late_starts, places),
        jax.ShapeDtypeStruct((clusters, 1, capacity), jnp.float32),
        *early,
        *late,
        soft_counts(early, starts, capacity),
    )
    back = lax.all_to_all(counts, ("owner", "helper"), split_axis=0, concat_axis=0, tiled=True)
    return select(back, slot, capacity)


def body_by_owner(embeddings, cluster_id):
    doc_count, feature_count = embeddings.shape
    owners, helpers = lax.axis_size("owner"), lax.axis_size("helper")
    clusters = CL_OWN * owners
    capacity = 2 * doc_count // clusters
    mine = lax.axis_index("helper") % CL_OWN

    def partner(x):
        return lax.ppermute(x, "helper", [(i, i ^ 1) for i in range(helpers)])

    outgoing, slot = call_kernel(
        "route",
        functools.partial(route_kernel, clusters, capacity),
        [
            jax.ShapeDtypeStruct((clusters * capacity, feature_count), jnp.bfloat16),
            jax.ShapeDtypeStruct((1, doc_count), jnp.int32),
        ],
        embeddings,
        cluster_id.reshape(1, doc_count),
    )
    outgoing = outgoing.reshape(owners, CL_OWN, capacity, feature_count)
    arrived = lax.all_to_all(outgoing, "owner", split_axis=0, concat_axis=0, tiled=True)
    kept = lax.dynamic_index_in_dim(arrived, mine, 1, keepdims=False)
    given = partner(lax.dynamic_index_in_dim(arrived, 1 - mine, 1, keepdims=False))
    own = jnp.stack([kept, given]).reshape(CL_OWN * owners * capacity, feature_count)
    others = [swap_cores(own)]
    for step in range(CL_OWN, helpers, CL_OWN):
        turn = [(i, (i + step) % helpers) for i in range(helpers)]
        others += [lax.ppermute(x, "helper", turn) for x in (own, others[0])]
    counts = soft_counts([own, *others], [0], own.shape[0])
    counts = counts.reshape(CL_OWN, owners, capacity)
    kept, given = counts[0], partner(counts[1])
    counts = jnp.where(mine == 0, jnp.stack([kept, given], 1), jnp.stack([given, kept], 1))
    back = lax.all_to_all(counts, "owner", split_axis=0, concat_axis=0, tiled=True)
    return select(back.reshape(clusters, 1, capacity), slot, capacity)


def solution(mesh):
    in_specs = (
        P(("groups", "owner", "helper", "sub"), None),
        P(("groups", "owner", "helper", "sub")),
    )
    out_specs = P(("groups", "owner", "helper", "sub"))
    body = body_by_chip if mesh.shape["helper"] == CL_OWN else body_by_owner
    return jax.shard_map(body, mesh=mesh, in_specs=in_specs, out_specs=out_specs, check_vma=False)
```

```python
import functools
import math

import jax
import jax.numpy as jnp
from jax import lax
from jax.experimental import pallas as pl
from jax.experimental.pallas import tpu as pltpu
from jax.sharding import PartitionSpec as P

CL_OWN = 2

epsilon = 1e-06
threshold = 0.8
sharpness = 0.05

EMPTY = 4.0
TILE = 256
VMEM = pl.BlockSpec(memory_space=pltpu.VMEM)


def chip_index():
    return lax.axis_index("owner") * CL_OWN + lax.axis_index("helper")


def slots_of(ids, clusters, capacity):
    doc_count = ids.shape[1]
    member = lax.broadcasted_iota(jnp.int32, (clusters, doc_count), 0) == ids
    earlier = lax.broadcasted_iota(jnp.int32, (doc_count, doc_count), 0) < (
        lax.broadcasted_iota(jnp.int32, (doc_count, doc_count), 1)
    )
    ahead = jnp.dot(
        member.astype(jnp.bfloat16), earlier.astype(jnp.bfloat16), preferred_element_type=jnp.float32
    )
    rank = jnp.sum(jnp.where(member, ahead, 0.0), axis=0, keepdims=True).astype(jnp.int32)
    return ids * capacity + rank


def lay(rows_ref, slot, slots):
    doc_count, feature_count = rows_ref.shape
    dispatch = lax.broadcasted_iota(jnp.int32, (slots, doc_count), 0) == slot
    filled = jnp.sum(dispatch.astype(jnp.float32), axis=1, keepdims=True) > 0
    laid = jnp.dot(
        dispatch.astype(jnp.bfloat16), rows_ref[...], preferred_element_type=jnp.float32
    )
    factor = lax.rsqrt(
        jnp.mean(laid * laid, axis=-1, keepdims=True) + epsilon
    ) * feature_count ** (-0.5)
    lane = lax.broadcasted_iota(jnp.int32, laid.shape, 1)
    return jnp.where(filled | (lane > 0), laid * factor, EMPTY).astype(jnp.bfloat16)


def steps_of(owner, sends):
    middle = (owner == 1) | (owner == 2)
    if isinstance(owner, int):
        near, far = (2, 1) if middle else (1, 2)
    else:
        near, far = jnp.where(middle, 2, 1), jnp.where(middle, 1, 2)
    return [3, 0, near, far] if sends else [3, 0, far, near]


def slots_of_steps(slot, capacity):
    by_distance = slot ^ (chip_index() * capacity)
    distance = by_distance // capacity
    rank = by_distance - distance * capacity
    step = jnp.full_like(slot, -1)
    for k, far in enumerate(steps_of(lax.axis_index("owner"), True)):
        step = jnp.where(distance == far * CL_OWN + lax.axis_index("sub"), k, step)
    return jnp.where(step < 0, -1, step * capacity + rank)


def route_own_kernel(clusters, capacity, rows_ref, ids_ref, laid_ref, slot_ref):
    slot = slots_of(ids_ref[...], clusters, capacity)
    slot_ref[...] = slot
    laid_ref[...] = lay(rows_ref, slots_of_steps(slot, capacity), laid_ref.shape[0])


def route_other_kernel(clusters, capacity, rows_ref, ids_ref, laid_ref, *piece_refs):
    slot = slots_of_steps(slots_of(ids_ref[...], clusters, capacity), capacity)
    laid = lay(rows_ref, slot, laid_ref.shape[0])
    for p, piece in enumerate(piece_refs):
        rows = slice(p * capacity, (p + 1) * capacity)
        piece[:capacity] = laid_ref[rows]
        piece[capacity:] = laid[rows]


def route_kernel(clusters, capacity, rows_ref, ids_ref, piece_ref, slot_ref):
    slot = slots_of(ids_ref[...], clusters, capacity)
    slot_ref[...] = slot
    piece_ref[...] = lay(rows_ref, slot, piece_ref.shape[0])


def call_kernel(name, kernel, out_shape, *args, limit=32 * 2**20):
    return pl.pallas_call(
        kernel,
        out_shape=out_shape,
        in_specs=[VMEM] * len(args),
        out_specs=jax.tree.map(lambda _: VMEM, out_shape),
        compiler_params=pltpu.CompilerParams(vmem_limit_bytes=limit),
        name=name,
    )(*args)


def blocks(rows, starts, size):
    return jnp.concatenate([rows[start : start + size] for start in starts], axis=0)


def count_against(rows, own, starts, size):
    column = lax.broadcasted_iota(jnp.int32, (1, own.shape[0]), 1)
    itself = jnp.full_like(column, -1)
    for k, start in enumerate(starts):
        itself = jnp.where(column // size == k, column + (start - k * size), itself)
    slope = -math.log2(math.e) / sharpness
    total = jnp.zeros((1, own.shape[0]), jnp.float32)
    for first in range(0, rows.shape[0], TILE):
        other = rows[first : first + TILE]
        scores = lax.dot_general(
            other, own, (((1,), (1,)), ((), ())), preferred_element_type=jnp.float32
        )
        weights = 1.0 / (1.0 + jnp.exp2(scores * slope - threshold * slope))
        keep = other[:, :1].astype(jnp.float32) < 0.5 * EMPTY
        if starts:
            keep = keep & (lax.broadcasted_iota(jnp.int32, scores.shape, 0) + first != itself)
        total = total + jnp.sum(jnp.where(keep, weights, 0.0), axis=0, keepdims=True)
    return total


def count_kernel(starts, size, *refs):
    *piece_refs, count_ref = refs
    rows = jnp.concatenate([piece[...] for piece in piece_refs], axis=0)
    count_ref[...] = count_against(rows, blocks(rows, starts, size), starts, size)


def soft_counts(pieces, starts, size):
    out_shape = jax.ShapeDtypeStruct((1, len(starts) * size), jnp.float32)
    return call_kernel("count", functools.partial(count_kernel, starts, size), out_shape, *pieces)


def finish_kernel(starts, late_pieces, late_starts, places, *refs):
    *piece_refs, early_ref, count_ref = refs
    size = count_ref.shape[2]
    early = jnp.concatenate([piece[...] for piece in piece_refs[:-late_pieces]], axis=0)
    late = jnp.concatenate([piece[...] for piece in piece_refs[-late_pieces:]], axis=0)
    own = blocks(early, starts, size)
    late_own = blocks(late, late_starts, size)
    total = early_ref[...] + count_against(late, own, [], size)
    late_total = count_against(early, late_own, [], size) + count_against(
        late, late_own, late_starts, size
    )
    for k, place in enumerate(places()):
        source, j = (total, k) if k < len(starts) else (late_total, k - len(starts))
        count_ref[pl.ds(place, 1), 0, :] = source[:, j * size : (j + 1) * size]


def select_kernel(capacity, counts_ref, slot_ref, out_ref):
    counts = counts_ref[:, 0, :]
    slot = slot_ref[...]
    doc_count = slot.shape[1]
    block = slot // capacity
    rank = slot - block * capacity
    hot = (lax.broadcasted_iota(jnp.int32, (capacity, doc_count), 0) == rank).astype(jnp.float32)
    by_block = jnp.dot(
        counts, hot, precision=lax.Precision.HIGHEST, preferred_element_type=jnp.float32
    )
    chosen = lax.broadcasted_iota(jnp.int32, by_block.shape, 0) == block
    out_ref[...] = jnp.sum(jnp.where(chosen, by_block, 0.0), axis=0, keepdims=True)


def select(counts, slot, capacity):
    out_shape = jax.ShapeDtypeStruct(slot.shape, jnp.float32)
    kernel = functools.partial(select_kernel, capacity)
    return call_kernel("select", kernel, out_shape, counts, slot, limit=8 * 2**20)[0]


def swap_cores(x):
    cores = lax.axis_size("sub")
    return lax.ppermute(x, "sub", [(i, i ^ 1) for i in range(cores)])


def body_by_chip(embeddings, cluster_id):
    doc_count, feature_count = embeddings.shape
    clusters = CL_OWN * lax.axis_size("owner")
    capacity = 2 * doc_count // clusters
    cores = lax.axis_size("sub")
    steps = clusters // cores

    def across(x, step):
        pairs = []
        for chip in range(clusters):
            distance = steps_of(chip // CL_OWN, True)[step] * CL_OWN
            for core in range(cores):
                pairs.append((chip * cores + core, (chip ^ (distance + core)) * cores + core))
        return lax.ppermute(x, ("owner", "helper", "sub"), pairs)

    ids = cluster_id.reshape(1, doc_count)
    other_rows, other_ids = swap_cores(embeddings), swap_cores(ids)
    own_laid, slot = call_kernel(
        "route_own",
        functools.partial(route_own_kernel, clusters, capacity),
        [
            jax.ShapeDtypeStruct((steps * capacity, feature_count), jnp.bfloat16),
            jax.ShapeDtypeStruct((1, doc_count), jnp.int32),
        ],
        embeddings,
        ids,
    )
    pieces = call_kernel(
        "route_other",
        functools.partial(route_other_kernel, clusters, capacity),
        [jax.ShapeDtypeStruct((cores * capacity, feature_count), jnp.bfloat16)] * steps,
        other_rows,
        other_ids,
        own_laid,
    )
    arrived = [across(piece, step) for step, piece in enumerate(pieces)]
    swapped = [swap_cores(x) for x in arrived]

    early = arrived[:-1] + swapped[:-1]
    late = [arrived[-1], swapped[-1]]
    span = cores * capacity
    starts = [k * span for k in range(steps - 1)]
    starts += [k * span + capacity for k in range(steps - 1, 2 * (steps - 1))]
    late_starts = [0, span + capacity]

    def places():
        chip, core = chip_index(), lax.axis_index("sub")
        far = [chip ^ (d * CL_OWN) for d in steps_of(lax.axis_index("owner"), False)]
        own, other = [x ^ core for x in far], [x ^ (1 - core) for x in far]
        return own[:-1] + other[:-1] + [own[-1], other[-1]]

    counts = call_kernel(
        "finish",
        functools.partial(finish_kernel, starts, len(late), late_starts, places),
        jax.ShapeDtypeStruct((clusters, 1, capacity), jnp.float32),
        *early,
        *late,
        soft_counts(early, starts, capacity),
    )
    back = lax.all_to_all(counts, ("owner", "helper"), split_axis=0, concat_axis=0, tiled=True)
    return select(back, slot, capacity)


def body_by_owner(embeddings, cluster_id):
    doc_count, feature_count = embeddings.shape
    owners, helpers = lax.axis_size("owner"), lax.axis_size("helper")
    clusters = CL_OWN * owners
    capacity = 2 * doc_count // clusters
    mine = lax.axis_index("helper") % CL_OWN

    def partner(x):
        return lax.ppermute(x, "helper", [(i, i ^ 1) for i in range(helpers)])

    outgoing, slot = call_kernel(
        "route",
        functools.partial(route_kernel, clusters, capacity),
        [
            jax.ShapeDtypeStruct((clusters * capacity, feature_count), jnp.bfloat16),
            jax.ShapeDtypeStruct((1, doc_count), jnp.int32),
        ],
        embeddings,
        cluster_id.reshape(1, doc_count),
    )
    outgoing = outgoing.reshape(owners, CL_OWN, capacity, feature_count)
    arrived = lax.all_to_all(outgoing, "owner", split_axis=0, concat_axis=0, tiled=True)
    kept = lax.dynamic_index_in_dim(arrived, mine, 1, keepdims=False)
    given = partner(lax.dynamic_index_in_dim(arrived, 1 - mine, 1, keepdims=False))
    own = jnp.stack([kept, given]).reshape(CL_OWN * owners * capacity, feature_count)
    others = [swap_cores(own)]
    for step in range(CL_OWN, helpers, CL_OWN):
        turn = [(i, (i + step) % helpers) for i in range(helpers)]
        others += [lax.ppermute(x, "helper", turn) for x in (own, others[0])]
    counts = soft_counts([own, *others], [0], own.shape[0])
    counts = counts.reshape(CL_OWN, owners, capacity)
    kept, given = counts[0], partner(counts[1])
    counts = jnp.where(mine == 0, jnp.stack([kept, given], 1), jnp.stack([given, kept], 1))
    back = lax.all_to_all(counts, "owner", split_axis=0, concat_axis=0, tiled=True)
    return select(back.reshape(clusters, 1, capacity), slot, capacity)


def solution(mesh):
    in_specs = (
        P(("groups", "owner", "helper", "sub"), None),
        P(("groups", "owner", "helper", "sub")),
    )
    out_specs = P(("groups", "owner", "helper", "sub"))
    line_of_chips = mesh.shape["owner"] == 4 and mesh.shape["helper"] == CL_OWN
    body = body_by_chip if line_of_chips and mesh.shape["sub"] == 2 else body_by_owner
    return jax.shard_map(body, mesh=mesh, in_specs=in_specs, out_specs=out_specs, check_vma=False)
```

```python
import functools
import math

import jax
import jax.numpy as jnp
from jax import lax
from jax.experimental import pallas as pl
from jax.experimental.pallas import tpu as pltpu
from jax.sharding import PartitionSpec as P

CL_OWN = 2

epsilon = 1e-06
threshold = 0.8
sharpness = 0.05

EMPTY = 4.0
TILE = 256
VMEM = pl.BlockSpec(memory_space=pltpu.VMEM)


def chip_index():
    return lax.axis_index("owner") * CL_OWN + lax.axis_index("helper")


def slots_of(ids, clusters, capacity):
    doc_count = ids.shape[1]
    member = lax.broadcasted_iota(jnp.int32, (clusters, doc_count), 0) == ids
    earlier = lax.broadcasted_iota(jnp.int32, (doc_count, doc_count), 0) < (
        lax.broadcasted_iota(jnp.int32, (doc_count, doc_count), 1)
    )
    ahead = jnp.dot(
        member.astype(jnp.bfloat16), earlier.astype(jnp.bfloat16), preferred_element_type=jnp.float32
    )
    rank = jnp.sum(jnp.where(member, ahead, 0.0), axis=0, keepdims=True).astype(jnp.int32)
    return ids * capacity + rank


def lay(rows_ref, slot, slots):
    doc_count, feature_count = rows_ref.shape
    dispatch = lax.broadcasted_iota(jnp.int32, (slots, doc_count), 0) == slot
    filled = jnp.sum(dispatch.astype(jnp.float32), axis=1, keepdims=True) > 0
    laid = jnp.dot(
        dispatch.astype(jnp.bfloat16), rows_ref[...], preferred_element_type=jnp.float32
    )
    factor = lax.rsqrt(
        jnp.mean(laid * laid, axis=-1, keepdims=True) + epsilon
    ) * feature_count ** (-0.5)
    lane = lax.broadcasted_iota(jnp.int32, laid.shape, 1)
    return jnp.where(filled | (lane > 0), laid * factor, EMPTY).astype(jnp.bfloat16)


def slots_of_steps(slot, capacity, steps):
    cores = lax.axis_size("sub")
    by_distance = slot ^ (chip_index() * capacity)
    distance = by_distance // capacity
    rank = by_distance - distance * capacity
    step = jnp.full_like(slot, -1)
    for place, p in enumerate(steps):
        step = jnp.where(distance == p * cores + lax.axis_index("sub"), place, step)
    return jnp.where(step < 0, -1, step * capacity + rank)


def route_first_kernel(clusters, capacity, step, rows_ref, ids_ref, piece_ref, slot_ref):
    slot = slots_of(ids_ref[...], clusters, capacity)
    slot_ref[...] = slot
    piece_ref[...] = lay(rows_ref, slots_of_steps(slot, capacity, [step]), capacity)


def route_rest_kernel(clusters, capacity, first, steps, *refs):
    own_rows, other_rows, own_slot, other_ids, first_ref, *piece_refs = refs
    slot = slots_of_steps(own_slot[...], capacity, steps)
    laid = lay(own_rows, slot, len(steps) * capacity)
    for k, piece in enumerate(piece_refs):
        piece[:capacity] = laid[k * capacity : (k + 1) * capacity]
    slot = slots_of(other_ids[...], clusters, capacity)
    slot = slots_of_steps(slot, capacity, [first, *steps])
    laid = lay(other_rows, slot, (1 + len(steps)) * capacity)
    first_ref[...] = laid[:capacity]
    for k, piece in enumerate(piece_refs):
        piece[capacity:] = laid[(k + 1) * capacity : (k + 2) * capacity]


def route_kernel(clusters, capacity, rows_ref, ids_ref, piece_ref, slot_ref):
    slot = slots_of(ids_ref[...], clusters, capacity)
    slot_ref[...] = slot
    piece_ref[...] = lay(rows_ref, slot, piece_ref.shape[0])


def call_kernel(name, kernel, out_shape, *args, limit=32 * 2**20, flops=0):
    cost = pl.CostEstimate(flops=flops, bytes_accessed=0, transcendentals=0) if flops else None
    return pl.pallas_call(
        kernel,
        out_shape=out_shape,
        in_specs=[VMEM] * len(args),
        out_specs=jax.tree.map(lambda _: VMEM, out_shape),
        compiler_params=pltpu.CompilerParams(vmem_limit_bytes=limit),
        cost_estimate=cost,
        name=name,
    )(*args)


def join_kernel(first_ref, second_ref, out_ref):
    rows = first_ref.shape[0]
    out_ref[:rows] = first_ref[...]
    out_ref[rows:] = second_ref[...]


def blocks(rows, starts, size):
    return jnp.concatenate([rows[start : start + size] for start in starts], axis=0)


def count_against(rows, own, starts, size):
    column = lax.broadcasted_iota(jnp.int32, (1, own.shape[0]), 1)
    itself = jnp.full_like(column, -1)
    for k, start in enumerate(starts):
        itself = jnp.where(column // size == k, column + (start - k * size), itself)
    slope = -math.log2(math.e) / sharpness
    total = jnp.zeros((1, own.shape[0]), jnp.float32)
    for first in range(0, rows.shape[0], TILE):
        other = rows[first : first + TILE]
        scores = lax.dot_general(
            other, own, (((1,), (1,)), ((), ())), preferred_element_type=jnp.float32
        )
        weights = 1.0 / (1.0 + jnp.exp2(scores * slope - threshold * slope))
        keep = other[:, :1].astype(jnp.float32) < 0.5 * EMPTY
        if starts:
            keep = keep & (lax.broadcasted_iota(jnp.int32, scores.shape, 0) + first != itself)
        total = total + jnp.sum(jnp.where(keep, weights, 0.0), axis=0, keepdims=True)
    return total


def count_kernel(starts, size, *refs):
    *piece_refs, count_ref = refs
    rows = jnp.concatenate([piece[...] for piece in piece_refs], axis=0)
    count_ref[...] = count_against(rows, blocks(rows, starts, size), starts, size)


def soft_counts(pieces, starts, size):
    out_shape = jax.ShapeDtypeStruct((1, len(starts) * size), jnp.float32)
    return call_kernel("count", functools.partial(count_kernel, starts, size), out_shape, *pieces)


def finish_kernel(starts, late_pieces, late_starts, places, *refs):
    *piece_refs, early_ref, count_ref = refs
    size = count_ref.shape[2]
    early = jnp.concatenate([piece[...] for piece in piece_refs[:-late_pieces]], axis=0)
    late = jnp.concatenate([piece[...] for piece in piece_refs[-late_pieces:]], axis=0)
    own = blocks(early, starts, size)
    late_own = blocks(late, late_starts, size)
    total = early_ref[...] + count_against(late, own, [], size)
    late_total = count_against(early, late_own, [], size) + count_against(
        late, late_own, late_starts, size
    )
    for k, place in enumerate(places()):
        source, j = (total, k) if k < len(starts) else (late_total, k - len(starts))
        count_ref[pl.ds(place, 1), 0, :] = source[:, j * size : (j + 1) * size]


def select_kernel(capacity, counts_ref, slot_ref, out_ref):
    counts = counts_ref[:, 0, :]
    slot = slot_ref[...]
    doc_count = slot.shape[1]
    block = slot // capacity
    rank = slot - block * capacity
    hot = (lax.broadcasted_iota(jnp.int32, (capacity, doc_count), 0) == rank).astype(jnp.float32)
    by_block = jnp.dot(
        counts, hot, precision=lax.Precision.HIGHEST, preferred_element_type=jnp.float32
    )
    chosen = lax.broadcasted_iota(jnp.int32, by_block.shape, 0) == block
    out_ref[...] = jnp.sum(jnp.where(chosen, by_block, 0.0), axis=0, keepdims=True)


def select(counts, slot, capacity):
    out_shape = jax.ShapeDtypeStruct(slot.shape, jnp.float32)
    kernel = functools.partial(select_kernel, capacity)
    return call_kernel("select", kernel, out_shape, counts, slot, limit=8 * 2**20)[0]


def swap_cores(x):
    cores = lax.axis_size("sub")
    return lax.ppermute(x, "sub", [(i, i ^ 1) for i in range(cores)])


def body_by_chip(embeddings, cluster_id):
    doc_count, feature_count = embeddings.shape
    clusters = CL_OWN * lax.axis_size("owner")
    capacity = 2 * doc_count // clusters
    cores = lax.axis_size("sub")
    steps = clusters // cores

    def across(x, p):
        pairs = [
            (chip * cores + core, (chip ^ (p * cores + core)) * cores + core)
            for chip in range(clusters)
            for core in range(cores)
        ]
        return lax.ppermute(x, ("owner", "helper", "sub"), pairs)

    ids = cluster_id.reshape(1, doc_count)
    other_rows, other_ids = swap_cores(embeddings), swap_cores(ids)
    first, last = steps // 2, steps - 1
    middle = [p for p in range(steps) if p not in (first, last)]
    half = jax.ShapeDtypeStruct((capacity, feature_count), jnp.bfloat16)
    whole = jax.ShapeDtypeStruct((cores * capacity, feature_count), jnp.bfloat16)

    first_own, slot = call_kernel(
        "route_first",
        functools.partial(route_first_kernel, clusters, capacity, first),
        [half, jax.ShapeDtypeStruct((1, doc_count), jnp.int32)],
        embeddings,
        ids,
    )
    first_own = across(first_own, first)
    first_other, *rest = call_kernel(
        "route_rest",
        functools.partial(route_rest_kernel, clusters, capacity, first, [*middle, last]),
        [half] + [whole] * (steps - 1),
        embeddings,
        other_rows,
        slot,
        other_ids,
    )
    first_other = across(first_other, first)
    rest = [across(piece, p) for piece, p in zip(rest, [*middle, last])]

    first_both = call_kernel("join", join_kernel, whole, first_own, first_other, flops=10**10)
    early = [first_both, *rest[:-1]]
    early += [swap_cores(x) for x in early]
    late = [rest[-1], swap_cores(rest[-1])]
    span = cores * capacity
    half_way = span * (steps - 1)
    starts = [k * span for k in range(steps - 1)]
    starts += [half_way + start + capacity for start in starts]
    late_starts = [0, span + capacity]

    def places():
        chip, core = chip_index(), lax.axis_index("sub")
        return (
            [chip ^ (p * cores + core) for p in (first, *middle)]
            + [chip ^ (p * cores + 1 - core) for p in (first, *middle)]
            + [chip ^ (last * cores + core), chip ^ (last * cores + 1 - core)]
        )

    counts = call_kernel(
        "finish",
        functools.partial(finish_kernel, starts, len(late), late_starts, places),
        jax.ShapeDtypeStruct((clusters, 1, capacity), jnp.float32),
        *early,
        *late,
        soft_counts(early, starts, capacity),
    )
    back = lax.all_to_all(counts, ("owner", "helper"), split_axis=0, concat_axis=0, tiled=True)
    return select(back, slot, capacity)


def body_by_owner(embeddings, cluster_id):
    doc_count, feature_count = embeddings.shape
    owners, helpers = lax.axis_size("owner"), lax.axis_size("helper")
    clusters = CL_OWN * owners
    capacity = 2 * doc_count // clusters
    mine = lax.axis_index("helper") % CL_OWN

    def partner(x):
        return lax.ppermute(x, "helper", [(i, i ^ 1) for i in range(helpers)])

    outgoing, slot = call_kernel(
        "route",
        functools.partial(route_kernel, clusters, capacity),
        [
            jax.ShapeDtypeStruct((clusters * capacity, feature_count), jnp.bfloat16),
            jax.ShapeDtypeStruct((1, doc_count), jnp.int32),
        ],
        embeddings,
        cluster_id.reshape(1, doc_count),
    )
    outgoing = outgoing.reshape(owners, CL_OWN, capacity, feature_count)
    arrived = lax.all_to_all(outgoing, "owner", split_axis=0, concat_axis=0, tiled=True)
    kept = lax.dynamic_index_in_dim(arrived, mine, 1, keepdims=False)
    given = partner(lax.dynamic_index_in_dim(arrived, 1 - mine, 1, keepdims=False))
    own = jnp.stack([kept, given]).reshape(CL_OWN * owners * capacity, feature_count)
    others = [swap_cores(own)]
    for step in range(CL_OWN, helpers, CL_OWN):
        turn = [(i, (i + step) % helpers) for i in range(helpers)]
        others += [lax.ppermute(x, "helper", turn) for x in (own, others[0])]
    counts = soft_counts([own, *others], [0], own.shape[0])
    counts = counts.reshape(CL_OWN, owners, capacity)
    kept, given = counts[0], partner(counts[1])
    counts = jnp.where(mine == 0, jnp.stack([kept, given], 1), jnp.stack([given, kept], 1))
    back = lax.all_to_all(counts, "owner", split_axis=0, concat_axis=0, tiled=True)
    return select(back.reshape(clusters, 1, capacity), slot, capacity)


def solution(mesh):
    in_specs = (
        P(("groups", "owner", "helper", "sub"), None),
        P(("groups", "owner", "helper", "sub")),
    )
    out_specs = P(("groups", "owner", "helper", "sub"))
    body = body_by_chip if mesh.shape["helper"] == CL_OWN else body_by_owner
    return jax.shard_map(body, mesh=mesh, in_specs=in_specs, out_specs=out_specs, check_vma=False)
```

```python
import functools
import math

import jax
import jax.numpy as jnp
from jax import lax
from jax.experimental import pallas as pl
from jax.experimental.pallas import tpu as pltpu
from jax.sharding import PartitionSpec as P

CL_OWN = 2

epsilon = 1e-06
threshold = 0.8
sharpness = 0.05

EMPTY = 4.0
TILE = 256
VMEM = pl.BlockSpec(memory_space=pltpu.VMEM)


def chip_index():
    return lax.axis_index("owner") * CL_OWN + lax.axis_index("helper")


def slots_of(ids, clusters, capacity):
    doc_count = ids.shape[1]
    member = lax.broadcasted_iota(jnp.int32, (clusters, doc_count), 0) == ids
    earlier = lax.broadcasted_iota(jnp.int32, (doc_count, doc_count), 0) < (
        lax.broadcasted_iota(jnp.int32, (doc_count, doc_count), 1)
    )
    ahead = jnp.dot(
        member.astype(jnp.bfloat16), earlier.astype(jnp.bfloat16), preferred_element_type=jnp.float32
    )
    rank = jnp.sum(jnp.where(member, ahead, 0.0), axis=0, keepdims=True).astype(jnp.int32)
    return ids * capacity + rank


def lay(rows_ref, slot, slots):
    doc_count, feature_count = rows_ref.shape
    dispatch = lax.broadcasted_iota(jnp.int32, (slots, doc_count), 0) == slot
    filled = jnp.sum(dispatch.astype(jnp.float32), axis=1, keepdims=True) > 0
    laid = jnp.dot(
        dispatch.astype(jnp.bfloat16), rows_ref[...], preferred_element_type=jnp.float32
    )
    factor = lax.rsqrt(
        jnp.mean(laid * laid, axis=-1, keepdims=True) + epsilon
    ) * feature_count ** (-0.5)
    lane = lax.broadcasted_iota(jnp.int32, laid.shape, 1)
    return jnp.where(filled | (lane > 0), laid * factor, EMPTY).astype(jnp.bfloat16)


def slots_of_steps(slot, capacity, steps):
    cores = lax.axis_size("sub")
    by_distance = slot ^ (chip_index() * capacity)
    distance = by_distance // capacity
    rank = by_distance - distance * capacity
    step = jnp.full_like(slot, -1)
    for place, p in enumerate(steps):
        step = jnp.where(distance == p * cores + lax.axis_index("sub"), place, step)
    return jnp.where(step < 0, -1, step * capacity + rank)


def route_first_kernel(clusters, capacity, step, rows_ref, ids_ref, piece_ref, slot_ref):
    slot = slots_of(ids_ref[...], clusters, capacity)
    slot_ref[...] = slot
    piece_ref[...] = lay(rows_ref, slots_of_steps(slot, capacity, [step]), capacity)


def route_rest_kernel(clusters, capacity, halves, steps, *refs):
    own_rows, other_rows, own_slot, other_ids, *piece_refs = refs
    half_refs, whole_refs = piece_refs[: len(halves)], piece_refs[len(halves) :]
    slot = slots_of_steps(own_slot[...], capacity, steps)
    laid = lay(own_rows, slot, len(steps) * capacity)
    for k, piece in enumerate(whole_refs):
        piece[:capacity] = laid[k * capacity : (k + 1) * capacity]
    slot = slots_of(other_ids[...], clusters, capacity)
    slot = slots_of_steps(slot, capacity, [*halves, *steps])
    laid = lay(other_rows, slot, (len(halves) + len(steps)) * capacity)
    for k, piece in enumerate(half_refs):
        piece[...] = laid[k * capacity : (k + 1) * capacity]
    for k, piece in enumerate(whole_refs, len(halves)):
        piece[capacity:] = laid[k * capacity : (k + 1) * capacity]


def route_kernel(clusters, capacity, rows_ref, ids_ref, piece_ref, slot_ref):
    slot = slots_of(ids_ref[...], clusters, capacity)
    slot_ref[...] = slot
    piece_ref[...] = lay(rows_ref, slot, piece_ref.shape[0])


def call_kernel(name, kernel, out_shape, *args, limit=32 * 2**20, flops=0):
    cost = pl.CostEstimate(flops=flops, bytes_accessed=0, transcendentals=0) if flops else None
    return pl.pallas_call(
        kernel,
        out_shape=out_shape,
        in_specs=[VMEM] * len(args),
        out_specs=jax.tree.map(lambda _: VMEM, out_shape),
        compiler_params=pltpu.CompilerParams(vmem_limit_bytes=limit),
        cost_estimate=cost,
        name=name,
    )(*args)


def join_kernel(first_ref, second_ref, out_ref):
    rows = first_ref.shape[0]
    out_ref[:rows] = first_ref[...]
    out_ref[rows:] = second_ref[...]


def blocks(rows, starts, size):
    return jnp.concatenate([rows[start : start + size] for start in starts], axis=0)


def count_against(rows, own, starts, size):
    column = lax.broadcasted_iota(jnp.int32, (1, own.shape[0]), 1)
    itself = jnp.full_like(column, -1)
    for k, start in enumerate(starts):
        itself = jnp.where(column // size == k, column + (start - k * size), itself)
    slope = -math.log2(math.e) / sharpness
    total = jnp.zeros((1, own.shape[0]), jnp.float32)
    for first in range(0, rows.shape[0], TILE):
        other = rows[first : first + TILE]
        scores = lax.dot_general(
            other, own, (((1,), (1,)), ((), ())), preferred_element_type=jnp.float32
        )
        weights = 1.0 / (1.0 + jnp.exp2(scores * slope - threshold * slope))
        keep = other[:, :1].astype(jnp.float32) < 0.5 * EMPTY
        if starts:
            keep = keep & (lax.broadcasted_iota(jnp.int32, scores.shape, 0) + first != itself)
        total = total + jnp.sum(jnp.where(keep, weights, 0.0), axis=0, keepdims=True)
    return total


def count_kernel(starts, size, *refs):
    *piece_refs, count_ref = refs
    rows = jnp.concatenate([piece[...] for piece in piece_refs], axis=0)
    count_ref[...] = count_against(rows, blocks(rows, starts, size), starts, size)


def soft_counts(pieces, starts, size):
    out_shape = jax.ShapeDtypeStruct((1, len(starts) * size), jnp.float32)
    return call_kernel("count", functools.partial(count_kernel, starts, size), out_shape, *pieces)


def finish_kernel(starts, late_pieces, late_starts, places, *refs):
    *piece_refs, early_ref, count_ref = refs
    size = count_ref.shape[2]
    early = jnp.concatenate([piece[...] for piece in piece_refs[:-late_pieces]], axis=0)
    late = jnp.concatenate([piece[...] for piece in piece_refs[-late_pieces:]], axis=0)
    own = blocks(early, starts, size)
    late_own = blocks(late, late_starts, size)
    total = early_ref[...] + count_against(late, own, [], size)
    late_total = count_against(early, late_own, [], size) + count_against(
        late, late_own, late_starts, size
    )
    for k, place in enumerate(places()):
        source, j = (total, k) if k < len(starts) else (late_total, k - len(starts))
        count_ref[pl.ds(place, 1), 0, :] = source[:, j * size : (j + 1) * size]


def select_kernel(capacity, counts_ref, slot_ref, out_ref):
    counts = counts_ref[:, 0, :]
    slot = slot_ref[...]
    doc_count = slot.shape[1]
    block = slot // capacity
    rank = slot - block * capacity
    hot = (lax.broadcasted_iota(jnp.int32, (capacity, doc_count), 0) == rank).astype(jnp.float32)
    by_block = jnp.dot(
        counts, hot, precision=lax.Precision.HIGHEST, preferred_element_type=jnp.float32
    )
    chosen = lax.broadcasted_iota(jnp.int32, by_block.shape, 0) == block
    out_ref[...] = jnp.sum(jnp.where(chosen, by_block, 0.0), axis=0, keepdims=True)


def select(counts, slot, capacity):
    out_shape = jax.ShapeDtypeStruct(slot.shape, jnp.float32)
    kernel = functools.partial(select_kernel, capacity)
    return call_kernel("select", kernel, out_shape, counts, slot, limit=8 * 2**20)[0]


def swap_cores(x):
    cores = lax.axis_size("sub")
    return lax.ppermute(x, "sub", [(i, i ^ 1) for i in range(cores)])


def body_by_chip(embeddings, cluster_id):
    doc_count, feature_count = embeddings.shape
    clusters = CL_OWN * lax.axis_size("owner")
    capacity = 2 * doc_count // clusters
    cores = lax.axis_size("sub")
    steps = clusters // cores

    def across(x, p):
        pairs = [
            (chip * cores + core, (chip ^ (p * cores + core)) * cores + core)
            for chip in range(clusters)
            for core in range(cores)
        ]
        return lax.ppermute(x, ("owner", "helper", "sub"), pairs)

    ids = cluster_id.reshape(1, doc_count)
    other_rows, other_ids = swap_cores(embeddings), swap_cores(ids)
    first, last = steps // 2, steps - 1
    middle = [p for p in range(steps) if p not in (first, last)]
    half = jax.ShapeDtypeStruct((capacity, feature_count), jnp.bfloat16)
    whole = jax.ShapeDtypeStruct((cores * capacity, feature_count), jnp.bfloat16)

    first_own, slot = call_kernel(
        "route_first",
        functools.partial(route_first_kernel, clusters, capacity, first),
        [half, jax.ShapeDtypeStruct((1, doc_count), jnp.int32)],
        embeddings,
        ids,
    )
    first_own = across(first_own, first)

    def route_rest(name, halves, steps):
        return call_kernel(
            name,
            functools.partial(route_rest_kernel, clusters, capacity, halves, steps),
            [half] * len(halves) + [whole] * len(steps),
            embeddings,
            other_rows,
            slot,
            other_ids,
        )

    first_other, last_piece = route_rest("route_far", [first], [last])
    first_other, last_piece = across(first_other, first), across(last_piece, last)
    near = route_rest("route_near", [], middle)
    near = [across(piece, p) for piece, p in zip(near, middle)]

    first_both = call_kernel("join", join_kernel, whole, first_own, first_other, flops=10**10)
    early = [first_both, *near]
    early += [swap_cores(x) for x in early]
    late = [last_piece, swap_cores(last_piece)]
    span = cores * capacity
    half_way = span * (steps - 1)
    starts = [k * span for k in range(steps - 1)]
    starts += [half_way + start + capacity for start in starts]
    late_starts = [0, span + capacity]

    def places():
        chip, core = chip_index(), lax.axis_index("sub")
        return (
            [chip ^ (p * cores + core) for p in (first, *middle)]
            + [chip ^ (p * cores + 1 - core) for p in (first, *middle)]
            + [chip ^ (last * cores + core), chip ^ (last * cores + 1 - core)]
        )

    counts = call_kernel(
        "finish",
        functools.partial(finish_kernel, starts, len(late), late_starts, places),
        jax.ShapeDtypeStruct((clusters, 1, capacity), jnp.float32),
        *early,
        *late,
        soft_counts(early, starts, capacity),
    )
    back = lax.all_to_all(counts, ("owner", "helper"), split_axis=0, concat_axis=0, tiled=True)
    return select(back, slot, capacity)


def body_by_owner(embeddings, cluster_id):
    doc_count, feature_count = embeddings.shape
    owners, helpers = lax.axis_size("owner"), lax.axis_size("helper")
    clusters = CL_OWN * owners
    capacity = 2 * doc_count // clusters
    mine = lax.axis_index("helper") % CL_OWN

    def partner(x):
        return lax.ppermute(x, "helper", [(i, i ^ 1) for i in range(helpers)])

    outgoing, slot = call_kernel(
        "route",
        functools.partial(route_kernel, clusters, capacity),
        [
            jax.ShapeDtypeStruct((clusters * capacity, feature_count), jnp.bfloat16),
            jax.ShapeDtypeStruct((1, doc_count), jnp.int32),
        ],
        embeddings,
        cluster_id.reshape(1, doc_count),
    )
    outgoing = outgoing.reshape(owners, CL_OWN, capacity, feature_count)
    arrived = lax.all_to_all(outgoing, "owner", split_axis=0, concat_axis=0, tiled=True)
    kept = lax.dynamic_index_in_dim(arrived, mine, 1, keepdims=False)
    given = partner(lax.dynamic_index_in_dim(arrived, 1 - mine, 1, keepdims=False))
    own = jnp.stack([kept, given]).reshape(CL_OWN * owners * capacity, feature_count)
    others = [swap_cores(own)]
    for step in range(CL_OWN, helpers, CL_OWN):
        turn = [(i, (i + step) % helpers) for i in range(helpers)]
        others += [lax.ppermute(x, "helper", turn) for x in (own, others[0])]
    counts = soft_counts([own, *others], [0], own.shape[0])
    counts = counts.reshape(CL_OWN, owners, capacity)
    kept, given = counts[0], partner(counts[1])
    counts = jnp.where(mine == 0, jnp.stack([kept, given], 1), jnp.stack([given, kept], 1))
    back = lax.all_to_all(counts, "owner", split_axis=0, concat_axis=0, tiled=True)
    return select(back.reshape(clusters, 1, capacity), slot, capacity)


def solution(mesh):
    in_specs = (
        P(("groups", "owner", "helper", "sub"), None),
        P(("groups", "owner", "helper", "sub")),
    )
    out_specs = P(("groups", "owner", "helper", "sub"))
    body = body_by_chip if mesh.shape["helper"] == CL_OWN else body_by_owner
    return jax.shard_map(body, mesh=mesh, in_specs=in_specs, out_specs=out_specs, check_vma=False)
```

```python
import functools
import math

import jax
import jax.numpy as jnp
from jax import lax
from jax.experimental import pallas as pl
from jax.experimental.pallas import tpu as pltpu
from jax.sharding import PartitionSpec as P

CL_OWN = 2

epsilon = 1e-06
threshold = 0.8
sharpness = 0.05

EMPTY = 4.0
TILE = 256
CHUNKS = 4
VMEM = pl.BlockSpec(memory_space=pltpu.VMEM)
ANY = pl.BlockSpec(memory_space=pl.ANY)


def chip_index():
    return lax.axis_index("owner") * CL_OWN + lax.axis_index("helper")


def slots_of(ids, clusters, capacity):
    doc_count = ids.shape[1]
    member = lax.broadcasted_iota(jnp.int32, (clusters, doc_count), 0) == ids
    earlier = lax.broadcasted_iota(jnp.int32, (doc_count, doc_count), 0) < (
        lax.broadcasted_iota(jnp.int32, (doc_count, doc_count), 1)
    )
    ahead = jnp.dot(
        member.astype(jnp.bfloat16), earlier.astype(jnp.bfloat16), preferred_element_type=jnp.float32
    )
    rank = jnp.sum(jnp.where(member, ahead, 0.0), axis=0, keepdims=True).astype(jnp.int32)
    return ids * capacity + rank


def mark_and_scale(laid, filled):
    factor = lax.rsqrt(
        jnp.mean(laid * laid, axis=-1, keepdims=True) + epsilon
    ) * laid.shape[1] ** (-0.5)
    lane = lax.broadcasted_iota(jnp.int32, laid.shape, 1)
    return jnp.where(filled | (lane > 0), laid * factor, EMPTY).astype(jnp.bfloat16)


def dispatch_of(slot, slots):
    dispatch = lax.broadcasted_iota(jnp.int32, (slots, slot.shape[1]), 0) == slot
    filled = jnp.sum(dispatch.astype(jnp.float32), axis=1, keepdims=True) > 0
    return dispatch.astype(jnp.bfloat16), filled


def lay(rows_ref, slot, slots):
    dispatch, filled = dispatch_of(slot, slots)
    laid = jnp.dot(dispatch, rows_ref[...], preferred_element_type=jnp.float32)
    return mark_and_scale(laid, filled)


def slots_of_steps(slot, capacity, steps):
    cores = lax.axis_size("sub")
    by_distance = slot ^ (chip_index() * capacity)
    distance = by_distance // capacity
    rank = by_distance - distance * capacity
    step = jnp.full_like(slot, -1)
    for place, p in enumerate(steps):
        step = jnp.where(distance == p * cores + lax.axis_index("sub"), place, step)
    return jnp.where(step < 0, -1, step * capacity + rank)


def route_first_kernel(clusters, capacity, step, *refs):
    rows_ref, ids_ref, piece_ref, slot_ref, rows, ids, row_sems, ids_sem = refs
    ids_copy = pltpu.make_async_copy(ids_ref, ids, ids_sem)
    ids_copy.start()
    chunk = rows.shape[0] // CHUNKS
    parts = [pl.ds(k * chunk, chunk) for k in range(CHUNKS)]
    copies = [
        pltpu.make_async_copy(rows_ref.at[part], rows.at[part], row_sems.at[k])
        for k, part in enumerate(parts)
    ]
    for copy in copies:
        copy.start()
    ids_copy.wait()
    slot = slots_of(ids[...], clusters, capacity)
    slot_ref[...] = slot
    dispatch, filled = dispatch_of(slots_of_steps(slot, capacity, [step]), capacity)
    laid = jnp.zeros(piece_ref.shape, jnp.float32)
    for k, copy in enumerate(copies):
        copy.wait()
        columns = slice(k * chunk, (k + 1) * chunk)
        laid = laid + jnp.dot(
            dispatch[:, columns], rows[columns], preferred_element_type=jnp.float32
        )
    piece_ref[...] = mark_and_scale(laid, filled)


def route_rest_kernel(clusters, capacity, first, steps, *refs):
    own_rows, other_rows, own_slot, other_ids, first_ref, *piece_refs = refs
    slot = slots_of_steps(own_slot[...], capacity, steps)
    laid = lay(own_rows, slot, len(steps) * capacity)
    for k, piece in enumerate(piece_refs):
        piece[:capacity] = laid[k * capacity : (k + 1) * capacity]
    slot = slots_of(other_ids[...], clusters, capacity)
    slot = slots_of_steps(slot, capacity, [first, *steps])
    laid = lay(other_rows, slot, (1 + len(steps)) * capacity)
    first_ref[...] = laid[:capacity]
    for k, piece in enumerate(piece_refs):
        piece[capacity:] = laid[(k + 1) * capacity : (k + 2) * capacity]


def route_kernel(clusters, capacity, rows_ref, ids_ref, piece_ref, slot_ref):
    slot = slots_of(ids_ref[...], clusters, capacity)
    slot_ref[...] = slot
    piece_ref[...] = lay(rows_ref, slot, piece_ref.shape[0])


def call_kernel(name, kernel, out_shape, *args, limit=32 * 2**20, flops=0, scratch=()):
    cost = pl.CostEstimate(flops=flops, bytes_accessed=0, transcendentals=0) if flops else None
    return pl.pallas_call(
        kernel,
        out_shape=out_shape,
        in_specs=[ANY if scratch else VMEM] * len(args),
        out_specs=jax.tree.map(lambda _: VMEM, out_shape),
        scratch_shapes=scratch,
        compiler_params=pltpu.CompilerParams(vmem_limit_bytes=limit),
        cost_estimate=cost,
        name=name,
    )(*args)


def join_kernel(first_ref, second_ref, out_ref):
    rows = first_ref.shape[0]
    out_ref[:rows] = first_ref[...]
    out_ref[rows:] = second_ref[...]


def blocks(rows, starts, size):
    return jnp.concatenate([rows[start : start + size] for start in starts], axis=0)


def count_against(rows, own, starts, size):
    column = lax.broadcasted_iota(jnp.int32, (1, own.shape[0]), 1)
    itself = jnp.full_like(column, -1)
    for k, start in enumerate(starts):
        itself = jnp.where(column // size == k, column + (start - k * size), itself)
    slope = -math.log2(math.e) / sharpness
    total = jnp.zeros((1, own.shape[0]), jnp.float32)
    for first in range(0, rows.shape[0], TILE):
        other = rows[first : first + TILE]
        scores = lax.dot_general(
            other, own, (((1,), (1,)), ((), ())), preferred_element_type=jnp.float32
        )
        weights = 1.0 / (1.0 + jnp.exp2(scores * slope - threshold * slope))
        keep = other[:, :1].astype(jnp.float32) < 0.5 * EMPTY
        if starts:
            keep = keep & (lax.broadcasted_iota(jnp.int32, scores.shape, 0) + first != itself)
        total = total + jnp.sum(jnp.where(keep, weights, 0.0), axis=0, keepdims=True)
    return total


def count_kernel(starts, size, *refs):
    *piece_refs, count_ref = refs
    rows = jnp.concatenate([piece[...] for piece in piece_refs], axis=0)
    count_ref[...] = count_against(rows, blocks(rows, starts, size), starts, size)


def soft_counts(pieces, starts, size):
    out_shape = jax.ShapeDtypeStruct((1, len(starts) * size), jnp.float32)
    return call_kernel("count", functools.partial(count_kernel, starts, size), out_shape, *pieces)


def finish_kernel(starts, late_pieces, late_starts, places, *refs):
    *piece_refs, early_ref, count_ref = refs
    size = count_ref.shape[2]
    early = jnp.concatenate([piece[...] for piece in piece_refs[:-late_pieces]], axis=0)
    late = jnp.concatenate([piece[...] for piece in piece_refs[-late_pieces:]], axis=0)
    own = blocks(early, starts, size)
    late_own = blocks(late, late_starts, size)
    total = early_ref[...] + count_against(late, own, [], size)
    late_total = count_against(early, late_own, [], size) + count_against(
        late, late_own, late_starts, size
    )
    for k, place in enumerate(places()):
        source, j = (total, k) if k < len(starts) else (late_total, k - len(starts))
        count_ref[pl.ds(place, 1), 0, :] = source[:, j * size : (j + 1) * size]


def select_kernel(capacity, counts_ref, slot_ref, out_ref):
    counts = counts_ref[:, 0, :]
    slot = slot_ref[...]
    doc_count = slot.shape[1]
    block = slot // capacity
    rank = slot - block * capacity
    hot = (lax.broadcasted_iota(jnp.int32, (capacity, doc_count), 0) == rank).astype(jnp.float32)
    by_block = jnp.dot(
        counts, hot, precision=lax.Precision.HIGHEST, preferred_element_type=jnp.float32
    )
    chosen = lax.broadcasted_iota(jnp.int32, by_block.shape, 0) == block
    out_ref[...] = jnp.sum(jnp.where(chosen, by_block, 0.0), axis=0, keepdims=True)


def select(counts, slot, capacity):
    out_shape = jax.ShapeDtypeStruct(slot.shape, jnp.float32)
    kernel = functools.partial(select_kernel, capacity)
    return call_kernel("select", kernel, out_shape, counts, slot, limit=8 * 2**20)[0]


def swap_cores(x):
    cores = lax.axis_size("sub")
    return lax.ppermute(x, "sub", [(i, i ^ 1) for i in range(cores)])


def body_by_chip(embeddings, cluster_id):
    doc_count, feature_count = embeddings.shape
    clusters = CL_OWN * lax.axis_size("owner")
    capacity = 2 * doc_count // clusters
    cores = lax.axis_size("sub")
    steps = clusters // cores

    def across(x, p):
        pairs = [
            (chip * cores + core, (chip ^ (p * cores + core)) * cores + core)
            for chip in range(clusters)
            for core in range(cores)
        ]
        return lax.ppermute(x, ("owner", "helper", "sub"), pairs)

    ids = cluster_id.reshape(1, doc_count)
    other_rows, other_ids = swap_cores(embeddings), swap_cores(ids)
    first, last = steps // 2, steps - 1
    middle = [p for p in range(steps) if p not in (first, last)]
    half = jax.ShapeDtypeStruct((capacity, feature_count), jnp.bfloat16)
    whole = jax.ShapeDtypeStruct((cores * capacity, feature_count), jnp.bfloat16)

    first_own, slot = call_kernel(
        "route_first",
        functools.partial(route_first_kernel, clusters, capacity, first),
        [half, jax.ShapeDtypeStruct((1, doc_count), jnp.int32)],
        embeddings,
        ids,
        limit=60 * 2**20,
        scratch=[
            pltpu.VMEM((doc_count, feature_count), jnp.bfloat16),
            pltpu.VMEM((1, doc_count), jnp.int32),
            pltpu.SemaphoreType.DMA((CHUNKS,)),
            pltpu.SemaphoreType.DMA,
        ],
    )
    first_own = across(first_own, first)
    first_other, *rest = call_kernel(
        "route_rest",
        functools.partial(route_rest_kernel, clusters, capacity, first, [*middle, last]),
        [half] + [whole] * (steps - 1),
        embeddings,
        other_rows,
        slot,
        other_ids,
    )
    first_other = across(first_other, first)
    rest = [across(piece, p) for piece, p in zip(rest, [*middle, last])]

    first_both = call_kernel("join", join_kernel, whole, first_own, first_other, flops=10**10)
    early = [first_both, *rest[:-1]]
    early += [swap_cores(x) for x in early]
    late = [rest[-1], swap_cores(rest[-1])]
    span = cores * capacity
    half_way = span * (steps - 1)
    starts = [k * span for k in range(steps - 1)]
    starts += [half_way + start + capacity for start in starts]
    late_starts = [0, span + capacity]

    def places():
        chip, core = chip_index(), lax.axis_index("sub")
        return (
            [chip ^ (p * cores + core) for p in (first, *middle)]
            + [chip ^ (p * cores + 1 - core) for p in (first, *middle)]
            + [chip ^ (last * cores + core), chip ^ (last * cores + 1 - core)]
        )

    counts = call_kernel(
        "finish",
        functools.partial(finish_kernel, starts, len(late), late_starts, places),
        jax.ShapeDtypeStruct((clusters, 1, capacity), jnp.float32),
        *early,
        *late,
        soft_counts(early, starts, capacity),
    )
    back = lax.all_to_all(counts, ("owner", "helper"), split_axis=0, concat_axis=0, tiled=True)
    return select(back, slot, capacity)


def body_by_owner(embeddings, cluster_id):
    doc_count, feature_count = embeddings.shape
    owners, helpers = lax.axis_size("owner"), lax.axis_size("helper")
    clusters = CL_OWN * owners
    capacity = 2 * doc_count // clusters
    mine = lax.axis_index("helper") % CL_OWN

    def partner(x):
        return lax.ppermute(x, "helper", [(i, i ^ 1) for i in range(helpers)])

    outgoing, slot = call_kernel(
        "route",
        functools.partial(route_kernel, clusters, capacity),
        [
            jax.ShapeDtypeStruct((clusters * capacity, feature_count), jnp.bfloat16),
            jax.ShapeDtypeStruct((1, doc_count), jnp.int32),
        ],
        embeddings,
        cluster_id.reshape(1, doc_count),
    )
    outgoing = outgoing.reshape(owners, CL_OWN, capacity, feature_count)
    arrived = lax.all_to_all(outgoing, "owner", split_axis=0, concat_axis=0, tiled=True)
    kept = lax.dynamic_index_in_dim(arrived, mine, 1, keepdims=False)
    given = partner(lax.dynamic_index_in_dim(arrived, 1 - mine, 1, keepdims=False))
    own = jnp.stack([kept, given]).reshape(CL_OWN * owners * capacity, feature_count)
    others = [swap_cores(own)]
    for step in range(CL_OWN, helpers, CL_OWN):
        turn = [(i, (i + step) % helpers) for i in range(helpers)]
        others += [lax.ppermute(x, "helper", turn) for x in (own, others[0])]
    counts = soft_counts([own, *others], [0], own.shape[0])
    counts = counts.reshape(CL_OWN, owners, capacity)
    kept, given = counts[0], partner(counts[1])
    counts = jnp.where(mine == 0, jnp.stack([kept, given], 1), jnp.stack([given, kept], 1))
    back = lax.all_to_all(counts, "owner", split_axis=0, concat_axis=0, tiled=True)
    return select(back.reshape(clusters, 1, capacity), slot, capacity)


def solution(mesh):
    in_specs = (
        P(("groups", "owner", "helper", "sub"), None),
        P(("groups", "owner", "helper", "sub")),
    )
    out_specs = P(("groups", "owner", "helper", "sub"))
    body = body_by_chip if mesh.shape["helper"] == CL_OWN else body_by_owner
    return jax.shard_map(body, mesh=mesh, in_specs=in_specs, out_specs=out_specs, check_vma=False)
```

```python
import functools
import math

import jax
import jax.numpy as jnp
from jax import lax
from jax.experimental import pallas as pl
from jax.experimental.pallas import tpu as pltpu
from jax.sharding import PartitionSpec as P

CL_OWN = 2

epsilon = 1e-06
threshold = 0.8
sharpness = 0.05

EMPTY = 4.0
TILE = 256
VMEM = pl.BlockSpec(memory_space=pltpu.VMEM)


def slots_of(ids, clusters, capacity):
    doc_count = ids.shape[1]
    member = lax.broadcasted_iota(jnp.int32, (clusters, doc_count), 0) == ids
    earlier = lax.broadcasted_iota(jnp.int32, (doc_count, doc_count), 0) < (
        lax.broadcasted_iota(jnp.int32, (doc_count, doc_count), 1)
    )
    ahead = jnp.dot(
        member.astype(jnp.bfloat16), earlier.astype(jnp.bfloat16), preferred_element_type=jnp.float32
    )
    rank = jnp.sum(jnp.where(member, ahead, 0.0), axis=0, keepdims=True).astype(jnp.int32)
    return ids * capacity + rank


def lay(rows_ref, slot, slots):
    doc_count, feature_count = rows_ref.shape
    dispatch = lax.broadcasted_iota(jnp.int32, (slots, doc_count), 0) == slot
    filled = jnp.sum(dispatch.astype(jnp.float32), axis=1, keepdims=True) > 0
    laid = jnp.dot(
        dispatch.astype(jnp.bfloat16), rows_ref[...], preferred_element_type=jnp.float32
    )
    factor = lax.rsqrt(
        jnp.mean(laid * laid, axis=-1, keepdims=True) + epsilon
    ) * feature_count ** (-0.5)
    lane = lax.broadcasted_iota(jnp.int32, laid.shape, 1)
    return jnp.where(filled | (lane > 0), laid * factor, EMPTY).astype(jnp.bfloat16)


def route_kernel(clusters, capacity, rows_ref, ids_ref, piece_ref, slot_ref):
    slot = slots_of(ids_ref[...], clusters, capacity)
    slot_ref[...] = slot
    piece_ref[...] = lay(rows_ref, slot, piece_ref.shape[0])


def call_kernel(name, kernel, out_shape, *args, limit=32 * 2**20, flops=0):
    cost = pl.CostEstimate(flops=flops, bytes_accessed=0, transcendentals=0) if flops else None
    return pl.pallas_call(
        kernel,
        out_shape=out_shape,
        in_specs=[VMEM] * len(args),
        out_specs=jax.tree.map(lambda _: VMEM, out_shape),
        compiler_params=pltpu.CompilerParams(vmem_limit_bytes=limit),
        cost_estimate=cost,
        name=name,
    )(*args)


def unit_rows_of(rows):
    widened = rows.astype(jnp.float32)
    factor = lax.rsqrt(
        jnp.mean(widened * widened, axis=-1, keepdims=True) + epsilon
    ) * rows.shape[1] ** (-0.5)
    return (widened * factor).astype(jnp.bfloat16)


def weights_of(others, own):
    scores = lax.dot_general(
        others, own, (((1,), (1,)), ((), ())), preferred_element_type=jnp.float32
    )
    slope = -math.log2(math.e) / sharpness
    return 1.0 / (1.0 + jnp.exp2(scores * slope - threshold * slope))


def count_kernel(*refs):
    *piece_refs, count_ref = refs
    own = piece_refs[0][...]
    total = jnp.zeros((1, own.shape[0]), jnp.float32)
    for k, piece in enumerate(piece_refs):
        for first in range(0, piece.shape[0], TILE):
            other = piece[first : first + TILE]
            weights = weights_of(other, own)
            keep = other[:, :1].astype(jnp.float32) < 0.5 * EMPTY
            if k == 0:
                keep = keep & (
                    lax.broadcasted_iota(jnp.int32, weights.shape, 0) + first
                    != lax.broadcasted_iota(jnp.int32, weights.shape, 1)
                )
            total = total + jnp.sum(jnp.where(keep, weights, 0.0), axis=0, keepdims=True)
    count_ref[...] = total


def soft_counts(pieces):
    out_shape = jax.ShapeDtypeStruct((1, pieces[0].shape[0]), jnp.float32)
    return call_kernel("count", count_kernel, out_shape, *pieces)


def column_of(row):
    size = row.shape[1]
    diagonal = lax.broadcasted_iota(jnp.int32, (size, size), 0) == (
        lax.broadcasted_iota(jnp.int32, (size, size), 1)
    )
    return jnp.sum(jnp.where(diagonal, row, 0), axis=1, keepdims=True)


def pair_counts(others, other_ids, own, own_ids, itself=None):
    weights = weights_of(others, own)
    keep = column_of(other_ids) == own_ids
    if itself is not None:
        keep = keep & (
            lax.broadcasted_iota(jnp.int32, weights.shape, 0)
            != lax.broadcasted_iota(jnp.int32, weights.shape, 1) + itself
        )
    return jnp.sum(jnp.where(keep, weights, 0.0), axis=0, keepdims=True)


def pair_up_kernel(first_ref, second_ref, out_ref):
    rows = first_ref.shape[0]
    out_ref[:rows] = first_ref[...]
    out_ref[rows:] = second_ref[...]


def pair_up(first, second):
    out_shape = jax.ShapeDtypeStruct((2 * first.shape[0], first.shape[1]), first.dtype)
    return call_kernel("pair_up", pair_up_kernel, out_shape, first, second)


OWN, OTHER, END, END_OTHER = range(4)


def first_kernel(ids_ref, next_ids_ref, across_ids_ref, *refs):
    *piece_refs, across_ref, unit_ref, across_unit_ref = refs[:-3]
    count_refs = refs[-3:]
    own, own_other, next_own, next_other, end_a, end_b, end_other_a, end_other_b = piece_refs
    blocks = [
        ([own], ids_ref, OWN),
        ([end_a, end_b], ids_ref, END),
        ([own_other], ids_ref, OTHER),
        ([end_other_a, end_other_b], ids_ref, END_OTHER),
        ([next_own], next_ids_ref, OWN),
        ([next_other], next_ids_ref, OTHER),
    ]
    size = own.shape[0]
    for k, (pieces, _, _) in enumerate(blocks):
        first = k * size
        for piece in pieces:
            unit_ref[first : first + piece.shape[0]] = unit_rows_of(piece[...])
            first += piece.shape[0]
    across_unit_ref[...] = unit_rows_of(across_ref[...])
    wanted = [
        (unit_ref[:size], ids_ref[OWN : OWN + 1], 0),
        (unit_ref[size : 2 * size], ids_ref[END : END + 1], 1),
        (across_unit_ref[...], across_ids_ref[OWN : OWN + 1], -1),
    ]
    for j, (rows, row_ids, place) in enumerate(wanted):
        total = jnp.zeros((1, size), jnp.float32)
        for k, (_, block_ids, which) in enumerate(blocks):
            total = total + pair_counts(
                unit_ref[k * size : (k + 1) * size],
                block_ids[which : which + 1],
                rows,
                row_ids,
                0 if k == place else None,
            )
        count_refs[j][...] = total


def more_kernel(half, ids_ref, next_ids_ref, across_ids_ref, unit_ref, across_unit_ref, *refs):
    far, far_other, across_end, *refs = refs
    if half == 0:
        *refs, far_unit_ref, end_unit_ref = refs
    else:
        before_ref, before_end_ref, end_count_ref, *refs = refs
    *refs, end_out_ref = refs
    count_refs, out_refs = refs[:3], refs[3:]
    size = ids_ref.shape[1]
    part = far.shape[0]
    lanes = slice(half * part, (half + 1) * part)
    fresh = jnp.concatenate([unit_rows_of(far[...]), unit_rows_of(far_other[...])], axis=0)
    fresh_ids = jnp.concatenate(
        [next_ids_ref[END : END + 1, lanes], next_ids_ref[END_OTHER : END_OTHER + 1, lanes]], axis=1
    )
    end = unit_rows_of(across_end[...])
    end_ids = across_ids_ref[END : END + 1, lanes]
    wanted = [
        (unit_ref[:size], ids_ref[OWN : OWN + 1]),
        (unit_ref[size : 2 * size], ids_ref[END : END + 1]),
        (across_unit_ref[...], across_ids_ref[OWN : OWN + 1]),
    ]
    for j, (rows, row_ids) in enumerate(wanted):
        out_refs[j][...] = count_refs[j][...] + pair_counts(fresh, fresh_ids, rows, row_ids)

    def against_column(rows, row_ids):
        total = pair_counts(fresh, fresh_ids, rows, row_ids)
        blocks = [(ids_ref, OWN), (ids_ref, END), (ids_ref, OTHER), (ids_ref, END_OTHER)]
        blocks += [(next_ids_ref, OWN), (next_ids_ref, OTHER)]
        for k, (block_ids, which) in enumerate(blocks):
            total = total + pair_counts(
                unit_ref[k * size : (k + 1) * size], block_ids[which : which + 1], rows, row_ids
            )
        return total

    if half == 0:
        far_unit_ref[...] = fresh
        end_unit_ref[...] = end
        end_out_ref[...] = against_column(end, end_ids)
    else:
        before_ids = jnp.concatenate(
            [next_ids_ref[END : END + 1, :part], next_ids_ref[END_OTHER : END_OTHER + 1, :part]],
            axis=1,
        )
        end_out_ref[:, :part] = end_count_ref[...] + pair_counts(
            fresh, fresh_ids, before_end_ref[...], across_ids_ref[END : END + 1, :part]
        )
        end_out_ref[:, part:] = against_column(end, end_ids) + pair_counts(
            before_ref[...], before_ids, end, end_ids
        )


def add_kernel(counts_ref, x_ref, z_ref, xz_ref, out_ref):
    owner = lax.axis_index("owner")
    own = jnp.where((owner == 1) | (owner == 2), counts_ref[...], 0.0)
    out_ref[...] = own + x_ref[...] + z_ref[...] + xz_ref[...]


def select_kernel(capacity, counts_ref, slot_ref, out_ref):
    counts = counts_ref[:, 0, :]
    slot = slot_ref[...]
    doc_count = slot.shape[1]
    block = slot // capacity
    rank = slot - block * capacity
    hot = (lax.broadcasted_iota(jnp.int32, (capacity, doc_count), 0) == rank).astype(jnp.float32)
    by_block = jnp.dot(
        counts, hot, precision=lax.Precision.HIGHEST, preferred_element_type=jnp.float32
    )
    chosen = lax.broadcasted_iota(jnp.int32, by_block.shape, 0) == block
    out_ref[...] = jnp.sum(jnp.where(chosen, by_block, 0.0), axis=0, keepdims=True)


def select(counts, slot, capacity):
    out_shape = jax.ShapeDtypeStruct(slot.shape, jnp.float32)
    kernel = functools.partial(select_kernel, capacity)
    return call_kernel("select", kernel, out_shape, counts, slot, limit=8 * 2**20)[0]


def swap_cores(x):
    cores = lax.axis_size("sub")
    return lax.ppermute(x, "sub", [(i, i ^ 1) for i in range(cores)])


def body_by_column(embeddings, cluster_id):
    doc_count, feature_count = embeddings.shape
    helpers, cores = lax.axis_size("helper"), lax.axis_size("sub")
    part = doc_count // 2

    def send(x, hops, turn=0, swap=0):
        pairs = [
            (
                (here * helpers + h) * cores + c,
                (there * helpers + (h ^ turn)) * cores + (c ^ swap),
            )
            for here, there in hops
            for h in range(helpers)
            for c in range(cores)
        ]
        return lax.ppermute(x, ("owner", "helper", "sub"), pairs)

    inwards, outwards = [(0, 1), (3, 2)], [(1, 0), (2, 3)]
    middle, still = [(1, 2), (2, 1)], [(1, 1), (2, 2)]

    ids = cluster_id.reshape(1, doc_count)
    next_own = send(embeddings, middle)
    across = send(embeddings, still, turn=1)
    own_other = send(embeddings, still, swap=1)
    end = [send(embeddings[first : first + part], inwards) for first in (0, part)]
    here_ids = pair_up(ids, swap_cores(ids))
    here_ids = pair_up(here_ids, send(here_ids, inwards))
    next_ids = send(here_ids, middle)
    across_ids = send(here_ids, still, turn=1)
    end_other = [send(x, still, swap=1) for x in end]
    far = [send(x, middle) for x in end]
    across_end = [send(x, still, turn=1) for x in end]
    next_other = send(next_own, still, swap=1)
    far_other = [send(x, still, swap=1) for x in far]

    rows = functools.partial(jax.ShapeDtypeStruct, dtype=jnp.bfloat16)
    sums = functools.partial(jax.ShapeDtypeStruct, dtype=jnp.float32)
    all_ids = (here_ids, next_ids, across_ids)
    units, across_units, *counts = call_kernel(
        "first",
        first_kernel,
        [
            rows((6 * doc_count, feature_count)),
            rows((doc_count, feature_count)),
        ]
        + [sums((1, doc_count))] * 3,
        *all_ids,
        embeddings,
        own_other,
        next_own,
        next_other,
        *end,
        *end_other,
        across,
    )
    *counts, end_counts, far_units, end_units = call_kernel(
        "more",
        functools.partial(more_kernel, 0),
        [sums((1, doc_count))] * 3
        + [
            sums((1, part)),
            rows((2 * part, feature_count)),
            rows((part, feature_count)),
        ],
        *all_ids,
        units,
        across_units,
        far[0],
        far_other[0],
        across_end[0],
        *counts,
    )
    *counts, end_counts = call_kernel(
        "last",
        functools.partial(more_kernel, 1),
        [sums((1, doc_count))] * 4,
        *all_ids,
        units,
        across_units,
        far[1],
        far_other[1],
        across_end[1],
        far_units,
        end_units,
        end_counts,
        *counts,
    )
    own_counts, inner_counts, across_counts = counts
    return call_kernel(
        "add",
        add_kernel,
        sums((1, doc_count)),
        own_counts,
        send(across_counts, still, turn=1),
        send(inner_counts, outwards),
        send(end_counts, outwards, turn=1),
        limit=8 * 2**20,
    )[0]


def body_by_owner(embeddings, cluster_id):
    doc_count, feature_count = embeddings.shape
    owners, helpers = lax.axis_size("owner"), lax.axis_size("helper")
    clusters = CL_OWN * owners
    capacity = 2 * doc_count // clusters
    mine = lax.axis_index("helper") % CL_OWN

    def partner(x):
        return lax.ppermute(x, "helper", [(i, i ^ 1) for i in range(helpers)])

    outgoing, slot = call_kernel(
        "route",
        functools.partial(route_kernel, clusters, capacity),
        [
            jax.ShapeDtypeStruct((clusters * capacity, feature_count), jnp.bfloat16),
            jax.ShapeDtypeStruct((1, doc_count), jnp.int32),
        ],
        embeddings,
        cluster_id.reshape(1, doc_count),
    )
    outgoing = outgoing.reshape(owners, CL_OWN, capacity, feature_count)
    arrived = lax.all_to_all(outgoing, "owner", split_axis=0, concat_axis=0, tiled=True)
    kept = lax.dynamic_index_in_dim(arrived, mine, 1, keepdims=False)
    given = partner(lax.dynamic_index_in_dim(arrived, 1 - mine, 1, keepdims=False))
    own = jnp.stack([kept, given]).reshape(CL_OWN * owners * capacity, feature_count)
    others = [swap_cores(own)]
    for step in range(CL_OWN, helpers, CL_OWN):
        turn = [(i, (i + step) % helpers) for i in range(helpers)]
        others += [lax.ppermute(x, "helper", turn) for x in (own, others[0])]
    counts = soft_counts([own, *others])
    counts = counts.reshape(CL_OWN, owners, capacity)
    kept, given = counts[0], partner(counts[1])
    counts = jnp.where(mine == 0, jnp.stack([kept, given], 1), jnp.stack([given, kept], 1))
    back = lax.all_to_all(counts, "owner", split_axis=0, concat_axis=0, tiled=True)
    return select(back.reshape(clusters, 1, capacity), slot, capacity)


def solution(mesh):
    in_specs = (
        P(("groups", "owner", "helper", "sub"), None),
        P(("groups", "owner", "helper", "sub")),
    )
    out_specs = P(("groups", "owner", "helper", "sub"))
    columns = tuple(mesh.shape[axis] for axis in ("owner", "helper", "sub")) == (4, 2, 2)
    body = body_by_column if columns else body_by_owner
    return jax.shard_map(body, mesh=mesh, in_specs=in_specs, out_specs=out_specs, check_vma=False)
```

```python
import functools
import math

import jax
import jax.numpy as jnp
from jax import lax
from jax.experimental import pallas as pl
from jax.experimental.pallas import tpu as pltpu
from jax.sharding import PartitionSpec as P

CL_OWN = 2

epsilon = 1e-06
threshold = 0.8
sharpness = 0.05

EMPTY = 4.0
TILE = 256
ID_ROWS = 16
VMEM = pl.BlockSpec(memory_space=pltpu.VMEM)


def slots_of(ids, clusters, capacity):
    doc_count = ids.shape[1]
    member = lax.broadcasted_iota(jnp.int32, (clusters, doc_count), 0) == ids
    earlier = lax.broadcasted_iota(jnp.int32, (doc_count, doc_count), 0) < (
        lax.broadcasted_iota(jnp.int32, (doc_count, doc_count), 1)
    )
    ahead = jnp.dot(
        member.astype(jnp.bfloat16), earlier.astype(jnp.bfloat16), preferred_element_type=jnp.float32
    )
    rank = jnp.sum(jnp.where(member, ahead, 0.0), axis=0, keepdims=True).astype(jnp.int32)
    return ids * capacity + rank


def lay(rows_ref, slot, slots):
    doc_count, feature_count = rows_ref.shape
    dispatch = lax.broadcasted_iota(jnp.int32, (slots, doc_count), 0) == slot
    filled = jnp.sum(dispatch.astype(jnp.float32), axis=1, keepdims=True) > 0
    laid = jnp.dot(
        dispatch.astype(jnp.bfloat16), rows_ref[...], preferred_element_type=jnp.float32
    )
    factor = lax.rsqrt(
        jnp.mean(laid * laid, axis=-1, keepdims=True) + epsilon
    ) * feature_count ** (-0.5)
    lane = lax.broadcasted_iota(jnp.int32, laid.shape, 1)
    return jnp.where(filled | (lane > 0), laid * factor, EMPTY).astype(jnp.bfloat16)


def route_kernel(clusters, capacity, rows_ref, ids_ref, piece_ref, slot_ref):
    slot = slots_of(ids_ref[...], clusters, capacity)
    slot_ref[...] = slot
    piece_ref[...] = lay(rows_ref, slot, piece_ref.shape[0])


def call_kernel(name, kernel, out_shape, *args, limit=32 * 2**20, flops=0):
    cost = pl.CostEstimate(flops=flops, bytes_accessed=0, transcendentals=0) if flops else None
    return pl.pallas_call(
        kernel,
        out_shape=out_shape,
        in_specs=[VMEM] * len(args),
        out_specs=jax.tree.map(lambda _: VMEM, out_shape),
        compiler_params=pltpu.CompilerParams(vmem_limit_bytes=limit),
        cost_estimate=cost,
        name=name,
    )(*args)


def unit_rows_of(rows):
    widened = rows.astype(jnp.float32)
    factor = lax.rsqrt(
        jnp.mean(widened * widened, axis=-1, keepdims=True) + epsilon
    ) * rows.shape[1] ** (-0.5)
    return (widened * factor).astype(jnp.bfloat16)


def weights_of(others, own):
    scores = lax.dot_general(
        others, own, (((1,), (1,)), ((), ())), preferred_element_type=jnp.float32
    )
    slope = -math.log2(math.e) / sharpness
    return 1.0 / (1.0 + jnp.exp2(scores * slope - threshold * slope))


def count_kernel(*refs):
    *piece_refs, count_ref = refs
    own = piece_refs[0][...]
    total = jnp.zeros((1, own.shape[0]), jnp.float32)
    for k, piece in enumerate(piece_refs):
        for first in range(0, piece.shape[0], TILE):
            other = piece[first : first + TILE]
            weights = weights_of(other, own)
            keep = other[:, :1].astype(jnp.float32) < 0.5 * EMPTY
            if k == 0:
                keep = keep & (
                    lax.broadcasted_iota(jnp.int32, weights.shape, 0) + first
                    != lax.broadcasted_iota(jnp.int32, weights.shape, 1)
                )
            total = total + jnp.sum(jnp.where(keep, weights, 0.0), axis=0, keepdims=True)
    count_ref[...] = total


def soft_counts(pieces):
    out_shape = jax.ShapeDtypeStruct((1, pieces[0].shape[0]), jnp.float32)
    return call_kernel("count", count_kernel, out_shape, *pieces)


def column_of(row):
    size = row.shape[1]
    diagonal = lax.broadcasted_iota(jnp.int32, (size, size), 0) == (
        lax.broadcasted_iota(jnp.int32, (size, size), 1)
    )
    return jnp.sum(jnp.where(diagonal, row, 0.0), axis=1, keepdims=True)


def pair_counts(others, other_ids, own, own_ids, itself=None):
    weights = weights_of(others, own)
    keep = column_of(other_ids) == own_ids
    if itself is not None:
        keep = keep & (
            lax.broadcasted_iota(jnp.int32, weights.shape, 0)
            != lax.broadcasted_iota(jnp.int32, weights.shape, 1) + itself
        )
    return jnp.sum(jnp.where(keep, weights, 0.0), axis=0, keepdims=True)


def prepare_kernel(rows_ref, ids_ref, whole_ref, first_ref, second_ref):
    doc_count, feature_count = rows_ref.shape
    part = doc_count // 2
    unit = unit_rows_of(rows_ref[...])
    ids = ids_ref[...].astype(jnp.float32)
    for first, piece_ref in ((0, whole_ref), (0, first_ref), (part, second_ref)):
        count = piece_ref.shape[0] - ID_ROWS
        some = jnp.concatenate(
            [ids[:, first : first + count], jnp.zeros((1, feature_count - count), jnp.float32)], axis=1
        )
        piece_ref[:count] = unit[first : first + count]
        piece_ref[count:] = jnp.broadcast_to(some, (ID_ROWS, feature_count)).astype(jnp.bfloat16)


def both(*pieces):
    counts = [piece.shape[0] - ID_ROWS for piece in pieces]
    rows = [piece[:count] for piece, count in zip(pieces, counts)]
    ids = [piece[count:, :count].astype(jnp.float32)[:1] for piece, count in zip(pieces, counts)]
    return jnp.concatenate(rows, axis=0), jnp.concatenate(ids, axis=1)


def first_kernel(
    own, across, end_a, end_b, own_other, end_other_a, end_other_b, next_own, next_other, *count_refs
):
    wanted = [both(own), both(end_a, end_b), both(across)]
    blocks = [*wanted[:2], both(own_other), both(end_other_a, end_other_b)]
    blocks += [both(next_own), both(next_other)]
    for j, mine in enumerate(wanted):
        count_refs[j][...] = sum(
            pair_counts(*block, *mine, 0 if j == k < 2 else None) for k, block in enumerate(blocks)
        )


def more_kernel(
    half, own, across, end_a, end_b, own_other, end_other_a, end_other_b, next_own, next_other, *refs
):
    far_a, far_other_a, across_a, *refs = refs
    fresh, end = both(far_a, far_other_a), both(across_a)
    if half == 1:
        far_b, far_other_b, across_b, end_count_ref, *refs = refs
        before, end_before = fresh, end
        fresh, end = both(far_b, far_other_b), both(across_b)
    count_refs, out_refs, end_out_ref = refs[:3], refs[3:6], refs[6]
    wanted = [both(own), both(end_a, end_b), both(across)]
    for j, mine in enumerate(wanted):
        out_refs[j][...] = count_refs[j][...] + pair_counts(*fresh, *mine)
    blocks = [fresh, *wanted[:2], both(own_other), both(end_other_a, end_other_b)]
    blocks += [both(next_own), both(next_other)]
    if half == 0:
        end_out_ref[...] = sum(pair_counts(*block, *end) for block in blocks)
    else:
        part = end_count_ref.shape[1]
        end_out_ref[:, part:] = sum(pair_counts(*block, *end) for block in [*blocks, before])
        end_out_ref[:, :part] = end_count_ref[...] + pair_counts(*fresh, *end_before)


def add_kernel(counts_ref, x_ref, z_ref, xz_ref, out_ref):
    owner = lax.axis_index("owner")
    middle = (owner == 1) | (owner == 2)
    out_ref[...] = jnp.where(middle, counts_ref[...] + x_ref[...], z_ref[...] + xz_ref[...])


def select_kernel(capacity, counts_ref, slot_ref, out_ref):
    counts = counts_ref[:, 0, :]
    slot = slot_ref[...]
    doc_count = slot.shape[1]
    block = slot // capacity
    rank = slot - block * capacity
    hot = (lax.broadcasted_iota(jnp.int32, (capacity, doc_count), 0) == rank).astype(jnp.float32)
    by_block = jnp.dot(
        counts, hot, precision=lax.Precision.HIGHEST, preferred_element_type=jnp.float32
    )
    chosen = lax.broadcasted_iota(jnp.int32, by_block.shape, 0) == block
    out_ref[...] = jnp.sum(jnp.where(chosen, by_block, 0.0), axis=0, keepdims=True)


def select(counts, slot, capacity):
    out_shape = jax.ShapeDtypeStruct(slot.shape, jnp.float32)
    kernel = functools.partial(select_kernel, capacity)
    return call_kernel("select", kernel, out_shape, counts, slot, limit=8 * 2**20)[0]


def swap_cores(x):
    cores = lax.axis_size("sub")
    return lax.ppermute(x, "sub", [(i, i ^ 1) for i in range(cores)])


def body_by_column(embeddings, cluster_id):
    doc_count, feature_count = embeddings.shape
    helpers, cores = lax.axis_size("helper"), lax.axis_size("sub")
    part = doc_count // 2

    def send(x, owners=(0, 1, 2, 3), turn=0, swap=0):
        pairs = [
            (
                (here * helpers + h) * cores + c,
                (there * helpers + (h ^ turn)) * cores + (c ^ swap),
            )
            for here, there in enumerate(owners)
            for h in range(helpers)
            for c in range(cores)
        ]
        return lax.ppermute(x, ("owner", "helper", "sub"), pairs)

    neighbours, middle = (1, 0, 3, 2), (0, 2, 1, 3)

    def rows(count):
        return jax.ShapeDtypeStruct((count, feature_count), jnp.bfloat16)

    def sums(count):
        return jax.ShapeDtypeStruct((1, count), jnp.float32)

    own, own_a, own_b = call_kernel(
        "prepare",
        prepare_kernel,
        [rows(count + ID_ROWS) for count in (doc_count, part, part)],
        embeddings,
        cluster_id.reshape(1, doc_count),
    )
    next_own = send(own, middle)
    across = send(own, turn=1)
    end_a, end_b = send(own_a, neighbours), send(own_b, neighbours)
    own_other = send(own, swap=1)
    far_a, far_b = send(end_a, middle), send(end_b, middle)
    across_a, across_b = send(end_a, turn=1), send(end_b, turn=1)
    end_other_a, end_other_b = send(end_a, swap=1), send(end_b, swap=1)
    next_other = send(next_own, swap=1)

    column = (own, across, end_a, end_b, own_other, end_other_a, end_other_b, next_own, next_other)
    counts = call_kernel("first", first_kernel, [sums(doc_count)] * 3, *column,)
    far_other_a = send(far_a, swap=1)
    *counts, end_counts = call_kernel(
        "more",
        functools.partial(more_kernel, 0),
        [sums(doc_count)] * 3 + [sums(part)],
        *column,
        far_a,
        far_other_a,
        across_a,
        *counts,
    )
    far_b, _ = lax.optimization_barrier((far_b, counts[0]))
    far_other_b = send(far_b, swap=1)
    *counts, end_counts = call_kernel(
        "last",
        functools.partial(more_kernel, 1),
        [sums(doc_count)] * 4,
        *column,
        far_a,
        far_other_a,
        across_a,
        far_b,
        far_other_b,
        across_b,
        end_counts,
        *counts,
    )
    own_counts, inner_counts, across_counts = counts
    return call_kernel(
        "add",
        add_kernel,
        sums(doc_count),
        own_counts,
        send(across_counts, turn=1),
        send(inner_counts, neighbours),
        send(end_counts, neighbours, turn=1),
        limit=8 * 2**20,
    )[0]


def body_by_owner(embeddings, cluster_id):
    doc_count, feature_count = embeddings.shape
    owners, helpers = lax.axis_size("owner"), lax.axis_size("helper")
    clusters = CL_OWN * owners
    capacity = 2 * doc_count // clusters
    mine = lax.axis_index("helper") % CL_OWN

    def partner(x):
        return lax.ppermute(x, "helper", [(i, i ^ 1) for i in range(helpers)])

    outgoing, slot = call_kernel(
        "route",
        functools.partial(route_kernel, clusters, capacity),
        [
            jax.ShapeDtypeStruct((clusters * capacity, feature_count), jnp.bfloat16),
            jax.ShapeDtypeStruct((1, doc_count), jnp.int32),
        ],
        embeddings,
        cluster_id.reshape(1, doc_count),
    )
    outgoing = outgoing.reshape(owners, CL_OWN, capacity, feature_count)
    arrived = lax.all_to_all(outgoing, "owner", split_axis=0, concat_axis=0, tiled=True)
    kept = lax.dynamic_index_in_dim(arrived, mine, 1, keepdims=False)
    given = partner(lax.dynamic_index_in_dim(arrived, 1 - mine, 1, keepdims=False))
    own = jnp.stack([kept, given]).reshape(CL_OWN * owners * capacity, feature_count)
    others = [swap_cores(own)]
    for step in range(CL_OWN, helpers, CL_OWN):
        turn = [(i, (i + step) % helpers) for i in range(helpers)]
        others += [lax.ppermute(x, "helper", turn) for x in (own, others[0])]
    counts = soft_counts([own, *others])
    counts = counts.reshape(CL_OWN, owners, capacity)
    kept, given = counts[0], partner(counts[1])
    counts = jnp.where(mine == 0, jnp.stack([kept, given], 1), jnp.stack([given, kept], 1))
    back = lax.all_to_all(counts, "owner", split_axis=0, concat_axis=0, tiled=True)
    return select(back.reshape(clusters, 1, capacity), slot, capacity)


def solution(mesh):
    in_specs = (
        P(("groups", "owner", "helper", "sub"), None),
        P(("groups", "owner", "helper", "sub")),
    )
    out_specs = P(("groups", "owner", "helper", "sub"))
    columns = tuple(mesh.shape[axis] for axis in ("owner", "helper", "sub")) == (4, 2, 2)
    body = body_by_column if columns else body_by_owner
    return jax.shard_map(body, mesh=mesh, in_specs=in_specs, out_specs=out_specs, check_vma=False)
```

```python
import functools
import math

import jax
import jax.numpy as jnp
from jax import lax
from jax.experimental import pallas as pl
from jax.experimental.pallas import tpu as pltpu
from jax.sharding import PartitionSpec as P

CL_OWN = 2

epsilon = 1e-06
threshold = 0.8
sharpness = 0.05

EMPTY = 4.0
TILE = 256
VMEM = pl.BlockSpec(memory_space=pltpu.VMEM)


def chip_index():
    return lax.axis_index("owner") * CL_OWN + lax.axis_index("helper")


def slots_of(ids, clusters, capacity):
    doc_count = ids.shape[1]
    member = lax.broadcasted_iota(jnp.int32, (clusters, doc_count), 0) == ids
    earlier = lax.broadcasted_iota(jnp.int32, (doc_count, doc_count), 0) < (
        lax.broadcasted_iota(jnp.int32, (doc_count, doc_count), 1)
    )
    ahead = jnp.dot(
        member.astype(jnp.bfloat16), earlier.astype(jnp.bfloat16), preferred_element_type=jnp.float32
    )
    rank = jnp.sum(jnp.where(member, ahead, 0.0), axis=0, keepdims=True).astype(jnp.int32)
    return ids * capacity + rank


def lay(rows_ref, slot, slots):
    doc_count, feature_count = rows_ref.shape
    dispatch = lax.broadcasted_iota(jnp.int32, (slots, doc_count), 0) == slot
    filled = jnp.sum(dispatch.astype(jnp.float32), axis=1, keepdims=True) > 0
    laid = jnp.dot(
        dispatch.astype(jnp.bfloat16), rows_ref[...], preferred_element_type=jnp.float32
    )
    factor = lax.rsqrt(
        jnp.mean(laid * laid, axis=-1, keepdims=True) + epsilon
    ) * feature_count ** (-0.5)
    lane = lax.broadcasted_iota(jnp.int32, laid.shape, 1)
    return jnp.where(filled | (lane > 0), laid * factor, EMPTY).astype(jnp.bfloat16)


def slots_of_steps(slot, capacity, steps):
    cores = lax.axis_size("sub")
    by_distance = slot ^ (chip_index() * capacity)
    distance = by_distance // capacity
    rank = by_distance - distance * capacity
    step = jnp.full_like(slot, -1)
    for place, p in enumerate(steps):
        step = jnp.where(distance == p * cores + lax.axis_index("sub"), place, step)
    return jnp.where(step < 0, -1, step * capacity + rank)


def route_first_kernel(clusters, capacity, step, rows_ref, ids_ref, piece_ref, slot_ref):
    slot = slots_of(ids_ref[...], clusters, capacity)
    slot_ref[...] = slot
    piece_ref[...] = lay(rows_ref, slots_of_steps(slot, capacity, [step]), capacity)


def route_rest_kernel(clusters, capacity, first, steps, *refs):
    own_rows, other_rows, own_slot, other_ids, first_ref, *piece_refs = refs
    slot = slots_of_steps(own_slot[...], capacity, steps)
    laid = lay(own_rows, slot, len(steps) * capacity)
    for k, piece in enumerate(piece_refs):
        piece[:capacity] = laid[k * capacity : (k + 1) * capacity]
    slot = slots_of(other_ids[...], clusters, capacity)
    slot = slots_of_steps(slot, capacity, [first, *steps])
    laid = lay(other_rows, slot, (1 + len(steps)) * capacity)
    first_ref[...] = laid[:capacity]
    for k, piece in enumerate(piece_refs):
        piece[capacity:] = laid[(k + 1) * capacity : (k + 2) * capacity]


def route_kernel(clusters, capacity, rows_ref, ids_ref, piece_ref, slot_ref):
    slot = slots_of(ids_ref[...], clusters, capacity)
    slot_ref[...] = slot
    piece_ref[...] = lay(rows_ref, slot, piece_ref.shape[0])


def call_kernel(name, kernel, out_shape, *args, limit=32 * 2**20, flops=0):
    cost = pl.CostEstimate(flops=flops, bytes_accessed=0, transcendentals=0) if flops else None
    return pl.pallas_call(
        kernel,
        out_shape=out_shape,
        in_specs=[VMEM] * len(args),
        out_specs=jax.tree.map(lambda _: VMEM, out_shape),
        compiler_params=pltpu.CompilerParams(vmem_limit_bytes=limit),
        cost_estimate=cost,
        name=name,
    )(*args)


def join_kernel(first_ref, second_ref, out_ref):
    rows = first_ref.shape[0]
    out_ref[:rows] = first_ref[...]
    out_ref[rows:] = second_ref[...]


def blocks(rows, starts, size):
    return jnp.concatenate([rows[start : start + size] for start in starts], axis=0)


def count_against(rows, own, starts, size):
    column = lax.broadcasted_iota(jnp.int32, (1, own.shape[0]), 1)
    itself = jnp.full_like(column, -1)
    for k, start in enumerate(starts):
        itself = jnp.where(column // size == k, column + (start - k * size), itself)
    slope = -math.log2(math.e) / sharpness
    total = jnp.zeros((1, own.shape[0]), jnp.float32)
    for first in range(0, rows.shape[0], TILE):
        other = rows[first : first + TILE]
        scores = lax.dot_general(
            other, own, (((1,), (1,)), ((), ())), preferred_element_type=jnp.float32
        )
        weights = 1.0 / (1.0 + jnp.exp2(scores * slope - threshold * slope))
        keep = other[:, :1].astype(jnp.float32) < 0.5 * EMPTY
        if starts:
            keep = keep & (lax.broadcasted_iota(jnp.int32, scores.shape, 0) + first != itself)
        total = total + jnp.sum(jnp.where(keep, weights, 0.0), axis=0, keepdims=True)
    return total


def count_kernel(starts, size, *refs):
    *piece_refs, count_ref = refs
    rows = jnp.concatenate([piece[...] for piece in piece_refs], axis=0)
    count_ref[...] = count_against(rows, blocks(rows, starts, size), starts, size)


def soft_counts(pieces, starts, size):
    out_shape = jax.ShapeDtypeStruct((1, len(starts) * size), jnp.float32)
    return call_kernel("count", functools.partial(count_kernel, starts, size), out_shape, *pieces)


def finish_kernel(starts, late_pieces, late_starts, distances, *refs):
    *piece_refs, early_ref = refs[:-2]
    halves = refs[-2:]
    size = halves[0].shape[1]
    early = jnp.concatenate([piece[...] for piece in piece_refs[:-late_pieces]], axis=0)
    late = jnp.concatenate([piece[...] for piece in piece_refs[-late_pieces:]], axis=0)
    own = blocks(early, starts, size)
    late_own = blocks(late, late_starts, size)
    total = early_ref[...] + count_against(late, own, [], size)
    late_total = count_against(early, late_own, [], size) + count_against(
        late, late_own, late_starts, size
    )
    for k, distance in enumerate(distances()):
        source, j = (total, k) if k < len(starts) else (late_total, k - len(starts))
        block = source[:, j * size : (j + 1) * size]
        keep_ref, send_ref = halves
        half = keep_ref.shape[0]
        for ref, first in ((keep_ref, 0), (send_ref, half)):

            @pl.when((distance >= first) & (distance < first + half))
            def _(ref=ref, first=first, block=block, distance=distance):
                ref[pl.ds(distance - first, 1), :] = block


def deal_kernel(width, keep_ref, got_ref, stay_ref, send_ref):
    blocks = jnp.concatenate([keep_ref[...], got_ref[...]], axis=0)
    stay, send = [], []
    for first in range(0, blocks.shape[0], 2 * width):
        stay.append(blocks[first : first + width])
        send.append(blocks[first + width : first + 2 * width])
    stay_ref[...] = jnp.concatenate(stay, axis=0)
    send_ref[...] = jnp.concatenate(send, axis=0)


def select_kernel(capacity, counts_ref, slot_ref, out_ref):
    counts = counts_ref[:, 0, :]
    slot = slot_ref[...]
    doc_count = slot.shape[1]
    block = slot // capacity
    rank = slot - block * capacity
    hot = (lax.broadcasted_iota(jnp.int32, (capacity, doc_count), 0) == rank).astype(jnp.float32)
    by_block = jnp.dot(
        counts, hot, precision=lax.Precision.HIGHEST, preferred_element_type=jnp.float32
    )
    chosen = lax.broadcasted_iota(jnp.int32, by_block.shape, 0) == block
    out_ref[...] = jnp.sum(jnp.where(chosen, by_block, 0.0), axis=0, keepdims=True)


def select(counts, slot, capacity):
    out_shape = jax.ShapeDtypeStruct(slot.shape, jnp.float32)
    kernel = functools.partial(select_kernel, capacity)
    return call_kernel("select", kernel, out_shape, counts, slot, limit=8 * 2**20)[0]


def choose_kernel(capacity, near_ref, far_ref, slot_ref, out_ref):
    counts = jnp.concatenate([near_ref[...], far_ref[...]], axis=0)
    slot = slot_ref[...]
    block = slot // capacity
    rank = slot - block * capacity
    hot = lax.broadcasted_iota(jnp.int32, (capacity, slot.shape[1]), 0) == rank
    by_block = jnp.dot(
        counts,
        hot.astype(jnp.float32),
        precision=lax.Precision.HIGHEST,
        preferred_element_type=jnp.float32,
    )
    row = lax.broadcasted_iota(jnp.int32, by_block.shape, 0)
    distance = ((row & 1) << 2) | (row & 2) | (row >> 2)
    chosen = distance == block ^ chip_index()
    out_ref[...] = jnp.sum(jnp.where(chosen, by_block, 0.0), axis=0, keepdims=True)


def swap_cores(x):
    cores = lax.axis_size("sub")
    return lax.ppermute(x, "sub", [(i, i ^ 1) for i in range(cores)])


def body_by_chip(embeddings, cluster_id):
    doc_count, feature_count = embeddings.shape
    clusters = CL_OWN * lax.axis_size("owner")
    capacity = 2 * doc_count // clusters
    cores = lax.axis_size("sub")
    steps = clusters // cores

    def across(x, p):
        pairs = [
            (chip * cores + core, (chip ^ (p * cores + core)) * cores + core)
            for chip in range(clusters)
            for core in range(cores)
        ]
        return lax.ppermute(x, ("owner", "helper", "sub"), pairs)

    def swap_chips(x, distance):
        pairs = [(chip, chip ^ distance) for chip in range(clusters)]
        return lax.ppermute(x, ("owner", "helper"), pairs)

    ids = cluster_id.reshape(1, doc_count)
    other_rows, other_ids = swap_cores(embeddings), swap_cores(ids)
    first, last = steps // 2, steps - 1
    middle = [p for p in range(steps) if p not in (first, last)]
    half = jax.ShapeDtypeStruct((capacity, feature_count), jnp.bfloat16)
    whole = jax.ShapeDtypeStruct((cores * capacity, feature_count), jnp.bfloat16)

    first_own, slot = call_kernel(
        "route_first",
        functools.partial(route_first_kernel, clusters, capacity, first),
        [half, jax.ShapeDtypeStruct((1, doc_count), jnp.int32)],
        embeddings,
        ids,
    )
    first_own = across(first_own, first)
    first_other, *rest = call_kernel(
        "route_rest",
        functools.partial(route_rest_kernel, clusters, capacity, first, [*middle, last]),
        [half] + [whole] * (steps - 1),
        embeddings,
        other_rows,
        slot,
        other_ids,
    )
    first_other = across(first_other, first)
    rest = [across(piece, p) for piece, p in zip(rest, [*middle, last])]

    first_both = call_kernel("join", join_kernel, whole, first_own, first_other, flops=10**10)
    early = [first_both, *rest[:-1]]
    early += [swap_cores(x) for x in early]
    late = [rest[-1], swap_cores(rest[-1])]
    span = cores * capacity
    half_way = span * (steps - 1)
    starts = [k * span for k in range(steps - 1)]
    starts += [half_way + start + capacity for start in starts]
    late_starts = [0, span + capacity]

    def distances():
        core = lax.axis_index("sub")
        own = [p * cores + core for p in (first, *middle, last)]
        other = [p * cores + 1 - core for p in (first, *middle, last)]
        return own[:-1] + other[:-1] + [own[-1], other[-1]]

    half_counts = [jax.ShapeDtypeStruct((clusters // 2, capacity), jnp.float32)] * 2
    keep, send = call_kernel(
        "finish",
        functools.partial(finish_kernel, starts, len(late), late_starts, distances),
        half_counts,
        *early,
        *late,
        soft_counts(early, starts, capacity),
    )
    got = swap_chips(send, 4)
    keep, send = call_kernel("deal", functools.partial(deal_kernel, 2), half_counts, keep, got)
    got = swap_chips(send, 2)
    keep, send = call_kernel("deal", functools.partial(deal_kernel, 1), half_counts, keep, got)
    got = swap_chips(send, 1)
    return call_kernel(
        "choose",
        functools.partial(choose_kernel, capacity),
        jax.ShapeDtypeStruct(slot.shape, jnp.float32),
        keep,
        got,
        slot,
        limit=8 * 2**20,
    )[0]


def body_by_owner(embeddings, cluster_id):
    doc_count, feature_count = embeddings.shape
    owners, helpers = lax.axis_size("owner"), lax.axis_size("helper")
    clusters = CL_OWN * owners
    capacity = 2 * doc_count // clusters
    mine = lax.axis_index("helper") % CL_OWN

    def partner(x):
        return lax.ppermute(x, "helper", [(i, i ^ 1) for i in range(helpers)])

    outgoing, slot = call_kernel(
        "route",
        functools.partial(route_kernel, clusters, capacity),
        [
            jax.ShapeDtypeStruct((clusters * capacity, feature_count), jnp.bfloat16),
            jax.ShapeDtypeStruct((1, doc_count), jnp.int32),
        ],
        embeddings,
        cluster_id.reshape(1, doc_count),
    )
    outgoing = outgoing.reshape(owners, CL_OWN, capacity, feature_count)
    arrived = lax.all_to_all(outgoing, "owner", split_axis=0, concat_axis=0, tiled=True)
    kept = lax.dynamic_index_in_dim(arrived, mine, 1, keepdims=False)
    given = partner(lax.dynamic_index_in_dim(arrived, 1 - mine, 1, keepdims=False))
    own = jnp.stack([kept, given]).reshape(CL_OWN * owners * capacity, feature_count)
    others = [swap_cores(own)]
    for step in range(CL_OWN, helpers, CL_OWN):
        turn = [(i, (i + step) % helpers) for i in range(helpers)]
        others += [lax.ppermute(x, "helper", turn) for x in (own, others[0])]
    counts = soft_counts([own, *others], [0], own.shape[0])
    counts = counts.reshape(CL_OWN, owners, capacity)
    kept, given = counts[0], partner(counts[1])
    counts = jnp.where(mine == 0, jnp.stack([kept, given], 1), jnp.stack([given, kept], 1))
    back = lax.all_to_all(counts, "owner", split_axis=0, concat_axis=0, tiled=True)
    return select(back.reshape(clusters, 1, capacity), slot, capacity)


def solution(mesh):
    in_specs = (
        P(("groups", "owner", "helper", "sub"), None),
        P(("groups", "owner", "helper", "sub")),
    )
    out_specs = P(("groups", "owner", "helper", "sub"))
    chips = tuple(mesh.shape[axis] for axis in ("owner", "helper", "sub"))
    body = body_by_chip if chips == (4, CL_OWN, 2) else body_by_owner
    return jax.shard_map(body, mesh=mesh, in_specs=in_specs, out_specs=out_specs, check_vma=False)
```

```python
import functools
import math

import jax
import jax.numpy as jnp
from jax import lax
from jax.experimental import pallas as pl
from jax.experimental.pallas import tpu as pltpu
from jax.sharding import PartitionSpec as P

CL_OWN = 2

epsilon = 1e-06
threshold = 0.8
sharpness = 0.05

EMPTY = 4.0
TILE = 256
VMEM = pl.BlockSpec(memory_space=pltpu.VMEM)


def chip_index():
    return lax.axis_index("owner") * CL_OWN + lax.axis_index("helper")


def slots_of(ids, clusters, capacity):
    doc_count = ids.shape[1]
    member = lax.broadcasted_iota(jnp.int32, (clusters, doc_count), 0) == ids
    earlier = lax.broadcasted_iota(jnp.int32, (doc_count, doc_count), 0) < (
        lax.broadcasted_iota(jnp.int32, (doc_count, doc_count), 1)
    )
    ahead = jnp.dot(
        member.astype(jnp.bfloat16), earlier.astype(jnp.bfloat16), preferred_element_type=jnp.float32
    )
    rank = jnp.sum(jnp.where(member, ahead, 0.0), axis=0, keepdims=True).astype(jnp.int32)
    return ids * capacity + rank


def lay(rows_ref, slot, slots):
    doc_count, feature_count = rows_ref.shape
    dispatch = lax.broadcasted_iota(jnp.int32, (slots, doc_count), 0) == slot
    filled = jnp.sum(dispatch.astype(jnp.float32), axis=1, keepdims=True) > 0
    laid = jnp.dot(
        dispatch.astype(jnp.bfloat16), rows_ref[...], preferred_element_type=jnp.float32
    )
    factor = lax.rsqrt(
        jnp.mean(laid * laid, axis=-1, keepdims=True) + epsilon
    ) * feature_count ** (-0.5)
    lane = lax.broadcasted_iota(jnp.int32, laid.shape, 1)
    return jnp.where(filled | (lane > 0), laid * factor, EMPTY).astype(jnp.bfloat16)


def slots_of_steps(slot, capacity, steps):
    half = CL_OWN * lax.axis_size("owner") // lax.axis_size("sub")
    by_distance = slot ^ (chip_index() * capacity)
    distance = by_distance // capacity
    rank = by_distance - distance * capacity
    step = jnp.full_like(slot, -1)
    for place, p in enumerate(steps):
        step = jnp.where(distance == p + half * lax.axis_index("sub"), place, step)
    return jnp.where(step < 0, -1, step * capacity + rank)


def route_first_kernel(clusters, capacity, step, rows_ref, ids_ref, piece_ref, slot_ref):
    slot = slots_of(ids_ref[...], clusters, capacity)
    slot_ref[...] = slot
    piece_ref[...] = lay(rows_ref, slots_of_steps(slot, capacity, [step]), capacity)


def route_rest_kernel(clusters, capacity, first, steps, *refs):
    own_rows, other_rows, own_slot, other_ids, first_ref, *piece_refs = refs
    slot = slots_of_steps(own_slot[...], capacity, steps)
    laid = lay(own_rows, slot, len(steps) * capacity)
    for k, piece in enumerate(piece_refs):
        piece[:capacity] = laid[k * capacity : (k + 1) * capacity]
    slot = slots_of(other_ids[...], clusters, capacity)
    slot = slots_of_steps(slot, capacity, [first, *steps])
    laid = lay(other_rows, slot, (1 + len(steps)) * capacity)
    first_ref[...] = laid[:capacity]
    for k, piece in enumerate(piece_refs):
        piece[capacity:] = laid[(k + 1) * capacity : (k + 2) * capacity]


def route_kernel(clusters, capacity, rows_ref, ids_ref, piece_ref, slot_ref):
    slot = slots_of(ids_ref[...], clusters, capacity)
    slot_ref[...] = slot
    piece_ref[...] = lay(rows_ref, slot, piece_ref.shape[0])


def call_kernel(name, kernel, out_shape, *args, limit=32 * 2**20, flops=0):
    cost = pl.CostEstimate(flops=flops, bytes_accessed=0, transcendentals=0) if flops else None
    return pl.pallas_call(
        kernel,
        out_shape=out_shape,
        in_specs=[VMEM] * len(args),
        out_specs=jax.tree.map(lambda _: VMEM, out_shape),
        compiler_params=pltpu.CompilerParams(vmem_limit_bytes=limit),
        cost_estimate=cost,
        name=name,
    )(*args)


def join_kernel(first_ref, second_ref, out_ref):
    rows = first_ref.shape[0]
    out_ref[:rows] = first_ref[...]
    out_ref[rows:] = second_ref[...]


def blocks(rows, starts, size):
    return jnp.concatenate([rows[start : start + size] for start in starts], axis=0)


def count_against(rows, own, starts, size):
    column = lax.broadcasted_iota(jnp.int32, (1, own.shape[0]), 1)
    itself = jnp.full_like(column, -1)
    for k, start in enumerate(starts):
        itself = jnp.where(column // size == k, column + (start - k * size), itself)
    slope = -math.log2(math.e) / sharpness
    total = jnp.zeros((1, own.shape[0]), jnp.float32)
    for first in range(0, rows.shape[0], TILE):
        other = rows[first : first + TILE]
        scores = lax.dot_general(
            other, own, (((1,), (1,)), ((), ())), preferred_element_type=jnp.float32
        )
        weights = 1.0 / (1.0 + jnp.exp2(scores * slope - threshold * slope))
        keep = other[:, :1].astype(jnp.float32) < 0.5 * EMPTY
        if starts:
            keep = keep & (lax.broadcasted_iota(jnp.int32, scores.shape, 0) + first != itself)
        total = total + jnp.sum(jnp.where(keep, weights, 0.0), axis=0, keepdims=True)
    return total


def count_kernel(starts, size, *refs):
    *piece_refs, count_ref = refs
    rows = jnp.concatenate([piece[...] for piece in piece_refs], axis=0)
    count_ref[...] = count_against(rows, blocks(rows, starts, size), starts, size)


def soft_counts(pieces, starts, size):
    out_shape = jax.ShapeDtypeStruct((1, len(starts) * size), jnp.float32)
    return call_kernel("count", functools.partial(count_kernel, starts, size), out_shape, *pieces)


def finish_kernel(starts, late_pieces, late_starts, places, *refs):
    *piece_refs, early_ref, count_ref = refs
    size = count_ref.shape[2]
    early = jnp.concatenate([piece[...] for piece in piece_refs[:-late_pieces]], axis=0)
    late = jnp.concatenate([piece[...] for piece in piece_refs[-late_pieces:]], axis=0)
    own = blocks(early, starts, size)
    late_own = blocks(late, late_starts, size)
    total = early_ref[...] + count_against(late, own, [], size)
    late_total = count_against(early, late_own, [], size) + count_against(
        late, late_own, late_starts, size
    )
    for k, place in enumerate(places()):
        source, j = (total, k) if k < len(starts) else (late_total, k - len(starts))
        count_ref[pl.ds(place, 1), 0, :] = source[:, j * size : (j + 1) * size]


def select_kernel(capacity, counts_ref, slot_ref, out_ref):
    counts = counts_ref[:, 0, :]
    slot = slot_ref[...]
    doc_count = slot.shape[1]
    block = slot // capacity
    rank = slot - block * capacity
    hot = (lax.broadcasted_iota(jnp.int32, (capacity, doc_count), 0) == rank).astype(jnp.float32)
    by_block = jnp.dot(
        counts, hot, precision=lax.Precision.HIGHEST, preferred_element_type=jnp.float32
    )
    chosen = lax.broadcasted_iota(jnp.int32, by_block.shape, 0) == block
    out_ref[...] = jnp.sum(jnp.where(chosen, by_block, 0.0), axis=0, keepdims=True)


def select(counts, slot, capacity):
    out_shape = jax.ShapeDtypeStruct(slot.shape, jnp.float32)
    kernel = functools.partial(select_kernel, capacity)
    return call_kernel("select", kernel, out_shape, counts, slot, limit=8 * 2**20)[0]


def swap_cores(x):
    cores = lax.axis_size("sub")
    return lax.ppermute(x, "sub", [(i, i ^ 1) for i in range(cores)])


def body_by_chip(embeddings, cluster_id):
    doc_count, feature_count = embeddings.shape
    clusters = CL_OWN * lax.axis_size("owner")
    capacity = 2 * doc_count // clusters
    cores = lax.axis_size("sub")
    steps = clusters // cores

    def across(x, p):
        pairs = [
            (chip * cores + core, (chip ^ (p + steps * core)) * cores + core)
            for chip in range(clusters)
            for core in range(cores)
        ]
        return lax.ppermute(x, ("owner", "helper", "sub"), pairs)

    ids = cluster_id.reshape(1, doc_count)
    other_rows, other_ids = swap_cores(embeddings), swap_cores(ids)
    first, last = 0, steps - 1
    middle = [p for p in range(steps) if p not in (first, last)]
    half = jax.ShapeDtypeStruct((capacity, feature_count), jnp.bfloat16)
    whole = jax.ShapeDtypeStruct((cores * capacity, feature_count), jnp.bfloat16)

    first_own, slot = call_kernel(
        "route_first",
        functools.partial(route_first_kernel, clusters, capacity, first),
        [half, jax.ShapeDtypeStruct((1, doc_count), jnp.int32)],
        embeddings,
        ids,
    )
    first_own = across(first_own, first)
    first_other, *rest = call_kernel(
        "route_rest",
        functools.partial(route_rest_kernel, clusters, capacity, first, [*middle, last]),
        [half] + [whole] * (steps - 1),
        embeddings,
        other_rows,
        slot,
        other_ids,
    )
    first_other = across(first_other, first)
    rest = [across(piece, p) for piece, p in zip(rest, [*middle, last])]

    first_both = call_kernel("join", join_kernel, whole, first_own, first_other, flops=10**10)
    early = [first_both, *rest[:-1]]
    early += [swap_cores(x) for x in early]
    late = [rest[-1], swap_cores(rest[-1])]
    span = cores * capacity
    half_way = span * (steps - 1)
    starts = [k * span for k in range(steps - 1)]
    starts += [half_way + start + capacity for start in starts]
    late_starts = [0, span + capacity]

    def places():
        chip, core = chip_index(), lax.axis_index("sub")
        return (
            [chip ^ (p + steps * core) for p in (first, *middle)]
            + [chip ^ (p + steps * (1 - core)) for p in (first, *middle)]
            + [chip ^ (last + steps * core), chip ^ (last + steps * (1 - core))]
        )

    counts = call_kernel(
        "finish",
        functools.partial(finish_kernel, starts, len(late), late_starts, places),
        jax.ShapeDtypeStruct((clusters, 1, capacity), jnp.float32),
        *early,
        *late,
        soft_counts(early, starts, capacity),
    )
    back = lax.all_to_all(counts, ("owner", "helper"), split_axis=0, concat_axis=0, tiled=True)
    return select(back, slot, capacity)


def body_by_owner(embeddings, cluster_id):
    doc_count, feature_count = embeddings.shape
    owners, helpers = lax.axis_size("owner"), lax.axis_size("helper")
    clusters = CL_OWN * owners
    capacity = 2 * doc_count // clusters
    mine = lax.axis_index("helper") % CL_OWN

    def partner(x):
        return lax.ppermute(x, "helper", [(i, i ^ 1) for i in range(helpers)])

    outgoing, slot = call_kernel(
        "route",
        functools.partial(route_kernel, clusters, capacity),
        [
            jax.ShapeDtypeStruct((clusters * capacity, feature_count), jnp.bfloat16),
            jax.ShapeDtypeStruct((1, doc_count), jnp.int32),
        ],
        embeddings,
        cluster_id.reshape(1, doc_count),
    )
    outgoing = outgoing.reshape(owners, CL_OWN, capacity, feature_count)
    arrived = lax.all_to_all(outgoing, "owner", split_axis=0, concat_axis=0, tiled=True)
    kept = lax.dynamic_index_in_dim(arrived, mine, 1, keepdims=False)
    given = partner(lax.dynamic_index_in_dim(arrived, 1 - mine, 1, keepdims=False))
    own = jnp.stack([kept, given]).reshape(CL_OWN * owners * capacity, feature_count)
    others = [swap_cores(own)]
    for step in range(CL_OWN, helpers, CL_OWN):
        turn = [(i, (i + step) % helpers) for i in range(helpers)]
        others += [lax.ppermute(x, "helper", turn) for x in (own, others[0])]
    counts = soft_counts([own, *others], [0], own.shape[0])
    counts = counts.reshape(CL_OWN, owners, capacity)
    kept, given = counts[0], partner(counts[1])
    counts = jnp.where(mine == 0, jnp.stack([kept, given], 1), jnp.stack([given, kept], 1))
    back = lax.all_to_all(counts, "owner", split_axis=0, concat_axis=0, tiled=True)
    return select(back.reshape(clusters, 1, capacity), slot, capacity)


def solution(mesh):
    in_specs = (
        P(("groups", "owner", "helper", "sub"), None),
        P(("groups", "owner", "helper", "sub")),
    )
    out_specs = P(("groups", "owner", "helper", "sub"))
    body = body_by_chip if mesh.shape["helper"] == CL_OWN else body_by_owner
    return jax.shard_map(body, mesh=mesh, in_specs=in_specs, out_specs=out_specs, check_vma=False)
```

```python
import functools
import math

import jax
import jax.numpy as jnp
from jax import lax
from jax.experimental import pallas as pl
from jax.experimental.pallas import tpu as pltpu
from jax.sharding import PartitionSpec as P

CL_OWN = 2

epsilon = 1e-06
threshold = 0.8
sharpness = 0.05

EMPTY = 4.0
TILE = 256
ID_ROWS = 16
VMEM = pl.BlockSpec(memory_space=pltpu.VMEM)


def slots_of(ids, clusters, capacity):
    doc_count = ids.shape[1]
    member = lax.broadcasted_iota(jnp.int32, (clusters, doc_count), 0) == ids
    earlier = lax.broadcasted_iota(jnp.int32, (doc_count, doc_count), 0) < (
        lax.broadcasted_iota(jnp.int32, (doc_count, doc_count), 1)
    )
    ahead = jnp.dot(
        member.astype(jnp.bfloat16), earlier.astype(jnp.bfloat16), preferred_element_type=jnp.float32
    )
    rank = jnp.sum(jnp.where(member, ahead, 0.0), axis=0, keepdims=True).astype(jnp.int32)
    return ids * capacity + rank


def lay(rows_ref, slot, slots):
    doc_count, feature_count = rows_ref.shape
    dispatch = lax.broadcasted_iota(jnp.int32, (slots, doc_count), 0) == slot
    filled = jnp.sum(dispatch.astype(jnp.float32), axis=1, keepdims=True) > 0
    laid = jnp.dot(
        dispatch.astype(jnp.bfloat16), rows_ref[...], preferred_element_type=jnp.float32
    )
    factor = lax.rsqrt(
        jnp.mean(laid * laid, axis=-1, keepdims=True) + epsilon
    ) * feature_count ** (-0.5)
    lane = lax.broadcasted_iota(jnp.int32, laid.shape, 1)
    return jnp.where(filled | (lane > 0), laid * factor, EMPTY).astype(jnp.bfloat16)


def route_kernel(clusters, capacity, rows_ref, ids_ref, piece_ref, slot_ref):
    slot = slots_of(ids_ref[...], clusters, capacity)
    slot_ref[...] = slot
    piece_ref[...] = lay(rows_ref, slot, piece_ref.shape[0])


def call_kernel(name, kernel, out_shape, *args, limit=32 * 2**20, flops=0):
    cost = pl.CostEstimate(flops=flops, bytes_accessed=0, transcendentals=0) if flops else None
    return pl.pallas_call(
        kernel,
        out_shape=out_shape,
        in_specs=[VMEM] * len(args),
        out_specs=jax.tree.map(lambda _: VMEM, out_shape),
        compiler_params=pltpu.CompilerParams(vmem_limit_bytes=limit),
        cost_estimate=cost,
        name=name,
    )(*args)


def unit_rows_of(rows):
    widened = rows.astype(jnp.float32)
    factor = lax.rsqrt(
        jnp.mean(widened * widened, axis=-1, keepdims=True) + epsilon
    ) * rows.shape[1] ** (-0.5)
    return (widened * factor).astype(jnp.bfloat16)


def weights_of(others, own):
    scores = lax.dot_general(
        others, own, (((1,), (1,)), ((), ())), preferred_element_type=jnp.float32
    )
    slope = -math.log2(math.e) / sharpness
    return 1.0 / (1.0 + jnp.exp2(scores * slope - threshold * slope))


def count_kernel(*refs):
    *piece_refs, count_ref = refs
    own = piece_refs[0][...]
    total = jnp.zeros((1, own.shape[0]), jnp.float32)
    for k, piece in enumerate(piece_refs):
        for first in range(0, piece.shape[0], TILE):
            other = piece[first : first + TILE]
            weights = weights_of(other, own)
            keep = other[:, :1].astype(jnp.float32) < 0.5 * EMPTY
            if k == 0:
                keep = keep & (
                    lax.broadcasted_iota(jnp.int32, weights.shape, 0) + first
                    != lax.broadcasted_iota(jnp.int32, weights.shape, 1)
                )
            total = total + jnp.sum(jnp.where(keep, weights, 0.0), axis=0, keepdims=True)
    count_ref[...] = total


def soft_counts(pieces):
    out_shape = jax.ShapeDtypeStruct((1, pieces[0].shape[0]), jnp.float32)
    return call_kernel("count", count_kernel, out_shape, *pieces)


def column_of(row):
    size = row.shape[1]
    diagonal = lax.broadcasted_iota(jnp.int32, (size, size), 0) == (
        lax.broadcasted_iota(jnp.int32, (size, size), 1)
    )
    return jnp.sum(jnp.where(diagonal, row, 0.0), axis=1, keepdims=True)


def pair_counts(others, other_ids, own, own_ids, itself=None):
    weights = weights_of(others, own)
    keep = column_of(other_ids) == own_ids
    if itself is not None:
        keep = keep & (
            lax.broadcasted_iota(jnp.int32, weights.shape, 0)
            != lax.broadcasted_iota(jnp.int32, weights.shape, 1) + itself
        )
    return jnp.sum(jnp.where(keep, weights, 0.0), axis=0, keepdims=True)


def prepare_kernel(rows_ref, ids_ref, piece_ref):
    doc_count, feature_count = rows_ref.shape
    ids = jnp.concatenate(
        [ids_ref[...].astype(jnp.float32), jnp.zeros((1, feature_count - doc_count), jnp.float32)],
        axis=1,
    )
    piece_ref[:doc_count] = unit_rows_of(rows_ref[...])
    piece_ref[doc_count:] = jnp.broadcast_to(ids, (ID_ROWS, feature_count)).astype(jnp.bfloat16)


def split(piece):
    count = piece.shape[0] - ID_ROWS
    return piece[:count], piece[count:, :count].astype(jnp.float32)[:1]


def count_all(others, wanted, same):
    return [
        sum(
            pair_counts(*other, *mine, 0 if same.get(j) == k else None)
            for k, other in enumerate(others)
        )
        for j, mine in enumerate(wanted)
    ]


def counts_kernel(others, same, *refs):
    *block_refs, out_ref = refs
    blocks = [split(block) for block in block_refs]
    wanted = [blocks[k] for k in same] + blocks[others:]
    totals = count_all(blocks[:others], wanted, {j: k for j, k in enumerate(same)})
    for j, total in enumerate(totals):
        out_ref[j : j + 1] = total


def halve_kernel(piece_ref, first_ref, second_ref):
    count = piece_ref.shape[0] - ID_ROWS
    part = count // 2
    for k, half_ref in enumerate((first_ref, second_ref)):
        rows = slice(k * part, (k + 1) * part)
        half_ref[:part] = piece_ref[rows]
        half_ref[part:] = jnp.zeros_like(half_ref[part:])
        half_ref[part:, :part] = piece_ref[count:, rows]


def joined(*pieces):
    rows, ids = zip(*[split(piece) for piece in pieces])
    return jnp.concatenate(rows, axis=0), jnp.concatenate(ids, axis=1)


def more_kernel(own, end, next_own, x_end, x_end_oa, x_end_ob, out_ref):
    others = [split(own), split(end), split(next_own)]
    for j, total in enumerate(count_all(others, [split(x_end), joined(x_end_oa, x_end_ob)], {})):
        out_ref[j : j + 1] = total


def last_kernel(far_ref, *refs):
    *block_refs, x_end_oa, x_end_ob, before_ref, across_ref, here_ref, there_ref = refs
    wanted = [split(block) for block in block_refs] + [joined(x_end_oa, x_end_ob)]
    for j, total in enumerate(count_all([split(far_ref)], wanted, {})):
        out_ref, row = (here_ref, j) if j < 4 else (there_ref, j - 4)
        old = across_ref[j // 4 : j // 4 + 1] if row == 3 else before_ref[j - j // 4 : j - j // 4 + 1]
        out_ref[row : row + 1] = old + total


def cores_kernel(here_ref, back_ref, stay_ref, go_ref):
    total = here_ref[...] + back_ref[...]
    stay_ref[...] = total[:2]
    go_ref[...] = total[2:]


def across_kernel(stay_ref, back_ref, own_ref, end_ref):
    total = stay_ref[...] + back_ref[...]
    own_ref[...] = total[:1]
    end_ref[...] = total[1:]


def choose_kernel(own_ref, end_ref, out_ref):
    owner = lax.axis_index("owner")
    out_ref[...] = jnp.where((owner == 1) | (owner == 2), own_ref[...], end_ref[...])


def select_kernel(capacity, counts_ref, slot_ref, out_ref):
    counts = counts_ref[:, 0, :]
    slot = slot_ref[...]
    doc_count = slot.shape[1]
    block = slot // capacity
    rank = slot - block * capacity
    hot = (lax.broadcasted_iota(jnp.int32, (capacity, doc_count), 0) == rank).astype(jnp.float32)
    by_block = jnp.dot(
        counts, hot, precision=lax.Precision.HIGHEST, preferred_element_type=jnp.float32
    )
    chosen = lax.broadcasted_iota(jnp.int32, by_block.shape, 0) == block
    out_ref[...] = jnp.sum(jnp.where(chosen, by_block, 0.0), axis=0, keepdims=True)


def select(counts, slot, capacity):
    out_shape = jax.ShapeDtypeStruct(slot.shape, jnp.float32)
    kernel = functools.partial(select_kernel, capacity)
    return call_kernel("select", kernel, out_shape, counts, slot, limit=8 * 2**20)[0]


def swap_cores(x):
    cores = lax.axis_size("sub")
    return lax.ppermute(x, "sub", [(i, i ^ 1) for i in range(cores)])


def body_by_column(embeddings, cluster_id):
    doc_count, feature_count = embeddings.shape
    helpers, cores = lax.axis_size("helper"), lax.axis_size("sub")

    def send(x, owners=(0, 1, 2, 3), turns=(0, 0, 0, 0), swap=0):
        pairs = [
            (
                (here * helpers + h) * cores + c,
                (there * helpers + (h ^ turn)) * cores + (c ^ swap),
            )
            for here, (there, turn) in enumerate(zip(owners, turns))
            for h in range(helpers)
            for c in range(cores)
        ]
        return lax.ppermute(x, ("owner", "helper", "sub"), pairs)

    def along(x):
        return send(x, owners=(1, 0, 3, 2))

    def middle(x):
        return send(x, owners=(0, 2, 1, 3), turns=(1, 0, 0, 1))

    def across(x):
        return send(x, turns=(1, 1, 1, 1))

    def other(x):
        return send(x, swap=1)

    def sums(count, blocks=1):
        return jax.ShapeDtypeStruct((blocks, count), jnp.float32)

    own = call_kernel(
        "prepare",
        prepare_kernel,
        jax.ShapeDtypeStruct((doc_count + ID_ROWS, feature_count), jnp.bfloat16),
        embeddings,
        cluster_id.reshape(1, doc_count),
    )
    x, end, next_own, own_o = across(own), along(own), middle(own), other(own)
    far, x_end = middle(end), across(end)
    end_o, x_o = other(end), other(x)

    before = call_kernel(
        "first",
        functools.partial(counts_kernel, 3, (0, 1)),
        sums(doc_count, 6),
        own,
        end,
        next_own,
        x,
        own_o,
        end_o,
        x_o,
    )
    late_x_end, _ = lax.optimization_barrier((x_end, before))
    half = jax.ShapeDtypeStruct((doc_count // 2 + ID_ROWS, feature_count), jnp.bfloat16)
    x_end_o = [other(x) for x in call_kernel("halve", halve_kernel, [half] * 2, late_x_end)]
    before_x = call_kernel(
        "more",
        more_kernel,
        sums(doc_count, 2),
        own,
        end,
        next_own,
        x_end,
        *x_end_o,
    )
    here, there = call_kernel(
        "last",
        last_kernel,
        [sums(doc_count, 4)] * 2,
        far,
        own,
        end,
        x,
        x_end,
        own_o,
        end_o,
        x_o,
        *x_end_o,
        before,
        before_x,
    )
    stay, go = call_kernel("cores", cores_kernel, [sums(doc_count, 2)] * 2, here, other(there))
    own_sum, end_sum = call_kernel(
        "across", across_kernel, [sums(doc_count)] * 2, stay, across(go)
    )
    return call_kernel(
        "choose", choose_kernel, sums(doc_count), own_sum, along(end_sum), limit=8 * 2**20
    )[0]


def body_by_owner(embeddings, cluster_id):
    doc_count, feature_count = embeddings.shape
    owners, helpers = lax.axis_size("owner"), lax.axis_size("helper")
    clusters = CL_OWN * owners
    capacity = 2 * doc_count // clusters
    mine = lax.axis_index("helper") % CL_OWN

    def partner(x):
        return lax.ppermute(x, "helper", [(i, i ^ 1) for i in range(helpers)])

    outgoing, slot = call_kernel(
        "route",
        functools.partial(route_kernel, clusters, capacity),
        [
            jax.ShapeDtypeStruct((clusters * capacity, feature_count), jnp.bfloat16),
            jax.ShapeDtypeStruct((1, doc_count), jnp.int32),
        ],
        embeddings,
        cluster_id.reshape(1, doc_count),
    )
    outgoing = outgoing.reshape(owners, CL_OWN, capacity, feature_count)
    arrived = lax.all_to_all(outgoing, "owner", split_axis=0, concat_axis=0, tiled=True)
    kept = lax.dynamic_index_in_dim(arrived, mine, 1, keepdims=False)
    given = partner(lax.dynamic_index_in_dim(arrived, 1 - mine, 1, keepdims=False))
    own = jnp.stack([kept, given]).reshape(CL_OWN * owners * capacity, feature_count)
    others = [swap_cores(own)]
    for step in range(CL_OWN, helpers, CL_OWN):
        turn = [(i, (i + step) % helpers) for i in range(helpers)]
        others += [lax.ppermute(x, "helper", turn) for x in (own, others[0])]
    counts = soft_counts([own, *others])
    counts = counts.reshape(CL_OWN, owners, capacity)
    kept, given = counts[0], partner(counts[1])
    counts = jnp.where(mine == 0, jnp.stack([kept, given], 1), jnp.stack([given, kept], 1))
    back = lax.all_to_all(counts, "owner", split_axis=0, concat_axis=0, tiled=True)
    return select(back.reshape(clusters, 1, capacity), slot, capacity)


def solution(mesh):
    in_specs = (
        P(("groups", "owner", "helper", "sub"), None),
        P(("groups", "owner", "helper", "sub")),
    )
    out_specs = P(("groups", "owner", "helper", "sub"))
    columns = tuple(mesh.shape[axis] for axis in ("owner", "helper", "sub")) == (4, 2, 2)
    body = body_by_column if columns else body_by_owner
    return jax.shard_map(body, mesh=mesh, in_specs=in_specs, out_specs=out_specs, check_vma=False)
```

```python
import functools
import math

import jax
import jax.numpy as jnp
from jax import lax
from jax.experimental import pallas as pl
from jax.experimental.pallas import tpu as pltpu
from jax.sharding import PartitionSpec as P

CL_OWN = 2

epsilon = 1e-06
threshold = 0.8
sharpness = 0.05

EMPTY = 4.0
TILE = 256
ID_ROWS = 16
VMEM = pl.BlockSpec(memory_space=pltpu.VMEM)


def slots_of(ids, clusters, capacity):
    doc_count = ids.shape[1]
    member = lax.broadcasted_iota(jnp.int32, (clusters, doc_count), 0) == ids
    earlier = lax.broadcasted_iota(jnp.int32, (doc_count, doc_count), 0) < (
        lax.broadcasted_iota(jnp.int32, (doc_count, doc_count), 1)
    )
    ahead = jnp.dot(
        member.astype(jnp.bfloat16), earlier.astype(jnp.bfloat16), preferred_element_type=jnp.float32
    )
    rank = jnp.sum(jnp.where(member, ahead, 0.0), axis=0, keepdims=True).astype(jnp.int32)
    return ids * capacity + rank


def lay(rows_ref, slot, slots):
    doc_count, feature_count = rows_ref.shape
    dispatch = lax.broadcasted_iota(jnp.int32, (slots, doc_count), 0) == slot
    filled = jnp.sum(dispatch.astype(jnp.float32), axis=1, keepdims=True) > 0
    laid = jnp.dot(
        dispatch.astype(jnp.bfloat16), rows_ref[...], preferred_element_type=jnp.float32
    )
    factor = lax.rsqrt(
        jnp.mean(laid * laid, axis=-1, keepdims=True) + epsilon
    ) * feature_count ** (-0.5)
    lane = lax.broadcasted_iota(jnp.int32, laid.shape, 1)
    return jnp.where(filled | (lane > 0), laid * factor, EMPTY).astype(jnp.bfloat16)


def route_kernel(clusters, capacity, rows_ref, ids_ref, piece_ref, slot_ref):
    slot = slots_of(ids_ref[...], clusters, capacity)
    slot_ref[...] = slot
    piece_ref[...] = lay(rows_ref, slot, piece_ref.shape[0])


def call_kernel(name, kernel, out_shape, *args, limit=32 * 2**20, flops=0):
    cost = pl.CostEstimate(flops=flops, bytes_accessed=0, transcendentals=0) if flops else None
    return pl.pallas_call(
        kernel,
        out_shape=out_shape,
        in_specs=[VMEM] * len(args),
        out_specs=jax.tree.map(lambda _: VMEM, out_shape),
        compiler_params=pltpu.CompilerParams(vmem_limit_bytes=limit),
        cost_estimate=cost,
        name=name,
    )(*args)


def unit_rows_of(rows):
    widened = rows.astype(jnp.float32)
    factor = lax.rsqrt(
        jnp.mean(widened * widened, axis=-1, keepdims=True) + epsilon
    ) * rows.shape[1] ** (-0.5)
    return (widened * factor).astype(jnp.bfloat16)


def weights_of(others, own):
    scores = lax.dot_general(
        others, own, (((1,), (1,)), ((), ())), preferred_element_type=jnp.float32
    )
    slope = -math.log2(math.e) / sharpness
    return 1.0 / (1.0 + jnp.exp2(scores * slope - threshold * slope))


def count_kernel(*refs):
    *piece_refs, count_ref = refs
    own = piece_refs[0][...]
    total = jnp.zeros((1, own.shape[0]), jnp.float32)
    for k, piece in enumerate(piece_refs):
        for first in range(0, piece.shape[0], TILE):
            other = piece[first : first + TILE]
            weights = weights_of(other, own)
            keep = other[:, :1].astype(jnp.float32) < 0.5 * EMPTY
            if k == 0:
                keep = keep & (
                    lax.broadcasted_iota(jnp.int32, weights.shape, 0) + first
                    != lax.broadcasted_iota(jnp.int32, weights.shape, 1)
                )
            total = total + jnp.sum(jnp.where(keep, weights, 0.0), axis=0, keepdims=True)
    count_ref[...] = total


def soft_counts(pieces):
    out_shape = jax.ShapeDtypeStruct((1, pieces[0].shape[0]), jnp.float32)
    return call_kernel("count", count_kernel, out_shape, *pieces)


def column_of(row):
    size = row.shape[1]
    diagonal = lax.broadcasted_iota(jnp.int32, (size, size), 0) == (
        lax.broadcasted_iota(jnp.int32, (size, size), 1)
    )
    return jnp.sum(jnp.where(diagonal, row, 0.0), axis=1, keepdims=True)


def pair_counts(others, other_ids, own, own_ids, itself=None):
    weights = weights_of(others, own)
    keep = column_of(other_ids) == own_ids
    if itself is not None:
        keep = keep & (
            lax.broadcasted_iota(jnp.int32, weights.shape, 0)
            != lax.broadcasted_iota(jnp.int32, weights.shape, 1) + itself
        )
    return jnp.sum(jnp.where(keep, weights, 0.0), axis=0, keepdims=True)


def prepare_kernel(rows_ref, ids_ref, piece_ref):
    doc_count, feature_count = rows_ref.shape
    ids = jnp.concatenate(
        [ids_ref[...].astype(jnp.float32), jnp.zeros((1, feature_count - doc_count), jnp.float32)],
        axis=1,
    )
    piece_ref[:doc_count] = unit_rows_of(rows_ref[...])
    piece_ref[doc_count:] = jnp.broadcast_to(ids, (ID_ROWS, feature_count)).astype(jnp.bfloat16)


def split(piece):
    count = piece.shape[0] - ID_ROWS
    return piece[:count], piece[count:, :count].astype(jnp.float32)[:1]


def count_all(others, wanted, same):
    return [
        sum(
            pair_counts(*other, *mine, 0 if same.get(j) == k else None)
            for k, other in enumerate(others)
        )
        for j, mine in enumerate(wanted)
    ]


def counts_kernel(others, same, *refs):
    *block_refs, out_ref = refs
    blocks = [split(block) for block in block_refs]
    wanted = [blocks[k] for k in same] + blocks[others:]
    totals = count_all(blocks[:others], wanted, {j: k for j, k in enumerate(same)})
    for j, total in enumerate(totals):
        out_ref[j : j + 1] = total


def half_kernel(which, piece_ref, half_ref):
    count = piece_ref.shape[0] - ID_ROWS
    part = count // 2
    rows = slice(which * part, (which + 1) * part)
    half_ref[:part] = piece_ref[rows]
    half_ref[part:] = jnp.zeros_like(half_ref[part:])
    half_ref[part:, :part] = piece_ref[count:, rows]


def joined(*pieces):
    rows, ids = zip(*[split(piece) for piece in pieces])
    return jnp.concatenate(rows, axis=0), jnp.concatenate(ids, axis=1)


def more_kernel(own, end, next_own, x_end_a, x_end_b, x_end_oa, x_end_ob, out_ref):
    others = [split(own), split(end), split(next_own)]
    wanted = [joined(x_end_a, x_end_b), joined(x_end_oa, x_end_ob)]
    for j, total in enumerate(count_all(others, wanted, {})):
        out_ref[j : j + 1] = total


def last_kernel(far_ref, *refs):
    own, end, x, x_end_a, x_end_b, own_o, end_o, x_o, x_end_oa, x_end_ob, *refs = refs
    before_ref, across_ref, here_ref, there_ref = refs
    wanted = [split(own), split(end), split(x), joined(x_end_a, x_end_b)]
    wanted += [split(own_o), split(end_o), split(x_o), joined(x_end_oa, x_end_ob)]
    for j, total in enumerate(count_all([split(far_ref)], wanted, {})):
        out_ref, row = (here_ref, j) if j < 4 else (there_ref, j - 4)
        old = across_ref[j // 4 : j // 4 + 1] if row == 3 else before_ref[j - j // 4 : j - j // 4 + 1]
        out_ref[row : row + 1] = old + total


def cores_kernel(here_ref, back_ref, stay_ref, go_ref):
    total = here_ref[...] + back_ref[...]
    stay_ref[...] = total[:2]
    go_ref[...] = total[2:]


def across_kernel(stay_ref, back_ref, own_ref, end_ref):
    total = stay_ref[...] + back_ref[...]
    own_ref[...] = total[:1]
    end_ref[...] = total[1:]


def choose_kernel(own_ref, end_ref, out_ref):
    owner = lax.axis_index("owner")
    out_ref[...] = jnp.where((owner == 1) | (owner == 2), own_ref[...], end_ref[...])


def select_kernel(capacity, counts_ref, slot_ref, out_ref):
    counts = counts_ref[:, 0, :]
    slot = slot_ref[...]
    doc_count = slot.shape[1]
    block = slot // capacity
    rank = slot - block * capacity
    hot = (lax.broadcasted_iota(jnp.int32, (capacity, doc_count), 0) == rank).astype(jnp.float32)
    by_block = jnp.dot(
        counts, hot, precision=lax.Precision.HIGHEST, preferred_element_type=jnp.float32
    )
    chosen = lax.broadcasted_iota(jnp.int32, by_block.shape, 0) == block
    out_ref[...] = jnp.sum(jnp.where(chosen, by_block, 0.0), axis=0, keepdims=True)


def select(counts, slot, capacity):
    out_shape = jax.ShapeDtypeStruct(slot.shape, jnp.float32)
    kernel = functools.partial(select_kernel, capacity)
    return call_kernel("select", kernel, out_shape, counts, slot, limit=8 * 2**20)[0]


def swap_cores(x):
    cores = lax.axis_size("sub")
    return lax.ppermute(x, "sub", [(i, i ^ 1) for i in range(cores)])


def body_by_column(embeddings, cluster_id):
    doc_count, feature_count = embeddings.shape
    helpers, cores = lax.axis_size("helper"), lax.axis_size("sub")

    def send(x, owners=(0, 1, 2, 3), turns=(0, 0, 0, 0), swaps=(0, 0, 0, 0)):
        pairs = [
            (
                (here * helpers + h) * cores + c,
                (there * helpers + (h ^ turn)) * cores + (c ^ swap),
            )
            for here, (there, turn, swap) in enumerate(zip(owners, turns, swaps))
            for h in range(helpers)
            for c in range(cores)
        ]
        return lax.ppermute(x, ("owner", "helper", "sub"), pairs)

    def along(x):
        return send(x, owners=(1, 0, 3, 2))

    def middle(x):
        return send(x, owners=(0, 2, 1, 3), swaps=(1, 0, 0, 1))

    def across(x):
        return send(x, turns=(1, 1, 1, 1))

    def middle_across(x):
        return send(x, turns=(0, 1, 1, 0), swaps=(1, 0, 0, 1))

    def other(x):
        return send(x, swaps=(1, 1, 1, 1))

    def sums(count, blocks=1):
        return jax.ShapeDtypeStruct((blocks, count), jnp.float32)

    own = call_kernel(
        "prepare",
        prepare_kernel,
        jax.ShapeDtypeStruct((doc_count + ID_ROWS, feature_count), jnp.bfloat16),
        embeddings,
        cluster_id.reshape(1, doc_count),
    )
    next_own, end, x, own_o = middle(own), along(own), across(own), other(own)
    far = middle(end)
    half = jax.ShapeDtypeStruct((doc_count // 2 + ID_ROWS, feature_count), jnp.bfloat16)
    end_half = call_kernel("half", functools.partial(half_kernel, 0), half, end)
    x_half = call_kernel("half", functools.partial(half_kernel, 1), half, x)
    x_end = [middle_across(end_half), along(x_half)]
    end_o, x_o = other(end), other(x)
    x_end_o = [other(piece) for piece in x_end]

    before = call_kernel(
        "first",
        functools.partial(counts_kernel, 3, (0, 1)),
        sums(doc_count, 6),
        own,
        end,
        next_own,
        x,
        own_o,
        end_o,
        x_o,
    )
    before_x = call_kernel(
        "more", more_kernel, sums(doc_count, 2), own, end, next_own, *x_end, *x_end_o,
    )
    here, there = call_kernel(
        "last",
        last_kernel,
        [sums(doc_count, 4)] * 2,
        far,
        own,
        end,
        x,
        *x_end,
        own_o,
        end_o,
        x_o,
        *x_end_o,
        before,
        before_x,
    )
    stay, go = call_kernel("cores", cores_kernel, [sums(doc_count, 2)] * 2, here, other(there))
    own_sum, end_sum = call_kernel(
        "across", across_kernel, [sums(doc_count)] * 2, stay, middle_across(go)
    )
    return call_kernel(
        "choose", choose_kernel, sums(doc_count), own_sum, along(end_sum), limit=8 * 2**20
    )[0]


def body_by_owner(embeddings, cluster_id):
    doc_count, feature_count = embeddings.shape
    owners, helpers = lax.axis_size("owner"), lax.axis_size("helper")
    clusters = CL_OWN * owners
    capacity = 2 * doc_count // clusters
    mine = lax.axis_index("helper") % CL_OWN

    def partner(x):
        return lax.ppermute(x, "helper", [(i, i ^ 1) for i in range(helpers)])

    outgoing, slot = call_kernel(
        "route",
        functools.partial(route_kernel, clusters, capacity),
        [
            jax.ShapeDtypeStruct((clusters * capacity, feature_count), jnp.bfloat16),
            jax.ShapeDtypeStruct((1, doc_count), jnp.int32),
        ],
        embeddings,
        cluster_id.reshape(1, doc_count),
    )
    outgoing = outgoing.reshape(owners, CL_OWN, capacity, feature_count)
    arrived = lax.all_to_all(outgoing, "owner", split_axis=0, concat_axis=0, tiled=True)
    kept = lax.dynamic_index_in_dim(arrived, mine, 1, keepdims=False)
    given = partner(lax.dynamic_index_in_dim(arrived, 1 - mine, 1, keepdims=False))
    own = jnp.stack([kept, given]).reshape(CL_OWN * owners * capacity, feature_count)
    others = [swap_cores(own)]
    for step in range(CL_OWN, helpers, CL_OWN):
        turn = [(i, (i + step) % helpers) for i in range(helpers)]
        others += [lax.ppermute(x, "helper", turn) for x in (own, others[0])]
    counts = soft_counts([own, *others])
    counts = counts.reshape(CL_OWN, owners, capacity)
    kept, given = counts[0], partner(counts[1])
    counts = jnp.where(mine == 0, jnp.stack([kept, given], 1), jnp.stack([given, kept], 1))
    back = lax.all_to_all(counts, "owner", split_axis=0, concat_axis=0, tiled=True)
    return select(back.reshape(clusters, 1, capacity), slot, capacity)


def solution(mesh):
    in_specs = (
        P(("groups", "owner", "helper", "sub"), None),
        P(("groups", "owner", "helper", "sub")),
    )
    out_specs = P(("groups", "owner", "helper", "sub"))
    columns = tuple(mesh.shape[axis] for axis in ("owner", "helper", "sub")) == (4, 2, 2)
    body = body_by_column if columns else body_by_owner
    return jax.shard_map(body, mesh=mesh, in_specs=in_specs, out_specs=out_specs, check_vma=False)
```

```python
import functools
import math

import jax
import jax.numpy as jnp
from jax import lax
from jax.experimental import pallas as pl
from jax.experimental.pallas import tpu as pltpu
from jax.sharding import PartitionSpec as P

CL_OWN = 2

epsilon = 1e-06
threshold = 0.8
sharpness = 0.05

EMPTY = 4.0
TILE = 256
ID_ROWS = 16
VMEM = pl.BlockSpec(memory_space=pltpu.VMEM)


def slots_of(ids, clusters, capacity):
    doc_count = ids.shape[1]
    member = lax.broadcasted_iota(jnp.int32, (clusters, doc_count), 0) == ids
    earlier = lax.broadcasted_iota(jnp.int32, (doc_count, doc_count), 0) < (
        lax.broadcasted_iota(jnp.int32, (doc_count, doc_count), 1)
    )
    ahead = jnp.dot(
        member.astype(jnp.bfloat16), earlier.astype(jnp.bfloat16), preferred_element_type=jnp.float32
    )
    rank = jnp.sum(jnp.where(member, ahead, 0.0), axis=0, keepdims=True).astype(jnp.int32)
    return ids * capacity + rank


def lay(rows_ref, slot, slots):
    doc_count, feature_count = rows_ref.shape
    dispatch = lax.broadcasted_iota(jnp.int32, (slots, doc_count), 0) == slot
    filled = jnp.sum(dispatch.astype(jnp.float32), axis=1, keepdims=True) > 0
    laid = jnp.dot(
        dispatch.astype(jnp.bfloat16), rows_ref[...], preferred_element_type=jnp.float32
    )
    factor = lax.rsqrt(
        jnp.mean(laid * laid, axis=-1, keepdims=True) + epsilon
    ) * feature_count ** (-0.5)
    lane = lax.broadcasted_iota(jnp.int32, laid.shape, 1)
    return jnp.where(filled | (lane > 0), laid * factor, EMPTY).astype(jnp.bfloat16)


def route_kernel(clusters, capacity, rows_ref, ids_ref, piece_ref, slot_ref):
    slot = slots_of(ids_ref[...], clusters, capacity)
    slot_ref[...] = slot
    piece_ref[...] = lay(rows_ref, slot, piece_ref.shape[0])


def call_kernel(name, kernel, out_shape, *args, limit=32 * 2**20, flops=0):
    cost = pl.CostEstimate(flops=flops, bytes_accessed=0, transcendentals=0) if flops else None
    return pl.pallas_call(
        kernel,
        out_shape=out_shape,
        in_specs=[VMEM] * len(args),
        out_specs=jax.tree.map(lambda _: VMEM, out_shape),
        compiler_params=pltpu.CompilerParams(vmem_limit_bytes=limit),
        cost_estimate=cost,
        name=name,
    )(*args)


def unit_rows_of(rows):
    widened = rows.astype(jnp.float32)
    factor = lax.rsqrt(
        jnp.mean(widened * widened, axis=-1, keepdims=True) + epsilon
    ) * rows.shape[1] ** (-0.5)
    return (widened * factor).astype(jnp.bfloat16)


def weights_of(others, own):
    scores = lax.dot_general(
        others, own, (((1,), (1,)), ((), ())), preferred_element_type=jnp.float32
    )
    slope = -math.log2(math.e) / sharpness
    return 1.0 / (1.0 + jnp.exp2(scores * slope - threshold * slope))


def count_kernel(*refs):
    *piece_refs, count_ref = refs
    own = piece_refs[0][...]
    total = jnp.zeros((1, own.shape[0]), jnp.float32)
    for k, piece in enumerate(piece_refs):
        for first in range(0, piece.shape[0], TILE):
            other = piece[first : first + TILE]
            weights = weights_of(other, own)
            keep = other[:, :1].astype(jnp.float32) < 0.5 * EMPTY
            if k == 0:
                keep = keep & (
                    lax.broadcasted_iota(jnp.int32, weights.shape, 0) + first
                    != lax.broadcasted_iota(jnp.int32, weights.shape, 1)
                )
            total = total + jnp.sum(jnp.where(keep, weights, 0.0), axis=0, keepdims=True)
    count_ref[...] = total


def soft_counts(pieces):
    out_shape = jax.ShapeDtypeStruct((1, pieces[0].shape[0]), jnp.float32)
    return call_kernel("count", count_kernel, out_shape, *pieces)


def column_of(row):
    size = row.shape[1]
    diagonal = lax.broadcasted_iota(jnp.int32, (size, size), 0) == (
        lax.broadcasted_iota(jnp.int32, (size, size), 1)
    )
    return jnp.sum(jnp.where(diagonal, row, 0.0), axis=1, keepdims=True)


def pair_counts(others, other_ids, own, own_ids, itself=None):
    weights = weights_of(others, own)
    keep = column_of(other_ids) == own_ids
    if itself is not None:
        keep = keep & (
            lax.broadcasted_iota(jnp.int32, weights.shape, 0)
            != lax.broadcasted_iota(jnp.int32, weights.shape, 1) + itself
        )
    return jnp.sum(jnp.where(keep, weights, 0.0), axis=0, keepdims=True)


def prepare_kernel(rows_ref, ids_ref, *piece_refs):
    doc_count, feature_count = rows_ref.shape
    unit = unit_rows_of(rows_ref[...])
    ids = ids_ref[...].astype(jnp.float32)
    for piece_ref, first in zip(piece_refs, (0, 0, doc_count // 2)):
        count = piece_ref.shape[0] - ID_ROWS
        some = jnp.concatenate(
            [ids[:, first : first + count], jnp.zeros((1, feature_count - count), jnp.float32)], axis=1
        )
        piece_ref[:count] = unit[first : first + count]
        piece_ref[count:] = jnp.broadcast_to(some, (ID_ROWS, feature_count)).astype(jnp.bfloat16)


def split(piece):
    count = piece.shape[0] - ID_ROWS
    return piece[:count], piece[count:, :count].astype(jnp.float32)[:1]


def count_all(others, wanted, same):
    return [
        sum(
            pair_counts(*other, *mine, 0 if same.get(j) == k else None)
            for k, other in enumerate(others)
        )
        for j, mine in enumerate(wanted)
    ]


def first_kernel(own, end, next_own, x_a, x_b, own_o, end_o, x_oa, x_ob, out_ref):
    others = [split(own), split(end), split(next_own)]
    wanted = [*others[:2], joined(x_a, x_b), split(own_o), split(end_o), joined(x_oa, x_ob)]
    for j, total in enumerate(count_all(others, wanted, {0: 0, 1: 1})):
        out_ref[j : j + 1] = total


def half_kernel(piece_ref, half_ref):
    count = piece_ref.shape[0] - ID_ROWS
    part = half_ref.shape[0] - ID_ROWS
    half_ref[:part] = piece_ref[:part]
    half_ref[part:] = piece_ref[count:]


def joined(*pieces):
    rows, ids = zip(*[split(piece) for piece in pieces])
    return jnp.concatenate(rows, axis=0), jnp.concatenate(ids, axis=1)


def more_kernel(own, end, next_own, x_end_a, x_end_b, x_end_oa, x_end_ob, out_ref):
    others = [split(own), split(end), split(next_own)]
    wanted = [joined(x_end_a, x_end_b), joined(x_end_oa, x_end_ob)]
    for j, total in enumerate(count_all(others, wanted, {})):
        out_ref[j : j + 1] = total


def last_kernel(far_ref, *refs):
    own, end, x_a, x_b, x_end_a, x_end_b, *refs = refs
    own_o, end_o, x_oa, x_ob, x_end_oa, x_end_ob, before_ref, across_ref, out_ref = refs
    wanted = [split(own), split(end), joined(x_a, x_b), joined(x_end_a, x_end_b)]
    wanted += [split(own_o), split(end_o), joined(x_oa, x_ob), joined(x_end_oa, x_end_ob)]
    for j, total in enumerate(count_all([split(far_ref)], wanted, {})):
        kind = j % 4
        old_ref, row = (across_ref, j // 4) if kind == 3 else (before_ref, j - j // 4)
        out_ref[j : j + 1] = old_ref[row : row + 1] + total


def cores_kernel(here_ref, got_ref, stay_ref, go_ref):
    here, got = here_ref[...], got_ref[...]
    half = here.shape[0] // 2
    own, other = here[:half] + got[half:], here[half:] + got[:half]
    stay_ref[...] = jnp.concatenate([own[:2], other[:2]], axis=0)
    go_ref[...] = jnp.concatenate([own[2:], other[2:]], axis=0)


def across_kernel(stay_ref, got_ref, own_ref, end_ref):
    total = stay_ref[...] + got_ref[...]
    own_ref[...] = jnp.concatenate([total[:1], total[2:3]], axis=0)
    end_ref[...] = jnp.concatenate([total[1:2], total[3:]], axis=0)


def along_kernel(own_ref, end_ref, here_ref, there_ref):
    owner = lax.axis_index("owner")
    total = jnp.where((owner == 1) | (owner == 2), own_ref[...], end_ref[...])
    here_ref[...] = total[:1]
    there_ref[...] = total[1:]


def choose_kernel(here_ref, there_ref, out_ref):
    out_ref[...] = jnp.where(lax.axis_index("sub") == 1, here_ref[...], there_ref[...])


def select_kernel(capacity, counts_ref, slot_ref, out_ref):
    counts = counts_ref[:, 0, :]
    slot = slot_ref[...]
    doc_count = slot.shape[1]
    block = slot // capacity
    rank = slot - block * capacity
    hot = (lax.broadcasted_iota(jnp.int32, (capacity, doc_count), 0) == rank).astype(jnp.float32)
    by_block = jnp.dot(
        counts, hot, precision=lax.Precision.HIGHEST, preferred_element_type=jnp.float32
    )
    chosen = lax.broadcasted_iota(jnp.int32, by_block.shape, 0) == block
    out_ref[...] = jnp.sum(jnp.where(chosen, by_block, 0.0), axis=0, keepdims=True)


def select(counts, slot, capacity):
    out_shape = jax.ShapeDtypeStruct(slot.shape, jnp.float32)
    kernel = functools.partial(select_kernel, capacity)
    return call_kernel("select", kernel, out_shape, counts, slot, limit=8 * 2**20)[0]


def swap_cores(x):
    cores = lax.axis_size("sub")
    return lax.ppermute(x, "sub", [(i, i ^ 1) for i in range(cores)])


def body_by_column(embeddings, cluster_id):
    doc_count, feature_count = embeddings.shape
    helpers, cores = lax.axis_size("helper"), lax.axis_size("sub")

    def send(x, owners=(0, 1, 2, 3), turns=(0, 0, 0, 0), swaps=(0, 0, 0, 0), still=()):
        pairs = []
        for here, (there, turn, swap) in enumerate(zip(owners, turns, swaps)):
            for h in range(helpers):
                for c in range(cores):
                    source = (here * helpers + h) * cores + c
                    target = (there * helpers + (h ^ turn)) * cores + (c ^ swap)
                    pairs.append((source, source if c in still else target))
        return lax.ppermute(x, ("owner", "helper", "sub"), pairs)

    def along(x, still=()):
        return send(x, owners=(1, 0, 3, 2), still=still)

    def middle(x):
        return send(x, owners=(0, 2, 1, 3), swaps=(1, 0, 0, 1))

    def across(x, still=()):
        return send(x, turns=(1, 1, 1, 1), still=still)

    def middle_across(x):
        return send(x, turns=(0, 1, 1, 0), swaps=(1, 0, 0, 1))

    def other(x):
        return send(x, swaps=(1, 1, 1, 1))

    def sums(count, blocks=1):
        return jax.ShapeDtypeStruct((blocks, count), jnp.float32)

    part = doc_count // 2
    pieces = [
        jax.ShapeDtypeStruct((count + ID_ROWS, feature_count), jnp.bfloat16)
        for count in (doc_count, part, part)
    ]
    own, own_a, own_b = call_kernel(
        "prepare", prepare_kernel, pieces, embeddings, cluster_id.reshape(1, doc_count)
    )
    end, next_own, own_o = along(own), middle(own), other(own)
    x = [across(own_a), across(own_b)]
    far = middle(end)
    end_a = call_kernel("half", half_kernel, pieces[1], end)
    x_end = [middle_across(end_a), along(x[1])]
    end_o, x_o = other(end), [other(piece) for piece in x]
    x_end_o = [other(piece) for piece in x_end]

    before = call_kernel(
        "first",
        first_kernel,
        sums(doc_count, 6),
        own,
        end,
        next_own,
        *x,
        own_o,
        end_o,
        *x_o,
    )
    before_x = call_kernel(
        "more", more_kernel, sums(doc_count, 2), own, end, next_own, *x_end, *x_end_o,
    )
    here = call_kernel(
        "last",
        last_kernel,
        sums(doc_count, 8),
        far,
        own,
        end,
        *x,
        *x_end,
        own_o,
        end_o,
        *x_o,
        *x_end_o,
        before,
        before_x,
    )
    stay, go = call_kernel("cores", cores_kernel, [sums(doc_count, 4)] * 2, here, other(here))
    own_sum, end_sum = call_kernel(
        "across", across_kernel, [sums(doc_count, 2)] * 2, stay, across(go, still=(0,))
    )
    here, there = call_kernel(
        "along", along_kernel, [sums(doc_count)] * 2, own_sum, along(end_sum, still=(0,))
    )
    return call_kernel(
        "choose", choose_kernel, sums(doc_count), here, other(there), limit=8 * 2**20
    )[0]


def body_by_owner(embeddings, cluster_id):
    doc_count, feature_count = embeddings.shape
    owners, helpers = lax.axis_size("owner"), lax.axis_size("helper")
    clusters = CL_OWN * owners
    capacity = 2 * doc_count // clusters
    mine = lax.axis_index("helper") % CL_OWN

    def partner(x):
        return lax.ppermute(x, "helper", [(i, i ^ 1) for i in range(helpers)])

    outgoing, slot = call_kernel(
        "route",
        functools.partial(route_kernel, clusters, capacity),
        [
            jax.ShapeDtypeStruct((clusters * capacity, feature_count), jnp.bfloat16),
            jax.ShapeDtypeStruct((1, doc_count), jnp.int32),
        ],
        embeddings,
        cluster_id.reshape(1, doc_count),
    )
    outgoing = outgoing.reshape(owners, CL_OWN, capacity, feature_count)
    arrived = lax.all_to_all(outgoing, "owner", split_axis=0, concat_axis=0, tiled=True)
    kept = lax.dynamic_index_in_dim(arrived, mine, 1, keepdims=False)
    given = partner(lax.dynamic_index_in_dim(arrived, 1 - mine, 1, keepdims=False))
    own = jnp.stack([kept, given]).reshape(CL_OWN * owners * capacity, feature_count)
    others = [swap_cores(own)]
    for step in range(CL_OWN, helpers, CL_OWN):
        turn = [(i, (i + step) % helpers) for i in range(helpers)]
        others += [lax.ppermute(x, "helper", turn) for x in (own, others[0])]
    counts = soft_counts([own, *others])
    counts = counts.reshape(CL_OWN, owners, capacity)
    kept, given = counts[0], partner(counts[1])
    counts = jnp.where(mine == 0, jnp.stack([kept, given], 1), jnp.stack([given, kept], 1))
    back = lax.all_to_all(counts, "owner", split_axis=0, concat_axis=0, tiled=True)
    return select(back.reshape(clusters, 1, capacity), slot, capacity)


def solution(mesh):
    in_specs = (
        P(("groups", "owner", "helper", "sub"), None),
        P(("groups", "owner", "helper", "sub")),
    )
    out_specs = P(("groups", "owner", "helper", "sub"))
    columns = tuple(mesh.shape[axis] for axis in ("owner", "helper", "sub")) == (4, 2, 2)
    body = body_by_column if columns else body_by_owner
    return jax.shard_map(body, mesh=mesh, in_specs=in_specs, out_specs=out_specs, check_vma=False)
```

```python
import functools
import math

import jax
import jax.numpy as jnp
from jax import lax
from jax.experimental import pallas as pl
from jax.experimental.pallas import tpu as pltpu
from jax.sharding import PartitionSpec as P

CL_OWN = 2

epsilon = 1e-06
threshold = 0.8
sharpness = 0.05

EMPTY = 4.0
TILE = 256
VMEM = pl.BlockSpec(memory_space=pltpu.VMEM)


def chip_index():
    return lax.axis_index("owner") * CL_OWN + lax.axis_index("helper")


def slots_of(ids, clusters, capacity):
    doc_count = ids.shape[1]
    member = lax.broadcasted_iota(jnp.int32, (clusters, doc_count), 0) == ids
    earlier = lax.broadcasted_iota(jnp.int32, (doc_count, doc_count), 0) < (
        lax.broadcasted_iota(jnp.int32, (doc_count, doc_count), 1)
    )
    ahead = jnp.dot(
        member.astype(jnp.bfloat16), earlier.astype(jnp.bfloat16), preferred_element_type=jnp.float32
    )
    rank = jnp.sum(jnp.where(member, ahead, 0.0), axis=0, keepdims=True).astype(jnp.int32)
    return ids * capacity + rank


def lay(rows_ref, slot, slots):
    doc_count, feature_count = rows_ref.shape
    dispatch = lax.broadcasted_iota(jnp.int32, (slots, doc_count), 0) == slot
    filled = jnp.sum(dispatch.astype(jnp.float32), axis=1, keepdims=True) > 0
    laid = jnp.dot(
        dispatch.astype(jnp.bfloat16), rows_ref[...], preferred_element_type=jnp.float32
    )
    factor = lax.rsqrt(
        jnp.mean(laid * laid, axis=-1, keepdims=True) + epsilon
    ) * feature_count ** (-0.5)
    lane = lax.broadcasted_iota(jnp.int32, laid.shape, 1)
    return jnp.where(filled | (lane > 0), laid * factor, EMPTY).astype(jnp.bfloat16)


def slots_of_steps(slot, capacity, steps):
    cores = lax.axis_size("sub")
    by_distance = slot ^ (chip_index() * capacity)
    distance = by_distance // capacity
    rank = by_distance - distance * capacity
    step = jnp.full_like(slot, -1)
    for place, p in enumerate(steps):
        step = jnp.where(distance == p * cores + lax.axis_index("sub"), place, step)
    return jnp.where(step < 0, -1, step * capacity + rank)


def route_first_kernel(clusters, capacity, step, rows_ref, ids_ref, piece_ref, slot_ref):
    slot = slots_of(ids_ref[...], clusters, capacity)
    slot_ref[...] = slot
    piece_ref[...] = lay(rows_ref, slots_of_steps(slot, capacity, [step]), capacity)


def route_rest_kernel(clusters, capacity, first, steps, *refs):
    own_rows, other_rows, own_slot, other_ids, first_ref, *piece_refs = refs
    slot = slots_of_steps(own_slot[...], capacity, steps)
    laid = lay(own_rows, slot, len(steps) * capacity)
    for k, piece in enumerate(piece_refs):
        piece[:capacity] = laid[k * capacity : (k + 1) * capacity]
    slot = slots_of(other_ids[...], clusters, capacity)
    slot = slots_of_steps(slot, capacity, [first, *steps])
    laid = lay(other_rows, slot, (1 + len(steps)) * capacity)
    first_ref[...] = laid[:capacity]
    for k, piece in enumerate(piece_refs):
        piece[capacity:] = laid[(k + 1) * capacity : (k + 2) * capacity]


def route_kernel(clusters, capacity, rows_ref, ids_ref, piece_ref, slot_ref):
    slot = slots_of(ids_ref[...], clusters, capacity)
    slot_ref[...] = slot
    piece_ref[...] = lay(rows_ref, slot, piece_ref.shape[0])


def call_kernel(name, kernel, out_shape, *args, limit=32 * 2**20, flops=0):
    cost = pl.CostEstimate(flops=flops, bytes_accessed=0, transcendentals=0) if flops else None
    return pl.pallas_call(
        kernel,
        out_shape=out_shape,
        in_specs=[VMEM] * len(args),
        out_specs=jax.tree.map(lambda _: VMEM, out_shape),
        compiler_params=pltpu.CompilerParams(vmem_limit_bytes=limit),
        cost_estimate=cost,
        name=name,
    )(*args)


def join_kernel(first_ref, second_ref, out_ref):
    rows = first_ref.shape[0]
    out_ref[:rows] = first_ref[...]
    out_ref[rows:] = second_ref[...]


def count_against(pieces, own, size, starts=()):
    slope = -math.log2(math.e) / sharpness
    total = jnp.zeros((1, own.shape[0]), jnp.float32)
    first = 0
    for piece in pieces:
        for row in range(0, piece.shape[0], TILE):
            other = piece[row : row + TILE]
            count = other.shape[0]
            scores = lax.dot_general(
                other, own, (((1,), (1,)), ((), ())), preferred_element_type=jnp.float32
            )
            odds = 1.0 + jnp.minimum(jnp.exp2(scores * slope - threshold * slope), 1e30)
            weights = pl.reciprocal(odds, approx=True)
            weights = weights * (2.0 - odds * weights)
            weights = jnp.where(other[:, :1].astype(jnp.float32) < 0.5 * EMPTY, weights, 0.0)
            for k, start in enumerate(starts):
                if start + size > first and start < first + count:
                    itself = lax.broadcasted_iota(jnp.int32, weights.shape, 1) + (
                        start - k * size - first
                    )
                    inside = lax.broadcasted_iota(jnp.int32, weights.shape, 1) // size == k
                    same = lax.broadcasted_iota(jnp.int32, weights.shape, 0) == itself
                    weights = jnp.where(inside & same, 0.0, weights)
            total = total + jnp.sum(weights, axis=0, keepdims=True)
            first += count
    return total


def count_kernel(starts, size, *refs):
    *piece_refs, own_ref, count_ref = refs
    rows, first = [], 0
    for piece in piece_refs:
        for start in starts:
            if first <= start < first + piece.shape[0]:
                rows.append(piece[start - first : start - first + size])
        first += piece.shape[0]
    own = jnp.concatenate(rows, axis=0)
    own_ref[...] = own
    count_ref[...] = count_against(piece_refs, own, size, starts)


def soft_counts(pieces, starts, size):
    count = len(starts) * size
    return call_kernel(
        "count",
        functools.partial(count_kernel, starts, size),
        [
            jax.ShapeDtypeStruct((count, pieces[0].shape[1]), jnp.bfloat16),
            jax.ShapeDtypeStruct((1, count), jnp.float32),
        ],
        *pieces,
    )


def finish_kernel(size, places, *refs):
    *early_refs, here_ref, there_ref, own_ref, early_ref, count_ref = refs
    late_refs = [here_ref, there_ref]
    late_own = jnp.concatenate([here_ref[:size], there_ref[size:]], axis=0)
    starts = [0, here_ref.shape[0] + size]
    total = early_ref[...] + count_against(late_refs, own_ref[...], size)
    late_total = count_against(early_refs, late_own, size) + count_against(
        late_refs, late_own, size, starts
    )
    early_blocks = own_ref.shape[0] // size
    for k, place in enumerate(places()):
        source, j = (total, k) if k < early_blocks else (late_total, k - early_blocks)
        count_ref[pl.ds(place, 1), 0, :] = source[:, j * size : (j + 1) * size]


def select_kernel(capacity, counts_ref, slot_ref, out_ref):
    counts = counts_ref[:, 0, :]
    slot = slot_ref[...]
    doc_count = slot.shape[1]
    block = slot // capacity
    rank = slot - block * capacity
    hot = (lax.broadcasted_iota(jnp.int32, (capacity, doc_count), 0) == rank).astype(jnp.float32)
    by_block = jnp.dot(
        counts, hot, precision=lax.Precision.HIGHEST, preferred_element_type=jnp.float32
    )
    chosen = lax.broadcasted_iota(jnp.int32, by_block.shape, 0) == block
    out_ref[...] = jnp.sum(jnp.where(chosen, by_block, 0.0), axis=0, keepdims=True)


def select(counts, slot, capacity):
    out_shape = jax.ShapeDtypeStruct(slot.shape, jnp.float32)
    kernel = functools.partial(select_kernel, capacity)
    return call_kernel("select", kernel, out_shape, counts, slot, limit=8 * 2**20)[0]


def swap_cores(x):
    cores = lax.axis_size("sub")
    return lax.ppermute(x, "sub", [(i, i ^ 1) for i in range(cores)])


def body_by_chip(embeddings, cluster_id):
    doc_count, feature_count = embeddings.shape
    clusters = CL_OWN * lax.axis_size("owner")
    capacity = 2 * doc_count // clusters
    cores = lax.axis_size("sub")
    steps = clusters // cores

    def across(x, p):
        pairs = [
            (chip * cores + core, (chip ^ (p * cores + core)) * cores + core)
            for chip in range(clusters)
            for core in range(cores)
        ]
        return lax.ppermute(x, ("owner", "helper", "sub"), pairs)

    ids = cluster_id.reshape(1, doc_count)
    other_rows, other_ids = swap_cores(embeddings), swap_cores(ids)
    first, last = steps // 2, steps - 1
    middle = [p for p in range(steps) if p not in (first, last)]
    half = jax.ShapeDtypeStruct((capacity, feature_count), jnp.bfloat16)
    whole = jax.ShapeDtypeStruct((cores * capacity, feature_count), jnp.bfloat16)

    first_own, slot = call_kernel(
        "route_first",
        functools.partial(route_first_kernel, clusters, capacity, first),
        [half, jax.ShapeDtypeStruct((1, doc_count), jnp.int32)],
        embeddings,
        ids,
    )
    first_own = across(first_own, first)
    first_other, *rest = call_kernel(
        "route_rest",
        functools.partial(route_rest_kernel, clusters, capacity, first, [*middle, last]),
        [half] + [whole] * (steps - 1),
        embeddings,
        other_rows,
        slot,
        other_ids,
    )
    first_other = across(first_other, first)
    rest = [across(piece, p) for piece, p in zip(rest, [*middle, last])]

    first_both = call_kernel("join", join_kernel, whole, first_own, first_other, flops=10**10)
    early = [first_both, *rest[:-1]]
    early += [swap_cores(x) for x in early]
    late = [rest[-1], swap_cores(rest[-1])]
    span = cores * capacity
    half_way = span * (steps - 1)
    starts = [k * span for k in range(steps - 1)]
    starts += [half_way + start + capacity for start in starts]

    def places():
        chip, core = chip_index(), lax.axis_index("sub")
        return (
            [chip ^ (p * cores + core) for p in (first, *middle)]
            + [chip ^ (p * cores + 1 - core) for p in (first, *middle)]
            + [chip ^ (last * cores + core), chip ^ (last * cores + 1 - core)]
        )

    counts = call_kernel(
        "finish",
        functools.partial(finish_kernel, capacity, places),
        jax.ShapeDtypeStruct((clusters, 1, capacity), jnp.float32),
        *early,
        *late,
        *soft_counts(early, starts, capacity),
    )
    back = lax.all_to_all(counts, ("owner", "helper"), split_axis=0, concat_axis=0, tiled=True)
    return select(back, slot, capacity)


def body_by_owner(embeddings, cluster_id):
    doc_count, feature_count = embeddings.shape
    owners, helpers = lax.axis_size("owner"), lax.axis_size("helper")
    clusters = CL_OWN * owners
    capacity = 2 * doc_count // clusters
    mine = lax.axis_index("helper") % CL_OWN

    def partner(x):
        return lax.ppermute(x, "helper", [(i, i ^ 1) for i in range(helpers)])

    outgoing, slot = call_kernel(
        "route",
        functools.partial(route_kernel, clusters, capacity),
        [
            jax.ShapeDtypeStruct((clusters * capacity, feature_count), jnp.bfloat16),
            jax.ShapeDtypeStruct((1, doc_count), jnp.int32),
        ],
        embeddings,
        cluster_id.reshape(1, doc_count),
    )
    outgoing = outgoing.reshape(owners, CL_OWN, capacity, feature_count)
    arrived = lax.all_to_all(outgoing, "owner", split_axis=0, concat_axis=0, tiled=True)
    kept = lax.dynamic_index_in_dim(arrived, mine, 1, keepdims=False)
    given = partner(lax.dynamic_index_in_dim(arrived, 1 - mine, 1, keepdims=False))
    own = jnp.stack([kept, given]).reshape(CL_OWN * owners * capacity, feature_count)
    others = [swap_cores(own)]
    for step in range(CL_OWN, helpers, CL_OWN):
        turn = [(i, (i + step) % helpers) for i in range(helpers)]
        others += [lax.ppermute(x, "helper", turn) for x in (own, others[0])]
    _, counts = soft_counts([own, *others], [0], own.shape[0])
    counts = counts.reshape(CL_OWN, owners, capacity)
    kept, given = counts[0], partner(counts[1])
    counts = jnp.where(mine == 0, jnp.stack([kept, given], 1), jnp.stack([given, kept], 1))
    back = lax.all_to_all(counts, "owner", split_axis=0, concat_axis=0, tiled=True)
    return select(back.reshape(clusters, 1, capacity), slot, capacity)


def solution(mesh):
    in_specs = (
        P(("groups", "owner", "helper", "sub"), None),
        P(("groups", "owner", "helper", "sub")),
    )
    out_specs = P(("groups", "owner", "helper", "sub"))
    body = body_by_chip if mesh.shape["helper"] == CL_OWN else body_by_owner
    return jax.shard_map(body, mesh=mesh, in_specs=in_specs, out_specs=out_specs, check_vma=False)
```

```python
import functools
import math

import jax
import jax.numpy as jnp
from jax import lax
from jax.experimental import pallas as pl
from jax.experimental.pallas import tpu as pltpu
from jax.sharding import PartitionSpec as P

CL_OWN = 2

epsilon = 1e-06
threshold = 0.8
sharpness = 0.05

EMPTY = 4.0
TILE = 1024
VMEM = pl.BlockSpec(memory_space=pltpu.VMEM)


def chip_index():
    return lax.axis_index("owner") * CL_OWN + lax.axis_index("helper")


def slots_of(ids, clusters, capacity):
    doc_count = ids.shape[1]
    member = lax.broadcasted_iota(jnp.int32, (clusters, doc_count), 0) == ids
    earlier = lax.broadcasted_iota(jnp.int32, (doc_count, doc_count), 0) < (
        lax.broadcasted_iota(jnp.int32, (doc_count, doc_count), 1)
    )
    ahead = jnp.dot(
        member.astype(jnp.bfloat16), earlier.astype(jnp.bfloat16), preferred_element_type=jnp.float32
    )
    rank = jnp.sum(jnp.where(member, ahead, 0.0), axis=0, keepdims=True).astype(jnp.int32)
    return ids * capacity + rank


def lay(rows_ref, slot, slots):
    doc_count, feature_count = rows_ref.shape
    dispatch = lax.broadcasted_iota(jnp.int32, (slots, doc_count), 0) == slot
    filled = jnp.sum(dispatch.astype(jnp.float32), axis=1, keepdims=True) > 0
    laid = jnp.dot(
        dispatch.astype(jnp.bfloat16), rows_ref[...], preferred_element_type=jnp.float32
    )
    factor = lax.rsqrt(
        jnp.mean(laid * laid, axis=-1, keepdims=True) + epsilon
    ) * feature_count ** (-0.5)
    lane = lax.broadcasted_iota(jnp.int32, laid.shape, 1)
    return jnp.where(filled | (lane > 0), laid * factor, EMPTY).astype(jnp.bfloat16)


def slots_of_steps(slot, capacity, steps):
    cores = lax.axis_size("sub")
    by_distance = slot ^ (chip_index() * capacity)
    distance = by_distance // capacity
    rank = by_distance - distance * capacity
    step = jnp.full_like(slot, -1)
    for place, p in enumerate(steps):
        step = jnp.where(distance == p * cores + lax.axis_index("sub"), place, step)
    return jnp.where(step < 0, -1, step * capacity + rank)


def route_first_kernel(clusters, capacity, step, rows_ref, ids_ref, piece_ref, slot_ref):
    slot = slots_of(ids_ref[...], clusters, capacity)
    slot_ref[...] = slot
    piece_ref[...] = lay(rows_ref, slots_of_steps(slot, capacity, [step]), capacity)


def route_rest_kernel(clusters, capacity, first, steps, *refs):
    own_rows, other_rows, own_slot, other_ids, first_ref, *piece_refs = refs
    slot = slots_of_steps(own_slot[...], capacity, steps)
    laid = lay(own_rows, slot, len(steps) * capacity)
    for k, piece in enumerate(piece_refs):
        piece[:capacity] = laid[k * capacity : (k + 1) * capacity]
    slot = slots_of(other_ids[...], clusters, capacity)
    slot = slots_of_steps(slot, capacity, [first, *steps])
    laid = lay(other_rows, slot, (1 + len(steps)) * capacity)
    first_ref[...] = laid[:capacity]
    for k, piece in enumerate(piece_refs):
        piece[capacity:] = laid[(k + 1) * capacity : (k + 2) * capacity]


def route_kernel(clusters, capacity, rows_ref, ids_ref, piece_ref, slot_ref):
    slot = slots_of(ids_ref[...], clusters, capacity)
    slot_ref[...] = slot
    piece_ref[...] = lay(rows_ref, slot, piece_ref.shape[0])


def call_kernel(name, kernel, out_shape, *args, limit=32 * 2**20, flops=0):
    cost = pl.CostEstimate(flops=flops, bytes_accessed=0, transcendentals=0) if flops else None
    return pl.pallas_call(
        kernel,
        out_shape=out_shape,
        in_specs=[VMEM] * len(args),
        out_specs=jax.tree.map(lambda _: VMEM, out_shape),
        compiler_params=pltpu.CompilerParams(vmem_limit_bytes=limit),
        cost_estimate=cost,
        name=name,
    )(*args)


def join_kernel(first_ref, second_ref, out_ref):
    rows = first_ref.shape[0]
    out_ref[:rows] = first_ref[...]
    out_ref[rows:] = second_ref[...]


def blocks(rows, starts, size):
    return jnp.concatenate([rows[start : start + size] for start in starts], axis=0)


def count_against(rows, own, starts, size):
    column = lax.broadcasted_iota(jnp.int32, (1, own.shape[0]), 1)
    itself = jnp.full_like(column, -1)
    for k, start in enumerate(starts):
        itself = jnp.where(column // size == k, column + (start - k * size), itself)
    slope = -math.log2(math.e) / sharpness
    total = jnp.zeros((1, own.shape[0]), jnp.float32)
    for first in range(0, rows.shape[0], TILE):
        other = rows[first : first + TILE]
        scores = lax.dot_general(
            other, own, (((1,), (1,)), ((), ())), preferred_element_type=jnp.float32
        )
        weights = 1.0 / (1.0 + jnp.exp2(scores * slope - threshold * slope))
        keep = other[:, :1].astype(jnp.float32) < 0.5 * EMPTY
        if starts:
            keep = keep & (lax.broadcasted_iota(jnp.int32, scores.shape, 0) + first != itself)
        total = total + jnp.sum(jnp.where(keep, weights, 0.0), axis=0, keepdims=True)
    return total


def count_kernel(starts, size, *refs):
    *piece_refs, count_ref = refs
    rows = jnp.concatenate([piece[...] for piece in piece_refs], axis=0)
    count_ref[...] = count_against(rows, blocks(rows, starts, size), starts, size)


def soft_counts(pieces, starts, size):
    out_shape = jax.ShapeDtypeStruct((1, len(starts) * size), jnp.float32)
    return call_kernel("count", functools.partial(count_kernel, starts, size), out_shape, *pieces)


def finish_kernel(starts, late_pieces, late_starts, places, *refs):
    *piece_refs, early_ref, count_ref = refs
    size = count_ref.shape[2]
    early = jnp.concatenate([piece[...] for piece in piece_refs[:-late_pieces]], axis=0)
    late = jnp.concatenate([piece[...] for piece in piece_refs[-late_pieces:]], axis=0)
    own = blocks(early, starts, size)
    late_own = blocks(late, late_starts, size)
    total = early_ref[...] + count_against(late, own, [], size)
    late_total = count_against(early, late_own, [], size) + count_against(
        late, late_own, late_starts, size
    )
    for k, place in enumerate(places()):
        source, j = (total, k) if k < len(starts) else (late_total, k - len(starts))
        count_ref[pl.ds(place, 1), 0, :] = source[:, j * size : (j + 1) * size]


def select_kernel(capacity, counts_ref, slot_ref, out_ref):
    counts = counts_ref[:, 0, :]
    slot = slot_ref[...]
    doc_count = slot.shape[1]
    block = slot // capacity
    rank = slot - block * capacity
    hot = (lax.broadcasted_iota(jnp.int32, (capacity, doc_count), 0) == rank).astype(jnp.float32)
    by_block = jnp.dot(
        counts, hot, precision=lax.Precision.HIGHEST, preferred_element_type=jnp.float32
    )
    chosen = lax.broadcasted_iota(jnp.int32, by_block.shape, 0) == block
    out_ref[...] = jnp.sum(jnp.where(chosen, by_block, 0.0), axis=0, keepdims=True)


def select(counts, slot, capacity):
    out_shape = jax.ShapeDtypeStruct(slot.shape, jnp.float32)
    kernel = functools.partial(select_kernel, capacity)
    return call_kernel("select", kernel, out_shape, counts, slot, limit=8 * 2**20)[0]


def swap_cores(x):
    cores = lax.axis_size("sub")
    return lax.ppermute(x, "sub", [(i, i ^ 1) for i in range(cores)])


def body_by_chip(embeddings, cluster_id):
    doc_count, feature_count = embeddings.shape
    clusters = CL_OWN * lax.axis_size("owner")
    capacity = 2 * doc_count // clusters
    cores = lax.axis_size("sub")
    steps = clusters // cores

    def across(x, p):
        pairs = [
            (chip * cores + core, (chip ^ (p * cores + core)) * cores + core)
            for chip in range(clusters)
            for core in range(cores)
        ]
        return lax.ppermute(x, ("owner", "helper", "sub"), pairs)

    ids = cluster_id.reshape(1, doc_count)
    other_rows, other_ids = swap_cores(embeddings), swap_cores(ids)
    first, last = steps // 2, steps - 1
    middle = [p for p in range(steps) if p not in (first, last)]
    half = jax.ShapeDtypeStruct((capacity, feature_count), jnp.bfloat16)
    whole = jax.ShapeDtypeStruct((cores * capacity, feature_count), jnp.bfloat16)

    first_own, slot = call_kernel(
        "route_first",
        functools.partial(route_first_kernel, clusters, capacity, first),
        [half, jax.ShapeDtypeStruct((1, doc_count), jnp.int32)],
        embeddings,
        ids,
    )
    first_own = across(first_own, first)
    first_other, *rest = call_kernel(
        "route_rest",
        functools.partial(route_rest_kernel, clusters, capacity, first, [*middle, last]),
        [half] + [whole] * (steps - 1),
        embeddings,
        other_rows,
        slot,
        other_ids,
    )
    first_other = across(first_other, first)
    rest = [across(piece, p) for piece, p in zip(rest, [*middle, last])]

    first_both = call_kernel("join", join_kernel, whole, first_own, first_other, flops=10**10)
    early = [first_both, *rest[:-1]]
    early += [swap_cores(x) for x in early]
    late = [rest[-1], swap_cores(rest[-1])]
    span = cores * capacity
    half_way = span * (steps - 1)
    starts = [k * span for k in range(steps - 1)]
    starts += [half_way + start + capacity for start in starts]
    late_starts = [0, span + capacity]

    def places():
        chip, core = chip_index(), lax.axis_index("sub")
        return (
            [chip ^ (p * cores + core) for p in (first, *middle)]
            + [chip ^ (p * cores + 1 - core) for p in (first, *middle)]
            + [chip ^ (last * cores + core), chip ^ (last * cores + 1 - core)]
        )

    counts = call_kernel(
        "finish",
        functools.partial(finish_kernel, starts, len(late), late_starts, places),
        jax.ShapeDtypeStruct((clusters, 1, capacity), jnp.float32),
        *early,
        *late,
        soft_counts(early, starts, capacity),
    )
    back = lax.all_to_all(counts, ("owner", "helper"), split_axis=0, concat_axis=0, tiled=True)
    return select(back, slot, capacity)


def body_by_owner(embeddings, cluster_id):
    doc_count, feature_count = embeddings.shape
    owners, helpers = lax.axis_size("owner"), lax.axis_size("helper")
    clusters = CL_OWN * owners
    capacity = 2 * doc_count // clusters
    mine = lax.axis_index("helper") % CL_OWN

    def partner(x):
        return lax.ppermute(x, "helper", [(i, i ^ 1) for i in range(helpers)])

    outgoing, slot = call_kernel(
        "route",
        functools.partial(route_kernel, clusters, capacity),
        [
            jax.ShapeDtypeStruct((clusters * capacity, feature_count), jnp.bfloat16),
            jax.ShapeDtypeStruct((1, doc_count), jnp.int32),
        ],
        embeddings,
        cluster_id.reshape(1, doc_count),
    )
    outgoing = outgoing.reshape(owners, CL_OWN, capacity, feature_count)
    arrived = lax.all_to_all(outgoing, "owner", split_axis=0, concat_axis=0, tiled=True)
    kept = lax.dynamic_index_in_dim(arrived, mine, 1, keepdims=False)
    given = partner(lax.dynamic_index_in_dim(arrived, 1 - mine, 1, keepdims=False))
    own = jnp.stack([kept, given]).reshape(CL_OWN * owners * capacity, feature_count)
    others = [swap_cores(own)]
    for step in range(CL_OWN, helpers, CL_OWN):
        turn = [(i, (i + step) % helpers) for i in range(helpers)]
        others += [lax.ppermute(x, "helper", turn) for x in (own, others[0])]
    counts = soft_counts([own, *others], [0], own.shape[0])
    counts = counts.reshape(CL_OWN, owners, capacity)
    kept, given = counts[0], partner(counts[1])
    counts = jnp.where(mine == 0, jnp.stack([kept, given], 1), jnp.stack([given, kept], 1))
    back = lax.all_to_all(counts, "owner", split_axis=0, concat_axis=0, tiled=True)
    return select(back.reshape(clusters, 1, capacity), slot, capacity)


def solution(mesh):
    in_specs = (
        P(("groups", "owner", "helper", "sub"), None),
        P(("groups", "owner", "helper", "sub")),
    )
    out_specs = P(("groups", "owner", "helper", "sub"))
    body = body_by_chip if mesh.shape["helper"] == CL_OWN else body_by_owner
    return jax.shard_map(body, mesh=mesh, in_specs=in_specs, out_specs=out_specs, check_vma=False)
```

```python
import functools
import math

import jax
import jax.numpy as jnp
from jax import lax
from jax.experimental import pallas as pl
from jax.experimental.pallas import tpu as pltpu
from jax.sharding import PartitionSpec as P

CL_OWN = 2

epsilon = 1e-06
threshold = 0.8
sharpness = 0.05

EMPTY = 4.0
TILE = 1024
LANES = 128
VMEM = pl.BlockSpec(memory_space=pltpu.VMEM)


def chip_index():
    return lax.axis_index("owner") * CL_OWN + lax.axis_index("helper")


def slots_of(ids, clusters, capacity):
    doc_count = ids.shape[1]
    member = lax.broadcasted_iota(jnp.int32, (clusters, doc_count), 0) == ids
    earlier = lax.broadcasted_iota(jnp.int32, (doc_count, doc_count), 0) < (
        lax.broadcasted_iota(jnp.int32, (doc_count, doc_count), 1)
    )
    ahead = jnp.dot(
        member.astype(jnp.bfloat16), earlier.astype(jnp.bfloat16), preferred_element_type=jnp.float32
    )
    rank = jnp.sum(jnp.where(member, ahead, 0.0), axis=0, keepdims=True).astype(jnp.int32)
    return ids * capacity + rank


def lay(rows_ref, slot, slots):
    doc_count, feature_count = rows_ref.shape
    dispatch = lax.broadcasted_iota(jnp.int32, (slots, doc_count), 0) == slot
    filled = jnp.sum(dispatch.astype(jnp.float32), axis=1, keepdims=True) > 0
    laid = jnp.dot(
        dispatch.astype(jnp.bfloat16), rows_ref[...], preferred_element_type=jnp.float32
    )
    factor = lax.rsqrt(
        jnp.mean(laid * laid, axis=-1, keepdims=True) + epsilon
    ) * feature_count ** (-0.5)
    lane = lax.broadcasted_iota(jnp.int32, laid.shape, 1)
    return jnp.where(filled | (lane > 0), laid * factor, EMPTY).astype(jnp.bfloat16)


def slots_of_steps(slot, capacity, steps):
    cores = lax.axis_size("sub")
    by_distance = slot ^ (chip_index() * capacity)
    distance = by_distance // capacity
    rank = by_distance - distance * capacity
    step = jnp.full_like(slot, -1)
    for place, p in enumerate(steps):
        step = jnp.where(distance == p * cores + lax.axis_index("sub"), place, step)
    return jnp.where(step < 0, -1, step * capacity + rank)


def route_first_kernel(clusters, capacity, step, rows_ref, ids_ref, piece_ref, slot_ref):
    slot = slots_of(ids_ref[...], clusters, capacity)
    slot_ref[...] = slot
    piece_ref[...] = lay(rows_ref, slots_of_steps(slot, capacity, [step]), capacity)


def route_rest_kernel(clusters, capacity, first, steps, *refs):
    own_rows, other_rows, own_slot, other_ids, first_ref, *piece_refs = refs
    slot = slots_of_steps(own_slot[...], capacity, steps)
    laid = lay(own_rows, slot, len(steps) * capacity)
    for k, piece in enumerate(piece_refs):
        piece[:capacity] = laid[k * capacity : (k + 1) * capacity]
    slot = slots_of(other_ids[...], clusters, capacity)
    slot = slots_of_steps(slot, capacity, [first, *steps])
    laid = lay(other_rows, slot, (1 + len(steps)) * capacity)
    first_ref[...] = laid[:capacity]
    for k, piece in enumerate(piece_refs):
        piece[capacity:] = laid[(k + 1) * capacity : (k + 2) * capacity]


def route_kernel(clusters, capacity, rows_ref, ids_ref, piece_ref, slot_ref):
    slot = slots_of(ids_ref[...], clusters, capacity)
    slot_ref[...] = slot
    piece_ref[...] = lay(rows_ref, slot, piece_ref.shape[0])


def call_kernel(name, kernel, out_shape, *args, limit=32 * 2**20, flops=0):
    cost = pl.CostEstimate(flops=flops, bytes_accessed=0, transcendentals=0) if flops else None
    return pl.pallas_call(
        kernel,
        out_shape=out_shape,
        in_specs=[VMEM] * len(args),
        out_specs=jax.tree.map(lambda _: VMEM, out_shape),
        compiler_params=pltpu.CompilerParams(vmem_limit_bytes=limit),
        cost_estimate=cost,
        name=name,
    )(*args)


def join_kernel(first_ref, second_ref, out_ref):
    rows = first_ref.shape[0]
    out_ref[:rows] = first_ref[...]
    out_ref[rows:] = second_ref[...]


def blocks(rows, starts, size):
    return jnp.concatenate([rows[start : start + size] for start in starts], axis=0)


def count_against(rows, own, starts, size):
    column = lax.broadcasted_iota(jnp.int32, (1, own.shape[0]), 1)
    itself = jnp.full_like(column, -1)
    for k, start in enumerate(starts):
        itself = jnp.where(column // size == k, column + (start - k * size), itself)
    slope = -math.log2(math.e) / sharpness
    total = jnp.zeros((1, own.shape[0]), jnp.float32)
    for first in range(0, rows.shape[0], TILE):
        other = rows[first : first + TILE]
        scores = lax.dot_general(
            other, own, (((1,), (1,)), ((), ())), preferred_element_type=jnp.float32
        )
        weights = 1.0 / (1.0 + jnp.exp2(scores * slope - threshold * slope))
        keep = other[:, :1].astype(jnp.float32) < 0.5 * EMPTY
        if starts:
            keep = keep & (lax.broadcasted_iota(jnp.int32, scores.shape, 0) + first != itself)
        total = total + jnp.sum(jnp.where(keep, weights, 0.0), axis=0, keepdims=True)
    return total


def count_kernel(starts, size, *refs):
    *piece_refs, count_ref = refs
    rows = jnp.concatenate([piece[...] for piece in piece_refs], axis=0)
    count_ref[...] = count_against(rows, blocks(rows, starts, size), starts, size)


def soft_counts(pieces, starts, size):
    out_shape = jax.ShapeDtypeStruct((1, len(starts) * size), jnp.float32)
    return call_kernel("count", functools.partial(count_kernel, starts, size), out_shape, *pieces)


def finish_kernel(starts, late_pieces, late_starts, places, here_size, *refs):
    *piece_refs, early_ref, count_ref = refs
    size = here_size
    early = jnp.concatenate([piece[...] for piece in piece_refs[:-late_pieces]], axis=0)
    late = jnp.concatenate([piece[...] for piece in piece_refs[-late_pieces:]], axis=0)
    own = blocks(early, starts, size)
    late_own = blocks(late, late_starts, size)
    total = early_ref[...] + count_against(late, own, [], size)
    late_total = count_against(early, late_own, [], size) + count_against(
        late, late_own, late_starts, size
    )
    for k, place in enumerate(places()):
        source, j = (total, k) if k < len(starts) else (late_total, k - len(starts))
        block = source[:, j * size : (j + 1) * size]
        padding = jnp.zeros((1, count_ref.shape[2] - size), jnp.float32)
        count_ref[pl.ds(place, 1), 0, :] = jnp.concatenate([block, padding], axis=1)


def select_kernel(capacity, counts_ref, slot_ref, out_ref):
    counts = counts_ref[:, 0, :][:, :capacity]
    slot = slot_ref[...]
    doc_count = slot.shape[1]
    block = slot // capacity
    rank = slot - block * capacity
    hot = (lax.broadcasted_iota(jnp.int32, (capacity, doc_count), 0) == rank).astype(jnp.float32)
    by_block = jnp.dot(
        counts, hot, precision=lax.Precision.HIGHEST, preferred_element_type=jnp.float32
    )
    chosen = lax.broadcasted_iota(jnp.int32, by_block.shape, 0) == block
    out_ref[...] = jnp.sum(jnp.where(chosen, by_block, 0.0), axis=0, keepdims=True)


def select(counts, slot, capacity):
    out_shape = jax.ShapeDtypeStruct(slot.shape, jnp.float32)
    kernel = functools.partial(select_kernel, capacity)
    return call_kernel("select", kernel, out_shape, counts, slot, limit=8 * 2**20)[0]


def swap_cores(x):
    cores = lax.axis_size("sub")
    return lax.ppermute(x, "sub", [(i, i ^ 1) for i in range(cores)])


def body_by_chip(embeddings, cluster_id):
    doc_count, feature_count = embeddings.shape
    clusters = CL_OWN * lax.axis_size("owner")
    capacity = 2 * doc_count // clusters
    cores = lax.axis_size("sub")
    steps = clusters // cores

    def across(x, p):
        pairs = [
            (chip * cores + core, (chip ^ (p * cores + core)) * cores + core)
            for chip in range(clusters)
            for core in range(cores)
        ]
        return lax.ppermute(x, ("owner", "helper", "sub"), pairs)

    ids = cluster_id.reshape(1, doc_count)
    other_rows, other_ids = swap_cores(embeddings), swap_cores(ids)
    first, last = steps // 2, steps - 1
    middle = [p for p in range(steps) if p not in (first, last)]
    half = jax.ShapeDtypeStruct((capacity, feature_count), jnp.bfloat16)
    whole = jax.ShapeDtypeStruct((cores * capacity, feature_count), jnp.bfloat16)

    first_own, slot = call_kernel(
        "route_first",
        functools.partial(route_first_kernel, clusters, capacity, first),
        [half, jax.ShapeDtypeStruct((1, doc_count), jnp.int32)],
        embeddings,
        ids,
    )
    first_own = across(first_own, first)
    first_other, *rest = call_kernel(
        "route_rest",
        functools.partial(route_rest_kernel, clusters, capacity, first, [*middle, last]),
        [half] + [whole] * (steps - 1),
        embeddings,
        other_rows,
        slot,
        other_ids,
    )
    first_other = across(first_other, first)
    rest = [across(piece, p) for piece, p in zip(rest, [*middle, last])]

    first_both = call_kernel("join", join_kernel, whole, first_own, first_other, flops=10**10)
    early = [first_both, *rest[:-1]]
    early += [swap_cores(x) for x in early]
    late = [rest[-1], swap_cores(rest[-1])]
    span = cores * capacity
    half_way = span * (steps - 1)
    starts = [k * span for k in range(steps - 1)]
    starts += [half_way + start + capacity for start in starts]
    late_starts = [0, span + capacity]

    def places():
        chip, core = chip_index(), lax.axis_index("sub")
        return (
            [chip ^ (p * cores + core) for p in (first, *middle)]
            + [chip ^ (p * cores + 1 - core) for p in (first, *middle)]
            + [chip ^ (last * cores + core), chip ^ (last * cores + 1 - core)]
        )

    counts = call_kernel(
        "finish",
        functools.partial(finish_kernel, starts, len(late), late_starts, places, capacity),
        jax.ShapeDtypeStruct((clusters, 1, LANES), jnp.float32),
        *early,
        *late,
        soft_counts(early, starts, capacity),
    )
    back = lax.all_to_all(counts, ("owner", "helper"), split_axis=0, concat_axis=0, tiled=True)
    return select(back, slot, capacity)


def body_by_owner(embeddings, cluster_id):
    doc_count, feature_count = embeddings.shape
    owners, helpers = lax.axis_size("owner"), lax.axis_size("helper")
    clusters = CL_OWN * owners
    capacity = 2 * doc_count // clusters
    mine = lax.axis_index("helper") % CL_OWN

    def partner(x):
        return lax.ppermute(x, "helper", [(i, i ^ 1) for i in range(helpers)])

    outgoing, slot = call_kernel(
        "route",
        functools.partial(route_kernel, clusters, capacity),
        [
            jax.ShapeDtypeStruct((clusters * capacity, feature_count), jnp.bfloat16),
            jax.ShapeDtypeStruct((1, doc_count), jnp.int32),
        ],
        embeddings,
        cluster_id.reshape(1, doc_count),
    )
    outgoing = outgoing.reshape(owners, CL_OWN, capacity, feature_count)
    arrived = lax.all_to_all(outgoing, "owner", split_axis=0, concat_axis=0, tiled=True)
    kept = lax.dynamic_index_in_dim(arrived, mine, 1, keepdims=False)
    given = partner(lax.dynamic_index_in_dim(arrived, 1 - mine, 1, keepdims=False))
    own = jnp.stack([kept, given]).reshape(CL_OWN * owners * capacity, feature_count)
    others = [swap_cores(own)]
    for step in range(CL_OWN, helpers, CL_OWN):
        turn = [(i, (i + step) % helpers) for i in range(helpers)]
        others += [lax.ppermute(x, "helper", turn) for x in (own, others[0])]
    counts = soft_counts([own, *others], [0], own.shape[0])
    counts = counts.reshape(CL_OWN, owners, capacity)
    kept, given = counts[0], partner(counts[1])
    counts = jnp.where(mine == 0, jnp.stack([kept, given], 1), jnp.stack([given, kept], 1))
    back = lax.all_to_all(counts, "owner", split_axis=0, concat_axis=0, tiled=True)
    return select(back.reshape(clusters, 1, capacity), slot, capacity)


def solution(mesh):
    in_specs = (
        P(("groups", "owner", "helper", "sub"), None),
        P(("groups", "owner", "helper", "sub")),
    )
    out_specs = P(("groups", "owner", "helper", "sub"))
    body = body_by_chip if mesh.shape["helper"] == CL_OWN else body_by_owner
    return jax.shard_map(body, mesh=mesh, in_specs=in_specs, out_specs=out_specs, check_vma=False)
```

```python
import functools
import math

import jax
import jax.numpy as jnp
from jax import lax
from jax.experimental import pallas as pl
from jax.experimental.pallas import tpu as pltpu
from jax.sharding import PartitionSpec as P

CL_OWN = 2

epsilon = 1e-06
threshold = 0.8
sharpness = 0.05

EMPTY = 4.0
TILE = 1024
VMEM = pl.BlockSpec(memory_space=pltpu.VMEM)


def chip_index():
    return lax.axis_index("owner") * CL_OWN + lax.axis_index("helper")


def slots_of(ids, clusters, capacity):
    doc_count = ids.shape[1]
    member = lax.broadcasted_iota(jnp.int32, (clusters, doc_count), 0) == ids
    earlier = lax.broadcasted_iota(jnp.int32, (doc_count, doc_count), 0) < (
        lax.broadcasted_iota(jnp.int32, (doc_count, doc_count), 1)
    )
    ahead = jnp.dot(
        member.astype(jnp.bfloat16), earlier.astype(jnp.bfloat16), preferred_element_type=jnp.float32
    )
    rank = jnp.sum(jnp.where(member, ahead, 0.0), axis=0, keepdims=True).astype(jnp.int32)
    return ids * capacity + rank


def lay(rows_ref, slot, slots):
    doc_count, feature_count = rows_ref.shape
    dispatch = lax.broadcasted_iota(jnp.int32, (slots, doc_count), 0) == slot
    filled = jnp.sum(dispatch.astype(jnp.float32), axis=1, keepdims=True) > 0
    laid = jnp.dot(
        dispatch.astype(jnp.bfloat16), rows_ref[...], preferred_element_type=jnp.float32
    )
    factor = lax.rsqrt(
        jnp.mean(laid * laid, axis=-1, keepdims=True) + epsilon
    ) * feature_count ** (-0.5)
    lane = lax.broadcasted_iota(jnp.int32, laid.shape, 1)
    return jnp.where(filled | (lane > 0), laid * factor, EMPTY).astype(jnp.bfloat16)


def slots_of_steps(slot, capacity, steps):
    cores = lax.axis_size("sub")
    by_distance = slot ^ (chip_index() * capacity)
    distance = by_distance // capacity
    rank = by_distance - distance * capacity
    step = jnp.full_like(slot, -1)
    for place, p in enumerate(steps):
        step = jnp.where(distance == p * cores + lax.axis_index("sub"), place, step)
    return jnp.where(step < 0, -1, step * capacity + rank)


def route_first_kernel(clusters, capacity, step, rows_ref, ids_ref, piece_ref, slot_ref):
    slot = slots_of(ids_ref[...], clusters, capacity)
    slot_ref[...] = slot
    piece_ref[...] = lay(rows_ref, slots_of_steps(slot, capacity, [step]), capacity)


def route_rest_kernel(clusters, capacity, halves, steps, *refs):
    own_rows, other_rows, own_slot, other_ids, *piece_refs = refs
    half_refs, whole_refs = piece_refs[: len(halves)], piece_refs[len(halves) :]
    slot = slots_of_steps(own_slot[...], capacity, steps)
    laid = lay(own_rows, slot, len(steps) * capacity)
    for k, piece in enumerate(whole_refs):
        piece[:capacity] = laid[k * capacity : (k + 1) * capacity]
    slot = slots_of(other_ids[...], clusters, capacity)
    slot = slots_of_steps(slot, capacity, [*halves, *steps])
    laid = lay(other_rows, slot, (len(halves) + len(steps)) * capacity)
    for k, piece in enumerate(half_refs):
        piece[...] = laid[k * capacity : (k + 1) * capacity]
    for k, piece in enumerate(whole_refs, len(halves)):
        piece[capacity:] = laid[k * capacity : (k + 1) * capacity]


def route_kernel(clusters, capacity, rows_ref, ids_ref, piece_ref, slot_ref):
    slot = slots_of(ids_ref[...], clusters, capacity)
    slot_ref[...] = slot
    piece_ref[...] = lay(rows_ref, slot, piece_ref.shape[0])


def call_kernel(name, kernel, out_shape, *args, limit=32 * 2**20, flops=0):
    cost = pl.CostEstimate(flops=flops, bytes_accessed=0, transcendentals=0) if flops else None
    return pl.pallas_call(
        kernel,
        out_shape=out_shape,
        in_specs=[VMEM] * len(args),
        out_specs=jax.tree.map(lambda _: VMEM, out_shape),
        compiler_params=pltpu.CompilerParams(vmem_limit_bytes=limit),
        cost_estimate=cost,
        name=name,
    )(*args)


def join_kernel(first_ref, second_ref, out_ref):
    rows = first_ref.shape[0]
    out_ref[:rows] = first_ref[...]
    out_ref[rows:] = second_ref[...]


def relay_kernel(a_ref, b_ref, c_ref, d_ref):
    c_ref[...] = a_ref[...]
    d_ref[...] = b_ref[...]


def blocks(rows, starts, size):
    return jnp.concatenate([rows[start : start + size] for start in starts], axis=0)


def count_against(rows, own, starts, size):
    column = lax.broadcasted_iota(jnp.int32, (1, own.shape[0]), 1)
    itself = jnp.full_like(column, -1)
    for k, start in enumerate(starts):
        itself = jnp.where(column // size == k, column + (start - k * size), itself)
    slope = -math.log2(math.e) / sharpness
    total = jnp.zeros((1, own.shape[0]), jnp.float32)
    for first in range(0, rows.shape[0], TILE):
        other = rows[first : first + TILE]
        scores = lax.dot_general(
            other, own, (((1,), (1,)), ((), ())), preferred_element_type=jnp.float32
        )
        weights = 1.0 / (1.0 + jnp.exp2(scores * slope - threshold * slope))
        keep = other[:, :1].astype(jnp.float32) < 0.5 * EMPTY
        if starts:
            keep = keep & (lax.broadcasted_iota(jnp.int32, scores.shape, 0) + first != itself)
        total = total + jnp.sum(jnp.where(keep, weights, 0.0), axis=0, keepdims=True)
    return total


def count_kernel(starts, size, *refs):
    *piece_refs, count_ref = refs
    rows = jnp.concatenate([piece[...] for piece in piece_refs], axis=0)
    count_ref[...] = count_against(rows, blocks(rows, starts, size), starts, size)


def soft_counts(pieces, starts, size):
    out_shape = jax.ShapeDtypeStruct((1, len(starts) * size), jnp.float32)
    return call_kernel("count", functools.partial(count_kernel, starts, size), out_shape, *pieces)


def finish_kernel(starts, late_pieces, late_starts, places, *refs):
    *piece_refs, early_ref, count_ref = refs
    size = count_ref.shape[2]
    early = jnp.concatenate([piece[...] for piece in piece_refs[:-late_pieces]], axis=0)
    late = jnp.concatenate([piece[...] for piece in piece_refs[-late_pieces:]], axis=0)
    own = blocks(early, starts, size)
    late_own = blocks(late, late_starts, size)
    total = early_ref[...] + count_against(late, own, [], size)
    late_total = count_against(early, late_own, [], size) + count_against(
        late, late_own, late_starts, size
    )
    for k, place in enumerate(places()):
        source, j = (total, k) if k < len(starts) else (late_total, k - len(starts))
        count_ref[pl.ds(place, 1), 0, :] = source[:, j * size : (j + 1) * size]


def select_kernel(capacity, counts_ref, slot_ref, out_ref):
    counts = counts_ref[:, 0, :]
    slot = slot_ref[...]
    doc_count = slot.shape[1]
    block = slot // capacity
    rank = slot - block * capacity
    hot = (lax.broadcasted_iota(jnp.int32, (capacity, doc_count), 0) == rank).astype(jnp.float32)
    by_block = jnp.dot(
        counts, hot, precision=lax.Precision.HIGHEST, preferred_element_type=jnp.float32
    )
    chosen = lax.broadcasted_iota(jnp.int32, by_block.shape, 0) == block
    out_ref[...] = jnp.sum(jnp.where(chosen, by_block, 0.0), axis=0, keepdims=True)


def select(counts, slot, capacity):
    out_shape = jax.ShapeDtypeStruct(slot.shape, jnp.float32)
    kernel = functools.partial(select_kernel, capacity)
    return call_kernel("select", kernel, out_shape, counts, slot, limit=8 * 2**20)[0]


def swap_cores(x):
    cores = lax.axis_size("sub")
    return lax.ppermute(x, "sub", [(i, i ^ 1) for i in range(cores)])


def body_by_chip(embeddings, cluster_id):
    doc_count, feature_count = embeddings.shape
    clusters = CL_OWN * lax.axis_size("owner")
    capacity = 2 * doc_count // clusters
    cores = lax.axis_size("sub")
    steps = clusters // cores

    def across(x, p):
        pairs = [
            (chip * cores + core, (chip ^ (p * cores + core)) * cores + core)
            for chip in range(clusters)
            for core in range(cores)
        ]
        return lax.ppermute(x, ("owner", "helper", "sub"), pairs)

    ids = cluster_id.reshape(1, doc_count)
    other_rows, other_ids = swap_cores(embeddings), swap_cores(ids)
    first, last = steps // 2, steps - 1
    middle = [p for p in range(steps) if p not in (first, last)]
    half = jax.ShapeDtypeStruct((capacity, feature_count), jnp.bfloat16)
    whole = jax.ShapeDtypeStruct((cores * capacity, feature_count), jnp.bfloat16)

    first_own, slot = call_kernel(
        "route_first",
        functools.partial(route_first_kernel, clusters, capacity, first),
        [half, jax.ShapeDtypeStruct((1, doc_count), jnp.int32)],
        embeddings,
        ids,
    )
    first_own = across(first_own, first)

    def route_rest(name, halves, steps, slot, flops=0):
        return call_kernel(
            name,
            functools.partial(route_rest_kernel, clusters, capacity, halves, steps),
            [half] * len(halves) + [whole] * len(steps),
            embeddings,
            other_rows,
            slot,
            other_ids,
            flops=flops,
        )

    near = route_rest("route_near", [], middle, slot)
    later_slot, _ = lax.optimization_barrier((slot, near[0]))
    near = [across(piece, p) for piece, p in zip(near, middle)]
    near = call_kernel("relay", relay_kernel, [whole] * 2, *near, flops=10**10)
    first_other, last_piece = route_rest("route_far", [first], [last], later_slot, 10**10)
    first_other, last_piece = across(first_other, first), across(last_piece, last)

    first_both = call_kernel("join", join_kernel, whole, first_own, first_other, )
    early = [first_both, *near]
    early += [swap_cores(x) for x in early]
    late = [last_piece, swap_cores(last_piece)]
    span = cores * capacity
    half_way = span * (steps - 1)
    starts = [k * span for k in range(steps - 1)]
    starts += [half_way + start + capacity for start in starts]
    late_starts = [0, span + capacity]

    def places():
        chip, core = chip_index(), lax.axis_index("sub")
        return (
            [chip ^ (p * cores + core) for p in (first, *middle)]
            + [chip ^ (p * cores + 1 - core) for p in (first, *middle)]
            + [chip ^ (last * cores + core), chip ^ (last * cores + 1 - core)]
        )

    counts = call_kernel(
        "finish",
        functools.partial(finish_kernel, starts, len(late), late_starts, places),
        jax.ShapeDtypeStruct((clusters, 1, capacity), jnp.float32),
        *early,
        *late,
        soft_counts(early, starts, capacity),
    )
    back = lax.all_to_all(counts, ("owner", "helper"), split_axis=0, concat_axis=0, tiled=True)
    return select(back, slot, capacity)


def body_by_owner(embeddings, cluster_id):
    doc_count, feature_count = embeddings.shape
    owners, helpers = lax.axis_size("owner"), lax.axis_size("helper")
    clusters = CL_OWN * owners
    capacity = 2 * doc_count // clusters
    mine = lax.axis_index("helper") % CL_OWN

    def partner(x):
        return lax.ppermute(x, "helper", [(i, i ^ 1) for i in range(helpers)])

    outgoing, slot = call_kernel(
        "route",
        functools.partial(route_kernel, clusters, capacity),
        [
            jax.ShapeDtypeStruct((clusters * capacity, feature_count), jnp.bfloat16),
            jax.ShapeDtypeStruct((1, doc_count), jnp.int32),
        ],
        embeddings,
        cluster_id.reshape(1, doc_count),
    )
    outgoing = outgoing.reshape(owners, CL_OWN, capacity, feature_count)
    arrived = lax.all_to_all(outgoing, "owner", split_axis=0, concat_axis=0, tiled=True)
    kept = lax.dynamic_index_in_dim(arrived, mine, 1, keepdims=False)
    given = partner(lax.dynamic_index_in_dim(arrived, 1 - mine, 1, keepdims=False))
    own = jnp.stack([kept, given]).reshape(CL_OWN * owners * capacity, feature_count)
    others = [swap_cores(own)]
    for step in range(CL_OWN, helpers, CL_OWN):
        turn = [(i, (i + step) % helpers) for i in range(helpers)]
        others += [lax.ppermute(x, "helper", turn) for x in (own, others[0])]
    counts = soft_counts([own, *others], [0], own.shape[0])
    counts = counts.reshape(CL_OWN, owners, capacity)
    kept, given = counts[0], partner(counts[1])
    counts = jnp.where(mine == 0, jnp.stack([kept, given], 1), jnp.stack([given, kept], 1))
    back = lax.all_to_all(counts, "owner", split_axis=0, concat_axis=0, tiled=True)
    return select(back.reshape(clusters, 1, capacity), slot, capacity)


def solution(mesh):
    in_specs = (
        P(("groups", "owner", "helper", "sub"), None),
        P(("groups", "owner", "helper", "sub")),
    )
    out_specs = P(("groups", "owner", "helper", "sub"))
    body = body_by_chip if mesh.shape["helper"] == CL_OWN else body_by_owner
    return jax.shard_map(body, mesh=mesh, in_specs=in_specs, out_specs=out_specs, check_vma=False)
```

```python
import functools
import math

import jax
import jax.numpy as jnp
from jax import lax
from jax.experimental import pallas as pl
from jax.experimental.pallas import tpu as pltpu
from jax.sharding import PartitionSpec as P

CL_OWN = 2

epsilon = 1e-06
threshold = 0.8
sharpness = 0.05

EMPTY = 4.0
TILE = 1024
VMEM = pl.BlockSpec(memory_space=pltpu.VMEM)


def chip_index():
    return lax.axis_index("owner") * CL_OWN + lax.axis_index("helper")


def slots_of(ids, clusters, capacity):
    doc_count = ids.shape[1]
    member = lax.broadcasted_iota(jnp.int32, (clusters, doc_count), 0) == ids
    earlier = lax.broadcasted_iota(jnp.int32, (doc_count, doc_count), 0) < (
        lax.broadcasted_iota(jnp.int32, (doc_count, doc_count), 1)
    )
    ahead = jnp.dot(
        member.astype(jnp.bfloat16), earlier.astype(jnp.bfloat16), preferred_element_type=jnp.float32
    )
    rank = jnp.sum(jnp.where(member, ahead, 0.0), axis=0, keepdims=True).astype(jnp.int32)
    return ids * capacity + rank


def lay(rows_ref, slot, slots):
    doc_count, feature_count = rows_ref.shape
    dispatch = lax.broadcasted_iota(jnp.int32, (slots, doc_count), 0) == slot
    filled = jnp.sum(dispatch.astype(jnp.float32), axis=1, keepdims=True) > 0
    laid = jnp.dot(
        dispatch.astype(jnp.bfloat16), rows_ref[...], preferred_element_type=jnp.float32
    )
    factor = lax.rsqrt(
        jnp.mean(laid * laid, axis=-1, keepdims=True) + epsilon
    ) * feature_count ** (-0.5)
    lane = lax.broadcasted_iota(jnp.int32, laid.shape, 1)
    return jnp.where(filled | (lane > 0), laid * factor, EMPTY).astype(jnp.bfloat16)


def slots_of_steps(slot, capacity, steps):
    cores = lax.axis_size("sub")
    by_distance = slot ^ (chip_index() * capacity)
    distance = by_distance // capacity
    rank = by_distance - distance * capacity
    step = jnp.full_like(slot, -1)
    for place, p in enumerate(steps):
        step = jnp.where(distance == p * cores + lax.axis_index("sub"), place, step)
    return jnp.where(step < 0, -1, step * capacity + rank)


def route_first_kernel(clusters, capacity, step, rows_ref, ids_ref, piece_ref, slot_ref):
    slot = slots_of(ids_ref[...], clusters, capacity)
    slot_ref[...] = slot
    piece_ref[...] = lay(rows_ref, slots_of_steps(slot, capacity, [step]), capacity)


def route_rest_kernel(clusters, capacity, first, steps, *refs):
    own_rows, other_rows, own_slot, other_ids, first_ref, *piece_refs = refs
    slot = slots_of_steps(own_slot[...], capacity, steps)
    laid = lay(own_rows, slot, len(steps) * capacity)
    for k, piece in enumerate(piece_refs):
        piece[:capacity] = laid[k * capacity : (k + 1) * capacity]
    slot = slots_of(other_ids[...], clusters, capacity)
    slot = slots_of_steps(slot, capacity, [first, *steps])
    laid = lay(other_rows, slot, (1 + len(steps)) * capacity)
    first_ref[...] = laid[:capacity]
    for k, piece in enumerate(piece_refs):
        piece[capacity:] = laid[(k + 1) * capacity : (k + 2) * capacity]


def route_kernel(clusters, capacity, rows_ref, ids_ref, piece_ref, slot_ref):
    slot = slots_of(ids_ref[...], clusters, capacity)
    slot_ref[...] = slot
    piece_ref[...] = lay(rows_ref, slot, piece_ref.shape[0])


def call_kernel(name, kernel, out_shape, *args, limit=32 * 2**20, flops=0):
    cost = pl.CostEstimate(flops=flops, bytes_accessed=0, transcendentals=0) if flops else None
    return pl.pallas_call(
        kernel,
        out_shape=out_shape,
        in_specs=[VMEM] * len(args),
        out_specs=jax.tree.map(lambda _: VMEM, out_shape),
        compiler_params=pltpu.CompilerParams(vmem_limit_bytes=limit),
        cost_estimate=cost,
        name=name,
    )(*args)


def join_kernel(first_ref, second_ref, out_ref):
    rows = first_ref.shape[0]
    out_ref[:rows] = first_ref[...]
    out_ref[rows:] = second_ref[...]


def blocks(rows, starts, size):
    return jnp.concatenate([rows[start : start + size] for start in starts], axis=0)


def count_against(rows, own, starts, size):
    column = lax.broadcasted_iota(jnp.int32, (1, own.shape[0]), 1)
    itself = jnp.full_like(column, -1)
    for k, start in enumerate(starts):
        itself = jnp.where(column // size == k, column + (start - k * size), itself)
    slope = -math.log2(math.e) / sharpness
    total = jnp.zeros((1, own.shape[0]), jnp.float32)
    for first in range(0, rows.shape[0], TILE):
        other = rows[first : first + TILE]
        scores = lax.dot_general(
            other, own, (((1,), (1,)), ((), ())), preferred_element_type=jnp.float32
        )
        weights = 1.0 / (1.0 + jnp.exp2(scores * slope - threshold * slope))
        keep = other[:, :1].astype(jnp.float32) < 0.5 * EMPTY
        if starts:
            keep = keep & (lax.broadcasted_iota(jnp.int32, scores.shape, 0) + first != itself)
        total = total + jnp.sum(jnp.where(keep, weights, 0.0), axis=0, keepdims=True)
    return total


def count_kernel(starts, size, *refs):
    *piece_refs, count_ref = refs
    rows = jnp.concatenate([piece[...] for piece in piece_refs], axis=0)
    count_ref[...] = count_against(rows, blocks(rows, starts, size), starts, size)


def soft_counts(pieces, starts, size):
    out_shape = jax.ShapeDtypeStruct((1, len(starts) * size), jnp.float32)
    return call_kernel("count", functools.partial(count_kernel, starts, size), out_shape, *pieces)


def finish_kernel(starts, late_pieces, late_starts, places, *refs):
    *piece_refs, early_ref, count_ref = refs
    size = count_ref.shape[2]
    early = jnp.concatenate([piece[...] for piece in piece_refs[:-late_pieces]], axis=0)
    late = jnp.concatenate([piece[...] for piece in piece_refs[-late_pieces:]], axis=0)
    own = blocks(early, starts, size)
    late_own = blocks(late, late_starts, size)
    total = early_ref[...] + count_against(late, own, [], size)
    late_total = count_against(early, late_own, [], size) + count_against(
        late, late_own, late_starts, size
    )
    count_ref[...] = jnp.zeros_like(count_ref)
    for k, place in enumerate(places()):
        source, j = (total, k) if k < len(starts) else (late_total, k - len(starts))
        count_ref[pl.ds(place, 1), 0, :] = source[:, j * size : (j + 1) * size]


def select_kernel(clusters, capacity, counts_ref, slot_ref, out_ref):
    counts = counts_ref[:, 0, :]
    slot = slot_ref[...]
    doc_count = slot.shape[1]
    block = slot // capacity
    rank = slot - block * capacity
    hot = (lax.broadcasted_iota(jnp.int32, (capacity, doc_count), 0) == rank).astype(jnp.float32)
    by_block = jnp.dot(
        counts, hot, precision=lax.Precision.HIGHEST, preferred_element_type=jnp.float32
    )
    cores = counts.shape[0] // clusters
    core = lax.axis_index("sub") if cores > 1 else 0
    chosen = lax.broadcasted_iota(jnp.int32, by_block.shape, 0) == block * cores + core
    out_ref[...] = jnp.sum(jnp.where(chosen, by_block, 0.0), axis=0, keepdims=True)


def select(counts, slot, clusters, capacity):
    out_shape = jax.ShapeDtypeStruct(slot.shape, jnp.float32)
    kernel = functools.partial(select_kernel, clusters, capacity)
    return call_kernel("select", kernel, out_shape, counts, slot, limit=8 * 2**20)[0]


def swap_cores(x):
    cores = lax.axis_size("sub")
    return lax.ppermute(x, "sub", [(i, i ^ 1) for i in range(cores)])


def body_by_chip(embeddings, cluster_id):
    doc_count, feature_count = embeddings.shape
    clusters = CL_OWN * lax.axis_size("owner")
    capacity = 2 * doc_count // clusters
    cores = lax.axis_size("sub")
    steps = clusters // cores

    def across(x, p):
        pairs = [
            (chip * cores + core, (chip ^ (p * cores + core)) * cores + core)
            for chip in range(clusters)
            for core in range(cores)
        ]
        return lax.ppermute(x, ("owner", "helper", "sub"), pairs)

    ids = cluster_id.reshape(1, doc_count)
    other_rows, other_ids = swap_cores(embeddings), swap_cores(ids)
    first, last = steps // 2, steps - 1
    middle = [p for p in range(steps) if p not in (first, last)]
    half = jax.ShapeDtypeStruct((capacity, feature_count), jnp.bfloat16)
    whole = jax.ShapeDtypeStruct((cores * capacity, feature_count), jnp.bfloat16)

    first_own, slot = call_kernel(
        "route_first",
        functools.partial(route_first_kernel, clusters, capacity, first),
        [half, jax.ShapeDtypeStruct((1, doc_count), jnp.int32)],
        embeddings,
        ids,
    )
    first_own = across(first_own, first)
    first_other, *rest = call_kernel(
        "route_rest",
        functools.partial(route_rest_kernel, clusters, capacity, first, [*middle, last]),
        [half] + [whole] * (steps - 1),
        embeddings,
        other_rows,
        slot,
        other_ids,
    )
    first_other = across(first_other, first)
    rest = [across(piece, p) for piece, p in zip(rest, [*middle, last])]

    first_both = call_kernel("join", join_kernel, whole, first_own, first_other, flops=10**10)
    early = [first_both, *rest[:-1]]
    early += [swap_cores(x) for x in early]
    late = [rest[-1], swap_cores(rest[-1])]
    span = cores * capacity
    half_way = span * (steps - 1)
    starts = [k * span for k in range(steps - 1)]
    starts += [half_way + start + capacity for start in starts]
    late_starts = [0, span + capacity]

    def places():
        chip, core = chip_index(), lax.axis_index("sub")
        own = [chip ^ (p * cores + core) for p in (first, *middle, last)]
        other = [chip ^ (p * cores + 1 - core) for p in (first, *middle, last)]
        chips = own[:-1] + other[:-1] + [own[-1], other[-1]]
        return [there * cores + core for there in chips]

    counts = call_kernel(
        "finish",
        functools.partial(finish_kernel, starts, len(late), late_starts, places),
        jax.ShapeDtypeStruct((clusters * cores, 1, capacity), jnp.float32),
        *early,
        *late,
        soft_counts(early, starts, capacity),
    )
    back = lax.all_to_all(
        counts, ("owner", "helper", "sub"), split_axis=0, concat_axis=0, tiled=True
    )
    return select(back, slot, clusters, capacity)


def body_by_owner(embeddings, cluster_id):
    doc_count, feature_count = embeddings.shape
    owners, helpers = lax.axis_size("owner"), lax.axis_size("helper")
    clusters = CL_OWN * owners
    capacity = 2 * doc_count // clusters
    mine = lax.axis_index("helper") % CL_OWN

    def partner(x):
        return lax.ppermute(x, "helper", [(i, i ^ 1) for i in range(helpers)])

    outgoing, slot = call_kernel(
        "route",
        functools.partial(route_kernel, clusters, capacity),
        [
            jax.ShapeDtypeStruct((clusters * capacity, feature_count), jnp.bfloat16),
            jax.ShapeDtypeStruct((1, doc_count), jnp.int32),
        ],
        embeddings,
        cluster_id.reshape(1, doc_count),
    )
    outgoing = outgoing.reshape(owners, CL_OWN, capacity, feature_count)
    arrived = lax.all_to_all(outgoing, "owner", split_axis=0, concat_axis=0, tiled=True)
    kept = lax.dynamic_index_in_dim(arrived, mine, 1, keepdims=False)
    given = partner(lax.dynamic_index_in_dim(arrived, 1 - mine, 1, keepdims=False))
    own = jnp.stack([kept, given]).reshape(CL_OWN * owners * capacity, feature_count)
    others = [swap_cores(own)]
    for step in range(CL_OWN, helpers, CL_OWN):
        turn = [(i, (i + step) % helpers) for i in range(helpers)]
        others += [lax.ppermute(x, "helper", turn) for x in (own, others[0])]
    counts = soft_counts([own, *others], [0], own.shape[0])
    counts = counts.reshape(CL_OWN, owners, capacity)
    kept, given = counts[0], partner(counts[1])
    counts = jnp.where(mine == 0, jnp.stack([kept, given], 1), jnp.stack([given, kept], 1))
    back = lax.all_to_all(counts, "owner", split_axis=0, concat_axis=0, tiled=True)
    return select(back.reshape(clusters, 1, capacity), slot, clusters, capacity)


def solution(mesh):
    in_specs = (
        P(("groups", "owner", "helper", "sub"), None),
        P(("groups", "owner", "helper", "sub")),
    )
    out_specs = P(("groups", "owner", "helper", "sub"))
    body = body_by_chip if mesh.shape["helper"] == CL_OWN else body_by_owner
    return jax.shard_map(body, mesh=mesh, in_specs=in_specs, out_specs=out_specs, check_vma=False)
```

```python
import functools
import math

import jax
import jax.numpy as jnp
from jax import lax
from jax.experimental import pallas as pl
from jax.experimental.pallas import tpu as pltpu
from jax.sharding import PartitionSpec as P

CL_OWN = 2

epsilon = 1e-06
threshold = 0.8
sharpness = 0.05

EMPTY = 4.0
TILE = 1024
VMEM = pl.BlockSpec(memory_space=pltpu.VMEM)


def chip_index():
    return lax.axis_index("owner") * CL_OWN + lax.axis_index("helper")


def slots_of(ids, clusters, capacity):
    doc_count = ids.shape[1]
    member = lax.broadcasted_iota(jnp.int32, (clusters, doc_count), 0) == ids
    earlier = lax.broadcasted_iota(jnp.int32, (doc_count, doc_count), 0) < (
        lax.broadcasted_iota(jnp.int32, (doc_count, doc_count), 1)
    )
    ahead = jnp.dot(
        member.astype(jnp.bfloat16), earlier.astype(jnp.bfloat16), preferred_element_type=jnp.float32
    )
    rank = jnp.sum(jnp.where(member, ahead, 0.0), axis=0, keepdims=True).astype(jnp.int32)
    return ids * capacity + rank


def lay(rows_ref, slot, slots):
    doc_count, feature_count = rows_ref.shape
    dispatch = lax.broadcasted_iota(jnp.int32, (slots, doc_count), 0) == slot
    filled = jnp.sum(dispatch.astype(jnp.float32), axis=1, keepdims=True) > 0
    laid = jnp.dot(
        dispatch.astype(jnp.bfloat16), rows_ref[...], preferred_element_type=jnp.float32
    )
    factor = lax.rsqrt(
        jnp.mean(laid * laid, axis=-1, keepdims=True) + epsilon
    ) * feature_count ** (-0.5)
    lane = lax.broadcasted_iota(jnp.int32, laid.shape, 1)
    return jnp.where(filled | (lane > 0), laid * factor, EMPTY).astype(jnp.bfloat16)


def slots_of_steps(slot, capacity, steps):
    cores = lax.axis_size("sub")
    by_distance = slot ^ (chip_index() * capacity)
    distance = by_distance // capacity
    rank = by_distance - distance * capacity
    step = jnp.full_like(slot, -1)
    for place, p in enumerate(steps):
        step = jnp.where(distance == p * cores + lax.axis_index("sub"), place, step)
    return jnp.where(step < 0, -1, step * capacity + rank)


def route_first_kernel(clusters, capacity, step, rows_ref, ids_ref, piece_ref, slot_ref):
    slot = slots_of(ids_ref[...], clusters, capacity)
    slot_ref[...] = slot
    piece_ref[...] = lay(rows_ref, slots_of_steps(slot, capacity, [step]), capacity)


def route_rest_kernel(clusters, capacity, first, steps, *refs):
    own_rows, other_rows, own_slot, other_ids, first_ref, *piece_refs = refs
    slot = slots_of_steps(own_slot[...], capacity, steps)
    laid = lay(own_rows, slot, len(steps) * capacity)
    for k, piece in enumerate(piece_refs):
        piece[:capacity] = laid[k * capacity : (k + 1) * capacity]
    slot = slots_of(other_ids[...], clusters, capacity)
    slot = slots_of_steps(slot, capacity, [first, *steps])
    laid = lay(other_rows, slot, (1 + len(steps)) * capacity)
    first_ref[...] = laid[:capacity]
    for k, piece in enumerate(piece_refs):
        piece[capacity:] = laid[(k + 1) * capacity : (k + 2) * capacity]


def route_kernel(clusters, capacity, rows_ref, ids_ref, piece_ref, slot_ref):
    slot = slots_of(ids_ref[...], clusters, capacity)
    slot_ref[...] = slot
    piece_ref[...] = lay(rows_ref, slot, piece_ref.shape[0])


def call_kernel(name, kernel, out_shape, *args, limit=32 * 2**20, flops=0):
    cost = pl.CostEstimate(flops=flops, bytes_accessed=0, transcendentals=0) if flops else None
    return pl.pallas_call(
        kernel,
        out_shape=out_shape,
        in_specs=[VMEM] * len(args),
        out_specs=jax.tree.map(lambda _: VMEM, out_shape),
        compiler_params=pltpu.CompilerParams(vmem_limit_bytes=limit),
        cost_estimate=cost,
        name=name,
    )(*args)


def pass_kernel(*refs):
    half = len(refs) // 2
    for in_ref, out_ref in zip(refs[:half], refs[half:]):
        out_ref[...] = in_ref[...]


def halve_kernel(*refs):
    pieces = len(refs) // 3
    for k, piece in enumerate(refs[:pieces]):
        first, second = refs[pieces + 2 * k : pieces + 2 * k + 2]
        first[...] = piece[: first.shape[0]]
        second[...] = piece[first.shape[0] :]


def blocks(rows, starts, size):
    return jnp.concatenate([rows[start : start + size] for start in starts], axis=0)


def count_against(rows, own, starts, size):
    column = lax.broadcasted_iota(jnp.int32, (1, own.shape[0]), 1)
    itself = jnp.full_like(column, -1)
    for k, start in enumerate(starts):
        itself = jnp.where(column // size == k, column + (start - k * size), itself)
    slope = -math.log2(math.e) / sharpness
    total = jnp.zeros((1, own.shape[0]), jnp.float32)
    for first in range(0, rows.shape[0], TILE):
        other = rows[first : first + TILE]
        scores = lax.dot_general(
            other, own, (((1,), (1,)), ((), ())), preferred_element_type=jnp.float32
        )
        weights = 1.0 / (1.0 + jnp.exp2(scores * slope - threshold * slope))
        keep = other[:, :1].astype(jnp.float32) < 0.5 * EMPTY
        if starts:
            keep = keep & (lax.broadcasted_iota(jnp.int32, scores.shape, 0) + first != itself)
        total = total + jnp.sum(jnp.where(keep, weights, 0.0), axis=0, keepdims=True)
    return total


def count_kernel(starts, size, *refs):
    *piece_refs, count_ref = refs
    rows = jnp.concatenate([piece[...] for piece in piece_refs], axis=0)
    count_ref[...] = count_against(rows, blocks(rows, starts, size), starts, size)


def soft_counts(pieces, starts, size):
    out_shape = jax.ShapeDtypeStruct((1, len(starts) * size), jnp.float32)
    return call_kernel("count", functools.partial(count_kernel, starts, size), out_shape, *pieces)


def late_kernel(*refs):
    *piece_refs, late_ref, early_ref, own_ref = refs
    early = jnp.concatenate([piece[...] for piece in piece_refs], axis=0)
    late = late_ref[...]
    size = late.shape[0]
    early_ref[...] = count_against(late, early, [], size)
    own_ref[...] = count_against(early, late, [], size) + count_against(late, late, [0], size)


def finish_kernel(starts, places, late_ref, other_ref, counts_ref, early_ref, own_ref, out_ref):
    size = out_ref.shape[2]
    late = late_ref[...]
    own = own_ref[...] + count_against(other_ref[...], late, [], size)
    early = early_ref[...]
    blocks_early = early.shape[1] // size
    out_ref[...] = jnp.zeros_like(out_ref)
    for k, place in enumerate(places()):
        if k < blocks_early:
            block = early[:, k * size : (k + 1) * size]
            if k * size in starts:
                j = starts.index(k * size)
                block = block + counts_ref[:, j * size : (j + 1) * size]
        else:
            block = own[:, (k - blocks_early) * size : (k - blocks_early + 1) * size]
        out_ref[pl.ds(place, 1), 0, :] = block


def select_kernel(clusters, capacity, counts_ref, slot_ref, out_ref):
    counts = counts_ref[:, 0, :]
    slot = slot_ref[...]
    doc_count = slot.shape[1]
    block = slot // capacity
    rank = slot - block * capacity
    hot = (lax.broadcasted_iota(jnp.int32, (capacity, doc_count), 0) == rank).astype(jnp.float32)
    by_block = jnp.dot(
        counts, hot, precision=lax.Precision.HIGHEST, preferred_element_type=jnp.float32
    )
    parts = counts.shape[0] // clusters
    chosen = lax.broadcasted_iota(jnp.int32, by_block.shape, 0) // parts == block
    out_ref[...] = jnp.sum(jnp.where(chosen, by_block, 0.0), axis=0, keepdims=True)


def select(counts, slot, clusters, capacity):
    out_shape = jax.ShapeDtypeStruct(slot.shape, jnp.float32)
    kernel = functools.partial(select_kernel, clusters, capacity)
    return call_kernel("select", kernel, out_shape, counts, slot, limit=8 * 2**20)[0]


def swap_cores(x):
    cores = lax.axis_size("sub")
    return lax.ppermute(x, "sub", [(i, i ^ 1) for i in range(cores)])


def body_by_chip(embeddings, cluster_id):
    doc_count, feature_count = embeddings.shape
    clusters = CL_OWN * lax.axis_size("owner")
    capacity = 2 * doc_count // clusters
    cores = lax.axis_size("sub")
    steps = clusters // cores

    def across(x, p):
        pairs = [
            (chip * cores + core, (chip ^ (p * cores + core)) * cores + core)
            for chip in range(clusters)
            for core in range(cores)
        ]
        return lax.ppermute(x, ("owner", "helper", "sub"), pairs)

    ids = cluster_id.reshape(1, doc_count)
    other_rows, other_ids = swap_cores(embeddings), swap_cores(ids)
    first, last = steps // 2, steps - 1
    middle = [p for p in range(steps) if p not in (first, last)]
    half = jax.ShapeDtypeStruct((capacity, feature_count), jnp.bfloat16)
    whole = jax.ShapeDtypeStruct((cores * capacity, feature_count), jnp.bfloat16)

    first_own, slot = call_kernel(
        "route_first",
        functools.partial(route_first_kernel, clusters, capacity, first),
        [half, jax.ShapeDtypeStruct((1, doc_count), jnp.int32)],
        embeddings,
        ids,
    )
    first_own = across(first_own, first)
    first_other, *rest = call_kernel(
        "route_rest",
        functools.partial(route_rest_kernel, clusters, capacity, first, [*middle, last]),
        [half] + [whole] * (steps - 1),
        embeddings,
        other_rows,
        slot,
        other_ids,
    )
    first_other = across(first_other, first)
    rest = [across(piece, p) for piece, p in zip(rest, [*middle, last])]

    firsts = call_kernel(
        "pass", pass_kernel, [half] * 2, first_own, first_other, flops=10**10
    )
    *near, last_piece = rest
    halves = call_kernel("halve", halve_kernel, [half] * (2 * len(near)), *near, flops=10**10)
    early = [*firsts, *near]
    early += [swap_cores(x) for x in (*firsts, *halves)]

    span = cores * capacity
    half_way = span * (steps - 1)
    starts = [k * span for k in range(steps - 1)]
    starts += [half_way + start + capacity for start in starts]
    counts = soft_counts(early, starts, capacity)

    late_piece, _ = lax.optimization_barrier((last_piece, counts))
    late_other = swap_cores(late_piece)
    sums = [
        jax.ShapeDtypeStruct((1, 2 * half_way), jnp.float32),
        jax.ShapeDtypeStruct((1, span), jnp.float32),
    ]
    early_sums, own_sums = call_kernel("late", late_kernel, sums, *early, last_piece)

    def places():
        chip, core = chip_index(), lax.axis_index("sub")
        devices = []
        for here in (core, 1 - core):
            for p in (first, *middle):
                there = (chip ^ (p * cores + here)) * cores
                devices += [there + here, there + 1 - here]
        there = (chip ^ (last * cores + core)) * cores
        return devices + [there + core, there + 1 - core]

    counts = call_kernel(
        "finish",
        functools.partial(finish_kernel, starts, places),
        jax.ShapeDtypeStruct((clusters * cores, 1, capacity), jnp.float32),
        last_piece,
        late_other,
        counts,
        early_sums,
        own_sums,
    )
    back = lax.all_to_all(
        counts, ("owner", "helper", "sub"), split_axis=0, concat_axis=0, tiled=True
    )
    return select(back, slot, clusters, capacity)


def body_by_owner(embeddings, cluster_id):
    doc_count, feature_count = embeddings.shape
    owners, helpers = lax.axis_size("owner"), lax.axis_size("helper")
    clusters = CL_OWN * owners
    capacity = 2 * doc_count // clusters
    mine = lax.axis_index("helper") % CL_OWN

    def partner(x):
        return lax.ppermute(x, "helper", [(i, i ^ 1) for i in range(helpers)])

    outgoing, slot = call_kernel(
        "route",
        functools.partial(route_kernel, clusters, capacity),
        [
            jax.ShapeDtypeStruct((clusters * capacity, feature_count), jnp.bfloat16),
            jax.ShapeDtypeStruct((1, doc_count), jnp.int32),
        ],
        embeddings,
        cluster_id.reshape(1, doc_count),
    )
    outgoing = outgoing.reshape(owners, CL_OWN, capacity, feature_count)
    arrived = lax.all_to_all(outgoing, "owner", split_axis=0, concat_axis=0, tiled=True)
    kept = lax.dynamic_index_in_dim(arrived, mine, 1, keepdims=False)
    given = partner(lax.dynamic_index_in_dim(arrived, 1 - mine, 1, keepdims=False))
    own = jnp.stack([kept, given]).reshape(CL_OWN * owners * capacity, feature_count)
    others = [swap_cores(own)]
    for step in range(CL_OWN, helpers, CL_OWN):
        turn = [(i, (i + step) % helpers) for i in range(helpers)]
        others += [lax.ppermute(x, "helper", turn) for x in (own, others[0])]
    counts = soft_counts([own, *others], [0], own.shape[0])
    counts = counts.reshape(CL_OWN, owners, capacity)
    kept, given = counts[0], partner(counts[1])
    counts = jnp.where(mine == 0, jnp.stack([kept, given], 1), jnp.stack([given, kept], 1))
    back = lax.all_to_all(counts, "owner", split_axis=0, concat_axis=0, tiled=True)
    return select(back.reshape(clusters, 1, capacity), slot, clusters, capacity)


def solution(mesh):
    in_specs = (
        P(("groups", "owner", "helper", "sub"), None),
        P(("groups", "owner", "helper", "sub")),
    )
    out_specs = P(("groups", "owner", "helper", "sub"))
    body = body_by_chip if mesh.shape["helper"] == CL_OWN else body_by_owner
    return jax.shard_map(body, mesh=mesh, in_specs=in_specs, out_specs=out_specs, check_vma=False)
```

```python
import functools
import math

import jax
import jax.numpy as jnp
from jax import lax
from jax.experimental import pallas as pl
from jax.experimental.pallas import tpu as pltpu
from jax.sharding import PartitionSpec as P

CL_OWN = 2

epsilon = 1e-06
threshold = 0.8
sharpness = 0.05

EMPTY = 4.0
TILE = 1024
VMEM = pl.BlockSpec(memory_space=pltpu.VMEM)


def chip_index():
    return lax.axis_index("owner") * CL_OWN + lax.axis_index("helper")


def slots_of(ids, clusters, capacity):
    doc_count = ids.shape[1]
    member = lax.broadcasted_iota(jnp.int32, (clusters, doc_count), 0) == ids
    earlier = lax.broadcasted_iota(jnp.int32, (doc_count, doc_count), 0) < (
        lax.broadcasted_iota(jnp.int32, (doc_count, doc_count), 1)
    )
    ahead = jnp.dot(
        member.astype(jnp.bfloat16), earlier.astype(jnp.bfloat16), preferred_element_type=jnp.float32
    )
    rank = jnp.sum(jnp.where(member, ahead, 0.0), axis=0, keepdims=True).astype(jnp.int32)
    return ids * capacity + rank


def lay(rows_ref, slot, slots):
    doc_count, feature_count = rows_ref.shape
    dispatch = lax.broadcasted_iota(jnp.int32, (slots, doc_count), 0) == slot
    filled = jnp.sum(dispatch.astype(jnp.float32), axis=1, keepdims=True) > 0
    laid = jnp.dot(
        dispatch.astype(jnp.bfloat16), rows_ref[...], preferred_element_type=jnp.float32
    )
    factor = lax.rsqrt(
        jnp.mean(laid * laid, axis=-1, keepdims=True) + epsilon
    ) * feature_count ** (-0.5)
    lane = lax.broadcasted_iota(jnp.int32, laid.shape, 1)
    return jnp.where(filled | (lane > 0), laid * factor, EMPTY).astype(jnp.bfloat16)


def slots_of_steps(slot, capacity, steps):
    cores = lax.axis_size("sub")
    by_distance = slot ^ (chip_index() * capacity)
    distance = by_distance // capacity
    rank = by_distance - distance * capacity
    step = jnp.full_like(slot, -1)
    for place, p in enumerate(steps):
        step = jnp.where(distance == p * cores + lax.axis_index("sub"), place, step)
    return jnp.where(step < 0, -1, step * capacity + rank)


def route_first_kernel(clusters, capacity, step, rows_ref, ids_ref, piece_ref, slot_ref):
    slot = slots_of(ids_ref[...], clusters, capacity)
    slot_ref[...] = slot
    piece_ref[...] = lay(rows_ref, slots_of_steps(slot, capacity, [step]), capacity)


def route_rest_kernel(clusters, capacity, halves, steps, *refs):
    own_rows, other_rows, own_slot, other_ids, *piece_refs = refs
    half_refs, whole_refs = piece_refs[: len(halves)], piece_refs[len(halves) :]
    slot = slots_of_steps(own_slot[...], capacity, steps)
    laid = lay(own_rows, slot, len(steps) * capacity)
    for k, piece in enumerate(whole_refs):
        piece[:capacity] = laid[k * capacity : (k + 1) * capacity]
    slot = slots_of(other_ids[...], clusters, capacity)
    slot = slots_of_steps(slot, capacity, [*halves, *steps])
    laid = lay(other_rows, slot, (len(halves) + len(steps)) * capacity)
    for k, piece in enumerate(half_refs):
        piece[...] = laid[k * capacity : (k + 1) * capacity]
    for k, piece in enumerate(whole_refs, len(halves)):
        piece[capacity:] = laid[k * capacity : (k + 1) * capacity]


def route_kernel(clusters, capacity, rows_ref, ids_ref, piece_ref, slot_ref):
    slot = slots_of(ids_ref[...], clusters, capacity)
    slot_ref[...] = slot
    piece_ref[...] = lay(rows_ref, slot, piece_ref.shape[0])


def call_kernel(name, kernel, out_shape, *args, limit=32 * 2**20, flops=0):
    cost = pl.CostEstimate(flops=flops, bytes_accessed=0, transcendentals=0) if flops else None
    return pl.pallas_call(
        kernel,
        out_shape=out_shape,
        in_specs=[VMEM] * len(args),
        out_specs=jax.tree.map(lambda _: VMEM, out_shape),
        compiler_params=pltpu.CompilerParams(vmem_limit_bytes=limit),
        cost_estimate=cost,
        name=name,
    )(*args)


def pass_kernel(*refs):
    half = len(refs) // 2
    for in_ref, out_ref in zip(refs[:half], refs[half:]):
        out_ref[...] = in_ref[...]


def halve_kernel(*refs):
    pieces = len(refs) // 3
    for k, piece in enumerate(refs[:pieces]):
        first, second = refs[pieces + 2 * k : pieces + 2 * k + 2]
        first[...] = piece[: first.shape[0]]
        second[...] = piece[first.shape[0] :]


def blocks(rows, starts, size):
    return jnp.concatenate([rows[start : start + size] for start in starts], axis=0)


def count_against(rows, own, starts, size):
    column = lax.broadcasted_iota(jnp.int32, (1, own.shape[0]), 1)
    itself = jnp.full_like(column, -1)
    for k, start in enumerate(starts):
        itself = jnp.where(column // size == k, column + (start - k * size), itself)
    slope = -math.log2(math.e) / sharpness
    total = jnp.zeros((1, own.shape[0]), jnp.float32)
    for first in range(0, rows.shape[0], TILE):
        other = rows[first : first + TILE]
        scores = lax.dot_general(
            other, own, (((1,), (1,)), ((), ())), preferred_element_type=jnp.float32
        )
        weights = 1.0 / (1.0 + jnp.exp2(scores * slope - threshold * slope))
        keep = other[:, :1].astype(jnp.float32) < 0.5 * EMPTY
        if starts:
            keep = keep & (lax.broadcasted_iota(jnp.int32, scores.shape, 0) + first != itself)
        total = total + jnp.sum(jnp.where(keep, weights, 0.0), axis=0, keepdims=True)
    return total


def count_kernel(starts, size, *refs):
    *piece_refs, count_ref = refs
    rows = jnp.concatenate([piece[...] for piece in piece_refs], axis=0)
    count_ref[...] = count_against(rows, blocks(rows, starts, size), starts, size)


def soft_counts(pieces, starts, size):
    out_shape = jax.ShapeDtypeStruct((1, len(starts) * size), jnp.float32)
    return call_kernel("count", functools.partial(count_kernel, starts, size), out_shape, *pieces)


def late_kernel(*refs):
    *piece_refs, late_ref, early_ref, own_ref = refs
    early = jnp.concatenate([piece[...] for piece in piece_refs], axis=0)
    late = late_ref[...]
    size = late.shape[0]
    early_ref[...] = count_against(late, early, [], size)
    own_ref[...] = count_against(early, late, [], size) + count_against(late, late, [0], size)


def finish_kernel(starts, places, late_ref, other_ref, counts_ref, early_ref, own_ref, out_ref):
    size = out_ref.shape[2]
    late = late_ref[...]
    own = own_ref[...] + count_against(other_ref[...], late, [], size)
    early = early_ref[...]
    blocks_early = early.shape[1] // size
    out_ref[...] = jnp.zeros_like(out_ref)
    for k, place in enumerate(places()):
        if k < blocks_early:
            block = early[:, k * size : (k + 1) * size]
            if k * size in starts:
                j = starts.index(k * size)
                block = block + counts_ref[:, j * size : (j + 1) * size]
        else:
            block = own[:, (k - blocks_early) * size : (k - blocks_early + 1) * size]
        out_ref[pl.ds(place, 1), 0, :] = block


def select_kernel(clusters, capacity, counts_ref, slot_ref, out_ref):
    counts = counts_ref[:, 0, :]
    slot = slot_ref[...]
    doc_count = slot.shape[1]
    block = slot // capacity
    rank = slot - block * capacity
    hot = (lax.broadcasted_iota(jnp.int32, (capacity, doc_count), 0) == rank).astype(jnp.float32)
    by_block = jnp.dot(
        counts, hot, precision=lax.Precision.HIGHEST, preferred_element_type=jnp.float32
    )
    parts = counts.shape[0] // clusters
    chosen = lax.broadcasted_iota(jnp.int32, by_block.shape, 0) // parts == block
    out_ref[...] = jnp.sum(jnp.where(chosen, by_block, 0.0), axis=0, keepdims=True)


def select(counts, slot, clusters, capacity):
    out_shape = jax.ShapeDtypeStruct(slot.shape, jnp.float32)
    kernel = functools.partial(select_kernel, clusters, capacity)
    return call_kernel("select", kernel, out_shape, counts, slot, limit=8 * 2**20)[0]


def swap_cores(x):
    cores = lax.axis_size("sub")
    return lax.ppermute(x, "sub", [(i, i ^ 1) for i in range(cores)])


def body_by_chip(embeddings, cluster_id):
    doc_count, feature_count = embeddings.shape
    clusters = CL_OWN * lax.axis_size("owner")
    capacity = 2 * doc_count // clusters
    cores = lax.axis_size("sub")
    steps = clusters // cores

    def across(x, p):
        pairs = [
            (chip * cores + core, (chip ^ (p * cores + core)) * cores + core)
            for chip in range(clusters)
            for core in range(cores)
        ]
        return lax.ppermute(x, ("owner", "helper", "sub"), pairs)

    ids = cluster_id.reshape(1, doc_count)
    other_rows, other_ids = swap_cores(embeddings), swap_cores(ids)
    first, last = steps // 2, steps - 1
    middle = [p for p in range(steps) if p not in (first, last)]
    half = jax.ShapeDtypeStruct((capacity, feature_count), jnp.bfloat16)
    whole = jax.ShapeDtypeStruct((cores * capacity, feature_count), jnp.bfloat16)

    first_own, slot = call_kernel(
        "route_first",
        functools.partial(route_first_kernel, clusters, capacity, first),
        [half, jax.ShapeDtypeStruct((1, doc_count), jnp.int32)],
        embeddings,
        ids,
    )
    first_own = across(first_own, first)

    def route_rest(name, halves, steps, slot, flops=0):
        return call_kernel(
            name,
            functools.partial(route_rest_kernel, clusters, capacity, halves, steps),
            [half] * len(halves) + [whole] * len(steps),
            embeddings,
            other_rows,
            slot,
            other_ids,
            flops=flops,
        )

    near = route_rest("route_near", [], middle, slot)
    later_slot, _ = lax.optimization_barrier((slot, near[0]))
    near = [across(piece, p) for piece, p in zip(near, middle)]
    first_other, last_piece = route_rest("route_far", [first], [last], later_slot, 10**10)
    first_other, last_piece = across(first_other, first), across(last_piece, last)

    firsts = call_kernel(
        "pass", pass_kernel, [half] * 2, first_own, first_other
    )
    halves = call_kernel("halve", halve_kernel, [half] * (2 * len(near)), *near, flops=10**10)
    early = [*firsts, *near]
    early += [swap_cores(x) for x in (*firsts, *halves)]

    span = cores * capacity
    half_way = span * (steps - 1)
    starts = [k * span for k in range(steps - 1)]
    starts += [half_way + start + capacity for start in starts]
    counts = soft_counts(early, starts, capacity)

    late_piece, _ = lax.optimization_barrier((last_piece, counts))
    late_other = swap_cores(late_piece)
    sums = [
        jax.ShapeDtypeStruct((1, 2 * half_way), jnp.float32),
        jax.ShapeDtypeStruct((1, span), jnp.float32),
    ]
    early_sums, own_sums = call_kernel("late", late_kernel, sums, *early, last_piece)

    def places():
        chip, core = chip_index(), lax.axis_index("sub")
        devices = []
        for here in (core, 1 - core):
            for p in (first, *middle):
                there = (chip ^ (p * cores + here)) * cores
                devices += [there + here, there + 1 - here]
        there = (chip ^ (last * cores + core)) * cores
        return devices + [there + core, there + 1 - core]

    counts = call_kernel(
        "finish",
        functools.partial(finish_kernel, starts, places),
        jax.ShapeDtypeStruct((clusters * cores, 1, capacity), jnp.float32),
        last_piece,
        late_other,
        counts,
        early_sums,
        own_sums,
    )
    back = lax.all_to_all(
        counts, ("owner", "helper", "sub"), split_axis=0, concat_axis=0, tiled=True
    )
    return select(back, slot, clusters, capacity)


def body_by_owner(embeddings, cluster_id):
    doc_count, feature_count = embeddings.shape
    owners, helpers = lax.axis_size("owner"), lax.axis_size("helper")
    clusters = CL_OWN * owners
    capacity = 2 * doc_count // clusters
    mine = lax.axis_index("helper") % CL_OWN

    def partner(x):
        return lax.ppermute(x, "helper", [(i, i ^ 1) for i in range(helpers)])

    outgoing, slot = call_kernel(
        "route",
        functools.partial(route_kernel, clusters, capacity),
        [
            jax.ShapeDtypeStruct((clusters * capacity, feature_count), jnp.bfloat16),
            jax.ShapeDtypeStruct((1, doc_count), jnp.int32),
        ],
        embeddings,
        cluster_id.reshape(1, doc_count),
    )
    outgoing = outgoing.reshape(owners, CL_OWN, capacity, feature_count)
    arrived = lax.all_to_all(outgoing, "owner", split_axis=0, concat_axis=0, tiled=True)
    kept = lax.dynamic_index_in_dim(arrived, mine, 1, keepdims=False)
    given = partner(lax.dynamic_index_in_dim(arrived, 1 - mine, 1, keepdims=False))
    own = jnp.stack([kept, given]).reshape(CL_OWN * owners * capacity, feature_count)
    others = [swap_cores(own)]
    for step in range(CL_OWN, helpers, CL_OWN):
        turn = [(i, (i + step) % helpers) for i in range(helpers)]
        others += [lax.ppermute(x, "helper", turn) for x in (own, others[0])]
    counts = soft_counts([own, *others], [0], own.shape[0])
    counts = counts.reshape(CL_OWN, owners, capacity)
    kept, given = counts[0], partner(counts[1])
    counts = jnp.where(mine == 0, jnp.stack([kept, given], 1), jnp.stack([given, kept], 1))
    back = lax.all_to_all(counts, "owner", split_axis=0, concat_axis=0, tiled=True)
    return select(back.reshape(clusters, 1, capacity), slot, clusters, capacity)


def solution(mesh):
    in_specs = (
        P(("groups", "owner", "helper", "sub"), None),
        P(("groups", "owner", "helper", "sub")),
    )
    out_specs = P(("groups", "owner", "helper", "sub"))
    body = body_by_chip if mesh.shape["helper"] == CL_OWN else body_by_owner
    return jax.shard_map(body, mesh=mesh, in_specs=in_specs, out_specs=out_specs, check_vma=False)
```

```python
import functools
import math

import jax
import jax.numpy as jnp
from jax import lax
from jax.experimental import pallas as pl
from jax.experimental.pallas import tpu as pltpu
from jax.sharding import PartitionSpec as P

CL_OWN = 2

epsilon = 1e-06
threshold = 0.8
sharpness = 0.05

EMPTY = 4.0
TILE = 1024
VMEM = pl.BlockSpec(memory_space=pltpu.VMEM)


def chip_index():
    return lax.axis_index("owner") * CL_OWN + lax.axis_index("helper")


def slots_of(ids, clusters, capacity):
    doc_count = ids.shape[1]
    member = lax.broadcasted_iota(jnp.int32, (clusters, doc_count), 0) == ids
    earlier = lax.broadcasted_iota(jnp.int32, (doc_count, doc_count), 0) < (
        lax.broadcasted_iota(jnp.int32, (doc_count, doc_count), 1)
    )
    ahead = jnp.dot(
        member.astype(jnp.bfloat16), earlier.astype(jnp.bfloat16), preferred_element_type=jnp.float32
    )
    rank = jnp.sum(jnp.where(member, ahead, 0.0), axis=0, keepdims=True).astype(jnp.int32)
    return ids * capacity + rank


def lay(rows_ref, slot, slots):
    doc_count, feature_count = rows_ref.shape
    dispatch = lax.broadcasted_iota(jnp.int32, (slots, doc_count), 0) == slot
    filled = jnp.sum(dispatch.astype(jnp.float32), axis=1, keepdims=True) > 0
    laid = jnp.dot(
        dispatch.astype(jnp.bfloat16), rows_ref[...], preferred_element_type=jnp.float32
    )
    factor = lax.rsqrt(
        jnp.mean(laid * laid, axis=-1, keepdims=True) + epsilon
    ) * feature_count ** (-0.5)
    lane = lax.broadcasted_iota(jnp.int32, laid.shape, 1)
    return jnp.where(filled | (lane > 0), laid * factor, EMPTY).astype(jnp.bfloat16)


def slots_of_steps(slot, capacity, steps):
    cores = lax.axis_size("sub")
    by_distance = slot ^ (chip_index() * capacity)
    distance = by_distance // capacity
    rank = by_distance - distance * capacity
    step = jnp.full_like(slot, -1)
    for place, p in enumerate(steps):
        step = jnp.where(distance == p * cores + lax.axis_index("sub"), place, step)
    return jnp.where(step < 0, -1, step * capacity + rank)


def route_first_kernel(clusters, capacity, step, rows_ref, ids_ref, piece_ref, slot_ref):
    slot = slots_of(ids_ref[...], clusters, capacity)
    slot_ref[...] = slot
    piece_ref[...] = lay(rows_ref, slots_of_steps(slot, capacity, [step]), capacity)


def route_rest_kernel(clusters, capacity, halves, steps, *refs):
    own_rows, other_rows, own_slot, other_ids, *piece_refs = refs
    half_refs, whole_refs = piece_refs[: len(halves)], piece_refs[len(halves) :]
    slot = slots_of_steps(own_slot[...], capacity, steps)
    laid = lay(own_rows, slot, len(steps) * capacity)
    for k, piece in enumerate(whole_refs):
        piece[:capacity] = laid[k * capacity : (k + 1) * capacity]
    slot = slots_of(other_ids[...], clusters, capacity)
    slot = slots_of_steps(slot, capacity, [*halves, *steps])
    laid = lay(other_rows, slot, (len(halves) + len(steps)) * capacity)
    for k, piece in enumerate(half_refs):
        piece[...] = laid[k * capacity : (k + 1) * capacity]
    for k, piece in enumerate(whole_refs, len(halves)):
        piece[capacity:] = laid[k * capacity : (k + 1) * capacity]


def route_kernel(clusters, capacity, rows_ref, ids_ref, piece_ref, slot_ref):
    slot = slots_of(ids_ref[...], clusters, capacity)
    slot_ref[...] = slot
    piece_ref[...] = lay(rows_ref, slot, piece_ref.shape[0])


def call_kernel(name, kernel, out_shape, *args, limit=32 * 2**20, flops=0):
    cost = pl.CostEstimate(flops=flops, bytes_accessed=0, transcendentals=0) if flops else None
    return pl.pallas_call(
        kernel,
        out_shape=out_shape,
        in_specs=[VMEM] * len(args),
        out_specs=jax.tree.map(lambda _: VMEM, out_shape),
        compiler_params=pltpu.CompilerParams(vmem_limit_bytes=limit),
        cost_estimate=cost,
        name=name,
    )(*args)


def pass_kernel(*refs):
    half = len(refs) // 2
    for in_ref, out_ref in zip(refs[:half], refs[half:]):
        out_ref[...] = in_ref[...]


def regroup_kernel(pieces, *refs):
    rows = jnp.concatenate([ref[...] for ref in refs[:pieces]], axis=0)
    first = 0
    for part in refs[pieces:]:
        part[...] = rows[first : first + part.shape[0]]
        first += part.shape[0]


def blocks(rows, starts, size):
    return jnp.concatenate([rows[start : start + size] for start in starts], axis=0)


def count_against(rows, own, starts, size):
    column = lax.broadcasted_iota(jnp.int32, (1, own.shape[0]), 1)
    itself = jnp.full_like(column, -1)
    for k, start in enumerate(starts):
        itself = jnp.where(column // size == k, column + (start - k * size), itself)
    slope = -math.log2(math.e) / sharpness
    total = jnp.zeros((1, own.shape[0]), jnp.float32)
    for first in range(0, rows.shape[0], TILE):
        other = rows[first : first + TILE]
        scores = lax.dot_general(
            other, own, (((1,), (1,)), ((), ())), preferred_element_type=jnp.float32
        )
        weights = 1.0 / (1.0 + jnp.exp2(scores * slope - threshold * slope))
        keep = other[:, :1].astype(jnp.float32) < 0.5 * EMPTY
        if starts:
            keep = keep & (lax.broadcasted_iota(jnp.int32, scores.shape, 0) + first != itself)
        total = total + jnp.sum(jnp.where(keep, weights, 0.0), axis=0, keepdims=True)
    return total


def count_kernel(starts, size, *refs):
    *piece_refs, count_ref = refs
    rows = jnp.concatenate([piece[...] for piece in piece_refs], axis=0)
    count_ref[...] = count_against(rows, blocks(rows, starts, size), starts, size)


def soft_counts(pieces, starts, size):
    out_shape = jax.ShapeDtypeStruct((1, len(starts) * size), jnp.float32)
    return call_kernel("count", functools.partial(count_kernel, starts, size), out_shape, *pieces)


def late_kernel(*refs):
    *piece_refs, late_ref, early_ref, own_ref = refs
    early = jnp.concatenate([piece[...] for piece in piece_refs], axis=0)
    late = late_ref[...]
    size = late.shape[0]
    early_ref[...] = count_against(late, early, [], size)
    own_ref[...] = count_against(early, late, [], size) + count_against(late, late, [0], size)


def finish_kernel(starts, places, late_ref, other_ref, counts_ref, early_ref, own_ref, out_ref):
    size = out_ref.shape[2]
    late = late_ref[...]
    own = own_ref[...] + count_against(other_ref[...], late, [], size)
    early = early_ref[...]
    blocks_early = early.shape[1] // size
    out_ref[...] = jnp.zeros_like(out_ref)
    for k, place in enumerate(places()):
        if k < blocks_early:
            block = early[:, k * size : (k + 1) * size]
            if k * size in starts:
                j = starts.index(k * size)
                block = block + counts_ref[:, j * size : (j + 1) * size]
        else:
            block = own[:, (k - blocks_early) * size : (k - blocks_early + 1) * size]
        out_ref[pl.ds(place, 1), 0, :] = block


def select_kernel(clusters, capacity, counts_ref, slot_ref, out_ref):
    counts = counts_ref[:, 0, :]
    slot = slot_ref[...]
    doc_count = slot.shape[1]
    block = slot // capacity
    rank = slot - block * capacity
    hot = (lax.broadcasted_iota(jnp.int32, (capacity, doc_count), 0) == rank).astype(jnp.float32)
    by_block = jnp.dot(
        counts, hot, precision=lax.Precision.HIGHEST, preferred_element_type=jnp.float32
    )
    parts = counts.shape[0] // clusters
    chosen = lax.broadcasted_iota(jnp.int32, by_block.shape, 0) // parts == block
    out_ref[...] = jnp.sum(jnp.where(chosen, by_block, 0.0), axis=0, keepdims=True)


def select(counts, slot, clusters, capacity):
    out_shape = jax.ShapeDtypeStruct(slot.shape, jnp.float32)
    kernel = functools.partial(select_kernel, clusters, capacity)
    return call_kernel("select", kernel, out_shape, counts, slot, limit=8 * 2**20)[0]


def swap_cores(x):
    cores = lax.axis_size("sub")
    return lax.ppermute(x, "sub", [(i, i ^ 1) for i in range(cores)])


def body_by_chip(embeddings, cluster_id):
    doc_count, feature_count = embeddings.shape
    clusters = CL_OWN * lax.axis_size("owner")
    capacity = 2 * doc_count // clusters
    cores = lax.axis_size("sub")
    steps = clusters // cores

    def across(x, p):
        pairs = [
            (chip * cores + core, (chip ^ (p * cores + core)) * cores + core)
            for chip in range(clusters)
            for core in range(cores)
        ]
        return lax.ppermute(x, ("owner", "helper", "sub"), pairs)

    ids = cluster_id.reshape(1, doc_count)
    other_rows, other_ids = swap_cores(embeddings), swap_cores(ids)
    first, last = steps // 2, steps - 1
    middle = [p for p in range(steps) if p not in (first, last)]
    half = jax.ShapeDtypeStruct((capacity, feature_count), jnp.bfloat16)
    whole = jax.ShapeDtypeStruct((cores * capacity, feature_count), jnp.bfloat16)

    first_own, slot = call_kernel(
        "route_first",
        functools.partial(route_first_kernel, clusters, capacity, first),
        [half, jax.ShapeDtypeStruct((1, doc_count), jnp.int32)],
        embeddings,
        ids,
    )
    first_own = across(first_own, first)

    def route_rest(name, halves, steps, slot, flops=0):
        return call_kernel(
            name,
            functools.partial(route_rest_kernel, clusters, capacity, halves, steps),
            [half] * len(halves) + [whole] * len(steps),
            embeddings,
            other_rows,
            slot,
            other_ids,
            flops=flops,
        )

    near = route_rest("route_near", [], middle, slot)
    later_slot, _ = lax.optimization_barrier((slot, near[0]))
    near = [across(piece, p) for piece, p in zip(near, middle)]
    first_other, last_piece = route_rest("route_far", [first], [last], later_slot, 10**10)
    first_other, last_piece = across(first_other, first), across(last_piece, last)

    (first_own,) = call_kernel("pass", pass_kernel, [half], first_own)
    early = [first_own, first_other, *near]
    half_way = cores * capacity * (steps - 1)
    part = jax.ShapeDtypeStruct((half_way // 4, feature_count), jnp.bfloat16)
    parts = call_kernel(
        "regroup", functools.partial(regroup_kernel, len(early)), [part] * 4, *early, flops=10**10
    )
    early += [swap_cores(x) for x in parts]

    span = cores * capacity
    starts = [k * span for k in range(steps - 1)]
    starts += [half_way + start + capacity for start in starts]
    counts = soft_counts(early, starts, capacity)

    late_piece, _ = lax.optimization_barrier((last_piece, counts))
    late_other = swap_cores(late_piece)
    sums = [
        jax.ShapeDtypeStruct((1, 2 * half_way), jnp.float32),
        jax.ShapeDtypeStruct((1, span), jnp.float32),
    ]
    early_sums, own_sums = call_kernel("late", late_kernel, sums, *early, last_piece)

    def places():
        chip, core = chip_index(), lax.axis_index("sub")
        devices = []
        for here in (core, 1 - core):
            for p in (first, *middle):
                there = (chip ^ (p * cores + here)) * cores
                devices += [there + here, there + 1 - here]
        there = (chip ^ (last * cores + core)) * cores
        return devices + [there + core, there + 1 - core]

    counts = call_kernel(
        "finish",
        functools.partial(finish_kernel, starts, places),
        jax.ShapeDtypeStruct((clusters * cores, 1, capacity), jnp.float32),
        last_piece,
        late_other,
        counts,
        early_sums,
        own_sums,
    )
    back = lax.all_to_all(
        counts, ("owner", "helper", "sub"), split_axis=0, concat_axis=0, tiled=True
    )
    return select(back, slot, clusters, capacity)


def body_by_owner(embeddings, cluster_id):
    doc_count, feature_count = embeddings.shape
    owners, helpers = lax.axis_size("owner"), lax.axis_size("helper")
    clusters = CL_OWN * owners
    capacity = 2 * doc_count // clusters
    mine = lax.axis_index("helper") % CL_OWN

    def partner(x):
        return lax.ppermute(x, "helper", [(i, i ^ 1) for i in range(helpers)])

    outgoing, slot = call_kernel(
        "route",
        functools.partial(route_kernel, clusters, capacity),
        [
            jax.ShapeDtypeStruct((clusters * capacity, feature_count), jnp.bfloat16),
            jax.ShapeDtypeStruct((1, doc_count), jnp.int32),
        ],
        embeddings,
        cluster_id.reshape(1, doc_count),
    )
    outgoing = outgoing.reshape(owners, CL_OWN, capacity, feature_count)
    arrived = lax.all_to_all(outgoing, "owner", split_axis=0, concat_axis=0, tiled=True)
    kept = lax.dynamic_index_in_dim(arrived, mine, 1, keepdims=False)
    given = partner(lax.dynamic_index_in_dim(arrived, 1 - mine, 1, keepdims=False))
    own = jnp.stack([kept, given]).reshape(CL_OWN * owners * capacity, feature_count)
    others = [swap_cores(own)]
    for step in range(CL_OWN, helpers, CL_OWN):
        turn = [(i, (i + step) % helpers) for i in range(helpers)]
        others += [lax.ppermute(x, "helper", turn) for x in (own, others[0])]
    counts = soft_counts([own, *others], [0], own.shape[0])
    counts = counts.reshape(CL_OWN, owners, capacity)
    kept, given = counts[0], partner(counts[1])
    counts = jnp.where(mine == 0, jnp.stack([kept, given], 1), jnp.stack([given, kept], 1))
    back = lax.all_to_all(counts, "owner", split_axis=0, concat_axis=0, tiled=True)
    return select(back.reshape(clusters, 1, capacity), slot, clusters, capacity)


def solution(mesh):
    in_specs = (
        P(("groups", "owner", "helper", "sub"), None),
        P(("groups", "owner", "helper", "sub")),
    )
    out_specs = P(("groups", "owner", "helper", "sub"))
    body = body_by_chip if mesh.shape["helper"] == CL_OWN else body_by_owner
    return jax.shard_map(body, mesh=mesh, in_specs=in_specs, out_specs=out_specs, check_vma=False)
```

```python
import functools
import math

import jax
import jax.numpy as jnp
from jax import lax
from jax.experimental import pallas as pl
from jax.experimental.pallas import tpu as pltpu
from jax.sharding import PartitionSpec as P

CL_OWN = 2

epsilon = 1e-06
threshold = 0.8
sharpness = 0.05

EMPTY = 4.0
TILE = 1024
VMEM = pl.BlockSpec(memory_space=pltpu.VMEM)


def chip_index():
    return lax.axis_index("owner") * CL_OWN + lax.axis_index("helper")


def slots_of(ids, clusters, capacity):
    doc_count = ids.shape[1]
    member = lax.broadcasted_iota(jnp.int32, (clusters, doc_count), 0) == ids
    earlier = lax.broadcasted_iota(jnp.int32, (doc_count, doc_count), 0) < (
        lax.broadcasted_iota(jnp.int32, (doc_count, doc_count), 1)
    )
    ahead = jnp.dot(
        member.astype(jnp.bfloat16), earlier.astype(jnp.bfloat16), preferred_element_type=jnp.float32
    )
    rank = jnp.sum(jnp.where(member, ahead, 0.0), axis=0, keepdims=True).astype(jnp.int32)
    return ids * capacity + rank


def lay(rows_ref, slot, slots):
    doc_count, feature_count = rows_ref.shape
    dispatch = lax.broadcasted_iota(jnp.int32, (slots, doc_count), 0) == slot
    filled = jnp.sum(dispatch.astype(jnp.float32), axis=1, keepdims=True) > 0
    laid = jnp.dot(
        dispatch.astype(jnp.bfloat16), rows_ref[...], preferred_element_type=jnp.float32
    )
    factor = lax.rsqrt(
        jnp.mean(laid * laid, axis=-1, keepdims=True) + epsilon
    ) * feature_count ** (-0.5)
    lane = lax.broadcasted_iota(jnp.int32, laid.shape, 1)
    return jnp.where(filled | (lane > 0), laid * factor, EMPTY).astype(jnp.bfloat16)


def slots_of_steps(slot, capacity, steps):
    cores = lax.axis_size("sub")
    by_distance = slot ^ (chip_index() * capacity)
    distance = by_distance // capacity
    rank = by_distance - distance * capacity
    step = jnp.full_like(slot, -1)
    for place, p in enumerate(steps):
        step = jnp.where(distance == p * cores + lax.axis_index("sub"), place, step)
    return jnp.where(step < 0, -1, step * capacity + rank)


def route_first_kernel(clusters, capacity, step, rows_ref, ids_ref, piece_ref, slot_ref):
    slot = slots_of(ids_ref[...], clusters, capacity)
    slot_ref[...] = slot
    piece_ref[...] = lay(rows_ref, slots_of_steps(slot, capacity, [step]), capacity)


def route_rest_kernel(clusters, capacity, halves, steps, *refs):
    own_rows, other_rows, own_slot, other_ids, *piece_refs = refs
    half_refs, whole_refs = piece_refs[: len(halves)], piece_refs[len(halves) :]
    slot = slots_of_steps(own_slot[...], capacity, steps)
    laid = lay(own_rows, slot, len(steps) * capacity)
    for k, piece in enumerate(whole_refs):
        piece[:capacity] = laid[k * capacity : (k + 1) * capacity]
    slot = slots_of(other_ids[...], clusters, capacity)
    slot = slots_of_steps(slot, capacity, [*halves, *steps])
    laid = lay(other_rows, slot, (len(halves) + len(steps)) * capacity)
    for k, piece in enumerate(half_refs):
        piece[...] = laid[k * capacity : (k + 1) * capacity]
    for k, piece in enumerate(whole_refs, len(halves)):
        piece[capacity:] = laid[k * capacity : (k + 1) * capacity]


def route_kernel(clusters, capacity, rows_ref, ids_ref, piece_ref, slot_ref):
    slot = slots_of(ids_ref[...], clusters, capacity)
    slot_ref[...] = slot
    piece_ref[...] = lay(rows_ref, slot, piece_ref.shape[0])


def call_kernel(name, kernel, out_shape, *args, limit=32 * 2**20, flops=0):
    cost = pl.CostEstimate(flops=flops, bytes_accessed=0, transcendentals=0) if flops else None
    return pl.pallas_call(
        kernel,
        out_shape=out_shape,
        in_specs=[VMEM] * len(args),
        out_specs=jax.tree.map(lambda _: VMEM, out_shape),
        compiler_params=pltpu.CompilerParams(vmem_limit_bytes=limit),
        cost_estimate=cost,
        name=name,
    )(*args)


def pass_kernel(*refs):
    half = len(refs) // 2
    for in_ref, out_ref in zip(refs[:half], refs[half:]):
        out_ref[...] = in_ref[...]


def regroup_kernel(pieces, *refs):
    rows = jnp.concatenate([ref[...] for ref in refs[:pieces]], axis=0)
    first = 0
    for part in refs[pieces:]:
        part[...] = rows[first : first + part.shape[0]]
        first += part.shape[0]


def blocks(rows, starts, size):
    return jnp.concatenate([rows[start : start + size] for start in starts], axis=0)


def count_against(rows, own, starts, size):
    column = lax.broadcasted_iota(jnp.int32, (1, own.shape[0]), 1)
    itself = jnp.full_like(column, -1)
    for k, start in enumerate(starts):
        itself = jnp.where(column // size == k, column + (start - k * size), itself)
    slope = -math.log2(math.e) / sharpness
    total = jnp.zeros((1, own.shape[0]), jnp.float32)
    for first in range(0, rows.shape[0], TILE):
        other = rows[first : first + TILE]
        scores = lax.dot_general(
            other, own, (((1,), (1,)), ((), ())), preferred_element_type=jnp.float32
        )
        weights = 1.0 / (1.0 + jnp.exp2(scores * slope - threshold * slope))
        keep = other[:, :1].astype(jnp.float32) < 0.5 * EMPTY
        if starts:
            keep = keep & (lax.broadcasted_iota(jnp.int32, scores.shape, 0) + first != itself)
        total = total + jnp.sum(jnp.where(keep, weights, 0.0), axis=0, keepdims=True)
    return total


def count_kernel(starts, size, *refs):
    *piece_refs, count_ref = refs
    rows = jnp.concatenate([piece[...] for piece in piece_refs], axis=0)
    count_ref[...] = count_against(rows, blocks(rows, starts, size), starts, size)


def soft_counts(pieces, starts, size):
    out_shape = jax.ShapeDtypeStruct((1, len(starts) * size), jnp.float32)
    return call_kernel("count", functools.partial(count_kernel, starts, size), out_shape, *pieces)


def late_kernel(*refs):
    *piece_refs, late_ref, early_ref, own_ref = refs
    early = jnp.concatenate([piece[...] for piece in piece_refs], axis=0)
    late = late_ref[...]
    size = late.shape[0]
    early_ref[...] = count_against(late, early, [], size)
    own_ref[...] = count_against(early, late, [], size) + count_against(late, late, [0], size)


def finish_kernel(starts, places, late_ref, other_ref, counts_ref, early_ref, own_ref, out_ref):
    size = out_ref.shape[2]
    late = late_ref[...]
    own = own_ref[...] + count_against(other_ref[...], late, [], size)
    early = early_ref[...]
    blocks_early = early.shape[1] // size
    out_ref[...] = jnp.zeros_like(out_ref)
    for k, place in enumerate(places()):
        if k < blocks_early:
            block = early[:, k * size : (k + 1) * size]
            if k * size in starts:
                j = starts.index(k * size)
                block = block + counts_ref[:, j * size : (j + 1) * size]
        else:
            block = own[:, (k - blocks_early) * size : (k - blocks_early + 1) * size]
        out_ref[pl.ds(place, 1), 0, :] = block


def select_kernel(clusters, capacity, counts_ref, slot_ref, out_ref):
    counts = counts_ref[:, 0, :]
    slot = slot_ref[...]
    doc_count = slot.shape[1]
    block = slot // capacity
    rank = slot - block * capacity
    hot = (lax.broadcasted_iota(jnp.int32, (capacity, doc_count), 0) == rank).astype(jnp.float32)
    by_block = jnp.dot(
        counts, hot, precision=lax.Precision.HIGHEST, preferred_element_type=jnp.float32
    )
    parts = counts.shape[0] // clusters
    chosen = lax.broadcasted_iota(jnp.int32, by_block.shape, 0) // parts == block
    out_ref[...] = jnp.sum(jnp.where(chosen, by_block, 0.0), axis=0, keepdims=True)


def select(counts, slot, clusters, capacity):
    out_shape = jax.ShapeDtypeStruct(slot.shape, jnp.float32)
    kernel = functools.partial(select_kernel, clusters, capacity)
    return call_kernel("select", kernel, out_shape, counts, slot, limit=8 * 2**20)[0]


def swap_cores(x):
    cores = lax.axis_size("sub")
    return lax.ppermute(x, "sub", [(i, i ^ 1) for i in range(cores)])


def body_by_chip(embeddings, cluster_id):
    doc_count, feature_count = embeddings.shape
    clusters = CL_OWN * lax.axis_size("owner")
    capacity = 2 * doc_count // clusters
    cores = lax.axis_size("sub")
    steps = clusters // cores

    def across(x, p):
        pairs = [
            (chip * cores + core, (chip ^ (p * cores + core)) * cores + core)
            for chip in range(clusters)
            for core in range(cores)
        ]
        return lax.ppermute(x, ("owner", "helper", "sub"), pairs)

    ids = cluster_id.reshape(1, doc_count)
    other_rows, other_ids = swap_cores(embeddings), swap_cores(ids)
    first, last = steps - 1, steps // 2
    middle = [p for p in range(steps) if p not in (first, last)]
    half = jax.ShapeDtypeStruct((capacity, feature_count), jnp.bfloat16)
    whole = jax.ShapeDtypeStruct((cores * capacity, feature_count), jnp.bfloat16)

    first_own, slot = call_kernel(
        "route_first",
        functools.partial(route_first_kernel, clusters, capacity, first),
        [half, jax.ShapeDtypeStruct((1, doc_count), jnp.int32)],
        embeddings,
        ids,
    )
    first_own = across(first_own, first)

    def route_rest(name, halves, steps, slot, flops=0):
        return call_kernel(
            name,
            functools.partial(route_rest_kernel, clusters, capacity, halves, steps),
            [half] * len(halves) + [whole] * len(steps),
            embeddings,
            other_rows,
            slot,
            other_ids,
            flops=flops,
        )

    near = route_rest("route_near", [], middle, slot)
    later_slot, _ = lax.optimization_barrier((slot, near[0]))
    near = [across(piece, p) for piece, p in zip(near, middle)]
    first_other, last_piece = route_rest("route_far", [first], [last], later_slot, 10**10)
    first_other, last_piece = across(first_other, first), across(last_piece, last)

    (first_own,) = call_kernel("pass", pass_kernel, [half], first_own)
    early = [first_own, first_other, *near]
    half_way = cores * capacity * (steps - 1)
    part = jax.ShapeDtypeStruct((half_way // 4, feature_count), jnp.bfloat16)
    parts = call_kernel(
        "regroup", functools.partial(regroup_kernel, len(early)), [part] * 4, *early, flops=10**10
    )
    early += [swap_cores(x) for x in parts]

    span = cores * capacity
    starts = [k * span for k in range(steps - 1)]
    starts += [half_way + start + capacity for start in starts]
    counts = soft_counts(early, starts, capacity)

    late_piece, _ = lax.optimization_barrier((last_piece, counts))
    late_other = swap_cores(late_piece)
    sums = [
        jax.ShapeDtypeStruct((1, 2 * half_way), jnp.float32),
        jax.ShapeDtypeStruct((1, span), jnp.float32),
    ]
    early_sums, own_sums = call_kernel("late", late_kernel, sums, *early, last_piece)

    def places():
        chip, core = chip_index(), lax.axis_index("sub")
        devices = []
        for here in (core, 1 - core):
            for p in (first, *middle):
                there = (chip ^ (p * cores + here)) * cores
                devices += [there + here, there + 1 - here]
        there = (chip ^ (last * cores + core)) * cores
        return devices + [there + core, there + 1 - core]

    counts = call_kernel(
        "finish",
        functools.partial(finish_kernel, starts, places),
        jax.ShapeDtypeStruct((clusters * cores, 1, capacity), jnp.float32),
        last_piece,
        late_other,
        counts,
        early_sums,
        own_sums,
    )
    back = lax.all_to_all(
        counts, ("owner", "helper", "sub"), split_axis=0, concat_axis=0, tiled=True
    )
    return select(back, slot, clusters, capacity)


def body_by_owner(embeddings, cluster_id):
    doc_count, feature_count = embeddings.shape
    owners, helpers = lax.axis_size("owner"), lax.axis_size("helper")
    clusters = CL_OWN * owners
    capacity = 2 * doc_count // clusters
    mine = lax.axis_index("helper") % CL_OWN

    def partner(x):
        return lax.ppermute(x, "helper", [(i, i ^ 1) for i in range(helpers)])

    outgoing, slot = call_kernel(
        "route",
        functools.partial(route_kernel, clusters, capacity),
        [
            jax.ShapeDtypeStruct((clusters * capacity, feature_count), jnp.bfloat16),
            jax.ShapeDtypeStruct((1, doc_count), jnp.int32),
        ],
        embeddings,
        cluster_id.reshape(1, doc_count),
    )
    outgoing = outgoing.reshape(owners, CL_OWN, capacity, feature_count)
    arrived = lax.all_to_all(outgoing, "owner", split_axis=0, concat_axis=0, tiled=True)
    kept = lax.dynamic_index_in_dim(arrived, mine, 1, keepdims=False)
    given = partner(lax.dynamic_index_in_dim(arrived, 1 - mine, 1, keepdims=False))
    own = jnp.stack([kept, given]).reshape(CL_OWN * owners * capacity, feature_count)
    others = [swap_cores(own)]
    for step in range(CL_OWN, helpers, CL_OWN):
        turn = [(i, (i + step) % helpers) for i in range(helpers)]
        others += [lax.ppermute(x, "helper", turn) for x in (own, others[0])]
    counts = soft_counts([own, *others], [0], own.shape[0])
    counts = counts.reshape(CL_OWN, owners, capacity)
    kept, given = counts[0], partner(counts[1])
    counts = jnp.where(mine == 0, jnp.stack([kept, given], 1), jnp.stack([given, kept], 1))
    back = lax.all_to_all(counts, "owner", split_axis=0, concat_axis=0, tiled=True)
    return select(back.reshape(clusters, 1, capacity), slot, clusters, capacity)


def solution(mesh):
    in_specs = (
        P(("groups", "owner", "helper", "sub"), None),
        P(("groups", "owner", "helper", "sub")),
    )
    out_specs = P(("groups", "owner", "helper", "sub"))
    body = body_by_chip if mesh.shape["helper"] == CL_OWN else body_by_owner
    return jax.shard_map(body, mesh=mesh, in_specs=in_specs, out_specs=out_specs, check_vma=False)
```

```python
import functools
import math

import jax
import jax.numpy as jnp
from jax import lax
from jax.experimental import pallas as pl
from jax.experimental.pallas import tpu as pltpu
from jax.sharding import PartitionSpec as P

CL_OWN = 2

epsilon = 1e-06
threshold = 0.8
sharpness = 0.05

EMPTY = 4.0
TILE = 1024
VMEM = pl.BlockSpec(memory_space=pltpu.VMEM)


def chip_index():
    return lax.axis_index("owner") * CL_OWN + lax.axis_index("helper")


def slots_of(ids, clusters, capacity):
    doc_count = ids.shape[1]
    member = lax.broadcasted_iota(jnp.int32, (clusters, doc_count), 0) == ids
    earlier = lax.broadcasted_iota(jnp.int32, (doc_count, doc_count), 0) < (
        lax.broadcasted_iota(jnp.int32, (doc_count, doc_count), 1)
    )
    ahead = jnp.dot(
        member.astype(jnp.bfloat16), earlier.astype(jnp.bfloat16), preferred_element_type=jnp.float32
    )
    rank = jnp.sum(jnp.where(member, ahead, 0.0), axis=0, keepdims=True).astype(jnp.int32)
    return ids * capacity + rank


def lay(rows_ref, slot, slots):
    doc_count, feature_count = rows_ref.shape
    dispatch = lax.broadcasted_iota(jnp.int32, (slots, doc_count), 0) == slot
    filled = jnp.sum(dispatch.astype(jnp.float32), axis=1, keepdims=True) > 0
    laid = jnp.dot(
        dispatch.astype(jnp.bfloat16), rows_ref[...], preferred_element_type=jnp.float32
    )
    factor = lax.rsqrt(
        jnp.mean(laid * laid, axis=-1, keepdims=True) + epsilon
    ) * feature_count ** (-0.5)
    lane = lax.broadcasted_iota(jnp.int32, laid.shape, 1)
    return jnp.where(filled | (lane > 0), laid * factor, EMPTY).astype(jnp.bfloat16)


def slots_of_steps(slot, capacity, steps):
    cores = lax.axis_size("sub")
    by_distance = slot ^ (chip_index() * capacity)
    distance = by_distance // capacity
    rank = by_distance - distance * capacity
    step = jnp.full_like(slot, -1)
    for place, p in enumerate(steps):
        step = jnp.where(distance == p * cores + lax.axis_index("sub"), place, step)
    return jnp.where(step < 0, -1, step * capacity + rank)


def route_first_kernel(clusters, capacity, step, rows_ref, ids_ref, piece_ref, slot_ref):
    slot = slots_of(ids_ref[...], clusters, capacity)
    slot_ref[...] = slot
    piece_ref[...] = lay(rows_ref, slots_of_steps(slot, capacity, [step]), capacity)


def route_rest_kernel(clusters, capacity, first, steps, *refs):
    own_rows, other_rows, own_slot, other_ids, first_ref, *piece_refs = refs
    slot = slots_of_steps(own_slot[...], capacity, steps)
    laid = lay(own_rows, slot, len(steps) * capacity)
    for k, piece in enumerate(piece_refs):
        piece[:capacity] = laid[k * capacity : (k + 1) * capacity]
    slot = slots_of(other_ids[...], clusters, capacity)
    slot = slots_of_steps(slot, capacity, [first, *steps])
    laid = lay(other_rows, slot, (1 + len(steps)) * capacity)
    first_ref[...] = laid[:capacity]
    for k, piece in enumerate(piece_refs):
        piece[capacity:] = laid[(k + 1) * capacity : (k + 2) * capacity]


def route_kernel(clusters, capacity, rows_ref, ids_ref, piece_ref, slot_ref):
    slot = slots_of(ids_ref[...], clusters, capacity)
    slot_ref[...] = slot
    piece_ref[...] = lay(rows_ref, slot, piece_ref.shape[0])


def call_kernel(name, kernel, out_shape, *args, limit=32 * 2**20, flops=0):
    cost = pl.CostEstimate(flops=flops, bytes_accessed=0, transcendentals=0) if flops else None
    return pl.pallas_call(
        kernel,
        out_shape=out_shape,
        in_specs=[VMEM] * len(args),
        out_specs=jax.tree.map(lambda _: VMEM, out_shape),
        compiler_params=pltpu.CompilerParams(vmem_limit_bytes=limit),
        cost_estimate=cost,
        name=name,
    )(*args)


def pass_kernel(*refs):
    half = len(refs) // 2
    for in_ref, out_ref in zip(refs[:half], refs[half:]):
        out_ref[...] = in_ref[...]


def regroup_kernel(pieces, *refs):
    rows = jnp.concatenate([ref[...] for ref in refs[:pieces]], axis=0)
    first = 0
    for part in refs[pieces:]:
        part[...] = rows[first : first + part.shape[0]]
        first += part.shape[0]


def blocks(rows, starts, size):
    return jnp.concatenate([rows[start : start + size] for start in starts], axis=0)


def count_against(rows, own, starts, size):
    column = lax.broadcasted_iota(jnp.int32, (1, own.shape[0]), 1)
    itself = jnp.full_like(column, -1)
    for k, start in enumerate(starts):
        itself = jnp.where(column // size == k, column + (start - k * size), itself)
    slope = -math.log2(math.e) / sharpness
    total = jnp.zeros((1, own.shape[0]), jnp.float32)
    for first in range(0, rows.shape[0], TILE):
        other = rows[first : first + TILE]
        scores = lax.dot_general(
            other, own, (((1,), (1,)), ((), ())), preferred_element_type=jnp.float32
        )
        weights = 1.0 / (1.0 + jnp.exp2(scores * slope - threshold * slope))
        keep = other[:, :1].astype(jnp.float32) < 0.5 * EMPTY
        if starts:
            keep = keep & (lax.broadcasted_iota(jnp.int32, scores.shape, 0) + first != itself)
        total = total + jnp.sum(jnp.where(keep, weights, 0.0), axis=0, keepdims=True)
    return total


def count_kernel(starts, size, *refs):
    *piece_refs, count_ref = refs
    rows = jnp.concatenate([piece[...] for piece in piece_refs], axis=0)
    count_ref[...] = count_against(rows, blocks(rows, starts, size), starts, size)


def soft_counts(pieces, starts, size):
    out_shape = jax.ShapeDtypeStruct((1, len(starts) * size), jnp.float32)
    return call_kernel("count", functools.partial(count_kernel, starts, size), out_shape, *pieces)


def late_kernel(*refs):
    *piece_refs, late_ref, early_ref, own_ref = refs
    early = jnp.concatenate([piece[...] for piece in piece_refs], axis=0)
    late = late_ref[...]
    size = late.shape[0]
    early_ref[...] = count_against(late, early, [], size)
    own_ref[...] = count_against(early, late, [], size) + count_against(late, late, [0], size)


def finish_kernel(starts, places, late_ref, other_ref, counts_ref, early_ref, own_ref, out_ref):
    size = out_ref.shape[2]
    late = late_ref[...]
    own = own_ref[...] + count_against(other_ref[...], late, [], size)
    early = early_ref[...]
    blocks_early = early.shape[1] // size
    out_ref[...] = jnp.zeros_like(out_ref)
    for k, place in enumerate(places()):
        if k < blocks_early:
            block = early[:, k * size : (k + 1) * size]
            if k * size in starts:
                j = starts.index(k * size)
                block = block + counts_ref[:, j * size : (j + 1) * size]
        else:
            block = own[:, (k - blocks_early) * size : (k - blocks_early + 1) * size]
        out_ref[pl.ds(place, 1), 0, :] = block


def select_kernel(clusters, capacity, counts_ref, slot_ref, out_ref):
    counts = counts_ref[:, 0, :]
    slot = slot_ref[...]
    doc_count = slot.shape[1]
    block = slot // capacity
    rank = slot - block * capacity
    hot = (lax.broadcasted_iota(jnp.int32, (capacity, doc_count), 0) == rank).astype(jnp.float32)
    by_block = jnp.dot(
        counts, hot, precision=lax.Precision.HIGHEST, preferred_element_type=jnp.float32
    )
    parts = counts.shape[0] // clusters
    chosen = lax.broadcasted_iota(jnp.int32, by_block.shape, 0) // parts == block
    out_ref[...] = jnp.sum(jnp.where(chosen, by_block, 0.0), axis=0, keepdims=True)


def select(counts, slot, clusters, capacity):
    out_shape = jax.ShapeDtypeStruct(slot.shape, jnp.float32)
    kernel = functools.partial(select_kernel, clusters, capacity)
    return call_kernel("select", kernel, out_shape, counts, slot, limit=8 * 2**20)[0]


def swap_cores(x):
    cores = lax.axis_size("sub")
    return lax.ppermute(x, "sub", [(i, i ^ 1) for i in range(cores)])


def body_by_chip(embeddings, cluster_id):
    doc_count, feature_count = embeddings.shape
    clusters = CL_OWN * lax.axis_size("owner")
    capacity = 2 * doc_count // clusters
    cores = lax.axis_size("sub")
    steps = clusters // cores

    def across(x, p):
        pairs = [
            (chip * cores + core, (chip ^ (p * cores + core)) * cores + core)
            for chip in range(clusters)
            for core in range(cores)
        ]
        return lax.ppermute(x, ("owner", "helper", "sub"), pairs)

    ids = cluster_id.reshape(1, doc_count)
    other_rows, other_ids = swap_cores(embeddings), swap_cores(ids)
    first, last = steps // 2, steps - 1
    middle = [p for p in range(steps) if p not in (first, last)]
    half = jax.ShapeDtypeStruct((capacity, feature_count), jnp.bfloat16)
    whole = jax.ShapeDtypeStruct((cores * capacity, feature_count), jnp.bfloat16)

    first_own, slot = call_kernel(
        "route_first",
        functools.partial(route_first_kernel, clusters, capacity, first),
        [half, jax.ShapeDtypeStruct((1, doc_count), jnp.int32)],
        embeddings,
        ids,
    )
    first_own = across(first_own, first)
    first_other, *rest = call_kernel(
        "route_rest",
        functools.partial(route_rest_kernel, clusters, capacity, first, [*middle, last]),
        [half] + [whole] * (steps - 1),
        embeddings,
        other_rows,
        slot,
        other_ids,
    )
    first_other = across(first_other, first)
    rest = [across(piece, p) for piece, p in zip(rest, [*middle, last])]

    (first_own,) = call_kernel("pass", pass_kernel, [half], first_own, flops=2*10**9)
    *near, last_piece = rest
    early = [first_own, first_other, *near]
    half_way = cores * capacity * (steps - 1)
    part = jax.ShapeDtypeStruct((half_way // 4, feature_count), jnp.bfloat16)
    parts = call_kernel(
        "regroup", functools.partial(regroup_kernel, len(early)), [part] * 4, *early, flops=10**10
    )
    early += [swap_cores(x) for x in parts]

    span = cores * capacity
    starts = [k * span for k in range(steps - 1)]
    starts += [half_way + start + capacity for start in starts]
    counts = soft_counts(early, starts, capacity)

    late_piece, _ = lax.optimization_barrier((last_piece, counts))
    late_other = swap_cores(late_piece)
    sums = [
        jax.ShapeDtypeStruct((1, 2 * half_way), jnp.float32),
        jax.ShapeDtypeStruct((1, span), jnp.float32),
    ]
    early_sums, own_sums = call_kernel("late", late_kernel, sums, *early, last_piece)

    def places():
        chip, core = chip_index(), lax.axis_index("sub")
        devices = []
        for here in (core, 1 - core):
            for p in (first, *middle):
                there = (chip ^ (p * cores + here)) * cores
                devices += [there + here, there + 1 - here]
        there = (chip ^ (last * cores + core)) * cores
        return devices + [there + core, there + 1 - core]

    counts = call_kernel(
        "finish",
        functools.partial(finish_kernel, starts, places),
        jax.ShapeDtypeStruct((clusters * cores, 1, capacity), jnp.float32),
        last_piece,
        late_other,
        counts,
        early_sums,
        own_sums,
    )
    back = lax.all_to_all(
        counts, ("owner", "helper", "sub"), split_axis=0, concat_axis=0, tiled=True
    )
    return select(back, slot, clusters, capacity)


def body_by_owner(embeddings, cluster_id):
    doc_count, feature_count = embeddings.shape
    owners, helpers = lax.axis_size("owner"), lax.axis_size("helper")
    clusters = CL_OWN * owners
    capacity = 2 * doc_count // clusters
    mine = lax.axis_index("helper") % CL_OWN

    def partner(x):
        return lax.ppermute(x, "helper", [(i, i ^ 1) for i in range(helpers)])

    outgoing, slot = call_kernel(
        "route",
        functools.partial(route_kernel, clusters, capacity),
        [
            jax.ShapeDtypeStruct((clusters * capacity, feature_count), jnp.bfloat16),
            jax.ShapeDtypeStruct((1, doc_count), jnp.int32),
        ],
        embeddings,
        cluster_id.reshape(1, doc_count),
    )
    outgoing = outgoing.reshape(owners, CL_OWN, capacity, feature_count)
    arrived = lax.all_to_all(outgoing, "owner", split_axis=0, concat_axis=0, tiled=True)
    kept = lax.dynamic_index_in_dim(arrived, mine, 1, keepdims=False)
    given = partner(lax.dynamic_index_in_dim(arrived, 1 - mine, 1, keepdims=False))
    own = jnp.stack([kept, given]).reshape(CL_OWN * owners * capacity, feature_count)
    others = [swap_cores(own)]
    for step in range(CL_OWN, helpers, CL_OWN):
        turn = [(i, (i + step) % helpers) for i in range(helpers)]
        others += [lax.ppermute(x, "helper", turn) for x in (own, others[0])]
    counts = soft_counts([own, *others], [0], own.shape[0])
    counts = counts.reshape(CL_OWN, owners, capacity)
    kept, given = counts[0], partner(counts[1])
    counts = jnp.where(mine == 0, jnp.stack([kept, given], 1), jnp.stack([given, kept], 1))
    back = lax.all_to_all(counts, "owner", split_axis=0, concat_axis=0, tiled=True)
    return select(back.reshape(clusters, 1, capacity), slot, clusters, capacity)


def solution(mesh):
    in_specs = (
        P(("groups", "owner", "helper", "sub"), None),
        P(("groups", "owner", "helper", "sub")),
    )
    out_specs = P(("groups", "owner", "helper", "sub"))
    body = body_by_chip if mesh.shape["helper"] == CL_OWN else body_by_owner
    return jax.shard_map(body, mesh=mesh, in_specs=in_specs, out_specs=out_specs, check_vma=False)
```

```python
import functools
import math

import jax
import jax.numpy as jnp
from jax import lax
from jax.experimental import pallas as pl
from jax.experimental.pallas import tpu as pltpu
from jax.sharding import PartitionSpec as P

CL_OWN = 2

epsilon = 1e-06
threshold = 0.8
sharpness = 0.05

EMPTY = 4.0
TILE = 1024
VMEM = pl.BlockSpec(memory_space=pltpu.VMEM)


def chip_index():
    return lax.axis_index("owner") * CL_OWN + lax.axis_index("helper")


def slots_of(ids, clusters, capacity):
    doc_count = ids.shape[1]
    member = lax.broadcasted_iota(jnp.int32, (clusters, doc_count), 0) == ids
    earlier = lax.broadcasted_iota(jnp.int32, (doc_count, doc_count), 0) < (
        lax.broadcasted_iota(jnp.int32, (doc_count, doc_count), 1)
    )
    ahead = jnp.dot(
        member.astype(jnp.bfloat16), earlier.astype(jnp.bfloat16), preferred_element_type=jnp.float32
    )
    rank = jnp.sum(jnp.where(member, ahead, 0.0), axis=0, keepdims=True).astype(jnp.int32)
    return ids * capacity + rank


def lay(rows_ref, slot, slots):
    doc_count, feature_count = rows_ref.shape
    dispatch = lax.broadcasted_iota(jnp.int32, (slots, doc_count), 0) == slot
    filled = jnp.sum(dispatch.astype(jnp.float32), axis=1, keepdims=True) > 0
    laid = jnp.dot(
        dispatch.astype(jnp.bfloat16), rows_ref[...], preferred_element_type=jnp.float32
    )
    factor = lax.rsqrt(
        jnp.mean(laid * laid, axis=-1, keepdims=True) + epsilon
    ) * feature_count ** (-0.5)
    lane = lax.broadcasted_iota(jnp.int32, laid.shape, 1)
    return jnp.where(filled | (lane > 0), laid * factor, EMPTY).astype(jnp.bfloat16)


def slots_of_steps(slot, capacity, steps):
    cores = lax.axis_size("sub")
    by_distance = slot ^ (chip_index() * capacity)
    distance = by_distance // capacity
    rank = by_distance - distance * capacity
    step = jnp.full_like(slot, -1)
    for place, p in enumerate(steps):
        step = jnp.where(distance == p * cores + lax.axis_index("sub"), place, step)
    return jnp.where(step < 0, -1, step * capacity + rank)


def route_first_kernel(clusters, capacity, step, rows_ref, ids_ref, piece_ref, slot_ref):
    slot = slots_of(ids_ref[...], clusters, capacity)
    slot_ref[...] = slot
    piece_ref[...] = lay(rows_ref, slots_of_steps(slot, capacity, [step]), capacity)


def route_rest_kernel(clusters, capacity, halves, steps, *refs):
    own_rows, other_rows, own_slot, other_ids, *piece_refs = refs
    half_refs, whole_refs = piece_refs[: len(halves)], piece_refs[len(halves) :]
    slot = slots_of_steps(own_slot[...], capacity, steps)
    laid = lay(own_rows, slot, len(steps) * capacity)
    for k, piece in enumerate(whole_refs):
        piece[:capacity] = laid[k * capacity : (k + 1) * capacity]
    slot = slots_of(other_ids[...], clusters, capacity)
    slot = slots_of_steps(slot, capacity, [*halves, *steps])
    laid = lay(other_rows, slot, (len(halves) + len(steps)) * capacity)
    for k, piece in enumerate(half_refs):
        piece[...] = laid[k * capacity : (k + 1) * capacity]
    for k, piece in enumerate(whole_refs, len(halves)):
        piece[capacity:] = laid[k * capacity : (k + 1) * capacity]


def route_kernel(clusters, capacity, rows_ref, ids_ref, piece_ref, slot_ref):
    slot = slots_of(ids_ref[...], clusters, capacity)
    slot_ref[...] = slot
    piece_ref[...] = lay(rows_ref, slot, piece_ref.shape[0])


def call_kernel(name, kernel, out_shape, *args, limit=32 * 2**20, flops=0):
    cost = pl.CostEstimate(flops=flops, bytes_accessed=0, transcendentals=0) if flops else None
    return pl.pallas_call(
        kernel,
        out_shape=out_shape,
        in_specs=[VMEM] * len(args),
        out_specs=jax.tree.map(lambda _: VMEM, out_shape),
        compiler_params=pltpu.CompilerParams(vmem_limit_bytes=limit),
        cost_estimate=cost,
        name=name,
    )(*args)


def pass_kernel(*refs):
    half = len(refs) // 2
    for in_ref, out_ref in zip(refs[:half], refs[half:]):
        out_ref[...] = in_ref[...]


def regroup_kernel(pieces, *refs):
    rows = jnp.concatenate([ref[...] for ref in refs[:pieces]], axis=0)
    first = 0
    for part in refs[pieces:]:
        part[...] = rows[first : first + part.shape[0]]
        first += part.shape[0]


def blocks(rows, starts, size):
    return jnp.concatenate([rows[start : start + size] for start in starts], axis=0)


def count_against(rows, own, starts, size):
    column = lax.broadcasted_iota(jnp.int32, (1, own.shape[0]), 1)
    itself = jnp.full_like(column, -1)
    for k, start in enumerate(starts):
        itself = jnp.where(column // size == k, column + (start - k * size), itself)
    slope = -math.log2(math.e) / sharpness
    total = jnp.zeros((1, own.shape[0]), jnp.float32)
    for first in range(0, rows.shape[0], TILE):
        other = rows[first : first + TILE]
        scores = lax.dot_general(
            other, own, (((1,), (1,)), ((), ())), preferred_element_type=jnp.float32
        )
        weights = 1.0 / (1.0 + jnp.exp2(scores * slope - threshold * slope))
        keep = other[:, :1].astype(jnp.float32) < 0.5 * EMPTY
        if starts:
            keep = keep & (lax.broadcasted_iota(jnp.int32, scores.shape, 0) + first != itself)
        total = total + jnp.sum(jnp.where(keep, weights, 0.0), axis=0, keepdims=True)
    return total


def count_kernel(starts, size, *refs):
    *piece_refs, count_ref = refs
    rows = jnp.concatenate([piece[...] for piece in piece_refs], axis=0)
    count_ref[...] = count_against(rows, blocks(rows, starts, size), starts, size)


def soft_counts(pieces, starts, size):
    out_shape = jax.ShapeDtypeStruct((1, len(starts) * size), jnp.float32)
    return call_kernel("count", functools.partial(count_kernel, starts, size), out_shape, *pieces)


def late_kernel(*refs):
    *piece_refs, late_ref, early_ref, own_ref = refs
    early = jnp.concatenate([piece[...] for piece in piece_refs], axis=0)
    late = late_ref[...]
    size = late.shape[0]
    early_ref[...] = count_against(late, early, [], size)
    own_ref[...] = count_against(early, late, [], size) + count_against(late, late, [0], size)


def finish_kernel(starts, places, late_ref, other_ref, counts_ref, early_ref, own_ref, out_ref):
    size = out_ref.shape[2]
    late = late_ref[...]
    own = own_ref[...] + count_against(other_ref[...], late, [], size)
    early = early_ref[...]
    blocks_early = early.shape[1] // size
    out_ref[...] = jnp.zeros_like(out_ref)
    for k, place in enumerate(places()):
        if k < blocks_early:
            block = early[:, k * size : (k + 1) * size]
            if k * size in starts:
                j = starts.index(k * size)
                block = block + counts_ref[:, j * size : (j + 1) * size]
        else:
            block = own[:, (k - blocks_early) * size : (k - blocks_early + 1) * size]
        out_ref[pl.ds(place, 1), 0, :] = block


def select_kernel(clusters, capacity, counts_ref, slot_ref, out_ref):
    counts = counts_ref[:, 0, :]
    slot = slot_ref[...]
    doc_count = slot.shape[1]
    block = slot // capacity
    rank = slot - block * capacity
    hot = (lax.broadcasted_iota(jnp.int32, (capacity, doc_count), 0) == rank).astype(jnp.float32)
    by_block = jnp.dot(
        counts, hot, precision=lax.Precision.HIGHEST, preferred_element_type=jnp.float32
    )
    parts = counts.shape[0] // clusters
    chosen = lax.broadcasted_iota(jnp.int32, by_block.shape, 0) // parts == block
    out_ref[...] = jnp.sum(jnp.where(chosen, by_block, 0.0), axis=0, keepdims=True)


def select(counts, slot, clusters, capacity):
    out_shape = jax.ShapeDtypeStruct(slot.shape, jnp.float32)
    kernel = functools.partial(select_kernel, clusters, capacity)
    return call_kernel("select", kernel, out_shape, counts, slot, limit=8 * 2**20)[0]


def swap_cores(x):
    cores = lax.axis_size("sub")
    return lax.ppermute(x, "sub", [(i, i ^ 1) for i in range(cores)])


def body_by_chip(embeddings, cluster_id):
    doc_count, feature_count = embeddings.shape
    clusters = CL_OWN * lax.axis_size("owner")
    capacity = 2 * doc_count // clusters
    cores = lax.axis_size("sub")
    steps = clusters // cores

    def across(x, p):
        pairs = [
            (chip * cores + core, (chip ^ (p * cores + core)) * cores + core)
            for chip in range(clusters)
            for core in range(cores)
        ]
        return lax.ppermute(x, ("owner", "helper", "sub"), pairs)

    ids = cluster_id.reshape(1, doc_count)
    other_rows, other_ids = swap_cores(embeddings), swap_cores(ids)
    first, last = steps // 2, steps - 1
    middle = [p for p in reversed(range(steps)) if p not in (first, last)]
    half = jax.ShapeDtypeStruct((capacity, feature_count), jnp.bfloat16)
    whole = jax.ShapeDtypeStruct((cores * capacity, feature_count), jnp.bfloat16)

    first_own, slot = call_kernel(
        "route_first",
        functools.partial(route_first_kernel, clusters, capacity, first),
        [half, jax.ShapeDtypeStruct((1, doc_count), jnp.int32)],
        embeddings,
        ids,
    )
    first_own = across(first_own, first)

    def route_rest(name, halves, steps, slot, flops=0):
        return call_kernel(
            name,
            functools.partial(route_rest_kernel, clusters, capacity, halves, steps),
            [half] * len(halves) + [whole] * len(steps),
            embeddings,
            other_rows,
            slot,
            other_ids,
            flops=flops,
        )

    near = route_rest("route_near", [], middle, slot)
    later_slot, _ = lax.optimization_barrier((slot, near[0]))
    near = [across(piece, p) for piece, p in zip(near, middle)]
    first_other, last_piece = route_rest("route_far", [first], [last], later_slot, 10**10)
    first_other, last_piece = across(first_other, first), across(last_piece, last)

    (first_own,) = call_kernel("pass", pass_kernel, [half], first_own)
    early = [first_own, first_other, *near]
    half_way = cores * capacity * (steps - 1)
    part = jax.ShapeDtypeStruct((half_way // 4, feature_count), jnp.bfloat16)
    parts = call_kernel(
        "regroup", functools.partial(regroup_kernel, len(early)), [part] * 4, *early, flops=10**10
    )
    early += [swap_cores(x) for x in parts]

    span = cores * capacity
    starts = [k * span for k in range(steps - 1)]
    starts += [half_way + start + capacity for start in starts]
    counts = soft_counts(early, starts, capacity)

    late_piece, _ = lax.optimization_barrier((last_piece, counts))
    late_other = swap_cores(late_piece)
    sums = [
        jax.ShapeDtypeStruct((1, 2 * half_way), jnp.float32),
        jax.ShapeDtypeStruct((1, span), jnp.float32),
    ]
    early_sums, own_sums = call_kernel("late", late_kernel, sums, *early, last_piece)

    def places():
        chip, core = chip_index(), lax.axis_index("sub")
        devices = []
        for here in (core, 1 - core):
            for p in (first, *middle):
                there = (chip ^ (p * cores + here)) * cores
                devices += [there + here, there + 1 - here]
        there = (chip ^ (last * cores + core)) * cores
        return devices + [there + core, there + 1 - core]

    counts = call_kernel(
        "finish",
        functools.partial(finish_kernel, starts, places),
        jax.ShapeDtypeStruct((clusters * cores, 1, capacity), jnp.float32),
        last_piece,
        late_other,
        counts,
        early_sums,
        own_sums,
    )
    back = lax.all_to_all(
        counts, ("owner", "helper", "sub"), split_axis=0, concat_axis=0, tiled=True
    )
    return select(back, slot, clusters, capacity)


def body_by_owner(embeddings, cluster_id):
    doc_count, feature_count = embeddings.shape
    owners, helpers = lax.axis_size("owner"), lax.axis_size("helper")
    clusters = CL_OWN * owners
    capacity = 2 * doc_count // clusters
    mine = lax.axis_index("helper") % CL_OWN

    def partner(x):
        return lax.ppermute(x, "helper", [(i, i ^ 1) for i in range(helpers)])

    outgoing, slot = call_kernel(
        "route",
        functools.partial(route_kernel, clusters, capacity),
        [
            jax.ShapeDtypeStruct((clusters * capacity, feature_count), jnp.bfloat16),
            jax.ShapeDtypeStruct((1, doc_count), jnp.int32),
        ],
        embeddings,
        cluster_id.reshape(1, doc_count),
    )
    outgoing = outgoing.reshape(owners, CL_OWN, capacity, feature_count)
    arrived = lax.all_to_all(outgoing, "owner", split_axis=0, concat_axis=0, tiled=True)
    kept = lax.dynamic_index_in_dim(arrived, mine, 1, keepdims=False)
    given = partner(lax.dynamic_index_in_dim(arrived, 1 - mine, 1, keepdims=False))
    own = jnp.stack([kept, given]).reshape(CL_OWN * owners * capacity, feature_count)
    others = [swap_cores(own)]
    for step in range(CL_OWN, helpers, CL_OWN):
        turn = [(i, (i + step) % helpers) for i in range(helpers)]
        others += [lax.ppermute(x, "helper", turn) for x in (own, others[0])]
    counts = soft_counts([own, *others], [0], own.shape[0])
    counts = counts.reshape(CL_OWN, owners, capacity)
    kept, given = counts[0], partner(counts[1])
    counts = jnp.where(mine == 0, jnp.stack([kept, given], 1), jnp.stack([given, kept], 1))
    back = lax.all_to_all(counts, "owner", split_axis=0, concat_axis=0, tiled=True)
    return select(back.reshape(clusters, 1, capacity), slot, clusters, capacity)


def solution(mesh):
    in_specs = (
        P(("groups", "owner", "helper", "sub"), None),
        P(("groups", "owner", "helper", "sub")),
    )
    out_specs = P(("groups", "owner", "helper", "sub"))
    body = body_by_chip if mesh.shape["helper"] == CL_OWN else body_by_owner
    return jax.shard_map(body, mesh=mesh, in_specs=in_specs, out_specs=out_specs, check_vma=False)
```

```python
import functools
import math

import jax
import jax.numpy as jnp
from jax import lax
from jax.experimental import pallas as pl
from jax.experimental.pallas import tpu as pltpu
from jax.sharding import PartitionSpec as P

CL_OWN = 2

epsilon = 1e-06
threshold = 0.8
sharpness = 0.05

EMPTY = 4.0
TILE = 1024
VMEM = pl.BlockSpec(memory_space=pltpu.VMEM)


def chip_index():
    return lax.axis_index("owner") * CL_OWN + lax.axis_index("helper")


def slots_of(ids, clusters, capacity):
    doc_count = ids.shape[1]
    member = lax.broadcasted_iota(jnp.int32, (clusters, doc_count), 0) == ids
    earlier = lax.broadcasted_iota(jnp.int32, (doc_count, doc_count), 0) < (
        lax.broadcasted_iota(jnp.int32, (doc_count, doc_count), 1)
    )
    ahead = jnp.dot(
        member.astype(jnp.bfloat16), earlier.astype(jnp.bfloat16), preferred_element_type=jnp.float32
    )
    rank = jnp.sum(jnp.where(member, ahead, 0.0), axis=0, keepdims=True).astype(jnp.int32)
    return ids * capacity + rank


def lay(rows_ref, slot, slots):
    doc_count, feature_count = rows_ref.shape
    dispatch = lax.broadcasted_iota(jnp.int32, (slots, doc_count), 0) == slot
    filled = jnp.sum(dispatch.astype(jnp.float32), axis=1, keepdims=True) > 0
    laid = jnp.dot(
        dispatch.astype(jnp.bfloat16), rows_ref[...], preferred_element_type=jnp.float32
    )
    factor = lax.rsqrt(
        jnp.mean(laid * laid, axis=-1, keepdims=True) + epsilon
    ) * feature_count ** (-0.5)
    lane = lax.broadcasted_iota(jnp.int32, laid.shape, 1)
    return jnp.where(filled | (lane > 0), laid * factor, EMPTY).astype(jnp.bfloat16)


def slots_of_steps(slot, capacity, steps):
    cores = lax.axis_size("sub")
    by_distance = slot ^ (chip_index() * capacity)
    distance = by_distance // capacity
    rank = by_distance - distance * capacity
    step = jnp.full_like(slot, -1)
    for place, p in enumerate(steps):
        step = jnp.where(distance == p * cores + lax.axis_index("sub"), place, step)
    return jnp.where(step < 0, -1, step * capacity + rank)


def route_first_kernel(clusters, capacity, step, rows_ref, ids_ref, piece_ref, slot_ref):
    slot = slots_of(ids_ref[...], clusters, capacity)
    slot_ref[...] = slot
    piece_ref[...] = lay(rows_ref, slots_of_steps(slot, capacity, [step]), capacity)


def route_rest_kernel(clusters, capacity, halves, steps, *refs):
    own_rows, other_rows, own_slot, other_ids, *piece_refs = refs
    half_refs, whole_refs = piece_refs[: len(halves)], piece_refs[len(halves) :]
    slot = slots_of_steps(own_slot[...], capacity, steps)
    laid = lay(own_rows, slot, len(steps) * capacity)
    for k, piece in enumerate(whole_refs):
        piece[:capacity] = laid[k * capacity : (k + 1) * capacity]
    slot = slots_of(other_ids[...], clusters, capacity)
    slot = slots_of_steps(slot, capacity, [*halves, *steps])
    laid = lay(other_rows, slot, (len(halves) + len(steps)) * capacity)
    for k, piece in enumerate(half_refs):
        piece[...] = laid[k * capacity : (k + 1) * capacity]
    for k, piece in enumerate(whole_refs, len(halves)):
        piece[capacity:] = laid[k * capacity : (k + 1) * capacity]


def route_kernel(clusters, capacity, rows_ref, ids_ref, piece_ref, slot_ref):
    slot = slots_of(ids_ref[...], clusters, capacity)
    slot_ref[...] = slot
    piece_ref[...] = lay(rows_ref, slot, piece_ref.shape[0])


def call_kernel(name, kernel, out_shape, *args, limit=32 * 2**20, flops=0):
    cost = pl.CostEstimate(flops=flops, bytes_accessed=0, transcendentals=0) if flops else None
    return pl.pallas_call(
        kernel,
        out_shape=out_shape,
        in_specs=[VMEM] * len(args),
        out_specs=jax.tree.map(lambda _: VMEM, out_shape),
        compiler_params=pltpu.CompilerParams(vmem_limit_bytes=limit),
        cost_estimate=cost,
        name=name,
    )(*args)


def pass_kernel(*refs):
    half = len(refs) // 2
    for in_ref, out_ref in zip(refs[:half], refs[half:]):
        out_ref[...] = in_ref[...]


def regroup_kernel(pieces, *refs):
    rows = jnp.concatenate([ref[...] for ref in refs[:pieces]], axis=0)
    first = 0
    for part in refs[pieces:]:
        part[...] = rows[first : first + part.shape[0]]
        first += part.shape[0]


def blocks(rows, starts, size):
    return jnp.concatenate([rows[start : start + size] for start in starts], axis=0)


def count_against(rows, own, starts, size):
    column = lax.broadcasted_iota(jnp.int32, (1, own.shape[0]), 1)
    itself = jnp.full_like(column, -1)
    for k, start in enumerate(starts):
        itself = jnp.where(column // size == k, column + (start - k * size), itself)
    slope = -math.log2(math.e) / sharpness
    total = jnp.zeros((1, own.shape[0]), jnp.float32)
    for first in range(0, rows.shape[0], TILE):
        other = rows[first : first + TILE]
        scores = lax.dot_general(
            other, own, (((1,), (1,)), ((), ())), preferred_element_type=jnp.float32
        )
        weights = 1.0 / (1.0 + jnp.exp2(scores * slope - threshold * slope))
        keep = other[:, :1].astype(jnp.float32) < 0.5 * EMPTY
        if starts:
            keep = keep & (lax.broadcasted_iota(jnp.int32, scores.shape, 0) + first != itself)
        total = total + jnp.sum(jnp.where(keep, weights, 0.0), axis=0, keepdims=True)
    return total


def count_kernel(starts, size, *refs):
    *piece_refs, count_ref = refs
    rows = jnp.concatenate([piece[...] for piece in piece_refs], axis=0)
    count_ref[...] = count_against(rows, blocks(rows, starts, size), starts, size)


def soft_counts(pieces, starts, size):
    out_shape = jax.ShapeDtypeStruct((1, len(starts) * size), jnp.float32)
    return call_kernel("count", functools.partial(count_kernel, starts, size), out_shape, *pieces)


def cross_kernel(pieces, *refs):
    *piece_refs, before_ref, count_ref = refs
    own = jnp.concatenate([piece[...] for piece in piece_refs[:pieces]], axis=0)
    other = jnp.concatenate([piece[...] for piece in piece_refs[pieces:]], axis=0)
    count_ref[...] = before_ref[...] + count_against(other, own, [], own.shape[0])


def late_kernel(*refs):
    *piece_refs, late_ref, early_ref, own_ref = refs
    early = jnp.concatenate([piece[...] for piece in piece_refs], axis=0)
    late = late_ref[...]
    size = late.shape[0]
    early_ref[...] = count_against(late, early, [], size)
    own_ref[...] = count_against(early, late, [], size) + count_against(late, late, [0], size)


def finish_kernel(places, late_ref, other_ref, counts_ref, early_ref, own_ref, out_ref):
    size = out_ref.shape[2]
    late = late_ref[...]
    own = own_ref[...] + count_against(other_ref[...], late, [], size)
    early = early_ref[...]
    blocks_early = early.shape[1] // size
    out_ref[...] = jnp.zeros_like(out_ref)
    for k, place in enumerate(places()):
        if k < blocks_early:
            block = early[:, k * size : (k + 1) * size]
            if k * size < counts_ref.shape[1]:
                block = block + counts_ref[:, k * size : (k + 1) * size]
        else:
            block = own[:, (k - blocks_early) * size : (k - blocks_early + 1) * size]
        out_ref[pl.ds(place, 1), 0, :] = block


def select_kernel(clusters, capacity, counts_ref, slot_ref, out_ref):
    counts = counts_ref[:, 0, :]
    slot = slot_ref[...]
    doc_count = slot.shape[1]
    block = slot // capacity
    rank = slot - block * capacity
    hot = (lax.broadcasted_iota(jnp.int32, (capacity, doc_count), 0) == rank).astype(jnp.float32)
    by_block = jnp.dot(
        counts, hot, precision=lax.Precision.HIGHEST, preferred_element_type=jnp.float32
    )
    parts = counts.shape[0] // clusters
    chosen = lax.broadcasted_iota(jnp.int32, by_block.shape, 0) // parts == block
    out_ref[...] = jnp.sum(jnp.where(chosen, by_block, 0.0), axis=0, keepdims=True)


def select(counts, slot, clusters, capacity):
    out_shape = jax.ShapeDtypeStruct(slot.shape, jnp.float32)
    kernel = functools.partial(select_kernel, clusters, capacity)
    return call_kernel("select", kernel, out_shape, counts, slot, limit=8 * 2**20)[0]


def swap_cores(x):
    cores = lax.axis_size("sub")
    return lax.ppermute(x, "sub", [(i, i ^ 1) for i in range(cores)])


def body_by_chip(embeddings, cluster_id):
    doc_count, feature_count = embeddings.shape
    clusters = CL_OWN * lax.axis_size("owner")
    capacity = 2 * doc_count // clusters
    cores = lax.axis_size("sub")
    steps = clusters // cores

    def across(x, p):
        pairs = [
            (chip * cores + core, (chip ^ (p * cores + core)) * cores + core)
            for chip in range(clusters)
            for core in range(cores)
        ]
        return lax.ppermute(x, ("owner", "helper", "sub"), pairs)

    ids = cluster_id.reshape(1, doc_count)
    other_rows, other_ids = swap_cores(embeddings), swap_cores(ids)
    first, last = steps // 2, steps - 1
    middle = [p for p in range(steps) if p not in (first, last)]
    half = jax.ShapeDtypeStruct((capacity, feature_count), jnp.bfloat16)
    whole = jax.ShapeDtypeStruct((cores * capacity, feature_count), jnp.bfloat16)

    first_own, slot = call_kernel(
        "route_first",
        functools.partial(route_first_kernel, clusters, capacity, first),
        [half, jax.ShapeDtypeStruct((1, doc_count), jnp.int32)],
        embeddings,
        ids,
    )
    first_own = across(first_own, first)

    def route_rest(name, halves, steps, slot, flops=0):
        return call_kernel(
            name,
            functools.partial(route_rest_kernel, clusters, capacity, halves, steps),
            [half] * len(halves) + [whole] * len(steps),
            embeddings,
            other_rows,
            slot,
            other_ids,
            flops=flops,
        )

    near = route_rest("route_near", [], middle, slot)
    later_slot, _ = lax.optimization_barrier((slot, near[0]))
    near = [across(piece, p) for piece, p in zip(near, middle)]
    first_other, last_piece = route_rest("route_far", [first], [last], later_slot, 10**10)
    first_other, last_piece = across(first_other, first), across(last_piece, last)

    (first_own,) = call_kernel("pass", pass_kernel, [half], first_own)
    early = [first_own, first_other, *near]
    half_way = cores * capacity * (steps - 1)
    part = jax.ShapeDtypeStruct((half_way // 4, feature_count), jnp.bfloat16)
    parts = call_kernel(
        "regroup", functools.partial(regroup_kernel, len(early)), [part] * 4, *early, flops=10**10
    )
    swapped = [swap_cores(x) for x in parts]

    counts = soft_counts(early, [0], half_way)
    counts = call_kernel(
        "cross",
        functools.partial(cross_kernel, len(early)),
        jax.ShapeDtypeStruct((1, half_way), jnp.float32),
        *early,
        *swapped,
        counts,
    )
    early += swapped

    late_piece, _ = lax.optimization_barrier((last_piece, counts))
    late_other = swap_cores(late_piece)
    sums = [
        jax.ShapeDtypeStruct((1, 2 * half_way), jnp.float32),
        jax.ShapeDtypeStruct((1, cores * capacity), jnp.float32),
    ]
    early_sums, own_sums = call_kernel("late", late_kernel, sums, *early, last_piece)

    def places():
        chip, core = chip_index(), lax.axis_index("sub")
        devices = []
        for here in (core, 1 - core):
            for p in (first, *middle):
                there = (chip ^ (p * cores + here)) * cores
                devices += [there + here, there + 1 - here]
        there = (chip ^ (last * cores + core)) * cores
        return devices + [there + core, there + 1 - core]

    counts = call_kernel(
        "finish",
        functools.partial(finish_kernel, places),
        jax.ShapeDtypeStruct((clusters * cores, 1, capacity), jnp.float32),
        last_piece,
        late_other,
        counts,
        early_sums,
        own_sums,
    )
    back = lax.all_to_all(
        counts, ("owner", "helper", "sub"), split_axis=0, concat_axis=0, tiled=True
    )
    return select(back, slot, clusters, capacity)


def body_by_owner(embeddings, cluster_id):
    doc_count, feature_count = embeddings.shape
    owners, helpers = lax.axis_size("owner"), lax.axis_size("helper")
    clusters = CL_OWN * owners
    capacity = 2 * doc_count // clusters
    mine = lax.axis_index("helper") % CL_OWN

    def partner(x):
        return lax.ppermute(x, "helper", [(i, i ^ 1) for i in range(helpers)])

    outgoing, slot = call_kernel(
        "route",
        functools.partial(route_kernel, clusters, capacity),
        [
            jax.ShapeDtypeStruct((clusters * capacity, feature_count), jnp.bfloat16),
            jax.ShapeDtypeStruct((1, doc_count), jnp.int32),
        ],
        embeddings,
        cluster_id.reshape(1, doc_count),
    )
    outgoing = outgoing.reshape(owners, CL_OWN, capacity, feature_count)
    arrived = lax.all_to_all(outgoing, "owner", split_axis=0, concat_axis=0, tiled=True)
    kept = lax.dynamic_index_in_dim(arrived, mine, 1, keepdims=False)
    given = partner(lax.dynamic_index_in_dim(arrived, 1 - mine, 1, keepdims=False))
    own = jnp.stack([kept, given]).reshape(CL_OWN * owners * capacity, feature_count)
    others = [swap_cores(own)]
    for step in range(CL_OWN, helpers, CL_OWN):
        turn = [(i, (i + step) % helpers) for i in range(helpers)]
        others += [lax.ppermute(x, "helper", turn) for x in (own, others[0])]
    counts = soft_counts([own, *others], [0], own.shape[0])
    counts = counts.reshape(CL_OWN, owners, capacity)
    kept, given = counts[0], partner(counts[1])
    counts = jnp.where(mine == 0, jnp.stack([kept, given], 1), jnp.stack([given, kept], 1))
    back = lax.all_to_all(counts, "owner", split_axis=0, concat_axis=0, tiled=True)
    return select(back.reshape(clusters, 1, capacity), slot, clusters, capacity)


def solution(mesh):
    in_specs = (
        P(("groups", "owner", "helper", "sub"), None),
        P(("groups", "owner", "helper", "sub")),
    )
    out_specs = P(("groups", "owner", "helper", "sub"))
    body = body_by_chip if mesh.shape["helper"] == CL_OWN else body_by_owner
    return jax.shard_map(body, mesh=mesh, in_specs=in_specs, out_specs=out_specs, check_vma=False)
```

```python
import functools
import math

import jax
import jax.numpy as jnp
from jax import lax
from jax.experimental import pallas as pl
from jax.experimental.pallas import tpu as pltpu
from jax.sharding import PartitionSpec as P

CL_OWN = 2

epsilon = 1e-06
threshold = 0.8
sharpness = 0.05

EMPTY = 4.0
TILE = 1024
VMEM = pl.BlockSpec(memory_space=pltpu.VMEM)


def chip_index():
    return lax.axis_index("owner") * CL_OWN + lax.axis_index("helper")


def slots_of(ids, clusters, capacity):
    doc_count = ids.shape[1]
    member = lax.broadcasted_iota(jnp.int32, (clusters, doc_count), 0) == ids
    earlier = lax.broadcasted_iota(jnp.int32, (doc_count, doc_count), 0) < (
        lax.broadcasted_iota(jnp.int32, (doc_count, doc_count), 1)
    )
    ahead = jnp.dot(
        member.astype(jnp.bfloat16), earlier.astype(jnp.bfloat16), preferred_element_type=jnp.float32
    )
    rank = jnp.sum(jnp.where(member, ahead, 0.0), axis=0, keepdims=True).astype(jnp.int32)
    return ids * capacity + rank


def lay(rows_ref, slot, slots):
    doc_count, feature_count = rows_ref.shape
    dispatch = lax.broadcasted_iota(jnp.int32, (slots, doc_count), 0) == slot
    filled = jnp.sum(dispatch.astype(jnp.float32), axis=1, keepdims=True) > 0
    laid = jnp.dot(
        dispatch.astype(jnp.bfloat16), rows_ref[...], preferred_element_type=jnp.float32
    )
    factor = lax.rsqrt(
        jnp.mean(laid * laid, axis=-1, keepdims=True) + epsilon
    ) * feature_count ** (-0.5)
    lane = lax.broadcasted_iota(jnp.int32, laid.shape, 1)
    return jnp.where(filled | (lane > 0), laid * factor, EMPTY).astype(jnp.bfloat16)


def slots_of_steps(slot, capacity, steps):
    cores = lax.axis_size("sub")
    by_distance = slot ^ (chip_index() * capacity)
    distance = by_distance // capacity
    rank = by_distance - distance * capacity
    step = jnp.full_like(slot, -1)
    for place, p in enumerate(steps):
        step = jnp.where(distance == p * cores + lax.axis_index("sub"), place, step)
    return jnp.where(step < 0, -1, step * capacity + rank)


def route_first_kernel(clusters, capacity, step, rows_ref, ids_ref, piece_ref, slot_ref):
    slot = slots_of(ids_ref[...], clusters, capacity)
    slot_ref[...] = slot
    piece_ref[...] = lay(rows_ref, slots_of_steps(slot, capacity, [step]), capacity)


def route_rest_kernel(clusters, capacity, halves, steps, *refs):
    own_rows, other_rows, own_slot, other_ids, *piece_refs = refs
    half_refs, whole_refs = piece_refs[: len(halves)], piece_refs[len(halves) :]
    slot = slots_of_steps(own_slot[...], capacity, steps)
    laid = lay(own_rows, slot, len(steps) * capacity)
    for k, piece in enumerate(whole_refs):
        piece[:capacity] = laid[k * capacity : (k + 1) * capacity]
    slot = slots_of(other_ids[...], clusters, capacity)
    slot = slots_of_steps(slot, capacity, [*halves, *steps])
    laid = lay(other_rows, slot, (len(halves) + len(steps)) * capacity)
    for k, piece in enumerate(half_refs):
        piece[...] = laid[k * capacity : (k + 1) * capacity]
    for k, piece in enumerate(whole_refs, len(halves)):
        piece[capacity:] = laid[k * capacity : (k + 1) * capacity]


def route_kernel(clusters, capacity, rows_ref, ids_ref, piece_ref, slot_ref):
    slot = slots_of(ids_ref[...], clusters, capacity)
    slot_ref[...] = slot
    piece_ref[...] = lay(rows_ref, slot, piece_ref.shape[0])


def call_kernel(name, kernel, out_shape, *args, limit=32 * 2**20, flops=0):
    cost = pl.CostEstimate(flops=flops, bytes_accessed=0, transcendentals=0) if flops else None
    return pl.pallas_call(
        kernel,
        out_shape=out_shape,
        in_specs=[VMEM] * len(args),
        out_specs=jax.tree.map(lambda _: VMEM, out_shape),
        compiler_params=pltpu.CompilerParams(vmem_limit_bytes=limit),
        cost_estimate=cost,
        name=name,
    )(*args)


def pass_kernel(*refs):
    half = len(refs) // 2
    for in_ref, out_ref in zip(refs[:half], refs[half:]):
        out_ref[...] = in_ref[...]


def regroup_kernel(pieces, *refs):
    rows = jnp.concatenate([ref[...] for ref in refs[:pieces]], axis=0)
    first = 0
    for part in refs[pieces:]:
        part[...] = rows[first : first + part.shape[0]]
        first += part.shape[0]


def blocks(rows, starts, size):
    return jnp.concatenate([rows[start : start + size] for start in starts], axis=0)


def count_against(rows, own, starts, size):
    column = lax.broadcasted_iota(jnp.int32, (1, own.shape[0]), 1)
    itself = jnp.full_like(column, -1)
    for k, start in enumerate(starts):
        itself = jnp.where(column // size == k, column + (start - k * size), itself)
    slope = -math.log2(math.e) / sharpness
    total = jnp.zeros((1, own.shape[0]), jnp.float32)
    for first in range(0, rows.shape[0], TILE):
        other = rows[first : first + TILE]
        scores = lax.dot_general(
            other, own, (((1,), (1,)), ((), ())), preferred_element_type=jnp.float32
        )
        weights = 1.0 / (1.0 + jnp.exp2(scores * slope - threshold * slope))
        keep = other[:, :1].astype(jnp.float32) < 0.5 * EMPTY
        if starts:
            keep = keep & (lax.broadcasted_iota(jnp.int32, scores.shape, 0) + first != itself)
        total = total + jnp.sum(jnp.where(keep, weights, 0.0), axis=0, keepdims=True)
    return total


def count_kernel(starts, size, *refs):
    *piece_refs, count_ref = refs
    rows = jnp.concatenate([piece[...] for piece in piece_refs], axis=0)
    count_ref[...] = count_against(rows, blocks(rows, starts, size), starts, size)


def soft_counts(pieces, starts, size):
    out_shape = jax.ShapeDtypeStruct((1, len(starts) * size), jnp.float32)
    return call_kernel("count", functools.partial(count_kernel, starts, size), out_shape, *pieces)


def cross_kernel(pieces, *refs):
    *piece_refs, before_ref, count_ref = refs
    own = jnp.concatenate([piece[...] for piece in piece_refs[:pieces]], axis=0)
    other = jnp.concatenate([piece[...] for piece in piece_refs[pieces:]], axis=0)
    count_ref[...] = before_ref[...] + count_against(other, own, [], own.shape[0])


def late_kernel(*refs):
    *piece_refs, late_ref, early_ref, own_ref = refs
    early = jnp.concatenate([piece[...] for piece in piece_refs], axis=0)
    late = late_ref[...]
    size = late.shape[0]
    early_ref[...] = count_against(late, early, [], size)
    own_ref[...] = count_against(early, late, [], size) + count_against(late, late, [0], size)


def finish_kernel(places, late_ref, other_ref, counts_ref, early_ref, own_ref, out_ref):
    size = out_ref.shape[2]
    late = late_ref[...]
    own = own_ref[...] + count_against(other_ref[...], late, [], size)
    early = early_ref[...]
    blocks_early = early.shape[1] // size
    out_ref[...] = jnp.zeros_like(out_ref)
    for k, place in enumerate(places()):
        if k < blocks_early:
            block = early[:, k * size : (k + 1) * size]
            if k * size < counts_ref.shape[1]:
                block = block + counts_ref[:, k * size : (k + 1) * size]
        else:
            block = own[:, (k - blocks_early) * size : (k - blocks_early + 1) * size]
        out_ref[pl.ds(place, 1), 0, :] = block


def select_kernel(clusters, capacity, backwards, counts_ref, slot_ref, out_ref):
    counts = counts_ref[:, 0, :]
    slot = slot_ref[...]
    doc_count = slot.shape[1]
    block = slot // capacity
    rank = slot - block * capacity
    hot = (lax.broadcasted_iota(jnp.int32, (capacity, doc_count), 0) == rank).astype(jnp.float32)
    by_block = jnp.dot(
        counts, hot, precision=lax.Precision.HIGHEST, preferred_element_type=jnp.float32
    )
    parts = counts.shape[0] // clusters
    row = lax.broadcasted_iota(jnp.int32, by_block.shape, 0)
    if backwards:
        row = counts.shape[0] - 1 - row
    chosen = row // parts == block
    out_ref[...] = jnp.sum(jnp.where(chosen, by_block, 0.0), axis=0, keepdims=True)


def select(counts, slot, clusters, capacity, backwards=False):
    out_shape = jax.ShapeDtypeStruct(slot.shape, jnp.float32)
    kernel = functools.partial(select_kernel, clusters, capacity, backwards)
    return call_kernel("select", kernel, out_shape, counts, slot, limit=8 * 2**20)[0]


def swap_cores(x):
    cores = lax.axis_size("sub")
    return lax.ppermute(x, "sub", [(i, i ^ 1) for i in range(cores)])


def body_by_chip(embeddings, cluster_id):
    doc_count, feature_count = embeddings.shape
    clusters = CL_OWN * lax.axis_size("owner")
    capacity = 2 * doc_count // clusters
    cores = lax.axis_size("sub")
    steps = clusters // cores

    def across(x, p):
        pairs = [
            (chip * cores + core, (chip ^ (p * cores + core)) * cores + core)
            for chip in range(clusters)
            for core in range(cores)
        ]
        return lax.ppermute(x, ("owner", "helper", "sub"), pairs)

    ids = cluster_id.reshape(1, doc_count)
    other_rows, other_ids = swap_cores(embeddings), swap_cores(ids)
    first, last = steps // 2, steps - 1
    middle = [p for p in range(steps) if p not in (first, last)]
    half = jax.ShapeDtypeStruct((capacity, feature_count), jnp.bfloat16)
    whole = jax.ShapeDtypeStruct((cores * capacity, feature_count), jnp.bfloat16)

    first_own, slot = call_kernel(
        "route_first",
        functools.partial(route_first_kernel, clusters, capacity, first),
        [half, jax.ShapeDtypeStruct((1, doc_count), jnp.int32)],
        embeddings,
        ids,
    )
    first_own = across(first_own, first)

    def route_rest(name, halves, steps, slot, flops=0):
        return call_kernel(
            name,
            functools.partial(route_rest_kernel, clusters, capacity, halves, steps),
            [half] * len(halves) + [whole] * len(steps),
            embeddings,
            other_rows,
            slot,
            other_ids,
            flops=flops,
        )

    near = route_rest("route_near", [], middle, slot)
    later_slot, _ = lax.optimization_barrier((slot, near[0]))
    near = [across(piece, p) for piece, p in zip(near, middle)]
    first_other, last_piece = route_rest("route_far", [first], [last], later_slot, 10**10)
    first_other, last_piece = across(first_other, first), across(last_piece, last)

    (first_own,) = call_kernel("pass", pass_kernel, [half], first_own)
    early = [first_own, first_other, *near]
    half_way = cores * capacity * (steps - 1)
    part = jax.ShapeDtypeStruct((half_way // 4, feature_count), jnp.bfloat16)
    parts = call_kernel(
        "regroup", functools.partial(regroup_kernel, len(early)), [part] * 4, *early, flops=10**10
    )
    swapped = [swap_cores(x) for x in parts]

    counts = soft_counts(early, [0], half_way)
    counts = call_kernel(
        "cross",
        functools.partial(cross_kernel, len(early)),
        jax.ShapeDtypeStruct((1, half_way), jnp.float32),
        *early,
        *swapped,
        counts,
    )
    early += swapped

    late_piece, _ = lax.optimization_barrier((last_piece, counts))
    late_other = swap_cores(late_piece)
    sums = [
        jax.ShapeDtypeStruct((1, 2 * half_way), jnp.float32),
        jax.ShapeDtypeStruct((1, cores * capacity), jnp.float32),
    ]
    early_sums, own_sums = call_kernel("late", late_kernel, sums, *early, last_piece)

    def places():
        chip, core = chip_index(), lax.axis_index("sub")
        devices = []
        for here in (core, 1 - core):
            for p in (first, *middle):
                there = (chip ^ (p * cores + here)) * cores
                devices += [there + here, there + 1 - here]
        there = (chip ^ (last * cores + core)) * cores
        devices += [there + core, there + 1 - core]
        return [clusters * cores - 1 - device for device in devices]

    counts = call_kernel(
        "finish",
        functools.partial(finish_kernel, places),
        jax.ShapeDtypeStruct((clusters * cores, 1, capacity), jnp.float32),
        last_piece,
        late_other,
        counts,
        early_sums,
        own_sums,
    )
    back = lax.all_to_all(
        counts,
        ("owner", "helper", "sub"),
        split_axis=0,
        concat_axis=0,
        axis_index_groups=[list(reversed(range(clusters * cores)))],
        tiled=True,
    )
    return select(back, slot, clusters, capacity, backwards=True)


def body_by_owner(embeddings, cluster_id):
    doc_count, feature_count = embeddings.shape
    owners, helpers = lax.axis_size("owner"), lax.axis_size("helper")
    clusters = CL_OWN * owners
    capacity = 2 * doc_count // clusters
    mine = lax.axis_index("helper") % CL_OWN

    def partner(x):
        return lax.ppermute(x, "helper", [(i, i ^ 1) for i in range(helpers)])

    outgoing, slot = call_kernel(
        "route",
        functools.partial(route_kernel, clusters, capacity),
        [
            jax.ShapeDtypeStruct((clusters * capacity, feature_count), jnp.bfloat16),
            jax.ShapeDtypeStruct((1, doc_count), jnp.int32),
        ],
        embeddings,
        cluster_id.reshape(1, doc_count),
    )
    outgoing = outgoing.reshape(owners, CL_OWN, capacity, feature_count)
    arrived = lax.all_to_all(outgoing, "owner", split_axis=0, concat_axis=0, tiled=True)
    kept = lax.dynamic_index_in_dim(arrived, mine, 1, keepdims=False)
    given = partner(lax.dynamic_index_in_dim(arrived, 1 - mine, 1, keepdims=False))
    own = jnp.stack([kept, given]).reshape(CL_OWN * owners * capacity, feature_count)
    others = [swap_cores(own)]
    for step in range(CL_OWN, helpers, CL_OWN):
        turn = [(i, (i + step) % helpers) for i in range(helpers)]
        others += [lax.ppermute(x, "helper", turn) for x in (own, others[0])]
    counts = soft_counts([own, *others], [0], own.shape[0])
    counts = counts.reshape(CL_OWN, owners, capacity)
    kept, given = counts[0], partner(counts[1])
    counts = jnp.where(mine == 0, jnp.stack([kept, given], 1), jnp.stack([given, kept], 1))
    back = lax.all_to_all(counts, "owner", split_axis=0, concat_axis=0, tiled=True)
    return select(back.reshape(clusters, 1, capacity), slot, clusters, capacity)


def solution(mesh):
    in_specs = (
        P(("groups", "owner", "helper", "sub"), None),
        P(("groups", "owner", "helper", "sub")),
    )
    out_specs = P(("groups", "owner", "helper", "sub"))
    body = body_by_chip if mesh.shape["helper"] == CL_OWN else body_by_owner
    return jax.shard_map(body, mesh=mesh, in_specs=in_specs, out_specs=out_specs, check_vma=False)
```

```python
import functools
import math

import jax
import jax.numpy as jnp
from jax import lax
from jax.experimental import pallas as pl
from jax.experimental.pallas import tpu as pltpu
from jax.sharding import PartitionSpec as P

CL_OWN = 2

epsilon = 1e-06
threshold = 0.8
sharpness = 0.05

EMPTY = 4.0
TILE = 1024
VMEM = pl.BlockSpec(memory_space=pltpu.VMEM)


def chip_index():
    return lax.axis_index("owner") * CL_OWN + lax.axis_index("helper")


def place_of(device):
    last = CL_OWN * 2 - 1
    owner, rest = device // (last + 1), device % (last + 1)
    places = (3, 1, 0, 2)
    if isinstance(device, int):
        return places[owner] * (last + 1) + last - rest
    place = jnp.full_like(owner, places[0])
    for k in range(1, len(places)):
        place = jnp.where(owner == k, places[k], place)
    return place * (last + 1) + last - rest


def slots_of(ids, clusters, capacity):
    doc_count = ids.shape[1]
    member = lax.broadcasted_iota(jnp.int32, (clusters, doc_count), 0) == ids
    earlier = lax.broadcasted_iota(jnp.int32, (doc_count, doc_count), 0) < (
        lax.broadcasted_iota(jnp.int32, (doc_count, doc_count), 1)
    )
    ahead = jnp.dot(
        member.astype(jnp.bfloat16), earlier.astype(jnp.bfloat16), preferred_element_type=jnp.float32
    )
    rank = jnp.sum(jnp.where(member, ahead, 0.0), axis=0, keepdims=True).astype(jnp.int32)
    return ids * capacity + rank


def lay(rows_ref, slot, slots):
    doc_count, feature_count = rows_ref.shape
    dispatch = lax.broadcasted_iota(jnp.int32, (slots, doc_count), 0) == slot
    filled = jnp.sum(dispatch.astype(jnp.float32), axis=1, keepdims=True) > 0
    laid = jnp.dot(
        dispatch.astype(jnp.bfloat16), rows_ref[...], preferred_element_type=jnp.float32
    )
    factor = lax.rsqrt(
        jnp.mean(laid * laid, axis=-1, keepdims=True) + epsilon
    ) * feature_count ** (-0.5)
    lane = lax.broadcasted_iota(jnp.int32, laid.shape, 1)
    return jnp.where(filled | (lane > 0), laid * factor, EMPTY).astype(jnp.bfloat16)


def slots_of_steps(slot, capacity, steps):
    cores = lax.axis_size("sub")
    by_distance = slot ^ (chip_index() * capacity)
    distance = by_distance // capacity
    rank = by_distance - distance * capacity
    step = jnp.full_like(slot, -1)
    for place, p in enumerate(steps):
        step = jnp.where(distance == p * cores + lax.axis_index("sub"), place, step)
    return jnp.where(step < 0, -1, step * capacity + rank)


def route_first_kernel(clusters, capacity, step, rows_ref, ids_ref, piece_ref, slot_ref):
    slot = slots_of(ids_ref[...], clusters, capacity)
    slot_ref[...] = slot
    piece_ref[...] = lay(rows_ref, slots_of_steps(slot, capacity, [step]), capacity)


def route_rest_kernel(clusters, capacity, halves, steps, *refs):
    own_rows, other_rows, own_slot, other_ids, *piece_refs = refs
    half_refs, whole_refs = piece_refs[: len(halves)], piece_refs[len(halves) :]
    slot = slots_of_steps(own_slot[...], capacity, steps)
    laid = lay(own_rows, slot, len(steps) * capacity)
    for k, piece in enumerate(whole_refs):
        piece[:capacity] = laid[k * capacity : (k + 1) * capacity]
    slot = slots_of(other_ids[...], clusters, capacity)
    slot = slots_of_steps(slot, capacity, [*halves, *steps])
    laid = lay(other_rows, slot, (len(halves) + len(steps)) * capacity)
    for k, piece in enumerate(half_refs):
        piece[...] = laid[k * capacity : (k + 1) * capacity]
    for k, piece in enumerate(whole_refs, len(halves)):
        piece[capacity:] = laid[k * capacity : (k + 1) * capacity]


def route_kernel(clusters, capacity, rows_ref, ids_ref, piece_ref, slot_ref):
    slot = slots_of(ids_ref[...], clusters, capacity)
    slot_ref[...] = slot
    piece_ref[...] = lay(rows_ref, slot, piece_ref.shape[0])


def call_kernel(name, kernel, out_shape, *args, limit=32 * 2**20, flops=0):
    cost = pl.CostEstimate(flops=flops, bytes_accessed=0, transcendentals=0) if flops else None
    return pl.pallas_call(
        kernel,
        out_shape=out_shape,
        in_specs=[VMEM] * len(args),
        out_specs=jax.tree.map(lambda _: VMEM, out_shape),
        compiler_params=pltpu.CompilerParams(vmem_limit_bytes=limit),
        cost_estimate=cost,
        name=name,
    )(*args)


def pass_kernel(*refs):
    half = len(refs) // 2
    for in_ref, out_ref in zip(refs[:half], refs[half:]):
        out_ref[...] = in_ref[...]


def regroup_kernel(pieces, *refs):
    rows = jnp.concatenate([ref[...] for ref in refs[:pieces]], axis=0)
    first = 0
    for part in refs[pieces:]:
        part[...] = rows[first : first + part.shape[0]]
        first += part.shape[0]


def blocks(rows, starts, size):
    return jnp.concatenate([rows[start : start + size] for start in starts], axis=0)


def count_against(rows, own, starts, size):
    column = lax.broadcasted_iota(jnp.int32, (1, own.shape[0]), 1)
    itself = jnp.full_like(column, -1)
    for k, start in enumerate(starts):
        itself = jnp.where(column // size == k, column + (start - k * size), itself)
    slope = -math.log2(math.e) / sharpness
    total = jnp.zeros((1, own.shape[0]), jnp.float32)
    for first in range(0, rows.shape[0], TILE):
        other = rows[first : first + TILE]
        scores = lax.dot_general(
            other, own, (((1,), (1,)), ((), ())), preferred_element_type=jnp.float32
        )
        weights = 1.0 / (1.0 + jnp.exp2(scores * slope - threshold * slope))
        keep = other[:, :1].astype(jnp.float32) < 0.5 * EMPTY
        if starts:
            keep = keep & (lax.broadcasted_iota(jnp.int32, scores.shape, 0) + first != itself)
        total = total + jnp.sum(jnp.where(keep, weights, 0.0), axis=0, keepdims=True)
    return total


def count_kernel(starts, size, *refs):
    *piece_refs, count_ref = refs
    rows = jnp.concatenate([piece[...] for piece in piece_refs], axis=0)
    count_ref[...] = count_against(rows, blocks(rows, starts, size), starts, size)


def soft_counts(pieces, starts, size):
    out_shape = jax.ShapeDtypeStruct((1, len(starts) * size), jnp.float32)
    return call_kernel("count", functools.partial(count_kernel, starts, size), out_shape, *pieces)


def cross_kernel(pieces, *refs):
    *piece_refs, before_ref, count_ref = refs
    own = jnp.concatenate([piece[...] for piece in piece_refs[:pieces]], axis=0)
    other = jnp.concatenate([piece[...] for piece in piece_refs[pieces:]], axis=0)
    count_ref[...] = before_ref[...] + count_against(other, own, [], own.shape[0])


def late_kernel(*refs):
    *piece_refs, late_ref, early_ref, own_ref = refs
    early = jnp.concatenate([piece[...] for piece in piece_refs], axis=0)
    late = late_ref[...]
    size = late.shape[0]
    early_ref[...] = count_against(late, early, [], size)
    own_ref[...] = count_against(early, late, [], size) + count_against(late, late, [0], size)


def finish_kernel(places, late_ref, other_ref, counts_ref, early_ref, own_ref, out_ref):
    size = out_ref.shape[2]
    late = late_ref[...]
    own = own_ref[...] + count_against(other_ref[...], late, [], size)
    early = early_ref[...]
    blocks_early = early.shape[1] // size
    out_ref[...] = jnp.zeros_like(out_ref)
    for k, place in enumerate(places()):
        if k < blocks_early:
            block = early[:, k * size : (k + 1) * size]
            if k * size < counts_ref.shape[1]:
                block = block + counts_ref[:, k * size : (k + 1) * size]
        else:
            block = own[:, (k - blocks_early) * size : (k - blocks_early + 1) * size]
        out_ref[pl.ds(place, 1), 0, :] = block


def select_kernel(clusters, capacity, backwards, counts_ref, slot_ref, out_ref):
    counts = counts_ref[:, 0, :]
    slot = slot_ref[...]
    doc_count = slot.shape[1]
    block = slot // capacity
    rank = slot - block * capacity
    hot = (lax.broadcasted_iota(jnp.int32, (capacity, doc_count), 0) == rank).astype(jnp.float32)
    by_block = jnp.dot(
        counts, hot, precision=lax.Precision.HIGHEST, preferred_element_type=jnp.float32
    )
    parts = counts.shape[0] // clusters
    row = lax.broadcasted_iota(jnp.int32, by_block.shape, 0)
    if backwards:
        chosen = row // parts == place_of(block * parts) // parts
    else:
        chosen = row // parts == block
    out_ref[...] = jnp.sum(jnp.where(chosen, by_block, 0.0), axis=0, keepdims=True)


def select(counts, slot, clusters, capacity, backwards=False):
    out_shape = jax.ShapeDtypeStruct(slot.shape, jnp.float32)
    kernel = functools.partial(select_kernel, clusters, capacity, backwards)
    return call_kernel("select", kernel, out_shape, counts, slot, limit=8 * 2**20)[0]


def swap_cores(x):
    cores = lax.axis_size("sub")
    return lax.ppermute(x, "sub", [(i, i ^ 1) for i in range(cores)])


def body_by_chip(embeddings, cluster_id):
    doc_count, feature_count = embeddings.shape
    clusters = CL_OWN * lax.axis_size("owner")
    capacity = 2 * doc_count // clusters
    cores = lax.axis_size("sub")
    steps = clusters // cores

    def across(x, p):
        pairs = [
            (chip * cores + core, (chip ^ (p * cores + core)) * cores + core)
            for chip in range(clusters)
            for core in range(cores)
        ]
        return lax.ppermute(x, ("owner", "helper", "sub"), pairs)

    ids = cluster_id.reshape(1, doc_count)
    other_rows, other_ids = swap_cores(embeddings), swap_cores(ids)
    first, last = steps // 2, steps - 1
    middle = [p for p in range(steps) if p not in (first, last)]
    half = jax.ShapeDtypeStruct((capacity, feature_count), jnp.bfloat16)
    whole = jax.ShapeDtypeStruct((cores * capacity, feature_count), jnp.bfloat16)

    first_own, slot = call_kernel(
        "route_first",
        functools.partial(route_first_kernel, clusters, capacity, first),
        [half, jax.ShapeDtypeStruct((1, doc_count), jnp.int32)],
        embeddings,
        ids,
    )
    first_own = across(first_own, first)

    def route_rest(name, halves, steps, slot, flops=0):
        return call_kernel(
            name,
            functools.partial(route_rest_kernel, clusters, capacity, halves, steps),
            [half] * len(halves) + [whole] * len(steps),
            embeddings,
            other_rows,
            slot,
            other_ids,
            flops=flops,
        )

    near = route_rest("route_near", [], middle, slot)
    later_slot, _ = lax.optimization_barrier((slot, near[0]))
    near = [across(piece, p) for piece, p in zip(near, middle)]
    first_other, last_piece = route_rest("route_far", [first], [last], later_slot, 10**10)
    first_other, last_piece = across(first_other, first), across(last_piece, last)

    (first_own,) = call_kernel("pass", pass_kernel, [half], first_own)
    early = [first_own, first_other, *near]
    half_way = cores * capacity * (steps - 1)
    part = jax.ShapeDtypeStruct((half_way // 4, feature_count), jnp.bfloat16)
    parts = call_kernel(
        "regroup", functools.partial(regroup_kernel, len(early)), [part] * 4, *early, flops=10**10
    )
    swapped = [swap_cores(x) for x in parts]

    counts = soft_counts(early, [0], half_way)
    counts = call_kernel(
        "cross",
        functools.partial(cross_kernel, len(early)),
        jax.ShapeDtypeStruct((1, half_way), jnp.float32),
        *early,
        *swapped,
        counts,
    )
    early += swapped

    late_piece, _ = lax.optimization_barrier((last_piece, counts))
    late_other = swap_cores(late_piece)
    sums = [
        jax.ShapeDtypeStruct((1, 2 * half_way), jnp.float32),
        jax.ShapeDtypeStruct((1, cores * capacity), jnp.float32),
    ]
    early_sums, own_sums = call_kernel("late", late_kernel, sums, *early, last_piece)

    def places():
        chip, core = chip_index(), lax.axis_index("sub")
        devices = []
        for here in (core, 1 - core):
            for p in (first, *middle):
                there = (chip ^ (p * cores + here)) * cores
                devices += [there + here, there + 1 - here]
        there = (chip ^ (last * cores + core)) * cores
        devices += [there + core, there + 1 - core]
        return [place_of(device) for device in devices]

    counts = call_kernel(
        "finish",
        functools.partial(finish_kernel, places),
        jax.ShapeDtypeStruct((clusters * cores, 1, capacity), jnp.float32),
        last_piece,
        late_other,
        counts,
        early_sums,
        own_sums,
    )
    back = lax.all_to_all(
        counts,
        ("owner", "helper", "sub"),
        split_axis=0,
        concat_axis=0,
        axis_index_groups=[sorted(range(clusters * cores), key=place_of)],
        tiled=True,
    )
    return select(back, slot, clusters, capacity, backwards=True)


def body_by_owner(embeddings, cluster_id):
    doc_count, feature_count = embeddings.shape
    owners, helpers = lax.axis_size("owner"), lax.axis_size("helper")
    clusters = CL_OWN * owners
    capacity = 2 * doc_count // clusters
    mine = lax.axis_index("helper") % CL_OWN

    def partner(x):
        return lax.ppermute(x, "helper", [(i, i ^ 1) for i in range(helpers)])

    outgoing, slot = call_kernel(
        "route",
        functools.partial(route_kernel, clusters, capacity),
        [
            jax.ShapeDtypeStruct((clusters * capacity, feature_count), jnp.bfloat16),
            jax.ShapeDtypeStruct((1, doc_count), jnp.int32),
        ],
        embeddings,
        cluster_id.reshape(1, doc_count),
    )
    outgoing = outgoing.reshape(owners, CL_OWN, capacity, feature_count)
    arrived = lax.all_to_all(outgoing, "owner", split_axis=0, concat_axis=0, tiled=True)
    kept = lax.dynamic_index_in_dim(arrived, mine, 1, keepdims=False)
    given = partner(lax.dynamic_index_in_dim(arrived, 1 - mine, 1, keepdims=False))
    own = jnp.stack([kept, given]).reshape(CL_OWN * owners * capacity, feature_count)
    others = [swap_cores(own)]
    for step in range(CL_OWN, helpers, CL_OWN):
        turn = [(i, (i + step) % helpers) for i in range(helpers)]
        others += [lax.ppermute(x, "helper", turn) for x in (own, others[0])]
    counts = soft_counts([own, *others], [0], own.shape[0])
    counts = counts.reshape(CL_OWN, owners, capacity)
    kept, given = counts[0], partner(counts[1])
    counts = jnp.where(mine == 0, jnp.stack([kept, given], 1), jnp.stack([given, kept], 1))
    back = lax.all_to_all(counts, "owner", split_axis=0, concat_axis=0, tiled=True)
    return select(back.reshape(clusters, 1, capacity), slot, clusters, capacity)


def solution(mesh):
    in_specs = (
        P(("groups", "owner", "helper", "sub"), None),
        P(("groups", "owner", "helper", "sub")),
    )
    out_specs = P(("groups", "owner", "helper", "sub"))
    body = body_by_chip if mesh.shape["helper"] == CL_OWN else body_by_owner
    return jax.shard_map(body, mesh=mesh, in_specs=in_specs, out_specs=out_specs, check_vma=False)
```

```python
import functools
import math

import jax
import jax.numpy as jnp
from jax import lax
from jax.experimental import pallas as pl
from jax.experimental.pallas import tpu as pltpu
from jax.sharding import PartitionSpec as P

CL_OWN = 2

epsilon = 1e-06
threshold = 0.8
sharpness = 0.05

EMPTY = 4.0
TILE = 1024
VMEM = pl.BlockSpec(memory_space=pltpu.VMEM)


def chip_index():
    return lax.axis_index("owner") * CL_OWN + lax.axis_index("helper")


def place_of(device):
    chip, core = device // 2, device % 2
    owner, helper = chip // CL_OWN, chip % CL_OWN
    places = (3, 1, 0, 2)
    chips = CL_OWN * len(places)
    if isinstance(device, int):
        place = places[owner] * CL_OWN + CL_OWN - 1 - helper + chips * core
        return {chips - 1: 2 * chips - 1, 2 * chips - 1: chips - 1}.get(place, place)
    place = jnp.full_like(owner, places[0])
    for k in range(1, len(places)):
        place = jnp.where(owner == k, places[k], place)
    place = place * CL_OWN + CL_OWN - 1 - helper + chips * core
    return jnp.where(chip == 0, (2 - core) * chips - 1, place)


def slots_of(ids, clusters, capacity):
    doc_count = ids.shape[1]
    member = lax.broadcasted_iota(jnp.int32, (clusters, doc_count), 0) == ids
    earlier = lax.broadcasted_iota(jnp.int32, (doc_count, doc_count), 0) < (
        lax.broadcasted_iota(jnp.int32, (doc_count, doc_count), 1)
    )
    ahead = jnp.dot(
        member.astype(jnp.bfloat16), earlier.astype(jnp.bfloat16), preferred_element_type=jnp.float32
    )
    rank = jnp.sum(jnp.where(member, ahead, 0.0), axis=0, keepdims=True).astype(jnp.int32)
    return ids * capacity + rank


def lay(rows_ref, slot, slots):
    doc_count, feature_count = rows_ref.shape
    dispatch = lax.broadcasted_iota(jnp.int32, (slots, doc_count), 0) == slot
    filled = jnp.sum(dispatch.astype(jnp.float32), axis=1, keepdims=True) > 0
    laid = jnp.dot(
        dispatch.astype(jnp.bfloat16), rows_ref[...], preferred_element_type=jnp.float32
    )
    factor = lax.rsqrt(
        jnp.mean(laid * laid, axis=-1, keepdims=True) + epsilon
    ) * feature_count ** (-0.5)
    lane = lax.broadcasted_iota(jnp.int32, laid.shape, 1)
    return jnp.where(filled | (lane > 0), laid * factor, EMPTY).astype(jnp.bfloat16)


def slots_of_steps(slot, capacity, steps):
    cores = lax.axis_size("sub")
    by_distance = slot ^ (chip_index() * capacity)
    distance = by_distance // capacity
    rank = by_distance - distance * capacity
    step = jnp.full_like(slot, -1)
    for place, p in enumerate(steps):
        step = jnp.where(distance == p * cores + lax.axis_index("sub"), place, step)
    return jnp.where(step < 0, -1, step * capacity + rank)


def route_first_kernel(clusters, capacity, step, rows_ref, ids_ref, piece_ref, slot_ref):
    slot = slots_of(ids_ref[...], clusters, capacity)
    slot_ref[...] = slot
    piece_ref[...] = lay(rows_ref, slots_of_steps(slot, capacity, [step]), capacity)


def route_rest_kernel(clusters, capacity, halves, steps, *refs):
    own_rows, other_rows, own_slot, other_ids, *piece_refs = refs
    half_refs, whole_refs = piece_refs[: len(halves)], piece_refs[len(halves) :]
    slot = slots_of_steps(own_slot[...], capacity, steps)
    laid = lay(own_rows, slot, len(steps) * capacity)
    for k, piece in enumerate(whole_refs):
        piece[:capacity] = laid[k * capacity : (k + 1) * capacity]
    slot = slots_of(other_ids[...], clusters, capacity)
    slot = slots_of_steps(slot, capacity, [*halves, *steps])
    laid = lay(other_rows, slot, (len(halves) + len(steps)) * capacity)
    for k, piece in enumerate(half_refs):
        piece[...] = laid[k * capacity : (k + 1) * capacity]
    for k, piece in enumerate(whole_refs, len(halves)):
        piece[capacity:] = laid[k * capacity : (k + 1) * capacity]


def route_kernel(clusters, capacity, rows_ref, ids_ref, piece_ref, slot_ref):
    slot = slots_of(ids_ref[...], clusters, capacity)
    slot_ref[...] = slot
    piece_ref[...] = lay(rows_ref, slot, piece_ref.shape[0])


def call_kernel(name, kernel, out_shape, *args, limit=32 * 2**20, flops=0):
    cost = pl.CostEstimate(flops=flops, bytes_accessed=0, transcendentals=0) if flops else None
    return pl.pallas_call(
        kernel,
        out_shape=out_shape,
        in_specs=[VMEM] * len(args),
        out_specs=jax.tree.map(lambda _: VMEM, out_shape),
        compiler_params=pltpu.CompilerParams(vmem_limit_bytes=limit),
        cost_estimate=cost,
        name=name,
    )(*args)


def pass_kernel(*refs):
    half = len(refs) // 2
    for in_ref, out_ref in zip(refs[:half], refs[half:]):
        out_ref[...] = in_ref[...]


def regroup_kernel(pieces, *refs):
    rows = jnp.concatenate([ref[...] for ref in refs[:pieces]], axis=0)
    first = 0
    for part in refs[pieces:]:
        part[...] = rows[first : first + part.shape[0]]
        first += part.shape[0]


def blocks(rows, starts, size):
    return jnp.concatenate([rows[start : start + size] for start in starts], axis=0)


def count_against(rows, own, starts, size):
    column = lax.broadcasted_iota(jnp.int32, (1, own.shape[0]), 1)
    itself = jnp.full_like(column, -1)
    for k, start in enumerate(starts):
        itself = jnp.where(column // size == k, column + (start - k * size), itself)
    slope = -math.log2(math.e) / sharpness
    total = jnp.zeros((1, own.shape[0]), jnp.float32)
    for first in range(0, rows.shape[0], TILE):
        other = rows[first : first + TILE]
        scores = lax.dot_general(
            other, own, (((1,), (1,)), ((), ())), preferred_element_type=jnp.float32
        )
        weights = 1.0 / (1.0 + jnp.exp2(scores * slope - threshold * slope))
        keep = other[:, :1].astype(jnp.float32) < 0.5 * EMPTY
        if starts:
            keep = keep & (lax.broadcasted_iota(jnp.int32, scores.shape, 0) + first != itself)
        total = total + jnp.sum(jnp.where(keep, weights, 0.0), axis=0, keepdims=True)
    return total


def count_kernel(starts, size, *refs):
    *piece_refs, count_ref = refs
    rows = jnp.concatenate([piece[...] for piece in piece_refs], axis=0)
    count_ref[...] = count_against(rows, blocks(rows, starts, size), starts, size)


def soft_counts(pieces, starts, size):
    out_shape = jax.ShapeDtypeStruct((1, len(starts) * size), jnp.float32)
    return call_kernel("count", functools.partial(count_kernel, starts, size), out_shape, *pieces)


def cross_kernel(pieces, *refs):
    *piece_refs, before_ref, count_ref = refs
    own = jnp.concatenate([piece[...] for piece in piece_refs[:pieces]], axis=0)
    other = jnp.concatenate([piece[...] for piece in piece_refs[pieces:]], axis=0)
    count_ref[...] = before_ref[...] + count_against(other, own, [], own.shape[0])


def late_kernel(*refs):
    *piece_refs, late_ref, early_ref, own_ref = refs
    early = jnp.concatenate([piece[...] for piece in piece_refs], axis=0)
    late = late_ref[...]
    size = late.shape[0]
    early_ref[...] = count_against(late, early, [], size)
    own_ref[...] = count_against(early, late, [], size) + count_against(late, late, [0], size)


def finish_kernel(places, late_ref, other_ref, counts_ref, early_ref, own_ref, out_ref):
    size = out_ref.shape[2]
    late = late_ref[...]
    own = own_ref[...] + count_against(other_ref[...], late, [], size)
    early = early_ref[...]
    blocks_early = early.shape[1] // size
    out_ref[...] = jnp.zeros_like(out_ref)
    for k, place in enumerate(places()):
        if k < blocks_early:
            block = early[:, k * size : (k + 1) * size]
            if k * size < counts_ref.shape[1]:
                block = block + counts_ref[:, k * size : (k + 1) * size]
        else:
            block = own[:, (k - blocks_early) * size : (k - blocks_early + 1) * size]
        out_ref[pl.ds(place, 1), 0, :] = block


def select_kernel(clusters, capacity, backwards, counts_ref, slot_ref, out_ref):
    counts = counts_ref[:, 0, :]
    slot = slot_ref[...]
    doc_count = slot.shape[1]
    block = slot // capacity
    rank = slot - block * capacity
    hot = (lax.broadcasted_iota(jnp.int32, (capacity, doc_count), 0) == rank).astype(jnp.float32)
    by_block = jnp.dot(
        counts, hot, precision=lax.Precision.HIGHEST, preferred_element_type=jnp.float32
    )
    parts = counts.shape[0] // clusters
    row = lax.broadcasted_iota(jnp.int32, by_block.shape, 0)
    if backwards:
        chosen = row == place_of(block * parts)
        for part in range(1, parts):
            chosen = chosen | (row == place_of(block * parts + part))
    else:
        chosen = row // parts == block
    out_ref[...] = jnp.sum(jnp.where(chosen, by_block, 0.0), axis=0, keepdims=True)


def select(counts, slot, clusters, capacity, backwards=False):
    out_shape = jax.ShapeDtypeStruct(slot.shape, jnp.float32)
    kernel = functools.partial(select_kernel, clusters, capacity, backwards)
    return call_kernel("select", kernel, out_shape, counts, slot, limit=8 * 2**20)[0]


def swap_cores(x):
    cores = lax.axis_size("sub")
    return lax.ppermute(x, "sub", [(i, i ^ 1) for i in range(cores)])


def body_by_chip(embeddings, cluster_id):
    doc_count, feature_count = embeddings.shape
    clusters = CL_OWN * lax.axis_size("owner")
    capacity = 2 * doc_count // clusters
    cores = lax.axis_size("sub")
    steps = clusters // cores

    def across(x, p):
        pairs = [
            (chip * cores + core, (chip ^ (p * cores + core)) * cores + core)
            for chip in range(clusters)
            for core in range(cores)
        ]
        return lax.ppermute(x, ("owner", "helper", "sub"), pairs)

    ids = cluster_id.reshape(1, doc_count)
    other_rows, other_ids = swap_cores(embeddings), swap_cores(ids)
    first, last = steps // 2, steps - 1
    middle = [p for p in range(steps) if p not in (first, last)]
    half = jax.ShapeDtypeStruct((capacity, feature_count), jnp.bfloat16)
    whole = jax.ShapeDtypeStruct((cores * capacity, feature_count), jnp.bfloat16)

    first_own, slot = call_kernel(
        "route_first",
        functools.partial(route_first_kernel, clusters, capacity, first),
        [half, jax.ShapeDtypeStruct((1, doc_count), jnp.int32)],
        embeddings,
        ids,
    )
    first_own = across(first_own, first)

    def route_rest(name, halves, steps, slot, flops=0):
        return call_kernel(
            name,
            functools.partial(route_rest_kernel, clusters, capacity, halves, steps),
            [half] * len(halves) + [whole] * len(steps),
            embeddings,
            other_rows,
            slot,
            other_ids,
            flops=flops,
        )

    near = route_rest("route_near", [], middle, slot)
    later_slot, _ = lax.optimization_barrier((slot, near[0]))
    near = [across(piece, p) for piece, p in zip(near, middle)]
    first_other, last_piece = route_rest("route_far", [first], [last], later_slot, 10**10)
    first_other, last_piece = across(first_other, first), across(last_piece, last)

    (first_own,) = call_kernel("pass", pass_kernel, [half], first_own)
    early = [first_own, first_other, *near]
    half_way = cores * capacity * (steps - 1)
    part = jax.ShapeDtypeStruct((half_way // 4, feature_count), jnp.bfloat16)
    parts = call_kernel(
        "regroup", functools.partial(regroup_kernel, len(early)), [part] * 4, *early, flops=10**10
    )
    swapped = [swap_cores(x) for x in parts]

    counts = soft_counts(early, [0], half_way)
    counts = call_kernel(
        "cross",
        functools.partial(cross_kernel, len(early)),
        jax.ShapeDtypeStruct((1, half_way), jnp.float32),
        *early,
        *swapped,
        counts,
    )
    early += swapped

    late_piece, _ = lax.optimization_barrier((last_piece, counts))
    late_other = swap_cores(late_piece)
    sums = [
        jax.ShapeDtypeStruct((1, 2 * half_way), jnp.float32),
        jax.ShapeDtypeStruct((1, cores * capacity), jnp.float32),
    ]
    early_sums, own_sums = call_kernel("late", late_kernel, sums, *early, last_piece)

    def places():
        chip, core = chip_index(), lax.axis_index("sub")
        devices = []
        for here in (core, 1 - core):
            for p in (first, *middle):
                there = (chip ^ (p * cores + here)) * cores
                devices += [there + here, there + 1 - here]
        there = (chip ^ (last * cores + core)) * cores
        devices += [there + core, there + 1 - core]
        return [place_of(device) for device in devices]

    counts = call_kernel(
        "finish",
        functools.partial(finish_kernel, places),
        jax.ShapeDtypeStruct((clusters * cores, 1, capacity), jnp.float32),
        last_piece,
        late_other,
        counts,
        early_sums,
        own_sums,
    )
    back = lax.all_to_all(
        counts,
        ("owner", "helper", "sub"),
        split_axis=0,
        concat_axis=0,
        axis_index_groups=[sorted(range(clusters * cores), key=place_of)],
        tiled=True,
    )
    return select(back, slot, clusters, capacity, backwards=True)


def body_by_owner(embeddings, cluster_id):
    doc_count, feature_count = embeddings.shape
    owners, helpers = lax.axis_size("owner"), lax.axis_size("helper")
    clusters = CL_OWN * owners
    capacity = 2 * doc_count // clusters
    mine = lax.axis_index("helper") % CL_OWN

    def partner(x):
        return lax.ppermute(x, "helper", [(i, i ^ 1) for i in range(helpers)])

    outgoing, slot = call_kernel(
        "route",
        functools.partial(route_kernel, clusters, capacity),
        [
            jax.ShapeDtypeStruct((clusters * capacity, feature_count), jnp.bfloat16),
            jax.ShapeDtypeStruct((1, doc_count), jnp.int32),
        ],
        embeddings,
        cluster_id.reshape(1, doc_count),
    )
    outgoing = outgoing.reshape(owners, CL_OWN, capacity, feature_count)
    arrived = lax.all_to_all(outgoing, "owner", split_axis=0, concat_axis=0, tiled=True)
    kept = lax.dynamic_index_in_dim(arrived, mine, 1, keepdims=False)
    given = partner(lax.dynamic_index_in_dim(arrived, 1 - mine, 1, keepdims=False))
    own = jnp.stack([kept, given]).reshape(CL_OWN * owners * capacity, feature_count)
    others = [swap_cores(own)]
    for step in range(CL_OWN, helpers, CL_OWN):
        turn = [(i, (i + step) % helpers) for i in range(helpers)]
        others += [lax.ppermute(x, "helper", turn) for x in (own, others[0])]
    counts = soft_counts([own, *others], [0], own.shape[0])
    counts = counts.reshape(CL_OWN, owners, capacity)
    kept, given = counts[0], partner(counts[1])
    counts = jnp.where(mine == 0, jnp.stack([kept, given], 1), jnp.stack([given, kept], 1))
    back = lax.all_to_all(counts, "owner", split_axis=0, concat_axis=0, tiled=True)
    return select(back.reshape(clusters, 1, capacity), slot, clusters, capacity)


def solution(mesh):
    in_specs = (
        P(("groups", "owner", "helper", "sub"), None),
        P(("groups", "owner", "helper", "sub")),
    )
    out_specs = P(("groups", "owner", "helper", "sub"))
    body = body_by_chip if mesh.shape["helper"] == CL_OWN else body_by_owner
    return jax.shard_map(body, mesh=mesh, in_specs=in_specs, out_specs=out_specs, check_vma=False)
```

```python
import functools
import math

import jax
import jax.numpy as jnp
from jax import lax
from jax.experimental import pallas as pl
from jax.experimental.pallas import tpu as pltpu
from jax.sharding import PartitionSpec as P

CL_OWN = 2

epsilon = 1e-06
threshold = 0.8
sharpness = 0.05

EMPTY = 4.0
TILE = 1024
VMEM = pl.BlockSpec(memory_space=pltpu.VMEM)


def chip_index():
    return lax.axis_index("owner") * CL_OWN + lax.axis_index("helper")


def place_of(device):
    last = CL_OWN * 2 - 1
    owner, rest = device // (last + 1), device % (last + 1)
    places = (3, 1, 0, 2)
    if isinstance(device, int):
        return places[owner] * (last + 1) + last - rest
    place = jnp.full_like(owner, places[0])
    for k in range(1, len(places)):
        place = jnp.where(owner == k, places[k], place)
    return place * (last + 1) + last - rest


def slots_of(ids, clusters, capacity):
    doc_count = ids.shape[1]
    member = lax.broadcasted_iota(jnp.int32, (clusters, doc_count), 0) == ids
    earlier = lax.broadcasted_iota(jnp.int32, (doc_count, doc_count), 0) < (
        lax.broadcasted_iota(jnp.int32, (doc_count, doc_count), 1)
    )
    ahead = jnp.dot(
        member.astype(jnp.bfloat16), earlier.astype(jnp.bfloat16), preferred_element_type=jnp.float32
    )
    rank = jnp.sum(jnp.where(member, ahead, 0.0), axis=0, keepdims=True).astype(jnp.int32)
    return ids * capacity + rank


def lay(rows_ref, slot, slots):
    doc_count, feature_count = rows_ref.shape
    dispatch = lax.broadcasted_iota(jnp.int32, (slots, doc_count), 0) == slot
    filled = jnp.sum(dispatch.astype(jnp.float32), axis=1, keepdims=True) > 0
    laid = jnp.dot(
        dispatch.astype(jnp.bfloat16), rows_ref[...], preferred_element_type=jnp.float32
    )
    factor = lax.rsqrt(
        jnp.mean(laid * laid, axis=-1, keepdims=True) + epsilon
    ) * feature_count ** (-0.5)
    lane = lax.broadcasted_iota(jnp.int32, laid.shape, 1)
    return jnp.where(filled | (lane > 0), laid * factor, EMPTY).astype(jnp.bfloat16)


def slots_of_steps(slot, capacity, steps):
    cores = lax.axis_size("sub")
    by_distance = slot ^ (chip_index() * capacity)
    distance = by_distance // capacity
    rank = by_distance - distance * capacity
    step = jnp.full_like(slot, -1)
    for place, p in enumerate(steps):
        step = jnp.where(distance == p * cores + lax.axis_index("sub"), place, step)
    return jnp.where(step < 0, -1, step * capacity + rank)


def route_first_kernel(clusters, capacity, step, rows_ref, ids_ref, piece_ref, slot_ref):
    slot = slots_of(ids_ref[...], clusters, capacity)
    slot_ref[...] = slot
    piece_ref[...] = lay(rows_ref, slots_of_steps(slot, capacity, [step]), capacity)


def route_rest_kernel(clusters, capacity, halves, steps, *refs):
    own_rows, other_rows, own_slot, other_ids, *piece_refs = refs
    half_refs, whole_refs = piece_refs[: len(halves)], piece_refs[len(halves) :]
    slot = slots_of_steps(own_slot[...], capacity, steps)
    laid = lay(own_rows, slot, len(steps) * capacity)
    for k, piece in enumerate(whole_refs):
        piece[:capacity] = laid[k * capacity : (k + 1) * capacity]
    slot = slots_of(other_ids[...], clusters, capacity)
    slot = slots_of_steps(slot, capacity, [*halves, *steps])
    laid = lay(other_rows, slot, (len(halves) + len(steps)) * capacity)
    for k, piece in enumerate(half_refs):
        piece[...] = laid[k * capacity : (k + 1) * capacity]
    for k, piece in enumerate(whole_refs, len(halves)):
        piece[capacity:] = laid[k * capacity : (k + 1) * capacity]


def route_kernel(clusters, capacity, rows_ref, ids_ref, piece_ref, slot_ref):
    slot = slots_of(ids_ref[...], clusters, capacity)
    slot_ref[...] = slot
    piece_ref[...] = lay(rows_ref, slot, piece_ref.shape[0])


def call_kernel(name, kernel, out_shape, *args, limit=32 * 2**20, flops=0):
    cost = pl.CostEstimate(flops=flops, bytes_accessed=0, transcendentals=0) if flops else None
    return pl.pallas_call(
        kernel,
        out_shape=out_shape,
        in_specs=[VMEM] * len(args),
        out_specs=jax.tree.map(lambda _: VMEM, out_shape),
        compiler_params=pltpu.CompilerParams(vmem_limit_bytes=limit),
        cost_estimate=cost,
        name=name,
    )(*args)


def pass_kernel(*refs):
    half = len(refs) // 2
    for in_ref, out_ref in zip(refs[:half], refs[half:]):
        out_ref[...] = in_ref[...]


def regroup_kernel(pieces, *refs):
    rows = jnp.concatenate([ref[...] for ref in refs[:pieces]], axis=0)
    first = 0
    for part in refs[pieces:]:
        part[...] = rows[first : first + part.shape[0]]
        first += part.shape[0]


def blocks(rows, starts, size):
    return jnp.concatenate([rows[start : start + size] for start in starts], axis=0)


def count_against(rows, own, starts, size):
    column = lax.broadcasted_iota(jnp.int32, (1, own.shape[0]), 1)
    itself = jnp.full_like(column, -1)
    for k, start in enumerate(starts):
        itself = jnp.where(column // size == k, column + (start - k * size), itself)
    slope = -math.log2(math.e) / sharpness
    total = jnp.zeros((1, own.shape[0]), jnp.float32)
    for first in range(0, rows.shape[0], TILE):
        other = rows[first : first + TILE]
        scores = lax.dot_general(
            other, own, (((1,), (1,)), ((), ())), preferred_element_type=jnp.float32
        )
        weights = 1.0 / (1.0 + jnp.exp2(scores * slope - threshold * slope))
        keep = other[:, :1].astype(jnp.float32) < 0.5 * EMPTY
        if starts:
            keep = keep & (lax.broadcasted_iota(jnp.int32, scores.shape, 0) + first != itself)
        total = total + jnp.sum(jnp.where(keep, weights, 0.0), axis=0, keepdims=True)
    return total


def count_kernel(starts, size, *refs):
    *piece_refs, count_ref = refs
    rows = jnp.concatenate([piece[...] for piece in piece_refs], axis=0)
    count_ref[...] = count_against(rows, blocks(rows, starts, size), starts, size)


def soft_counts(pieces, starts, size):
    out_shape = jax.ShapeDtypeStruct((1, len(starts) * size), jnp.float32)
    return call_kernel("count", functools.partial(count_kernel, starts, size), out_shape, *pieces)


def cross_kernel(pieces, *refs):
    *piece_refs, before_ref, count_ref = refs
    own = jnp.concatenate([piece[...] for piece in piece_refs[:pieces]], axis=0)
    other = jnp.concatenate([piece[...] for piece in piece_refs[pieces:]], axis=0)
    count_ref[...] = before_ref[...] + count_against(other, own, [], own.shape[0])


def late_kernel(*refs):
    *piece_refs, late_ref, early_ref, own_ref = refs
    early = jnp.concatenate([piece[...] for piece in piece_refs], axis=0)
    late = late_ref[...]
    size = late.shape[0]
    early_ref[...] = count_against(late, early, [], size)
    own_ref[...] = count_against(early, late, [], size) + count_against(late, late, [0], size)


def finish_kernel(places, late_ref, other_ref, counts_ref, early_ref, own_ref, out_ref):
    size = out_ref.shape[2]
    late = late_ref[...]
    own = own_ref[...] + count_against(other_ref[...], late, [], size)
    early = early_ref[...]
    blocks_early = early.shape[1] // size
    out_ref[...] = jnp.zeros_like(out_ref)
    for k, place in enumerate(places()):
        if k < blocks_early:
            block = early[:, k * size : (k + 1) * size]
            if k * size < counts_ref.shape[1]:
                block = block + counts_ref[:, k * size : (k + 1) * size]
        else:
            block = own[:, (k - blocks_early) * size : (k - blocks_early + 1) * size]
        out_ref[pl.ds(place, 1), 0, :] = block


def select_kernel(clusters, capacity, backwards, counts_ref, slot_ref, out_ref):
    counts = counts_ref[:, 0, :]
    slot = slot_ref[...]
    doc_count = slot.shape[1]
    block = slot // capacity
    rank = slot - block * capacity
    hot = (lax.broadcasted_iota(jnp.int32, (capacity, doc_count), 0) == rank).astype(jnp.float32)
    by_block = jnp.dot(
        counts, hot, precision=lax.Precision.HIGHEST, preferred_element_type=jnp.float32
    )
    parts = counts.shape[0] // clusters
    row = lax.broadcasted_iota(jnp.int32, by_block.shape, 0)
    if backwards:
        chosen = row // parts == place_of(block * parts) // parts
    else:
        chosen = row // parts == block
    out_ref[...] = jnp.sum(jnp.where(chosen, by_block, 0.0), axis=0, keepdims=True)


def select(counts, slot, clusters, capacity, backwards=False):
    out_shape = jax.ShapeDtypeStruct(slot.shape, jnp.float32)
    kernel = functools.partial(select_kernel, clusters, capacity, backwards)
    return call_kernel("select", kernel, out_shape, counts, slot, limit=8 * 2**20)[0]


def swap_cores(x):
    cores = lax.axis_size("sub")
    return lax.ppermute(x, "sub", [(i, i ^ 1) for i in range(cores)])


def body_by_chip(embeddings, cluster_id):
    doc_count, feature_count = embeddings.shape
    clusters = CL_OWN * lax.axis_size("owner")
    capacity = 2 * doc_count // clusters
    cores = lax.axis_size("sub")
    steps = clusters // cores

    def across(x, p):
        pairs = [
            (chip * cores + core, (chip ^ (p * cores + core)) * cores + (core ^ (p == 0)))
            for chip in range(clusters)
            for core in range(cores)
        ]
        return lax.ppermute(x, ("owner", "helper", "sub"), pairs)

    ids = cluster_id.reshape(1, doc_count)
    other_rows, other_ids = swap_cores(embeddings), swap_cores(ids)
    first, last = steps // 2, steps - 1
    middle = [p for p in range(steps) if p not in (first, last)]
    half = jax.ShapeDtypeStruct((capacity, feature_count), jnp.bfloat16)
    whole = jax.ShapeDtypeStruct((cores * capacity, feature_count), jnp.bfloat16)

    first_own, slot = call_kernel(
        "route_first",
        functools.partial(route_first_kernel, clusters, capacity, first),
        [half, jax.ShapeDtypeStruct((1, doc_count), jnp.int32)],
        embeddings,
        ids,
    )
    first_own = across(first_own, first)

    def route_rest(name, halves, steps, slot, flops=0):
        return call_kernel(
            name,
            functools.partial(route_rest_kernel, clusters, capacity, halves, steps),
            [half] * len(halves) + [whole] * len(steps),
            embeddings,
            other_rows,
            slot,
            other_ids,
            flops=flops,
        )

    near = route_rest("route_near", [], middle, slot)
    later_slot, _ = lax.optimization_barrier((slot, near[0]))
    near = [across(piece, p) for piece, p in zip(near, middle)]
    first_other, last_piece = route_rest("route_far", [first], [last], later_slot, 10**10)
    first_other, last_piece = across(first_other, first), across(last_piece, last)

    (first_own,) = call_kernel("pass", pass_kernel, [half], first_own)
    early = [first_own, first_other, *near]
    half_way = cores * capacity * (steps - 1)
    part = jax.ShapeDtypeStruct((half_way // 4, feature_count), jnp.bfloat16)
    parts = call_kernel(
        "regroup", functools.partial(regroup_kernel, len(early)), [part] * 4, *early, flops=10**10
    )
    swapped = [swap_cores(x) for x in parts]

    counts = soft_counts(early, [0], half_way)
    counts = call_kernel(
        "cross",
        functools.partial(cross_kernel, len(early)),
        jax.ShapeDtypeStruct((1, half_way), jnp.float32),
        *early,
        *swapped,
        counts,
    )
    early += swapped

    late_piece, _ = lax.optimization_barrier((last_piece, counts))
    late_other = swap_cores(late_piece)
    sums = [
        jax.ShapeDtypeStruct((1, 2 * half_way), jnp.float32),
        jax.ShapeDtypeStruct((1, cores * capacity), jnp.float32),
    ]
    early_sums, own_sums = call_kernel("late", late_kernel, sums, *early, last_piece)

    def places():
        chip, core = chip_index(), lax.axis_index("sub")
        devices = []
        for here in (core, 1 - core):
            for p in (first, *middle):
                source = 1 - here if p == 0 else here
                there = (chip ^ (p * cores + source)) * cores
                devices += [there + source, there + 1 - source]
        there = (chip ^ (last * cores + core)) * cores
        devices += [there + core, there + 1 - core]
        return [place_of(device) for device in devices]

    counts = call_kernel(
        "finish",
        functools.partial(finish_kernel, places),
        jax.ShapeDtypeStruct((clusters * cores, 1, capacity), jnp.float32),
        last_piece,
        late_other,
        counts,
        early_sums,
        own_sums,
    )
    back = lax.all_to_all(
        counts,
        ("owner", "helper", "sub"),
        split_axis=0,
        concat_axis=0,
        axis_index_groups=[sorted(range(clusters * cores), key=place_of)],
        tiled=True,
    )
    return select(back, slot, clusters, capacity, backwards=True)


def body_by_owner(embeddings, cluster_id):
    doc_count, feature_count = embeddings.shape
    owners, helpers = lax.axis_size("owner"), lax.axis_size("helper")
    clusters = CL_OWN * owners
    capacity = 2 * doc_count // clusters
    mine = lax.axis_index("helper") % CL_OWN

    def partner(x):
        return lax.ppermute(x, "helper", [(i, i ^ 1) for i in range(helpers)])

    outgoing, slot = call_kernel(
        "route",
        functools.partial(route_kernel, clusters, capacity),
        [
            jax.ShapeDtypeStruct((clusters * capacity, feature_count), jnp.bfloat16),
            jax.ShapeDtypeStruct((1, doc_count), jnp.int32),
        ],
        embeddings,
        cluster_id.reshape(1, doc_count),
    )
    outgoing = outgoing.reshape(owners, CL_OWN, capacity, feature_count)
    arrived = lax.all_to_all(outgoing, "owner", split_axis=0, concat_axis=0, tiled=True)
    kept = lax.dynamic_index_in_dim(arrived, mine, 1, keepdims=False)
    given = partner(lax.dynamic_index_in_dim(arrived, 1 - mine, 1, keepdims=False))
    own = jnp.stack([kept, given]).reshape(CL_OWN * owners * capacity, feature_count)
    others = [swap_cores(own)]
    for step in range(CL_OWN, helpers, CL_OWN):
        turn = [(i, (i + step) % helpers) for i in range(helpers)]
        others += [lax.ppermute(x, "helper", turn) for x in (own, others[0])]
    counts = soft_counts([own, *others], [0], own.shape[0])
    counts = counts.reshape(CL_OWN, owners, capacity)
    kept, given = counts[0], partner(counts[1])
    counts = jnp.where(mine == 0, jnp.stack([kept, given], 1), jnp.stack([given, kept], 1))
    back = lax.all_to_all(counts, "owner", split_axis=0, concat_axis=0, tiled=True)
    return select(back.reshape(clusters, 1, capacity), slot, clusters, capacity)


def solution(mesh):
    in_specs = (
        P(("groups", "owner", "helper", "sub"), None),
        P(("groups", "owner", "helper", "sub")),
    )
    out_specs = P(("groups", "owner", "helper", "sub"))
    body = body_by_chip if mesh.shape["helper"] == CL_OWN else body_by_owner
    return jax.shard_map(body, mesh=mesh, in_specs=in_specs, out_specs=out_specs, check_vma=False)
```

```python
import functools
import math

import jax
import jax.numpy as jnp
from jax import lax
from jax.experimental import pallas as pl
from jax.experimental.pallas import tpu as pltpu
from jax.sharding import PartitionSpec as P

CL_OWN = 2

epsilon = 1e-06
threshold = 0.8
sharpness = 0.05

EMPTY = 4.0
TILE = 1024
VMEM = pl.BlockSpec(memory_space=pltpu.VMEM)


def chip_index():
    return lax.axis_index("owner") * CL_OWN + lax.axis_index("helper")


def slots_of(ids, clusters, capacity):
    doc_count = ids.shape[1]
    member = lax.broadcasted_iota(jnp.int32, (clusters, doc_count), 0) == ids
    earlier = lax.broadcasted_iota(jnp.int32, (doc_count, doc_count), 0) < (
        lax.broadcasted_iota(jnp.int32, (doc_count, doc_count), 1)
    )
    ahead = jnp.dot(
        member.astype(jnp.bfloat16), earlier.astype(jnp.bfloat16), preferred_element_type=jnp.float32
    )
    rank = jnp.sum(jnp.where(member, ahead, 0.0), axis=0, keepdims=True).astype(jnp.int32)
    return ids * capacity + rank


def lay(rows_ref, slot, slots):
    doc_count, feature_count = rows_ref.shape
    dispatch = lax.broadcasted_iota(jnp.int32, (slots, doc_count), 0) == slot
    filled = jnp.sum(dispatch.astype(jnp.float32), axis=1, keepdims=True) > 0
    laid = jnp.dot(
        dispatch.astype(jnp.bfloat16), rows_ref[...], preferred_element_type=jnp.float32
    )
    factor = lax.rsqrt(
        jnp.mean(laid * laid, axis=-1, keepdims=True) + epsilon
    ) * feature_count ** (-0.5)
    lane = lax.broadcasted_iota(jnp.int32, laid.shape, 1)
    return jnp.where(filled | (lane > 0), laid * factor, EMPTY).astype(jnp.bfloat16)


def slots_of_steps(slot, capacity, steps):
    cores = lax.axis_size("sub")
    by_distance = slot ^ (chip_index() * capacity)
    distance = by_distance // capacity
    rank = by_distance - distance * capacity
    step = jnp.full_like(slot, -1)
    for place, p in enumerate(steps):
        step = jnp.where(distance == p * cores + lax.axis_index("sub"), place, step)
    return jnp.where(step < 0, -1, step * capacity + rank)


def route_first_kernel(clusters, capacity, step, rows_ref, ids_ref, piece_ref, slot_ref):
    slot = slots_of(ids_ref[...], clusters, capacity)
    slot_ref[...] = slot
    piece_ref[...] = lay(rows_ref, slots_of_steps(slot, capacity, [step]), capacity)


def route_rest_kernel(clusters, capacity, halves, steps, *refs):
    own_rows, other_rows, own_slot, other_ids, *piece_refs = refs
    half_refs, whole_refs = piece_refs[: len(halves)], piece_refs[len(halves) :]
    slot = slots_of_steps(own_slot[...], capacity, steps)
    laid = lay(own_rows, slot, len(steps) * capacity)
    for k, piece in enumerate(whole_refs):
        piece[:capacity] = laid[k * capacity : (k + 1) * capacity]
    slot = slots_of(other_ids[...], clusters, capacity)
    slot = slots_of_steps(slot, capacity, [*halves, *steps])
    laid = lay(other_rows, slot, (len(halves) + len(steps)) * capacity)
    for k, piece in enumerate(half_refs):
        piece[...] = laid[k * capacity : (k + 1) * capacity]
    for k, piece in enumerate(whole_refs, len(halves)):
        piece[capacity:] = laid[k * capacity : (k + 1) * capacity]


def route_kernel(clusters, capacity, rows_ref, ids_ref, piece_ref, slot_ref):
    slot = slots_of(ids_ref[...], clusters, capacity)
    slot_ref[...] = slot
    piece_ref[...] = lay(rows_ref, slot, piece_ref.shape[0])


def call_kernel(name, kernel, out_shape, *args, limit=32 * 2**20, flops=0):
    cost = pl.CostEstimate(flops=flops, bytes_accessed=0, transcendentals=0) if flops else None
    return pl.pallas_call(
        kernel,
        out_shape=out_shape,
        in_specs=[VMEM] * len(args),
        out_specs=jax.tree.map(lambda _: VMEM, out_shape),
        compiler_params=pltpu.CompilerParams(vmem_limit_bytes=limit),
        cost_estimate=cost,
        name=name,
    )(*args)


def pass_kernel(*refs):
    half = len(refs) // 2
    for in_ref, out_ref in zip(refs[:half], refs[half:]):
        out_ref[...] = in_ref[...]


def regroup_kernel(pieces, *refs):
    rows = jnp.concatenate([ref[...] for ref in refs[:pieces]], axis=0)
    first = 0
    for part in refs[pieces:]:
        part[...] = rows[first : first + part.shape[0]]
        first += part.shape[0]


def blocks(rows, starts, size):
    return jnp.concatenate([rows[start : start + size] for start in starts], axis=0)


def count_against(rows, own, starts, size):
    column = lax.broadcasted_iota(jnp.int32, (1, own.shape[0]), 1)
    itself = jnp.full_like(column, -1)
    for k, start in enumerate(starts):
        itself = jnp.where(column // size == k, column + (start - k * size), itself)
    slope = -math.log2(math.e) / sharpness
    total = jnp.zeros((1, own.shape[0]), jnp.float32)
    for first in range(0, rows.shape[0], TILE):
        other = rows[first : first + TILE]
        scores = lax.dot_general(
            other, own, (((1,), (1,)), ((), ())), preferred_element_type=jnp.float32
        )
        weights = 1.0 / (1.0 + jnp.exp2(scores * slope - threshold * slope))
        keep = other[:, :1].astype(jnp.float32) < 0.5 * EMPTY
        if starts:
            keep = keep & (lax.broadcasted_iota(jnp.int32, scores.shape, 0) + first != itself)
        total = total + jnp.sum(jnp.where(keep, weights, 0.0), axis=0, keepdims=True)
    return total


def count_kernel(starts, size, *refs):
    *piece_refs, count_ref = refs
    rows = jnp.concatenate([piece[...] for piece in piece_refs], axis=0)
    count_ref[...] = count_against(rows, blocks(rows, starts, size), starts, size)


def soft_counts(pieces, starts, size):
    out_shape = jax.ShapeDtypeStruct((1, len(starts) * size), jnp.float32)
    return call_kernel("count", functools.partial(count_kernel, starts, size), out_shape, *pieces)


def cross_kernel(pieces, *refs):
    *piece_refs, before_ref, count_ref = refs
    own = jnp.concatenate([piece[...] for piece in piece_refs[:pieces]], axis=0)
    other = jnp.concatenate([piece[...] for piece in piece_refs[pieces:]], axis=0)
    count_ref[...] = before_ref[...] + count_against(other, own, [], own.shape[0])


def late_kernel(*refs):
    *piece_refs, late_ref, early_ref, own_ref = refs
    early = jnp.concatenate([piece[...] for piece in piece_refs], axis=0)
    late = late_ref[...]
    size = late.shape[0]
    early_ref[...] = count_against(late, early, [], size)
    own_ref[...] = count_against(early, late, [], size) + count_against(late, late, [0], size)


def finish_kernel(places, late_ref, other_ref, counts_ref, early_ref, own_ref, out_ref):
    size = out_ref.shape[2]
    late = late_ref[...]
    own = own_ref[...] + count_against(other_ref[...], late, [], size)
    early = early_ref[...]
    blocks_early = early.shape[1] // size
    out_ref[...] = jnp.zeros_like(out_ref)
    for k, place in enumerate(places()):
        if k < blocks_early:
            block = early[:, k * size : (k + 1) * size]
            if k * size < counts_ref.shape[1]:
                block = block + counts_ref[:, k * size : (k + 1) * size]
        else:
            block = own[:, (k - blocks_early) * size : (k - blocks_early + 1) * size]
        out_ref[pl.ds(place, 1), 0, :] = block


def select_kernel(clusters, capacity, backwards, counts_ref, slot_ref, out_ref):
    counts = counts_ref[:, 0, :]
    slot = slot_ref[...]
    doc_count = slot.shape[1]
    block = slot // capacity
    rank = slot - block * capacity
    hot = (lax.broadcasted_iota(jnp.int32, (capacity, doc_count), 0) == rank).astype(jnp.float32)
    by_block = jnp.dot(
        counts, hot, precision=lax.Precision.HIGHEST, preferred_element_type=jnp.float32
    )
    parts = counts.shape[0] // clusters
    row = lax.broadcasted_iota(jnp.int32, by_block.shape, 0)
    if backwards:
        row = counts.shape[0] - 1 - row
    chosen = row // parts == block
    out_ref[...] = jnp.sum(jnp.where(chosen, by_block, 0.0), axis=0, keepdims=True)


def select(counts, slot, clusters, capacity, backwards=False):
    out_shape = jax.ShapeDtypeStruct(slot.shape, jnp.float32)
    kernel = functools.partial(select_kernel, clusters, capacity, backwards)
    return call_kernel("select", kernel, out_shape, counts, slot, limit=8 * 2**20)[0]


def swap_cores(x):
    cores = lax.axis_size("sub")
    return lax.ppermute(x, "sub", [(i, i ^ 1) for i in range(cores)])


def body_by_chip(embeddings, cluster_id):
    doc_count, feature_count = embeddings.shape
    clusters = CL_OWN * lax.axis_size("owner")
    capacity = 2 * doc_count // clusters
    cores = lax.axis_size("sub")
    steps = clusters // cores

    def across(x, p):
        pairs = [
            (chip * cores + core, (chip ^ (p * cores + core)) * cores + core)
            for chip in range(clusters)
            for core in range(cores)
        ]
        return lax.ppermute(x, ("owner", "helper", "sub"), pairs)

    ids = cluster_id.reshape(1, doc_count)
    other_rows, other_ids = swap_cores(embeddings), swap_cores(ids)
    first, last = steps - 1, steps // 2
    middle = [p for p in range(steps) if p not in (first, last)]
    half = jax.ShapeDtypeStruct((capacity, feature_count), jnp.bfloat16)
    whole = jax.ShapeDtypeStruct((cores * capacity, feature_count), jnp.bfloat16)

    first_own, slot = call_kernel(
        "route_first",
        functools.partial(route_first_kernel, clusters, capacity, first),
        [half, jax.ShapeDtypeStruct((1, doc_count), jnp.int32)],
        embeddings,
        ids,
    )
    first_own = across(first_own, first)

    def route_rest(name, halves, steps, slot, flops=0):
        return call_kernel(
            name,
            functools.partial(route_rest_kernel, clusters, capacity, halves, steps),
            [half] * len(halves) + [whole] * len(steps),
            embeddings,
            other_rows,
            slot,
            other_ids,
            flops=flops,
        )

    near = route_rest("route_near", [], middle, slot)
    later_slot, _ = lax.optimization_barrier((slot, near[0]))
    near = [across(piece, p) for piece, p in zip(near, middle)]
    first_other, last_piece = route_rest("route_far", [first], [last], later_slot, 10**10)
    first_other, last_piece = across(first_other, first), across(last_piece, last)

    (first_own,) = call_kernel("pass", pass_kernel, [half], first_own)
    early = [first_own, first_other, *near]
    half_way = cores * capacity * (steps - 1)
    part = jax.ShapeDtypeStruct((half_way // 4, feature_count), jnp.bfloat16)
    parts = call_kernel(
        "regroup", functools.partial(regroup_kernel, len(early)), [part] * 4, *early, flops=10**10
    )
    swapped = [swap_cores(x) for x in parts]

    counts = soft_counts(early, [0], half_way)
    counts = call_kernel(
        "cross",
        functools.partial(cross_kernel, len(early)),
        jax.ShapeDtypeStruct((1, half_way), jnp.float32),
        *early,
        *swapped,
        counts,
    )
    early += swapped

    late_piece, _ = lax.optimization_barrier((last_piece, counts))
    late_other = swap_cores(late_piece)
    sums = [
        jax.ShapeDtypeStruct((1, 2 * half_way), jnp.float32),
        jax.ShapeDtypeStruct((1, cores * capacity), jnp.float32),
    ]
    early_sums, own_sums = call_kernel("late", late_kernel, sums, *early, last_piece)

    def places():
        chip, core = chip_index(), lax.axis_index("sub")
        devices = []
        for here in (core, 1 - core):
            for p in (first, *middle):
                there = (chip ^ (p * cores + here)) * cores
                devices += [there + here, there + 1 - here]
        there = (chip ^ (last * cores + core)) * cores
        devices += [there + core, there + 1 - core]
        return [clusters * cores - 1 - device for device in devices]

    counts = call_kernel(
        "finish",
        functools.partial(finish_kernel, places),
        jax.ShapeDtypeStruct((clusters * cores, 1, capacity), jnp.float32),
        last_piece,
        late_other,
        counts,
        early_sums,
        own_sums,
    )
    back = lax.all_to_all(
        counts,
        ("owner", "helper", "sub"),
        split_axis=0,
        concat_axis=0,
        axis_index_groups=[list(reversed(range(clusters * cores)))],
        tiled=True,
    )
    return select(back, slot, clusters, capacity, backwards=True)


def body_by_owner(embeddings, cluster_id):
    doc_count, feature_count = embeddings.shape
    owners, helpers = lax.axis_size("owner"), lax.axis_size("helper")
    clusters = CL_OWN * owners
    capacity = 2 * doc_count // clusters
    mine = lax.axis_index("helper") % CL_OWN

    def partner(x):
        return lax.ppermute(x, "helper", [(i, i ^ 1) for i in range(helpers)])

    outgoing, slot = call_kernel(
        "route",
        functools.partial(route_kernel, clusters, capacity),
        [
            jax.ShapeDtypeStruct((clusters * capacity, feature_count), jnp.bfloat16),
            jax.ShapeDtypeStruct((1, doc_count), jnp.int32),
        ],
        embeddings,
        cluster_id.reshape(1, doc_count),
    )
    outgoing = outgoing.reshape(owners, CL_OWN, capacity, feature_count)
    arrived = lax.all_to_all(outgoing, "owner", split_axis=0, concat_axis=0, tiled=True)
    kept = lax.dynamic_index_in_dim(arrived, mine, 1, keepdims=False)
    given = partner(lax.dynamic_index_in_dim(arrived, 1 - mine, 1, keepdims=False))
    own = jnp.stack([kept, given]).reshape(CL_OWN * owners * capacity, feature_count)
    others = [swap_cores(own)]
    for step in range(CL_OWN, helpers, CL_OWN):
        turn = [(i, (i + step) % helpers) for i in range(helpers)]
        others += [lax.ppermute(x, "helper", turn) for x in (own, others[0])]
    counts = soft_counts([own, *others], [0], own.shape[0])
    counts = counts.reshape(CL_OWN, owners, capacity)
    kept, given = counts[0], partner(counts[1])
    counts = jnp.where(mine == 0, jnp.stack([kept, given], 1), jnp.stack([given, kept], 1))
    back = lax.all_to_all(counts, "owner", split_axis=0, concat_axis=0, tiled=True)
    return select(back.reshape(clusters, 1, capacity), slot, clusters, capacity)


def solution(mesh):
    in_specs = (
        P(("groups", "owner", "helper", "sub"), None),
        P(("groups", "owner", "helper", "sub")),
    )
    out_specs = P(("groups", "owner", "helper", "sub"))
    body = body_by_chip if mesh.shape["helper"] == CL_OWN else body_by_owner
    return jax.shard_map(body, mesh=mesh, in_specs=in_specs, out_specs=out_specs, check_vma=False)
```

```python
import functools
import math

import jax
import jax.numpy as jnp
from jax import lax
from jax.experimental import pallas as pl
from jax.experimental.pallas import tpu as pltpu
from jax.sharding import PartitionSpec as P

CL_OWN = 2

epsilon = 1e-06
threshold = 0.8
sharpness = 0.05

EMPTY = 4.0
TILE = 1024
VMEM = pl.BlockSpec(memory_space=pltpu.VMEM)


def chip_index():
    return lax.axis_index("owner") * CL_OWN + lax.axis_index("helper")


def place_of(device):
    last = CL_OWN * 2 - 1
    owner, rest = device // (last + 1), device % (last + 1)
    places = (3, 1, 0, 2)
    if isinstance(device, int):
        return places[owner] * (last + 1) + last - rest
    place = jnp.full_like(owner, places[0])
    for k in range(1, len(places)):
        place = jnp.where(owner == k, places[k], place)
    return place * (last + 1) + last - rest


def slots_of(ids, clusters, capacity):
    doc_count = ids.shape[1]
    member = lax.broadcasted_iota(jnp.int32, (clusters, doc_count), 0) == ids
    earlier = lax.broadcasted_iota(jnp.int32, (doc_count, doc_count), 0) < (
        lax.broadcasted_iota(jnp.int32, (doc_count, doc_count), 1)
    )
    ahead = jnp.dot(
        member.astype(jnp.bfloat16), earlier.astype(jnp.bfloat16), preferred_element_type=jnp.float32
    )
    rank = jnp.sum(jnp.where(member, ahead, 0.0), axis=0, keepdims=True).astype(jnp.int32)
    return ids * capacity + rank


def lay(rows_ref, slot, slots):
    doc_count, feature_count = rows_ref.shape
    dispatch = lax.broadcasted_iota(jnp.int32, (slots, doc_count), 0) == slot
    filled = jnp.sum(dispatch.astype(jnp.float32), axis=1, keepdims=True) > 0
    laid = jnp.dot(
        dispatch.astype(jnp.bfloat16), rows_ref[...], preferred_element_type=jnp.float32
    )
    factor = lax.rsqrt(
        jnp.mean(laid * laid, axis=-1, keepdims=True) + epsilon
    ) * feature_count ** (-0.5)
    lane = lax.broadcasted_iota(jnp.int32, laid.shape, 1)
    return jnp.where(filled | (lane > 0), laid * factor, EMPTY).astype(jnp.bfloat16)


def slots_of_steps(slot, capacity, steps):
    cores = lax.axis_size("sub")
    by_distance = slot ^ (chip_index() * capacity)
    distance = by_distance // capacity
    rank = by_distance - distance * capacity
    step = jnp.full_like(slot, -1)
    for place, p in enumerate(steps):
        step = jnp.where(distance == p * cores + lax.axis_index("sub"), place, step)
    return jnp.where(step < 0, -1, step * capacity + rank)


def route_first_kernel(clusters, capacity, step, rows_ref, ids_ref, piece_ref, slot_ref):
    slot = slots_of(ids_ref[...], clusters, capacity)
    slot_ref[...] = slot
    piece_ref[...] = lay(rows_ref, slots_of_steps(slot, capacity, [step]), capacity)


def route_rest_kernel(clusters, capacity, halves, steps, *refs):
    own_rows, other_rows, own_slot, other_ids, *piece_refs = refs
    half_refs, whole_refs = piece_refs[: len(halves)], piece_refs[len(halves) :]
    slot = slots_of_steps(own_slot[...], capacity, steps)
    laid = lay(own_rows, slot, len(steps) * capacity)
    for k, piece in enumerate(whole_refs):
        piece[:capacity] = laid[k * capacity : (k + 1) * capacity]
    slot = slots_of(other_ids[...], clusters, capacity)
    slot = slots_of_steps(slot, capacity, [*halves, *steps])
    laid = lay(other_rows, slot, (len(halves) + len(steps)) * capacity)
    for k, piece in enumerate(half_refs):
        piece[...] = laid[k * capacity : (k + 1) * capacity]
    for k, piece in enumerate(whole_refs, len(halves)):
        piece[capacity:] = laid[k * capacity : (k + 1) * capacity]


def route_kernel(clusters, capacity, rows_ref, ids_ref, piece_ref, slot_ref):
    slot = slots_of(ids_ref[...], clusters, capacity)
    slot_ref[...] = slot
    piece_ref[...] = lay(rows_ref, slot, piece_ref.shape[0])


def call_kernel(name, kernel, out_shape, *args, limit=32 * 2**20, flops=0):
    cost = pl.CostEstimate(flops=flops, bytes_accessed=0, transcendentals=0) if flops else None
    return pl.pallas_call(
        kernel,
        out_shape=out_shape,
        in_specs=[VMEM] * len(args),
        out_specs=jax.tree.map(lambda _: VMEM, out_shape),
        compiler_params=pltpu.CompilerParams(vmem_limit_bytes=limit),
        cost_estimate=cost,
        name=name,
    )(*args)


def pass_kernel(*refs):
    half = len(refs) // 2
    for in_ref, out_ref in zip(refs[:half], refs[half:]):
        out_ref[...] = in_ref[...]


def regroup_kernel(pieces, *refs):
    rows = jnp.concatenate([ref[...] for ref in refs[:pieces]], axis=0)
    first = 0
    for part in refs[pieces:]:
        part[...] = rows[first : first + part.shape[0]]
        first += part.shape[0]


def blocks(rows, starts, size):
    return jnp.concatenate([rows[start : start + size] for start in starts], axis=0)


def count_against(rows, own, starts, size):
    column = lax.broadcasted_iota(jnp.int32, (1, own.shape[0]), 1)
    itself = jnp.full_like(column, -1)
    for k, start in enumerate(starts):
        itself = jnp.where(column // size == k, column + (start - k * size), itself)
    slope = -math.log2(math.e) / sharpness
    total = jnp.zeros((1, own.shape[0]), jnp.float32)
    for first in range(0, rows.shape[0], TILE):
        other = rows[first : first + TILE]
        scores = lax.dot_general(
            other, own, (((1,), (1,)), ((), ())), preferred_element_type=jnp.float32
        )
        weights = 1.0 / (1.0 + jnp.exp2(scores * slope - threshold * slope))
        keep = other[:, :1].astype(jnp.float32) < 0.5 * EMPTY
        if starts:
            keep = keep & (lax.broadcasted_iota(jnp.int32, scores.shape, 0) + first != itself)
        total = total + jnp.sum(jnp.where(keep, weights, 0.0), axis=0, keepdims=True)
    return total


def count_kernel(starts, size, *refs):
    *piece_refs, count_ref = refs
    rows = jnp.concatenate([piece[...] for piece in piece_refs], axis=0)
    count_ref[...] = count_against(rows, blocks(rows, starts, size), starts, size)


def soft_counts(pieces, starts, size):
    out_shape = jax.ShapeDtypeStruct((1, len(starts) * size), jnp.float32)
    return call_kernel("count", functools.partial(count_kernel, starts, size), out_shape, *pieces)


def cross_kernel(pieces, *refs):
    *piece_refs, before_ref, count_ref = refs
    own = jnp.concatenate([piece[...] for piece in piece_refs[:pieces]], axis=0)
    other = jnp.concatenate([piece[...] for piece in piece_refs[pieces:]], axis=0)
    count_ref[...] = before_ref[...] + count_against(other, own, [], own.shape[0])


def late_kernel(*refs):
    *piece_refs, late_ref, early_ref, own_ref = refs
    early = jnp.concatenate([piece[...] for piece in piece_refs], axis=0)
    late = late_ref[...]
    size = late.shape[0]
    early_ref[...] = count_against(late, early, [], size)
    own_ref[...] = count_against(early, late, [], size) + count_against(late, late, [0], size)


def finish_kernel(places, late_ref, other_ref, counts_ref, early_ref, own_ref, out_ref):
    size = out_ref.shape[2]
    late = late_ref[...]
    own = own_ref[...] + count_against(other_ref[...], late, [], size)
    early = early_ref[...]
    blocks_early = early.shape[1] // size
    out_ref[...] = jnp.zeros_like(out_ref)
    for k, place in enumerate(places()):
        if k < blocks_early:
            block = early[:, k * size : (k + 1) * size]
            if k * size < counts_ref.shape[1]:
                block = block + counts_ref[:, k * size : (k + 1) * size]
        else:
            block = own[:, (k - blocks_early) * size : (k - blocks_early + 1) * size]
        out_ref[pl.ds(place, 1), 0, :] = block


def select_kernel(clusters, capacity, backwards, counts_ref, slot_ref, out_ref):
    counts = counts_ref[:, 0, :]
    slot = slot_ref[...]
    doc_count = slot.shape[1]
    block = slot // capacity
    rank = slot - block * capacity
    hot = (lax.broadcasted_iota(jnp.int32, (capacity, doc_count), 0) == rank).astype(jnp.float32)
    by_block = jnp.dot(
        counts, hot, precision=lax.Precision.HIGHEST, preferred_element_type=jnp.float32
    )
    parts = counts.shape[0] // clusters
    row = lax.broadcasted_iota(jnp.int32, by_block.shape, 0)
    if backwards:
        chosen = row // parts == place_of(block * parts) // parts
    else:
        chosen = row // parts == block
    out_ref[...] = jnp.sum(jnp.where(chosen, by_block, 0.0), axis=0, keepdims=True)


def select(counts, slot, clusters, capacity, backwards=False):
    out_shape = jax.ShapeDtypeStruct(slot.shape, jnp.float32)
    kernel = functools.partial(select_kernel, clusters, capacity, backwards)
    return call_kernel("select", kernel, out_shape, counts, slot, limit=8 * 2**20)[0]


def swap_cores(x):
    cores = lax.axis_size("sub")
    return lax.ppermute(x, "sub", [(i, i ^ 1) for i in range(cores)])


def body_by_chip(embeddings, cluster_id):
    doc_count, feature_count = embeddings.shape
    clusters = CL_OWN * lax.axis_size("owner")
    capacity = 2 * doc_count // clusters
    cores = lax.axis_size("sub")
    steps = clusters // cores

    def across(x, p):
        pairs = [
            (chip * cores + core, (chip ^ (p * cores + core)) * cores + (core ^ (p == 0)))
            for chip in range(clusters)
            for core in range(cores)
        ]
        return lax.ppermute(x, ("owner", "helper", "sub"), pairs)

    ids = cluster_id.reshape(1, doc_count)
    other_rows, other_ids = swap_cores(embeddings), swap_cores(ids)
    first, last = steps // 2, steps - 1
    middle = [p for p in reversed(range(steps)) if p not in (first, last)]
    half = jax.ShapeDtypeStruct((capacity, feature_count), jnp.bfloat16)
    whole = jax.ShapeDtypeStruct((cores * capacity, feature_count), jnp.bfloat16)

    first_own, slot = call_kernel(
        "route_first",
        functools.partial(route_first_kernel, clusters, capacity, first),
        [half, jax.ShapeDtypeStruct((1, doc_count), jnp.int32)],
        embeddings,
        ids,
    )
    first_own = across(first_own, first)

    def route_rest(name, halves, steps, slot, flops=0):
        return call_kernel(
            name,
            functools.partial(route_rest_kernel, clusters, capacity, halves, steps),
            [half] * len(halves) + [whole] * len(steps),
            embeddings,
            other_rows,
            slot,
            other_ids,
            flops=flops,
        )

    near = route_rest("route_near", [], middle, slot)
    later_slot, _ = lax.optimization_barrier((slot, near[0]))
    near = [across(piece, p) for piece, p in zip(near, middle)]
    first_other, last_piece = route_rest("route_far", [first], [last], later_slot, 10**10)
    first_other, last_piece = across(first_other, first), across(last_piece, last)

    (first_own,) = call_kernel("pass", pass_kernel, [half], first_own)
    early = [first_own, first_other, *near]
    half_way = cores * capacity * (steps - 1)
    part = jax.ShapeDtypeStruct((half_way // 4, feature_count), jnp.bfloat16)
    parts = call_kernel(
        "regroup", functools.partial(regroup_kernel, len(early)), [part] * 4, *early, flops=10**10
    )
    swapped = [swap_cores(x) for x in parts]

    counts = soft_counts(early, [0], half_way)
    counts = call_kernel(
        "cross",
        functools.partial(cross_kernel, len(early)),
        jax.ShapeDtypeStruct((1, half_way), jnp.float32),
        *early,
        *swapped,
        counts,
    )
    early += swapped

    late_piece, _ = lax.optimization_barrier((last_piece, counts))
    late_other = swap_cores(late_piece)
    sums = [
        jax.ShapeDtypeStruct((1, 2 * half_way), jnp.float32),
        jax.ShapeDtypeStruct((1, cores * capacity), jnp.float32),
    ]
    early_sums, own_sums = call_kernel("late", late_kernel, sums, *early, last_piece)

    def places():
        chip, core = chip_index(), lax.axis_index("sub")
        devices = []
        for here in (core, 1 - core):
            for p in (first, *middle):
                source = 1 - here if p == 0 else here
                there = (chip ^ (p * cores + source)) * cores
                devices += [there + source, there + 1 - source]
        there = (chip ^ (last * cores + core)) * cores
        devices += [there + core, there + 1 - core]
        return [place_of(device) for device in devices]

    counts = call_kernel(
        "finish",
        functools.partial(finish_kernel, places),
        jax.ShapeDtypeStruct((clusters * cores, 1, capacity), jnp.float32),
        last_piece,
        late_other,
        counts,
        early_sums,
        own_sums,
    )
    back = lax.all_to_all(
        counts,
        ("owner", "helper", "sub"),
        split_axis=0,
        concat_axis=0,
        axis_index_groups=[sorted(range(clusters * cores), key=place_of)],
        tiled=True,
    )
    return select(back, slot, clusters, capacity, backwards=True)


def body_by_owner(embeddings, cluster_id):
    doc_count, feature_count = embeddings.shape
    owners, helpers = lax.axis_size("owner"), lax.axis_size("helper")
    clusters = CL_OWN * owners
    capacity = 2 * doc_count // clusters
    mine = lax.axis_index("helper") % CL_OWN

    def partner(x):
        return lax.ppermute(x, "helper", [(i, i ^ 1) for i in range(helpers)])

    outgoing, slot = call_kernel(
        "route",
        functools.partial(route_kernel, clusters, capacity),
        [
            jax.ShapeDtypeStruct((clusters * capacity, feature_count), jnp.bfloat16),
            jax.ShapeDtypeStruct((1, doc_count), jnp.int32),
        ],
        embeddings,
        cluster_id.reshape(1, doc_count),
    )
    outgoing = outgoing.reshape(owners, CL_OWN, capacity, feature_count)
    arrived = lax.all_to_all(outgoing, "owner", split_axis=0, concat_axis=0, tiled=True)
    kept = lax.dynamic_index_in_dim(arrived, mine, 1, keepdims=False)
    given = partner(lax.dynamic_index_in_dim(arrived, 1 - mine, 1, keepdims=False))
    own = jnp.stack([kept, given]).reshape(CL_OWN * owners * capacity, feature_count)
    others = [swap_cores(own)]
    for step in range(CL_OWN, helpers, CL_OWN):
        turn = [(i, (i + step) % helpers) for i in range(helpers)]
        others += [lax.ppermute(x, "helper", turn) for x in (own, others[0])]
    counts = soft_counts([own, *others], [0], own.shape[0])
    counts = counts.reshape(CL_OWN, owners, capacity)
    kept, given = counts[0], partner(counts[1])
    counts = jnp.where(mine == 0, jnp.stack([kept, given], 1), jnp.stack([given, kept], 1))
    back = lax.all_to_all(counts, "owner", split_axis=0, concat_axis=0, tiled=True)
    return select(back.reshape(clusters, 1, capacity), slot, clusters, capacity)


def solution(mesh):
    in_specs = (
        P(("groups", "owner", "helper", "sub"), None),
        P(("groups", "owner", "helper", "sub")),
    )
    out_specs = P(("groups", "owner", "helper", "sub"))
    body = body_by_chip if mesh.shape["helper"] == CL_OWN else body_by_owner
    return jax.shard_map(body, mesh=mesh, in_specs=in_specs, out_specs=out_specs, check_vma=False)
```

```python
import functools
import math

import jax
import jax.numpy as jnp
from jax import lax
from jax.experimental import pallas as pl
from jax.experimental.pallas import tpu as pltpu
from jax.sharding import PartitionSpec as P

CL_OWN = 2

epsilon = 1e-06
threshold = 0.8
sharpness = 0.05

EMPTY = 4.0
TILE = 1024
VMEM = pl.BlockSpec(memory_space=pltpu.VMEM)


def chip_index():
    return lax.axis_index("owner") * CL_OWN + lax.axis_index("helper")


def place_of(device):
    last = CL_OWN * 2 - 1
    owner, rest = device // (last + 1), device % (last + 1)
    places = (3, 1, 0, 2)
    if isinstance(device, int):
        return places[owner] * (last + 1) + last - rest
    place = jnp.full_like(owner, places[0])
    for k in range(1, len(places)):
        place = jnp.where(owner == k, places[k], place)
    return place * (last + 1) + last - rest


def slots_of(ids, clusters, capacity):
    doc_count = ids.shape[1]
    member = lax.broadcasted_iota(jnp.int32, (clusters, doc_count), 0) == ids
    earlier = lax.broadcasted_iota(jnp.int32, (doc_count, doc_count), 0) < (
        lax.broadcasted_iota(jnp.int32, (doc_count, doc_count), 1)
    )
    ahead = jnp.dot(
        member.astype(jnp.bfloat16), earlier.astype(jnp.bfloat16), preferred_element_type=jnp.float32
    )
    rank = jnp.sum(jnp.where(member, ahead, 0.0), axis=0, keepdims=True).astype(jnp.int32)
    return ids * capacity + rank


def lay(rows_ref, slot, slots):
    doc_count, feature_count = rows_ref.shape
    dispatch = lax.broadcasted_iota(jnp.int32, (slots, doc_count), 0) == slot
    filled = jnp.sum(dispatch.astype(jnp.float32), axis=1, keepdims=True) > 0
    laid = jnp.dot(
        dispatch.astype(jnp.bfloat16), rows_ref[...], preferred_element_type=jnp.float32
    )
    factor = lax.rsqrt(
        jnp.mean(laid * laid, axis=-1, keepdims=True) + epsilon
    ) * feature_count ** (-0.5)
    lane = lax.broadcasted_iota(jnp.int32, laid.shape, 1)
    return jnp.where(filled | (lane > 0), laid * factor, EMPTY).astype(jnp.bfloat16)


def slots_of_steps(slot, capacity, steps):
    cores = lax.axis_size("sub")
    by_distance = slot ^ (chip_index() * capacity)
    distance = by_distance // capacity
    rank = by_distance - distance * capacity
    step = jnp.full_like(slot, -1)
    for place, p in enumerate(steps):
        step = jnp.where(distance == p * cores + lax.axis_index("sub"), place, step)
    return jnp.where(step < 0, -1, step * capacity + rank)


def route_first_kernel(clusters, capacity, step, rows_ref, ids_ref, piece_ref, slot_ref):
    slot = slots_of(ids_ref[...], clusters, capacity)
    slot_ref[...] = slot
    piece_ref[...] = lay(rows_ref, slots_of_steps(slot, capacity, [step]), capacity)


def route_rest_kernel(clusters, capacity, halves, steps, *refs):
    own_rows, other_rows, own_slot, other_ids, *piece_refs = refs
    half_refs, whole_refs = piece_refs[: len(halves)], piece_refs[len(halves) :]
    slot = slots_of_steps(own_slot[...], capacity, steps)
    laid = lay(own_rows, slot, len(steps) * capacity)
    for k, piece in enumerate(whole_refs):
        piece[:capacity] = laid[k * capacity : (k + 1) * capacity]
    slot = slots_of(other_ids[...], clusters, capacity)
    slot = slots_of_steps(slot, capacity, [*halves, *steps])
    laid = lay(other_rows, slot, (len(halves) + len(steps)) * capacity)
    for k, piece in enumerate(half_refs):
        piece[...] = laid[k * capacity : (k + 1) * capacity]
    for k, piece in enumerate(whole_refs, len(halves)):
        piece[capacity:] = laid[k * capacity : (k + 1) * capacity]


def route_kernel(clusters, capacity, rows_ref, ids_ref, piece_ref, slot_ref):
    slot = slots_of(ids_ref[...], clusters, capacity)
    slot_ref[...] = slot
    piece_ref[...] = lay(rows_ref, slot, piece_ref.shape[0])


def call_kernel(name, kernel, out_shape, *args, limit=32 * 2**20, flops=0):
    cost = pl.CostEstimate(flops=flops, bytes_accessed=0, transcendentals=0) if flops else None
    return pl.pallas_call(
        kernel,
        out_shape=out_shape,
        in_specs=[VMEM] * len(args),
        out_specs=jax.tree.map(lambda _: VMEM, out_shape),
        compiler_params=pltpu.CompilerParams(vmem_limit_bytes=limit),
        cost_estimate=cost,
        name=name,
    )(*args)


def pass_kernel(*refs):
    half = len(refs) // 2
    for in_ref, out_ref in zip(refs[:half], refs[half:]):
        out_ref[...] = in_ref[...]


def regroup_kernel(pieces, *refs):
    rows = jnp.concatenate([ref[...] for ref in refs[:pieces]], axis=0)
    first = 0
    for part in refs[pieces:]:
        part[...] = rows[first : first + part.shape[0]]
        first += part.shape[0]


def blocks(rows, starts, size):
    return jnp.concatenate([rows[start : start + size] for start in starts], axis=0)


def count_against(rows, own, starts, size):
    column = lax.broadcasted_iota(jnp.int32, (1, own.shape[0]), 1)
    itself = jnp.full_like(column, -1)
    for k, start in enumerate(starts):
        itself = jnp.where(column // size == k, column + (start - k * size), itself)
    slope = -math.log2(math.e) / sharpness
    total = jnp.zeros((1, own.shape[0]), jnp.float32)
    for first in range(0, rows.shape[0], TILE):
        other = rows[first : first + TILE]
        scores = lax.dot_general(
            other, own, (((1,), (1,)), ((), ())), preferred_element_type=jnp.float32
        )
        weights = 1.0 / (1.0 + jnp.exp2(scores * slope - threshold * slope))
        keep = other[:, :1].astype(jnp.float32) < 0.5 * EMPTY
        if starts:
            keep = keep & (lax.broadcasted_iota(jnp.int32, scores.shape, 0) + first != itself)
        total = total + jnp.sum(jnp.where(keep, weights, 0.0), axis=0, keepdims=True)
    return total


def count_kernel(starts, size, *refs):
    *piece_refs, count_ref = refs
    rows = jnp.concatenate([piece[...] for piece in piece_refs], axis=0)
    count_ref[...] = count_against(rows, blocks(rows, starts, size), starts, size)


def soft_counts(pieces, starts, size):
    out_shape = jax.ShapeDtypeStruct((1, len(starts) * size), jnp.float32)
    return call_kernel("count", functools.partial(count_kernel, starts, size), out_shape, *pieces)


def cross_kernel(pieces, *refs):
    *piece_refs, before_ref, count_ref = refs
    own = jnp.concatenate([piece[...] for piece in piece_refs[:pieces]], axis=0)
    other = jnp.concatenate([piece[...] for piece in piece_refs[pieces:]], axis=0)
    count_ref[...] = before_ref[...] + count_against(other, own, [], own.shape[0])


def late_kernel(*refs):
    *piece_refs, late_ref, early_ref, own_ref = refs
    early = jnp.concatenate([piece[...] for piece in piece_refs], axis=0)
    late = late_ref[...]
    size = late.shape[0]
    early_ref[...] = count_against(late, early, [], size)
    own_ref[...] = count_against(early, late, [], size) + count_against(late, late, [0], size)


def finish_kernel(places, late_ref, other_ref, counts_ref, early_ref, own_ref, out_ref):
    size = out_ref.shape[2]
    late = late_ref[...]
    own = own_ref[...] + count_against(other_ref[...], late, [], size)
    early = early_ref[...]
    blocks_early = early.shape[1] // size
    out_ref[...] = jnp.zeros_like(out_ref)
    for k, place in enumerate(places()):
        if k < blocks_early:
            block = early[:, k * size : (k + 1) * size]
            if k * size < counts_ref.shape[1]:
                block = block + counts_ref[:, k * size : (k + 1) * size]
        else:
            block = own[:, (k - blocks_early) * size : (k - blocks_early + 1) * size]
        out_ref[pl.ds(place, 1), 0, :] = block


def select_kernel(clusters, capacity, backwards, counts_ref, slot_ref, out_ref):
    counts = counts_ref[:, 0, :]
    slot = slot_ref[...]
    doc_count = slot.shape[1]
    block = slot // capacity
    rank = slot - block * capacity
    hot = (lax.broadcasted_iota(jnp.int32, (capacity, doc_count), 0) == rank).astype(jnp.float32)
    parts = counts.shape[0] // clusters
    counts = jnp.sum(counts.reshape(clusters, parts, capacity), axis=1)
    by_block = jnp.dot(
        counts, hot, precision=lax.Precision.HIGHEST, preferred_element_type=jnp.float32
    )
    if backwards:
        block = place_of(block * parts) // parts
    chosen = lax.broadcasted_iota(jnp.int32, by_block.shape, 0) == block
    out_ref[...] = jnp.sum(jnp.where(chosen, by_block, 0.0), axis=0, keepdims=True)


def select(counts, slot, clusters, capacity, backwards=False):
    out_shape = jax.ShapeDtypeStruct(slot.shape, jnp.float32)
    kernel = functools.partial(select_kernel, clusters, capacity, backwards)
    return call_kernel("select", kernel, out_shape, counts, slot, limit=8 * 2**20)[0]


def swap_cores(x):
    cores = lax.axis_size("sub")
    return lax.ppermute(x, "sub", [(i, i ^ 1) for i in range(cores)])


def body_by_chip(embeddings, cluster_id):
    doc_count, feature_count = embeddings.shape
    clusters = CL_OWN * lax.axis_size("owner")
    capacity = 2 * doc_count // clusters
    cores = lax.axis_size("sub")
    steps = clusters // cores

    def across(x, p):
        pairs = [
            (chip * cores + core, (chip ^ (p * cores + core)) * cores + core)
            for chip in range(clusters)
            for core in range(cores)
        ]
        return lax.ppermute(x, ("owner", "helper", "sub"), pairs)

    ids = cluster_id.reshape(1, doc_count)
    other_rows, other_ids = swap_cores(embeddings), swap_cores(ids)
    first, last = steps // 2, steps - 1
    middle = [p for p in range(steps) if p not in (first, last)]
    half = jax.ShapeDtypeStruct((capacity, feature_count), jnp.bfloat16)
    whole = jax.ShapeDtypeStruct((cores * capacity, feature_count), jnp.bfloat16)

    first_own, slot = call_kernel(
        "route_first",
        functools.partial(route_first_kernel, clusters, capacity, first),
        [half, jax.ShapeDtypeStruct((1, doc_count), jnp.int32)],
        embeddings,
        ids,
    )
    first_own = across(first_own, first)

    def route_rest(name, halves, steps, slot, flops=0):
        return call_kernel(
            name,
            functools.partial(route_rest_kernel, clusters, capacity, halves, steps),
            [half] * len(halves) + [whole] * len(steps),
            embeddings,
            other_rows,
            slot,
            other_ids,
            flops=flops,
        )

    near = route_rest("route_near", [], middle, slot)
    later_slot, _ = lax.optimization_barrier((slot, near[0]))
    near = [across(piece, p) for piece, p in zip(near, middle)]
    first_other, last_piece = route_rest("route_far", [first], [last], later_slot, 10**10)
    first_other, last_piece = across(first_other, first), across(last_piece, last)

    (first_own,) = call_kernel("pass", pass_kernel, [half], first_own)
    early = [first_own, first_other, *near]
    half_way = cores * capacity * (steps - 1)
    part = jax.ShapeDtypeStruct((half_way // 4, feature_count), jnp.bfloat16)
    parts = call_kernel(
        "regroup", functools.partial(regroup_kernel, len(early)), [part] * 4, *early, flops=10**10
    )
    swapped = [swap_cores(x) for x in parts]

    counts = soft_counts(early, [0], half_way)
    counts = call_kernel(
        "cross",
        functools.partial(cross_kernel, len(early)),
        jax.ShapeDtypeStruct((1, half_way), jnp.float32),
        *early,
        *swapped,
        counts,
    )
    early += swapped

    late_piece, _ = lax.optimization_barrier((last_piece, counts))
    late_other = swap_cores(late_piece)
    sums = [
        jax.ShapeDtypeStruct((1, 2 * half_way), jnp.float32),
        jax.ShapeDtypeStruct((1, cores * capacity), jnp.float32),
    ]
    early_sums, own_sums = call_kernel("late", late_kernel, sums, *early, last_piece)

    def places():
        chip, core = chip_index(), lax.axis_index("sub")
        devices = []
        for here in (core, 1 - core):
            for p in (first, *middle):
                there = (chip ^ (p * cores + here)) * cores
                devices += [there + here, there + 1 - here]
        there = (chip ^ (last * cores + core)) * cores
        devices += [there + core, there + 1 - core]
        return [place_of(device) for device in devices]

    counts = call_kernel(
        "finish",
        functools.partial(finish_kernel, places),
        jax.ShapeDtypeStruct((clusters * cores, 1, capacity), jnp.float32),
        last_piece,
        late_other,
        counts,
        early_sums,
        own_sums,
    )
    back = lax.all_to_all(
        counts,
        ("owner", "helper", "sub"),
        split_axis=0,
        concat_axis=0,
        axis_index_groups=[sorted(range(clusters * cores), key=place_of)],
        tiled=True,
    )
    return select(back, slot, clusters, capacity, backwards=True)


def body_by_owner(embeddings, cluster_id):
    doc_count, feature_count = embeddings.shape
    owners, helpers = lax.axis_size("owner"), lax.axis_size("helper")
    clusters = CL_OWN * owners
    capacity = 2 * doc_count // clusters
    mine = lax.axis_index("helper") % CL_OWN

    def partner(x):
        return lax.ppermute(x, "helper", [(i, i ^ 1) for i in range(helpers)])

    outgoing, slot = call_kernel(
        "route",
        functools.partial(route_kernel, clusters, capacity),
        [
            jax.ShapeDtypeStruct((clusters * capacity, feature_count), jnp.bfloat16),
            jax.ShapeDtypeStruct((1, doc_count), jnp.int32),
        ],
        embeddings,
        cluster_id.reshape(1, doc_count),
    )
    outgoing = outgoing.reshape(owners, CL_OWN, capacity, feature_count)
    arrived = lax.all_to_all(outgoing, "owner", split_axis=0, concat_axis=0, tiled=True)
    kept = lax.dynamic_index_in_dim(arrived, mine, 1, keepdims=False)
    given = partner(lax.dynamic_index_in_dim(arrived, 1 - mine, 1, keepdims=False))
    own = jnp.stack([kept, given]).reshape(CL_OWN * owners * capacity, feature_count)
    others = [swap_cores(own)]
    for step in range(CL_OWN, helpers, CL_OWN):
        turn = [(i, (i + step) % helpers) for i in range(helpers)]
        others += [lax.ppermute(x, "helper", turn) for x in (own, others[0])]
    counts = soft_counts([own, *others], [0], own.shape[0])
    counts = counts.reshape(CL_OWN, owners, capacity)
    kept, given = counts[0], partner(counts[1])
    counts = jnp.where(mine == 0, jnp.stack([kept, given], 1), jnp.stack([given, kept], 1))
    back = lax.all_to_all(counts, "owner", split_axis=0, concat_axis=0, tiled=True)
    return select(back.reshape(clusters, 1, capacity), slot, clusters, capacity)


def solution(mesh):
    in_specs = (
        P(("groups", "owner", "helper", "sub"), None),
        P(("groups", "owner", "helper", "sub")),
    )
    out_specs = P(("groups", "owner", "helper", "sub"))
    body = body_by_chip if mesh.shape["helper"] == CL_OWN else body_by_owner
    return jax.shard_map(body, mesh=mesh, in_specs=in_specs, out_specs=out_specs, check_vma=False)
```

```python
import functools
import math

import jax
import jax.numpy as jnp
from jax import lax
from jax.experimental import pallas as pl
from jax.experimental.pallas import tpu as pltpu
from jax.sharding import PartitionSpec as P

CL_OWN = 2

epsilon = 1e-06
threshold = 0.8
sharpness = 0.05

EMPTY = 4.0
TILE = 1024
VMEM = pl.BlockSpec(memory_space=pltpu.VMEM)


def chip_index():
    return lax.axis_index("owner") * CL_OWN + lax.axis_index("helper")


def place_of(device):
    last = CL_OWN * 2 - 1
    owner, rest = device // (last + 1), device % (last + 1)
    places = (3, 2, 1, 0)
    if isinstance(device, int):
        return places[owner] * (last + 1) + last - rest
    place = jnp.full_like(owner, places[0])
    for k in range(1, len(places)):
        place = jnp.where(owner == k, places[k], place)
    return place * (last + 1) + last - rest


def slots_of(ids, clusters, capacity):
    doc_count = ids.shape[1]
    member = lax.broadcasted_iota(jnp.int32, (clusters, doc_count), 0) == ids
    earlier = lax.broadcasted_iota(jnp.int32, (doc_count, doc_count), 0) < (
        lax.broadcasted_iota(jnp.int32, (doc_count, doc_count), 1)
    )
    ahead = jnp.dot(
        member.astype(jnp.bfloat16), earlier.astype(jnp.bfloat16), preferred_element_type=jnp.float32
    )
    rank = jnp.sum(jnp.where(member, ahead, 0.0), axis=0, keepdims=True).astype(jnp.int32)
    return ids * capacity + rank


def lay(rows_ref, slot, slots):
    doc_count, feature_count = rows_ref.shape
    dispatch = lax.broadcasted_iota(jnp.int32, (slots, doc_count), 0) == slot
    filled = jnp.sum(dispatch.astype(jnp.float32), axis=1, keepdims=True) > 0
    laid = jnp.dot(
        dispatch.astype(jnp.bfloat16), rows_ref[...], preferred_element_type=jnp.float32
    )
    factor = lax.rsqrt(
        jnp.mean(laid * laid, axis=-1, keepdims=True) + epsilon
    ) * feature_count ** (-0.5)
    lane = lax.broadcasted_iota(jnp.int32, laid.shape, 1)
    return jnp.where(filled | (lane > 0), laid * factor, EMPTY).astype(jnp.bfloat16)


def slots_of_steps(slot, capacity, steps):
    cores = lax.axis_size("sub")
    by_distance = slot ^ (chip_index() * capacity)
    distance = by_distance // capacity
    rank = by_distance - distance * capacity
    step = jnp.full_like(slot, -1)
    for place, p in enumerate(steps):
        step = jnp.where(distance == p * cores + lax.axis_index("sub"), place, step)
    return jnp.where(step < 0, -1, step * capacity + rank)


def route_first_kernel(clusters, capacity, step, rows_ref, ids_ref, piece_ref, slot_ref):
    slot = slots_of(ids_ref[...], clusters, capacity)
    slot_ref[...] = slot
    piece_ref[...] = lay(rows_ref, slots_of_steps(slot, capacity, [step]), capacity)


def route_rest_kernel(clusters, capacity, halves, steps, *refs):
    own_rows, other_rows, own_slot, other_ids, *piece_refs = refs
    half_refs, whole_refs = piece_refs[: len(halves)], piece_refs[len(halves) :]
    slot = slots_of_steps(own_slot[...], capacity, steps)
    laid = lay(own_rows, slot, len(steps) * capacity)
    for k, piece in enumerate(whole_refs):
        piece[:capacity] = laid[k * capacity : (k + 1) * capacity]
    slot = slots_of(other_ids[...], clusters, capacity)
    slot = slots_of_steps(slot, capacity, [*halves, *steps])
    laid = lay(other_rows, slot, (len(halves) + len(steps)) * capacity)
    for k, piece in enumerate(half_refs):
        piece[...] = laid[k * capacity : (k + 1) * capacity]
    for k, piece in enumerate(whole_refs, len(halves)):
        piece[capacity:] = laid[k * capacity : (k + 1) * capacity]


def route_kernel(clusters, capacity, rows_ref, ids_ref, piece_ref, slot_ref):
    slot = slots_of(ids_ref[...], clusters, capacity)
    slot_ref[...] = slot
    piece_ref[...] = lay(rows_ref, slot, piece_ref.shape[0])


def call_kernel(name, kernel, out_shape, *args, limit=32 * 2**20, flops=0):
    cost = pl.CostEstimate(flops=flops, bytes_accessed=0, transcendentals=0) if flops else None
    return pl.pallas_call(
        kernel,
        out_shape=out_shape,
        in_specs=[VMEM] * len(args),
        out_specs=jax.tree.map(lambda _: VMEM, out_shape),
        compiler_params=pltpu.CompilerParams(vmem_limit_bytes=limit),
        cost_estimate=cost,
        name=name,
    )(*args)


def pass_kernel(*refs):
    half = len(refs) // 2
    for in_ref, out_ref in zip(refs[:half], refs[half:]):
        out_ref[...] = in_ref[...]


def regroup_kernel(pieces, *refs):
    rows = jnp.concatenate([ref[...] for ref in refs[:pieces]], axis=0)
    first = 0
    for part in refs[pieces:]:
        part[...] = rows[first : first + part.shape[0]]
        first += part.shape[0]


def blocks(rows, starts, size):
    return jnp.concatenate([rows[start : start + size] for start in starts], axis=0)


def count_against(rows, own, starts, size):
    column = lax.broadcasted_iota(jnp.int32, (1, own.shape[0]), 1)
    itself = jnp.full_like(column, -1)
    for k, start in enumerate(starts):
        itself = jnp.where(column // size == k, column + (start - k * size), itself)
    slope = -math.log2(math.e) / sharpness
    total = jnp.zeros((1, own.shape[0]), jnp.float32)
    for first in range(0, rows.shape[0], TILE):
        other = rows[first : first + TILE]
        scores = lax.dot_general(
            other, own, (((1,), (1,)), ((), ())), preferred_element_type=jnp.float32
        )
        weights = 1.0 / (1.0 + jnp.exp2(scores * slope - threshold * slope))
        keep = other[:, :1].astype(jnp.float32) < 0.5 * EMPTY
        if starts:
            keep = keep & (lax.broadcasted_iota(jnp.int32, scores.shape, 0) + first != itself)
        total = total + jnp.sum(jnp.where(keep, weights, 0.0), axis=0, keepdims=True)
    return total


def count_kernel(starts, size, *refs):
    *piece_refs, count_ref = refs
    rows = jnp.concatenate([piece[...] for piece in piece_refs], axis=0)
    count_ref[...] = count_against(rows, blocks(rows, starts, size), starts, size)


def soft_counts(pieces, starts, size):
    out_shape = jax.ShapeDtypeStruct((1, len(starts) * size), jnp.float32)
    return call_kernel("count", functools.partial(count_kernel, starts, size), out_shape, *pieces)


def cross_kernel(pieces, *refs):
    *piece_refs, before_ref, count_ref = refs
    own = jnp.concatenate([piece[...] for piece in piece_refs[:pieces]], axis=0)
    other = jnp.concatenate([piece[...] for piece in piece_refs[pieces:]], axis=0)
    count_ref[...] = before_ref[...] + count_against(other, own, [], own.shape[0])


def late_kernel(*refs):
    *piece_refs, late_ref, early_ref, own_ref = refs
    early = jnp.concatenate([piece[...] for piece in piece_refs], axis=0)
    late = late_ref[...]
    size = late.shape[0]
    early_ref[...] = count_against(late, early, [], size)
    own_ref[...] = count_against(early, late, [], size) + count_against(late, late, [0], size)


def finish_kernel(places, late_ref, other_ref, counts_ref, early_ref, own_ref, out_ref):
    size = out_ref.shape[2]
    late = late_ref[...]
    own = own_ref[...] + count_against(other_ref[...], late, [], size)
    early = early_ref[...]
    blocks_early = early.shape[1] // size
    out_ref[...] = jnp.zeros_like(out_ref)
    for k, place in enumerate(places()):
        if k < blocks_early:
            block = early[:, k * size : (k + 1) * size]
            if k * size < counts_ref.shape[1]:
                block = block + counts_ref[:, k * size : (k + 1) * size]
        else:
            block = own[:, (k - blocks_early) * size : (k - blocks_early + 1) * size]
        out_ref[pl.ds(place, 1), 0, :] = block


def select_kernel(clusters, capacity, backwards, counts_ref, slot_ref, out_ref):
    counts = counts_ref[:, 0, :]
    slot = slot_ref[...]
    doc_count = slot.shape[1]
    block = slot // capacity
    rank = slot - block * capacity
    hot = (lax.broadcasted_iota(jnp.int32, (capacity, doc_count), 0) == rank).astype(jnp.float32)
    by_block = jnp.dot(
        counts, hot, precision=lax.Precision.HIGHEST, preferred_element_type=jnp.float32
    )
    parts = counts.shape[0] // clusters
    row = lax.broadcasted_iota(jnp.int32, by_block.shape, 0)
    if backwards:
        chosen = row // parts == place_of(block * parts) // parts
    else:
        chosen = row // parts == block
    out_ref[...] = jnp.sum(jnp.where(chosen, by_block, 0.0), axis=0, keepdims=True)


def select(counts, slot, clusters, capacity, backwards=False):
    out_shape = jax.ShapeDtypeStruct(slot.shape, jnp.float32)
    kernel = functools.partial(select_kernel, clusters, capacity, backwards)
    return call_kernel("select", kernel, out_shape, counts, slot, limit=8 * 2**20)[0]


def swap_cores(x):
    cores = lax.axis_size("sub")
    return lax.ppermute(x, "sub", [(i, i ^ 1) for i in range(cores)])


def body_by_chip(embeddings, cluster_id):
    doc_count, feature_count = embeddings.shape
    clusters = CL_OWN * lax.axis_size("owner")
    capacity = 2 * doc_count // clusters
    cores = lax.axis_size("sub")
    steps = clusters // cores

    def across(x, p):
        pairs = [
            (chip * cores + core, (chip ^ (p * cores + core)) * cores + (core ^ (p == 0)))
            for chip in range(clusters)
            for core in range(cores)
        ]
        return lax.ppermute(x, ("owner", "helper", "sub"), pairs)

    ids = cluster_id.reshape(1, doc_count)
    other_rows, other_ids = swap_cores(embeddings), swap_cores(ids)
    first, last = steps // 2, steps - 1
    middle = [p for p in range(steps) if p not in (first, last)]
    half = jax.ShapeDtypeStruct((capacity, feature_count), jnp.bfloat16)
    whole = jax.ShapeDtypeStruct((cores * capacity, feature_count), jnp.bfloat16)

    first_own, slot = call_kernel(
        "route_first",
        functools.partial(route_first_kernel, clusters, capacity, first),
        [half, jax.ShapeDtypeStruct((1, doc_count), jnp.int32)],
        embeddings,
        ids,
    )
    first_own = across(first_own, first)

    def route_rest(name, halves, steps, slot, flops=0):
        return call_kernel(
            name,
            functools.partial(route_rest_kernel, clusters, capacity, halves, steps),
            [half] * len(halves) + [whole] * len(steps),
            embeddings,
            other_rows,
            slot,
            other_ids,
            flops=flops,
        )

    near = route_rest("route_near", [], middle, slot)
    later_slot, _ = lax.optimization_barrier((slot, near[0]))
    near = [across(piece, p) for piece, p in zip(near, middle)]
    first_other, last_piece = route_rest("route_far", [first], [last], later_slot, 10**10)
    first_other, last_piece = across(first_other, first), across(last_piece, last)

    (first_own,) = call_kernel("pass", pass_kernel, [half], first_own)
    early = [first_own, first_other, *near]
    half_way = cores * capacity * (steps - 1)
    part = jax.ShapeDtypeStruct((half_way // 4, feature_count), jnp.bfloat16)
    parts = call_kernel(
        "regroup", functools.partial(regroup_kernel, len(early)), [part] * 4, *early, flops=10**10
    )
    swapped = [swap_cores(x) for x in parts]

    counts = soft_counts(early, [0], half_way)
    counts = call_kernel(
        "cross",
        functools.partial(cross_kernel, len(early)),
        jax.ShapeDtypeStruct((1, half_way), jnp.float32),
        *early,
        *swapped,
        counts,
    )
    early += swapped

    late_piece, _ = lax.optimization_barrier((last_piece, counts))
    late_other = swap_cores(late_piece)
    sums = [
        jax.ShapeDtypeStruct((1, 2 * half_way), jnp.float32),
        jax.ShapeDtypeStruct((1, cores * capacity), jnp.float32),
    ]
    early_sums, own_sums = call_kernel("late", late_kernel, sums, *early, last_piece)

    def places():
        chip, core = chip_index(), lax.axis_index("sub")
        devices = []
        for here in (core, 1 - core):
            for p in (first, *middle):
                source = 1 - here if p == 0 else here
                there = (chip ^ (p * cores + source)) * cores
                devices += [there + source, there + 1 - source]
        there = (chip ^ (last * cores + core)) * cores
        devices += [there + core, there + 1 - core]
        return [place_of(device) for device in devices]

    counts = call_kernel(
        "finish",
        functools.partial(finish_kernel, places),
        jax.ShapeDtypeStruct((clusters * cores, 1, capacity), jnp.float32),
        last_piece,
        late_other,
        counts,
        early_sums,
        own_sums,
    )
    back = lax.all_to_all(
        counts,
        ("owner", "helper", "sub"),
        split_axis=0,
        concat_axis=0,
        axis_index_groups=[sorted(range(clusters * cores), key=place_of)],
        tiled=True,
    )
    return select(back, slot, clusters, capacity, backwards=True)


def body_by_owner(embeddings, cluster_id):
    doc_count, feature_count = embeddings.shape
    owners, helpers = lax.axis_size("owner"), lax.axis_size("helper")
    clusters = CL_OWN * owners
    capacity = 2 * doc_count // clusters
    mine = lax.axis_index("helper") % CL_OWN

    def partner(x):
        return lax.ppermute(x, "helper", [(i, i ^ 1) for i in range(helpers)])

    outgoing, slot = call_kernel(
        "route",
        functools.partial(route_kernel, clusters, capacity),
        [
            jax.ShapeDtypeStruct((clusters * capacity, feature_count), jnp.bfloat16),
            jax.ShapeDtypeStruct((1, doc_count), jnp.int32),
        ],
        embeddings,
        cluster_id.reshape(1, doc_count),
    )
    outgoing = outgoing.reshape(owners, CL_OWN, capacity, feature_count)
    arrived = lax.all_to_all(outgoing, "owner", split_axis=0, concat_axis=0, tiled=True)
    kept = lax.dynamic_index_in_dim(arrived, mine, 1, keepdims=False)
    given = partner(lax.dynamic_index_in_dim(arrived, 1 - mine, 1, keepdims=False))
    own = jnp.stack([kept, given]).reshape(CL_OWN * owners * capacity, feature_count)
    others = [swap_cores(own)]
    for step in range(CL_OWN, helpers, CL_OWN):
        turn = [(i, (i + step) % helpers) for i in range(helpers)]
        others += [lax.ppermute(x, "helper", turn) for x in (own, others[0])]
    counts = soft_counts([own, *others], [0], own.shape[0])
    counts = counts.reshape(CL_OWN, owners, capacity)
    kept, given = counts[0], partner(counts[1])
    counts = jnp.where(mine == 0, jnp.stack([kept, given], 1), jnp.stack([given, kept], 1))
    back = lax.all_to_all(counts, "owner", split_axis=0, concat_axis=0, tiled=True)
    return select(back.reshape(clusters, 1, capacity), slot, clusters, capacity)


def solution(mesh):
    in_specs = (
        P(("groups", "owner", "helper", "sub"), None),
        P(("groups", "owner", "helper", "sub")),
    )
    out_specs = P(("groups", "owner", "helper", "sub"))
    body = body_by_chip if mesh.shape["helper"] == CL_OWN else body_by_owner
    return jax.shard_map(body, mesh=mesh, in_specs=in_specs, out_specs=out_specs, check_vma=False)
```
